32 devices in a mesh: seq: 8 (over y, x, core), head: 4 (over z).
Axes of the slice: x: 2, y: 2, z: 4, core: 2. Of those that a mesh axis runs over, the one named last changes fastest.
Arguments:
- hidden_in: bfloat16 [4096, 1536], P('seq'), may hold values from -6 to 6
- cond: float32 [1024], replicated, may hold values from -6 to 6
- captions: bfloat16 [4, 128, 4096], replicated, may hold values from -6 to 6
- clip_lengths: int32 [4], replicated, may hold values from 1 to 3585, 4096 in all
- ada_weight: bfloat16 [1024, 6144], P(None, ('seq', 'head')), may hold values from -0.1875 to 0.1875
- norm_gains: float32 [4, 1536], replicated, may hold values from 0.5 to 1.5
- qk_gains: float32 [2, 64], replicated, may hold values from 0.1 to 1.9
- w_query: bfloat16 [1536, 1536], P('seq', 'head'), may hold values from -0.15625 to 0.15625
- w_key: bfloat16 [1536, 1536], P('seq', 'head'), may hold values from -0.15625 to 0.15625
- w_value: bfloat16 [1536, 1536], P('seq', 'head'), may hold values from -0.15625 to 0.15625
- w_out: bfloat16 [1536, 1536], P('head', 'seq'), may hold values from -0.15625 to 0.15625
- cross_gate: float32 [24], P('head'), may hold values from 0.3 to 1.5
- w_text_key: bfloat16 [4096, 1536], P('seq', 'head'), may hold values from -0.09375 to 0.09375
- w_text_value: bfloat16 [4096, 1536], P('seq', 'head'), may hold values from -0.09375 to 0.09375
- w_gate: bfloat16 [1536, 4096], P('seq', 'head'), may hold values from -0.15625 to 0.15625
- w_up: bfloat16 [1536, 4096], P('seq', 'head'), may hold values from -0.15625 to 0.15625
- w_down: bfloat16 [4096, 1536], P('head', 'seq'), may hold values from -0.09375 to 0.09375
- out_cotangent: bfloat16 [4096, 1536], P('seq'), may hold values from -6 to 6
Outputs:
- hidden_out: bfloat16 [4096, 1536], P('seq')
- input_grad: float32 [4096, 1536], P('seq')
- ada_grad: float32 [1024, 6144], P(None, ('seq', 'head'))
- norm_gains_grad: float32 [4, 1536], replicated
- qk_gains_grad: float32 [2, 64], replicated
- query_grad: float32 [1536, 1536], P('seq', 'head')
- key_grad: float32 [1536, 1536], P('seq', 'head')
- value_grad: float32 [1536, 1536], P('seq', 'head')
- out_grad: float32 [1536, 1536], P('head', 'seq')
- cross_gate_grad: float32 [24], P('head')
- text_key_grad: float32 [4096, 1536], P('seq', 'head')
- text_value_grad: float32 [4096, 1536], P('seq', 'head')
- gate_grad: float32 [1536, 4096], P('seq', 'head')
- up_grad: float32 [1536, 4096], P('seq', 'head')
- down_grad: float32 [4096, 1536], P('head', 'seq')
The draws below stay inside these ranges and needn't reach their ends.
Inputs may be any that keep to these rules, and one draw needn't show every extreme that they name: `clip_lengths`: the lengths sum to 4096; the longest clip has exactly 3585 tokens.
All inputs are finite; a program needn't handle non-finite values.
Results may differ from the reference program's by a relative error of at most 0.024.
Values may be sent and summed in bfloat16 or wider, within the bound.
No kernel may reach another device: no remote copies, remote signals or barrier semaphores. Data moves between devices by JAX's collectives and lax.ppermute only.
A program may use at most 192 MiB of HBM per device.

```python
import math
import jax
import jax.numpy as jnp
import numpy as np
from jax import lax

D = 1536
HEADS = 24
HD = 64
FF = 4096
TDIM = 4096
CDIM = 1024
TOK_DEV = 512
TEXT = 128
CLIPS = 4
TOKENS = 4096


def levels(key, extent, cuts, smallest, top_value):
    level = 1.0
    for dim, parts in cuts:
        steps = jax.random.uniform(jax.random.fold_in(jax.random.fold_in(key, 6), dim), (parts,), jnp.float32, smallest / len(cuts), top_value / len(cuts))
        level = level * jnp.repeat(jnp.exp(steps), extent[dim] // parts).reshape((-1,) + (1,) * (len(extent) - 1 - dim))
    return level


def split_up(count, total, reach, skew):
    weights = [(1 << 20) // math.isqrt(grade ** skew) + 1 for grade in range(2, count + 1)]
    surplus, given = total - reach - (count - 1), [1] * (count - 1)
    while surplus > 0:
        movable = [i for i in range(count - 1) if given[i] < reach]
        pool, left = sum([weights[i] for i in movable]), surplus
        for i in movable:
            extra = min(reach - given[i], max(1, left * weights[i] // pool), surplus)
            given[i] = given[i] + extra
            surplus = surplus - extra
    return np.array([reach] + given)


def ragged(key, number_of, total, limit, lean):
    if number_of == 2:
        one = jax.random.randint(key, (), max(1, total - limit), min(limit, total - 1) + 1)
        return jnp.stack([one, total - one])
    tallies = jnp.asarray(split_up(number_of, total, limit, lean), jnp.int32)
    couples = (number_of - 1) // 2
    giver, receiver = tallies[1:1 + 2 * couples:2], tallies[2:2 + 2 * couples:2]
    margin = jnp.minimum(giver - 1, limit - receiver)
    shifted = jax.random.randint(jax.random.fold_in(key, 1), (couples,), 0, 1 << 20) % (margin + 1)
    tallies = tallies.at[1:1 + 2 * couples:2].set(giver - shifted).at[2:2 + 2 * couples:2].set(receiver + shifted)
    return tallies[jax.random.permutation(jax.random.fold_in(key, 2), number_of)]


def normal_values(rng, extent, spread, limit, cuts=(), kind=jnp.bfloat16):
    values = spread * jax.random.normal(rng, extent, jnp.float32)
    if cuts:
        values = values * levels(rng, extent, cuts, -0.22, 0.18)
    return jnp.clip(values, -limit, limit).astype(kind)


def setup_inputs(seed: int = 0) -> dict:
    seeds = jax.random.split(jax.random.key(seed), 19)
    return {
        "hidden_in": normal_values(seeds[0], (TOKENS, D), 1.0, 6.0, ((0, 8),)),
        "cond": normal_values(seeds[1], (CDIM,), 1.0, 6.0, (), jnp.float32),
        "captions": normal_values(seeds[2], (CLIPS, TEXT, TDIM), 1.0, 6.0),
        "clip_lengths": ragged(seeds[3], CLIPS, TOKENS, TOKENS - TOK_DEV + 1, 0).astype(jnp.int32),
        "ada_weight": normal_values(seeds[4], (CDIM, 4 * D), CDIM ** -0.5, 0.1875, ((1, 32),)),
        "norm_gains": jnp.clip(1.0 + 0.1 * jax.random.normal(seeds[5], (4, D), jnp.float32), 0.5, 1.5),
        "qk_gains": jnp.clip(1.0 + 0.18 * jax.random.normal(seeds[6], (2, HD), jnp.float32), 0.1, 1.9),
        "w_query": normal_values(seeds[7], (D, D), D ** -0.5, 0.15625, ((0, 8), (1, 4))),
        "w_key": normal_values(seeds[8], (D, D), D ** -0.5, 0.15625, ((0, 8), (1, 4))),
        "w_value": normal_values(seeds[9], (D, D), D ** -0.5, 0.15625, ((0, 8), (1, 4))),
        "w_out": normal_values(seeds[10], (D, D), D ** -0.5, 0.15625, ((0, 4), (1, 8))),
        "cross_gate": jnp.clip(0.3 + 1.2 * jax.random.uniform(seeds[11], (HEADS,), jnp.float32) ** levels(seeds[11], (HEADS,), ((0, 4),), -0.2, 0.2), 0.3, 1.5),
        "w_text_key": normal_values(seeds[12], (TDIM, D), TDIM ** -0.5, 0.09375, ((0, 8), (1, 4))),
        "w_text_value": normal_values(seeds[13], (TDIM, D), TDIM ** -0.5, 0.09375, ((0, 8), (1, 4))),
        "w_gate": normal_values(seeds[14], (D, FF), D ** -0.5, 0.15625, ((0, 8), (1, 4))),
        "w_up": normal_values(seeds[15], (D, FF), D ** -0.5, 0.15625, ((0, 8), (1, 4))),
        "w_down": normal_values(seeds[16], (FF, D), FF ** -0.5, 0.09375, ((0, 4), (1, 8))),
        "out_cotangent": normal_values(seeds[17], (TOKENS, D), 1.0, 6.0, ((0, 8),)),
    }


highest = lax.Precision.HIGHEST

@jax.custom_vjp
def low(v):
    return lax.optimization_barrier(v.astype(jnp.bfloat16)).astype(jnp.float32)

@jax.custom_vjp
def low_back(v):
    return v

def low_keep(v):
    return (low(v), None)

def low_pass(kept, grad):
    return (grad,)

def back_keep(v):
    return (v, None)

def back_low(kept, grad):
    return (low(grad),)
low.defvjp(low_keep, low_pass)
low_back.defvjp(back_keep, back_low)

def mean_norm(value):
    return value * lax.rsqrt(lax.optimization_barrier(jnp.mean(value * value, axis=-1, keepdims=True)) + 1e-06)

def clip_places(clip_lengths, first, count):
    clip_ends = jnp.cumsum(clip_lengths, dtype=jnp.int32)
    starts = clip_ends - clip_lengths
    places = first + jnp.arange(count, dtype=jnp.int32)
    segment = lax.optimization_barrier(jnp.sum((places[:, None] >= clip_ends[None, :]).astype(jnp.int32), axis=1, dtype=jnp.int32))
    onehot = segment[:, None] == jnp.arange(clip_lengths.shape[0], dtype=jnp.int32)[None, :]
    position = places - lax.optimization_barrier(jnp.sum(jnp.where(onehot, starts[None, :], 0), axis=1, dtype=jnp.int32))
    return (segment, position)

def rotate_pairs(value, position):
    half_dim = value.shape[-1] // 2
    frequency = 10000.0 ** (-jnp.arange(half_dim, dtype=jnp.float32) / half_dim)
    angles = position.astype(jnp.float32)[:, None] * frequency[None, :]
    cosine = jnp.cos(angles)[:, None, :]
    sine_value = jnp.sin(angles)[:, None, :]
    first_half = value[..., :half_dim]
    second_half = value[..., half_dim:]
    return jnp.concatenate([first_half * cosine - second_half * sine_value, second_half * cosine + first_half * sine_value], axis=-1)

def head_norm(flat, gain):
    shaped = flat.reshape(flat.shape[0], -1, HD)
    return mean_norm(shaped) * gain

def softmax_rows(scores):
    top_score = lax.optimization_barrier(jnp.max(scores, axis=-1, keepdims=True))
    weights = jnp.exp(scores - top_score)
    return weights / lax.optimization_barrier(jnp.sum(weights, axis=-1, keepdims=True))

def reference(hidden_in, cond, captions, clip_lengths, ada_weight, norm_gains, qk_gains, w_query, w_key, w_value, w_out, cross_gate, w_text_key, w_text_value, w_gate, w_up, w_down, out_cotangent):
    all_rows = hidden_in.shape[0]
    segment, position = clip_places(clip_lengths, 0, all_rows)
    text_rows = captions.reshape(-1, captions.shape[2]).astype(jnp.float32)
    key_clip = jnp.arange(text_rows.shape[0], dtype=jnp.int32) // captions.shape[1]
    block_rows = min(512, all_rows)
    score_scale = HD ** (-0.5)

    def attend(query_block, segment_block, keys3, values3, text_keys3, text_values3):
        raw = low_back(jnp.einsum('qhd,khd->hqk', query_block, keys3, precision=highest))
        allowed = (segment_block[:, None] == segment[None, :])[None]
        probs = softmax_rows(jnp.where(allowed, score_scale * raw, -1e+30))
        self_part = jnp.einsum('hqk,khd->qhd', low(probs), values3, precision=highest)
        cross_raw = low_back(jnp.einsum('qhd,khd->hqk', query_block, text_keys3, precision=highest))
        cross_allowed = (segment_block[:, None] == key_clip[None, :])[None]
        cross_probs = softmax_rows(jnp.where(cross_allowed, score_scale * cross_raw, -1e+30))
        cross_part = jnp.einsum('hqk,khd->qhd', low(cross_probs), text_values3, precision=highest)
        return (self_part, cross_part)
    checked = jax.checkpoint(attend)

    def forward(x_value, ada_value, gains_value, qk_value, query_w, key_w, value_w, out_w, gate_value, text_key_w, text_value_w, gate_w, up_w, down_w):
        cond_act = low(jax.nn.silu(cond.astype(jnp.float32)))
        modulation = jnp.dot(cond_act[None, :], ada_value, precision=highest)[0]
        scale_a, gate_a, scale_f, gate_f = jnp.split(modulation, 4)
        act_a = low(mean_norm(x_value) * gains_value[0] * (1.0 + scale_a))
        query_pre = low_back(jnp.dot(act_a, query_w, precision=highest))
        key_pre = low_back(jnp.dot(act_a, key_w, precision=highest))
        value_pre = low_back(jnp.dot(act_a, value_w, precision=highest))
        queries = low(rotate_pairs(head_norm(query_pre, qk_value[0]), position))
        keys3 = low(rotate_pairs(head_norm(key_pre, qk_value[1]), position))
        values3 = low(value_pre).reshape(all_rows, -1, HD)
        text_key_pre = low_back(jnp.dot(text_rows, text_key_w, precision=highest))
        text_value_pre = low_back(jnp.dot(text_rows, text_value_w, precision=highest))
        text_keys3 = low(head_norm(text_key_pre, qk_value[1]))
        text_values3 = low(text_value_pre).reshape(text_rows.shape[0], -1, HD)
        heads = queries.shape[1]
        query_blocks = queries.reshape(all_rows // block_rows, block_rows, heads, HD)
        segment_blocks = segment.reshape(all_rows // block_rows, block_rows)
        self_out, cross_out = lax.map(lambda item: checked(item[0], item[1], keys3, values3, text_keys3, text_values3), (query_blocks, segment_blocks))
        self_out = low_back(self_out.reshape(all_rows, heads, HD))
        cross_out = low_back(cross_out.reshape(all_rows, heads, HD))
        mixed = low((self_out + jnp.tanh(gate_value)[None, :, None] * cross_out).reshape(all_rows, -1))
        attn = low_back(jnp.dot(mixed, out_w, precision=highest))
        middle = x_value + jnp.tanh(gate_a) * mean_norm(attn) * gains_value[1]
        act_f = low(mean_norm(middle) * gains_value[2] * (1.0 + scale_f))
        gate_pre = low_back(jnp.dot(act_f, gate_w, precision=highest))
        up_pre = low_back(jnp.dot(act_f, up_w, precision=highest))
        units = low(jax.nn.silu(gate_pre) * up_pre)
        ffn = low_back(jnp.dot(units, down_w, precision=highest))
        return middle + jnp.tanh(gate_f) * mean_norm(ffn) * gains_value[3]
    primals = (hidden_in.astype(jnp.float32), ada_weight.astype(jnp.float32), norm_gains, qk_gains, w_query.astype(jnp.float32), w_key.astype(jnp.float32), w_value.astype(jnp.float32), w_out.astype(jnp.float32), cross_gate, w_text_key.astype(jnp.float32), w_text_value.astype(jnp.float32), w_gate.astype(jnp.float32), w_up.astype(jnp.float32), w_down.astype(jnp.float32))
    result, pullback = jax.vjp(forward, *primals)
    grads = pullback(out_cotangent.astype(jnp.float32))
    return (result.astype(jnp.bfloat16), grads[0], grads[1], grads[2], grads[3], grads[4], grads[5], grads[6], grads[7], grads[8], grads[9], grads[10], grads[11], grads[12], grads[13])
```

```python
import functools
import jax
import jax.numpy as jnp
from jax import lax
from jax.experimental import pallas as pl
from jax.experimental.pallas import tpu as pltpu
from jax.sharding import PartitionSpec as P

HD = 64
MASK = 8192.0


def dot(a, b):
    return lax.dot_general(a, b, (((1,), (0,)), ((), ())), preferred_element_type=jnp.float32)


def split3(v):
    hi = v.astype(jnp.bfloat16).astype(jnp.float32)
    mid = (v - hi).astype(jnp.bfloat16).astype(jnp.float32)
    return hi, mid, v - hi - mid


def bounds(info, base, clips, ids):
    start = jnp.full(ids.shape, 1 << 30, jnp.int32)
    end = jnp.zeros(ids.shape, jnp.int32)
    for c in range(clips):
        start = jnp.where(ids == c, info[base + c], start)
        end = jnp.where(ids == c, info[base + clips + c], end)
    return start, end


def query_ext(info, clips, width, scale):
    ids = lax.broadcasted_iota(jnp.int32, (16, width), 0)
    place = info[0] + lax.broadcasted_iota(jnp.int32, (16, width), 1)
    start, end = bounds(info, 1, clips, ids)
    return jnp.where((place >= start) & (place < end), scale, 0.0)


def key_ext(info, clips, first, rows):
    ids = lax.broadcasted_iota(jnp.int32, (rows, 128), 1)
    place = first + lax.broadcasted_iota(jnp.int32, (rows, 128), 0)
    start, end = bounds(info, 1 + 2 * clips, clips, ids)
    inside = (place >= start) & (place < end)
    value = jnp.where(ids < clips, jnp.where(inside, 0.0, -1.0), jnp.where(ids < clips + 3, 1.0, 0.0))
    return value.astype(jnp.bfloat16)


def fill_ext(dst, h, src, tail):
    width = src.shape[1]
    half = h % 2
    zero = jnp.zeros((HD, width), jnp.bfloat16)
    dst[h, half * HD : half * HD + HD, :] = src[h * HD : h * HD + HD, :]
    dst[h, (1 - half) * HD : (1 - half) * HD + HD, :] = zero
    dst[h, 128:144, :] = tail.astype(jnp.bfloat16)
    dst[h, 144:256, :] = jnp.zeros((112, width), jnp.bfloat16)


def stack_rows(heads, rows, clips, width):
    ids = lax.broadcasted_iota(jnp.int32, (16, width), 0)
    total = jnp.zeros((16, width), jnp.float32)
    for k, row in enumerate(rows):
        total = jnp.where(ids == clips + k, jnp.broadcast_to(row, (16, width)), total)
    return total


def load_pieces(pieces, kv, sem):
    rows = pieces[0].shape[0]
    return [
        pltpu.make_async_copy(piece, kv.at[pl.ds(k * rows, rows), :], sem.at[k])
        for k, piece in enumerate(pieces)
    ]


def fwd_kernel(heads, clips, count, tile, info, qt, *rest):
    pieces, (out, qx, kv, sem) = rest[:count], rest[count:]
    copies = load_pieces(pieces, kv, sem)
    for c in copies:
        c.start()
    width = qt.shape[1]
    wide = qt.shape[0]
    ext = query_ext(info, clips, width, MASK)
    for h in range(heads):
        fill_ext(qx, h, qt, ext)
        out[h] = jnp.zeros((80, width), jnp.float32)
    for c in copies:
        c.wait()
    per = pieces[0].shape[0] // tile
    ones = jnp.ones((16, tile), jnp.bfloat16)

    def step(t, carry):
        rows = pl.ds(pl.multiple_of(t * tile, tile), tile)
        first = info[1 + 4 * clips + t // per] + lax.rem(t, per) * tile
        extra = key_ext(info, clips, first, tile)
        for p in range((heads + 1) // 2):
            kx = jnp.concatenate([kv[rows, p * 128 : p * 128 + 128], extra], axis=1)
            vt = kv[rows, wide + p * 128 : wide + p * 128 + 128].T
            for h in range(2 * p, min(2 * p + 2, heads)):
                half = h % 2
                probs = jnp.exp(dot(kx, qx[h])).astype(jnp.bfloat16)
                vx = jnp.concatenate([vt[half * HD : half * HD + HD, :], ones], axis=0)
                out[h] += dot(vx, probs)
        return carry

    lax.fori_loop(0, per * count, step, 0)


def attend(info, qt, pieces, heads, clips, tile=512):
    count = len(pieces)
    wide, width = qt.shape
    rows = pieces[0].shape[0]
    tile = min(tile, rows)
    return pl.pallas_call(
        functools.partial(fwd_kernel, heads, clips, count, tile),
        out_shape=jax.ShapeDtypeStruct((heads, 80, width), jnp.float32),
        in_specs=[pl.BlockSpec(memory_space=pltpu.SMEM), pl.BlockSpec(memory_space=pltpu.VMEM)]
        + [pl.BlockSpec(memory_space=pl.ANY)] * count,
        out_specs=pl.BlockSpec(memory_space=pltpu.VMEM),
        scratch_shapes=[
            pltpu.VMEM((heads, 256, width), jnp.bfloat16),
            pltpu.VMEM((count * rows, 2 * wide), jnp.bfloat16),
            pltpu.SemaphoreType.DMA((count,)),
        ],
        compiler_params=pltpu.CompilerParams(vmem_limit_bytes=48 << 20),
        cost_estimate=pl.CostEstimate(
            flops=4 * heads * width * rows * count * 256,
            bytes_accessed=count * rows * wide * 4 + 4 * heads * 80 * width,
            transcendentals=heads * width * rows * count,
        ),
        name="attend",
    )(info, qt, *pieces)


def bwd_kernel(heads, clips, count, tile, info, qt, dot_t, q_tok, do_tok, lse, delta, *rest):
    pieces, rest = rest[:count], rest[count:]
    dqt, grads, (qx, dox, qpad, dopad, kv, sem) = rest[0], rest[1:-6], rest[-6:]
    copies = load_pieces(pieces, kv, sem)
    for c in copies:
        c.start()
    wide, width = qt.shape
    ext = query_ext(info, clips, width, MASK)
    for h in range(heads):
        p, half = h // 2, h % 2
        fill_ext(qx, h, qt, ext - stack_rows(heads, split3(lse[h : h + 1, :]), clips, width))
        fill_ext(dox, h, dot_t, -stack_rows(heads, split3(delta[h : h + 1, :]), clips, width))
        lane = lax.broadcasted_iota(jnp.int32, (width, 128), 1) // HD
        zero = jnp.zeros((width, 128), jnp.bfloat16)
        qpad[h] = jnp.where(lane == half, q_tok[:, p * 128 : p * 128 + 128], zero)
        dopad[h] = jnp.where(lane == half, do_tok[:, p * 128 : p * 128 + 128], zero)
    dqt[...] = jnp.zeros((wide, width), jnp.float32)
    for c in copies:
        c.wait()
    per = pieces[0].shape[0] // tile

    def step(t, carry):
        rows = pl.ds(pl.multiple_of(t * tile, tile), tile)
        first = info[1 + 4 * clips + t // per] + lax.rem(t, per) * tile
        extra = key_ext(info, clips, first, tile)
        for p in range((heads + 1) // 2):
            cols = slice(p * 128, p * 128 + 128)
            vcols = slice(wide + p * 128, wide + p * 128 + 128)
            k_tile = kv[rows, cols]
            kx = jnp.concatenate([k_tile, extra], axis=1)
            vx = jnp.concatenate([kv[rows, vcols], extra], axis=1)
            kt = k_tile.T
            dk = jnp.zeros((tile, 128), jnp.float32)
            dv = jnp.zeros((tile, 128), jnp.float32)
            for h in range(2 * p, min(2 * p + 2, heads)):
                half = h % 2
                probs = jnp.exp(dot(kx, qx[h]))
                ds = (probs * dot(vx, dox[h])).astype(jnp.bfloat16)
                dqt[h * HD : h * HD + HD, :] += dot(kt[half * HD : half * HD + HD, :], ds)
                dk = dk + dot(ds, qpad[h])
                dv = dv + dot(probs.astype(jnp.bfloat16), dopad[h])
            for g, grad in enumerate(grads):

                @pl.when(t // (per * count // len(grads)) == g)
                def store(g=g, grad=grad, dk=dk, dv=dv, cols=cols, vcols=vcols):
                    start = (t - g * (per * count // len(grads))) * tile
                    here = pl.ds(pl.multiple_of(start, tile), tile)
                    grad[here, cols] = dk.astype(grad.dtype)
                    grad[here, vcols] = dv.astype(grad.dtype)

        return carry

    lax.fori_loop(0, per * count, step, 0)


def attend_back(info, qt, dot_t, q_tok, do_tok, lse, delta, pieces, heads, clips, kind, parts=1, tile=512):
    count = len(pieces)
    wide, width = qt.shape
    rows = pieces[0].shape[0]
    tile = min(tile, rows)
    return pl.pallas_call(
        functools.partial(bwd_kernel, heads, clips, count, tile),
        out_shape=(
            jax.ShapeDtypeStruct((wide, width), jnp.float32),
        )
        + (jax.ShapeDtypeStruct((count * rows // parts, 2 * wide), kind),) * parts,
        in_specs=[pl.BlockSpec(memory_space=pltpu.SMEM)]
        + [pl.BlockSpec(memory_space=pltpu.VMEM)] * 6
        + [pl.BlockSpec(memory_space=pl.ANY)] * count,
        out_specs=(pl.BlockSpec(memory_space=pltpu.VMEM),) * (1 + parts),
        scratch_shapes=[
            pltpu.VMEM((heads, 256, width), jnp.bfloat16),
            pltpu.VMEM((heads, 256, width), jnp.bfloat16),
            pltpu.VMEM((heads, width, 128), jnp.bfloat16),
            pltpu.VMEM((heads, width, 128), jnp.bfloat16),
            pltpu.VMEM((count * rows, 2 * wide), jnp.bfloat16),
            pltpu.SemaphoreType.DMA((count,)),
        ],
        compiler_params=pltpu.CompilerParams(vmem_limit_bytes=56 << 20),
        cost_estimate=pl.CostEstimate(
            flops=10 * heads * width * rows * count * 256,
            bytes_accessed=count * rows * wide * 8 + 4 * wide * width,
            transcendentals=heads * width * rows * count,
        ),
        name="attend_back",
    )(info, qt, dot_t, q_tok, do_tok, lse, delta, *pieces)


ROWS = (((1,), (1,)), ((), ()))
COLS = (((0,), (0,)), ((), ()))
f32 = jnp.float32
bf16 = jnp.bfloat16


def matmul(left, right, dims=None):
    if dims is None:
        return jnp.dot(left, right, preferred_element_type=f32)
    return lax.dot_general(left, right, dims, preferred_element_type=f32)


def first_way(i):
    return i ^ 2 if i % 2 == 0 else i ^ 4


def other_way(i):
    return i ^ 4 if i % 2 == 0 else i ^ 2


def swap(value, axis, count, to):
    return lax.ppermute(value, axis, [(i, to(i)) for i in range(count)])


def seq_roles(seq_index, seq_count):
    if seq_count != 8:
        return jnp.arange(seq_count, dtype=jnp.int32)
    peer = seq_index ^ 1

    def roles(i):
        even = i % 2 == 0
        return [i, jnp.where(even, i ^ 2, i ^ 4), jnp.where(even, i ^ 4, i ^ 2), i ^ 6]

    return jnp.stack(roles(seq_index) + roles(peer)).astype(jnp.int32)


def gather_pieces(block, seq_count):
    if seq_count != 8:
        whole = lax.all_gather(block, "seq", axis=0, tiled=False)
        return [whole[i] for i in range(seq_count)]
    near = swap(block, "seq", 8, first_way)
    next_ = swap(block, "seq", 8, other_way)
    far = swap(near, "seq", 8, other_way)
    mine = [block, near, next_, far]
    return mine + [swap(v, "seq", 8, lambda i: i ^ 1) for v in mine]


def place_kernel(count, rows, roles, *rest):
    pieces, out, sem = rest[:count], rest[count], rest[count + 1]
    copies = []
    for k in range(count):
        start = pl.multiple_of(roles[k] * rows, rows)
        copies.append(pltpu.make_async_copy(pieces[k], out.at[pl.ds(start, rows), :], sem.at[k]))
    for c in copies:
        c.start()
    for c in copies:
        c.wait()


def place(pieces, roles):
    count = len(pieces)
    rows, width = pieces[0].shape
    return pl.pallas_call(
        functools.partial(place_kernel, count, rows),
        out_shape=jax.ShapeDtypeStruct((count * rows, width), pieces[0].dtype),
        in_specs=[pl.BlockSpec(memory_space=pltpu.SMEM)]
        + [pl.BlockSpec(memory_space=pl.ANY)] * count,
        out_specs=pl.BlockSpec(memory_space=pltpu.VMEM),
        scratch_shapes=[pltpu.SemaphoreType.DMA((count,))],
        compiler_params=pltpu.CompilerParams(vmem_limit_bytes=32 << 20),
        cost_estimate=pl.CostEstimate(flops=0, bytes_accessed=4 * count * rows * width, transcendentals=0),
        name="place",
    )(roles, *pieces)


def scatter_sum(part, seq_index, seq_count):
    if seq_count != 8:
        return lax.psum_scatter(part, "seq", scatter_dimension=0, tiled=True).astype(f32)
    rows = part.shape[0] // 8
    blocks = part.reshape(4, 2, rows, part.shape[1])
    core, chip = seq_index % 2, seq_index // 2
    theirs = lax.dynamic_index_in_dim(blocks, 1 - core, 1, False)
    got = swap(theirs, "seq", 8, lambda i: i ^ 1)
    mine = (lax.dynamic_index_in_dim(blocks, core, 1, False).astype(f32) + got.astype(f32)).astype(bf16)
    pick = lambda c: lax.dynamic_index_in_dim(mine, c, 0, False)
    near = jnp.where(core == 0, chip ^ 1, chip ^ 2)
    next_ = jnp.where(core == 0, chip ^ 2, chip ^ 1)
    first = swap(jnp.stack([pick(chip ^ 3), pick(next_)]), "seq", 8, other_way)
    second = (pick(near).astype(f32) + first[0].astype(f32)).astype(bf16)
    second = swap(second, "seq", 8, first_way)
    return pick(chip).astype(f32) + first[1].astype(f32) + second.astype(f32)


def sum_all(value, axes):
    for axis, count in axes:
        if count & (count - 1):
            value = lax.psum(value, axis)
            continue
        bit = 1
        while bit < count:
            value = value + swap(value, axis, count, lambda i, bit=bit: i ^ bit)
            bit *= 2
    return value


def head_sum(chunks, head_index, head_count):
    if head_count != 4:
        return [lax.psum(c, "head") for c in chunks]
    end = (head_index == 0) | (head_index == 3)
    inner, middle, totals = [], [], []
    for k, chunk in enumerate(chunks):
        if k >= 2:
            chunk, _ = lax.optimization_barrier((chunk, middle[k - 2]))
        got = lax.ppermute(chunk, "head", [(0, 1), (3, 2)])
        middle.append((chunk.astype(f32) + got.astype(f32)).astype(bf16))
    for k, part in enumerate(middle):
        got = lax.ppermute(part, "head", [(1, 2), (2, 1)])
        total = (part.astype(f32) + got.astype(f32)).astype(bf16)
        back = lax.ppermute(total, "head", [(1, 0), (2, 3)])
        totals.append(jnp.where(end, back, total))
    return totals


def head_sum_rows(value, head_index, head_count, parts=4):
    rows = value.shape[0] // parts
    value = value.astype(bf16)
    chunks = [value[k * rows : (k + 1) * rows] for k in range(parts)]
    return jnp.concatenate(head_sum(chunks, head_index, head_count), axis=0)


def head_mean(value):
    row = lax.broadcasted_iota(jnp.int32, (128, 128), 0) // HD
    col = lax.broadcasted_iota(jnp.int32, (128, 128), 1) // HD
    ones = jnp.where(row == col, 1.0 / HD, 0.0).astype(bf16)
    hi, mid, lo = split3(value)
    return dot(hi.astype(bf16), ones) + dot(mid.astype(bf16), ones) + dot(lo.astype(bf16), ones)


def partner(value):
    lane = lax.broadcasted_iota(jnp.int32, value.shape, 1) % HD
    return jnp.where(lane < HD // 2, pltpu.roll(value, 128 - HD // 2, 1), pltpu.roll(value, HD // 2, 1))


def norm_kernel(pre, gain, cos, sin, out):
    for p in range(pre.shape[1] // 128):
        cols = slice(p * 128, p * 128 + 128)
        value = pre[:, cols]
        value = value * lax.rsqrt(head_mean(value * value) + 1e-6) * gain[...]
        out[:, cols] = (value * cos[...] + partner(value) * sin[...]).astype(out.dtype)


def norm_rope(pre, gain, cos, sin):
    return pl.pallas_call(
        norm_kernel,
        out_shape=jax.ShapeDtypeStruct(pre.shape, bf16),
        name="norm_rope",
        compiler_params=pltpu.CompilerParams(vmem_limit_bytes=32 << 20),
    )(pre, gain, cos, sin)


def norm_back_kernel(pre, gain, cos, sin, grad, out, gain_grad):
    total = jnp.zeros((1, 128), f32)
    for p in range(pre.shape[1] // 128):
        cols = slice(p * 128, p * 128 + 128)
        value = pre[:, cols]
        scale = lax.rsqrt(head_mean(value * value) + 1e-6)
        normed = value * scale
        g = grad[:, cols]
        g = g * cos[...] - partner(g) * sin[...]
        total = total + jnp.sum(g * normed, axis=0, keepdims=True)
        g = g * gain[...]
        out[:, cols] = (scale * (g - normed * head_mean(g * normed))).astype(out.dtype)
    gain_grad[...] = total


def norm_rope_back(pre, gain, cos, sin, grad, kind):
    return pl.pallas_call(
        norm_back_kernel,
        out_shape=(jax.ShapeDtypeStruct(pre.shape, kind), jax.ShapeDtypeStruct((1, 128), f32)),
        name="norm_rope_back",
        compiler_params=pltpu.CompilerParams(vmem_limit_bytes=32 << 20),
    )(pre, gain, cos, sin, grad)


def mean_norm(value):
    return value * lax.rsqrt(jnp.mean(value * value, axis=-1, keepdims=True) + 1e-06)


def attn_input(x_value, gain_value, scale_value):
    return mean_norm(x_value) * gain_value * (1.0 + scale_value)


def branch_tail(x_value, branch, gain_value, gate_value):
    return x_value + jnp.tanh(gate_value) * mean_norm(branch) * gain_value


def swiglu_units(gate_pre, up_pre):
    return jax.nn.silu(gate_pre) * up_pre


def per_device(
    seq_count,
    head_count,
    hidden_in,
    cond,
    captions,
    clip_lengths,
    ada_weight,
    norm_gains,
    qk_gains,
    w_query,
    w_key,
    w_value,
    w_out,
    cross_gate,
    w_text_key,
    w_text_value,
    w_gate,
    w_up,
    w_down,
    out_cotangent,
):
    local_rows, model_width = hidden_in.shape
    seq_index = lax.axis_index("seq")
    head_index = lax.axis_index("head")
    clips = clip_lengths.shape[0]
    cols = w_query.shape[1]
    heads = cols // HD
    wide = (cols + 127) // 128 * 128
    units = w_gate.shape[1]
    roles = seq_roles(seq_index, seq_count)
    pad = lambda v: jnp.pad(v, ((0, 0), (0, wide - cols))) if wide > cols else v
    cut = lambda v: v[:, :cols]

    cond_act = jax.nn.silu(cond).astype(bf16)
    piece_width = ada_weight.shape[1]
    mod_piece = matmul(cond_act[None, :], ada_weight)
    mine = lax.broadcasted_iota(jnp.int32, (seq_count * head_count, 1), 0) == seq_index * head_count + head_index
    modulation = sum_all(
        jnp.where(mine, mod_piece, 0.0), (("seq", seq_count), ("head", head_count))
    ).reshape(-1)
    scale_a, gate_a, scale_f, gate_f = jnp.split(modulation, 4)

    w_qkv = place(
        gather_pieces(jnp.concatenate([pad(w_query), pad(w_key), pad(w_value)], axis=1), seq_count), roles
    )
    text_rows = captions.reshape(-1, captions.shape[2])
    text_count = text_rows.shape[0]
    slab_width = text_rows.shape[1] // seq_count
    own_text = lax.dynamic_slice_in_dim(text_rows, seq_index * slab_width, slab_width, 1)
    w_text = jnp.concatenate([pad(w_text_key), pad(w_text_value)], axis=1)
    text_pre = lax.psum(matmul(own_text, w_text).astype(bf16), "seq")
    gate_w = lax.all_gather(w_gate, "seq", axis=0, tiled=True)
    up_w = lax.all_gather(w_up, "seq", axis=0, tiled=True)
    down_t = lax.all_gather(w_down.T, "seq", axis=0, tiled=True)

    clip_ends = jnp.cumsum(clip_lengths, dtype=jnp.int32)
    starts = clip_ends - clip_lengths
    text_ids = jnp.arange(clips, dtype=jnp.int32) * captions.shape[1]
    first_row = seq_index * local_rows
    place_info = jnp.concatenate([first_row[None], starts, clip_ends]).astype(jnp.int32)
    text_info = jnp.concatenate(
        [place_info, text_ids, text_ids + captions.shape[1], jnp.zeros((1,), jnp.int32)]
    )

    def self_info(which):
        return jnp.concatenate([place_info, starts, clip_ends, roles[which] * local_rows])

    places = first_row + jnp.arange(local_rows, dtype=jnp.int32)
    inside = (places[:, None] >= starts[None, :]) & (places[:, None] < clip_ends[None, :])
    position = places - jnp.sum(jnp.where(inside, starts[None, :], 0), axis=1, dtype=jnp.int32)
    lane = jnp.arange(128)
    frequency = 10000.0 ** (-(lane % (HD // 2)).astype(f32) / (HD // 2))
    angles = position.astype(f32)[:, None] * frequency[None, :]
    cos = jnp.cos(angles)
    sin = jnp.where(lane % HD < HD // 2, -1.0, 1.0)[None, :] * jnp.sin(angles)
    flat = (jnp.ones((text_count, 128), f32), jnp.zeros((text_count, 128), f32))
    query_gain = jnp.tile(qk_gains[0], 2)[None, :]
    key_gain = jnp.tile(qk_gains[1], 2)[None, :]

    x_float = hidden_in.astype(f32)
    normed_a, pull_in_a = jax.vjp(attn_input, x_float, norm_gains[0], scale_a)
    act_a = normed_a.astype(bf16)
    pre = matmul(act_a, w_qkv)
    query_pre, key_pre, value_pre = pre[:, :wide], pre[:, wide : 2 * wide], pre[:, 2 * wide :]
    queries = norm_rope(query_pre, query_gain, cos, sin) * jnp.asarray(HD**-0.5, bf16)
    keys = norm_rope(key_pre, key_gain, cos, sin)
    query_t = queries.T
    pieces = gather_pieces(jnp.concatenate([keys, value_pre.astype(bf16)], axis=1), seq_count)
    out_in, _ = lax.optimization_barrier((w_out.T, pieces[-1]))
    out_t = place(gather_pieces(out_in, seq_count), roles)
    text_key_pre = text_pre[:, :wide].astype(f32)
    text_keys = norm_rope(text_key_pre, key_gain, *flat)
    text_piece = jnp.concatenate([text_keys, text_pre[:, wide:]], axis=1)
    if seq_count == 8:
        groups = ((0, 4), (1, 2, 5, 6), (3, 7))
    else:
        groups = (tuple(range(seq_count)),)
    sums = 0.0
    for group in groups:
        sums = sums + attend(
            self_info(jnp.array(group)), query_t, [pieces[g] for g in group], heads, clips
        )
    cross_sums = attend(text_info, query_t, [text_piece], heads, clips)
    self_den, cross_den = sums[:, HD], cross_sums[:, HD]
    self_lse, cross_lse = jnp.log(self_den), jnp.log(cross_den)
    self_out = sums[:, :HD] / self_den[:, None]
    cross_out = cross_sums[:, :HD] / cross_den[:, None]
    gate_local = jnp.tanh(cross_gate)[:, None, None]
    mixed = (self_out + gate_local * cross_out).astype(bf16).reshape(cols, local_rows)
    attn_part = matmul(mixed, cut(out_t), (((0,), (1,)), ((), ())))
    attn_sum = head_sum_rows(attn_part, head_index, head_count).astype(f32)

    x_mid, pull_tail_a = jax.vjp(branch_tail, x_float, attn_sum, norm_gains[1], gate_a)
    normed_f, pull_in_f = jax.vjp(attn_input, x_mid, norm_gains[2], scale_f)
    act_f = normed_f.astype(bf16)
    gate_pre = matmul(act_f, gate_w)
    up_pre = matmul(act_f, up_w)
    unit_value, unit_pull = jax.vjp(swiglu_units, gate_pre, up_pre)
    hidden_units = unit_value.astype(bf16)
    ffn_sum = head_sum_rows(matmul(hidden_units, down_t, ROWS), head_index, head_count).astype(f32)
    out_value, pull_tail_f = jax.vjp(branch_tail, x_mid, ffn_sum, norm_gains[3], gate_f)
    hidden_out = out_value.astype(bf16)
    grad_mid, grad_ffn, grad_gain_fo, grad_gate_f = pull_tail_f(out_cotangent.astype(f32))
    grad_ffn_low = grad_ffn.astype(bf16)
    grad_units = matmul(grad_ffn_low, down_t)
    grad_gate_pre, grad_up_pre = unit_pull(grad_units)
    grad_gate_low = grad_gate_pre.astype(bf16)
    grad_up_low = grad_up_pre.astype(bf16)
    grad_act_f = head_sum_rows(
        matmul(grad_gate_low, gate_w, ROWS) + matmul(grad_up_low, up_w, ROWS), head_index, head_count
    ).astype(f32)
    down_part = matmul(grad_ffn_low, hidden_units, COLS).astype(bf16)
    gate_part = matmul(act_f, grad_gate_low, COLS).astype(bf16)
    up_part = matmul(act_f, grad_up_low, COLS).astype(bf16)
    down_grad = lax.psum_scatter(down_part, "seq", scatter_dimension=0, tiled=True).astype(f32).T
    gate_grad = lax.psum_scatter(gate_part, "seq", scatter_dimension=0, tiled=True).astype(f32)
    up_grad = lax.psum_scatter(up_part, "seq", scatter_dimension=0, tiled=True).astype(f32)

    grad_mid_f, grad_gain_fi, grad_scale_f = pull_in_f(grad_act_f)
    grad_x_tail, grad_attn, grad_gain_ao, grad_gate_a = pull_tail_a(grad_mid + grad_mid_f)
    grad_attn_low = grad_attn.astype(bf16)
    grad_mixed = matmul(out_t, grad_attn_low, (((0,), (1,)), ((), ())))[:cols]
    grad_mixed = grad_mixed.reshape(heads, HD, local_rows)
    out_part = matmul(grad_attn_low, mixed, (((0,), (1,)), ((), ()))).astype(bf16)
    grad_self = grad_mixed.astype(bf16)
    grad_cross = (gate_local * grad_mixed).astype(bf16)
    cross_gate_part = jnp.sum(grad_mixed * cross_out, axis=(1, 2)) * (1.0 - gate_local[:, 0, 0] ** 2)
    cross_delta = jnp.sum(grad_cross.astype(f32) * cross_out, axis=1)
    self_delta = jnp.sum(grad_self.astype(f32) * self_out, axis=1)
    pad_rows = lambda v: jnp.pad(v.reshape(cols, local_rows), ((0, wide - cols), (0, 0)))
    grad_self_t, grad_cross_t = pad_rows(grad_self), pad_rows(grad_cross)
    grad_self_tok, grad_cross_tok = grad_self_t.T, grad_cross_t.T
    cross_dq, cross_kv = attend_back(
        text_info, query_t, grad_cross_t, queries, grad_cross_tok, cross_lse, cross_delta,
        [text_piece], heads, clips, f32,
    )

    def back(group, parts):
        return attend_back(
            self_info(jnp.array(group)), query_t, grad_self_t, queries, grad_self_tok, self_lse, self_delta,
            [pieces[g] for g in group], heads, clips, bf16, parts,
        )

    if seq_count == 8:
        core = lambda v: swap(v, "seq", 8, lambda i: i ^ 1).astype(f32)
        dq1, kv_mine, kv_theirs = back((3, 2, 7, 6), 2)
        total = (kv_mine.astype(f32) + core(kv_theirs)).astype(bf16)
        first = swap(total, "seq", 8, other_way).astype(f32)
        dq2, kv_mine, kv_theirs = back((1, 5), 2)
        total = (kv_mine.astype(f32) + core(kv_theirs) + first[:local_rows]).astype(bf16)
        second = swap(total, "seq", 8, first_way).astype(f32)
        dq3, kv_mine, kv_theirs = back((0, 4), 2)
        own_kv = kv_mine.astype(f32) + core(kv_theirs) + first[local_rows:] + second
        query_grad_t = dq1 + dq2 + dq3
    else:
        query_grad_t, kv_all = back(tuple(range(seq_count)), 1)
        own_kv = lax.psum_scatter(kv_all, "seq", scatter_dimension=0, tiled=True).astype(f32)
    query_total = ((query_grad_t + cross_dq) * HD**-0.5).T
    query_low, grad_query_gain = norm_rope_back(query_pre, query_gain, cos, sin, query_total, bf16)
    key_low, grad_key_gain = norm_rope_back(key_pre, key_gain, cos, sin, own_kv[:, :wide], bf16)
    text_low, grad_text_gain = norm_rope_back(text_key_pre, key_gain, *flat, cross_kv[:, :wide], bf16)
    qkv_low = jnp.concatenate([query_low, key_low, own_kv[:, wide:].astype(bf16)], axis=1)
    act_part = matmul(qkv_low, w_qkv, ROWS)
    grad_act_a = head_sum_rows(act_part, head_index, head_count).astype(f32)
    qkv_part = matmul(act_a, qkv_low, COLS).astype(bf16)
    own_qkv = scatter_sum(jnp.concatenate([qkv_part, out_part], axis=1), seq_index, seq_count)
    grad_x_in, grad_gain_ai, grad_scale_a = pull_in_a(grad_act_a)
    input_grad = grad_x_tail + grad_x_in

    fold = lambda v: v[0, :HD] + v[0, HD:]
    gains = jnp.stack([fold(grad_query_gain), fold(grad_key_gain + grad_text_gain)])
    gains = sum_all(gains, (("head", head_count),))
    flat_sum = jnp.concatenate(
        [grad_scale_a, grad_gate_a, grad_scale_f, grad_gate_f, grad_gain_ai, grad_gain_ao, grad_gain_fi, grad_gain_fo]
        + [gains.reshape(-1), cross_gate_part]
    )
    flat_sum = sum_all(flat_sum, (("seq", seq_count),))
    mod_grad = flat_sum[: 4 * model_width]
    norm_gains_grad = flat_sum[4 * model_width : 8 * model_width].reshape(4, model_width)
    qk_gains_grad = flat_sum[8 * model_width : 8 * model_width + 2 * HD].reshape(2, HD)
    cross_gate_grad = flat_sum[8 * model_width + 2 * HD :]
    own_mod = lax.dynamic_slice_in_dim(
        mod_grad, (seq_index * head_count + head_index) * piece_width, piece_width
    )
    ada_grad = cond_act.astype(f32)[:, None] * own_mod[None, :]
    text_total = lax.psum(jnp.concatenate([text_low, cross_kv[:, wide:].astype(bf16)], axis=1), "seq")
    text_grad = matmul(own_text, text_total, COLS)
    return (
        hidden_out,
        input_grad,
        ada_grad,
        norm_gains_grad,
        qk_gains_grad,
        cut(own_qkv[:, :wide]),
        cut(own_qkv[:, wide : 2 * wide]),
        cut(own_qkv[:, 2 * wide : 3 * wide]),
        own_qkv[:, 3 * wide :].T,
        cross_gate_grad,
        cut(text_grad[:, :wide]),
        cut(text_grad[:, wide:]),
        gate_grad,
        up_grad,
        down_grad,
    )


def solution(mesh):
    in_specs = (
        P("seq", None),
        P(),
        P(),
        P(),
        P(None, ("seq", "head")),
        P(),
        P(),
        P("seq", "head"),
        P("seq", "head"),
        P("seq", "head"),
        P("head", "seq"),
        P("head"),
        P("seq", "head"),
        P("seq", "head"),
        P("seq", "head"),
        P("seq", "head"),
        P("head", "seq"),
        P("seq", None),
    )
    out_specs = (
        P("seq", None),
        P("seq", None),
        P(None, ("seq", "head")),
        P(),
        P(),
        P("seq", "head"),
        P("seq", "head"),
        P("seq", "head"),
        P("head", "seq"),
        P("head"),
        P("seq", "head"),
        P("seq", "head"),
        P("seq", "head"),
        P("seq", "head"),
        P("head", "seq"),
    )
    body = functools.partial(per_device, mesh.shape["seq"], mesh.shape["head"])
    return jax.shard_map(body, mesh=mesh, in_specs=in_specs, out_specs=out_specs, check_vma=False)
```

```python
import functools
import jax
import jax.numpy as jnp
from jax import lax
from jax.experimental import pallas as pl
from jax.experimental.pallas import tpu as pltpu
from jax.sharding import PartitionSpec as P

HD = 64
MASK = 8192.0
CHEAP = pl.CostEstimate(flops=1, bytes_accessed=1, transcendentals=0)
ATTEND_MIB = 60
BACK_MIB = 60
SMALL_MIB = 16


def dot(a, b):
    return lax.dot_general(a, b, (((1,), (0,)), ((), ())), preferred_element_type=jnp.float32)


def split3(v):
    hi = v.astype(jnp.bfloat16).astype(jnp.float32)
    mid = (v - hi).astype(jnp.bfloat16).astype(jnp.float32)
    return hi, mid, v - hi - mid


def bounds(info, base, clips, ids):
    start = jnp.full(ids.shape, 1 << 30, jnp.int32)
    end = jnp.zeros(ids.shape, jnp.int32)
    for c in range(clips):
        start = jnp.where(ids == c, info[base + c], start)
        end = jnp.where(ids == c, info[base + clips + c], end)
    return start, end


def query_ext(info, clips, width, scale):
    ids = lax.broadcasted_iota(jnp.int32, (16, width), 0)
    place = info[0] + lax.broadcasted_iota(jnp.int32, (16, width), 1)
    start, end = bounds(info, 1, clips, ids)
    return jnp.where((place >= start) & (place < end), scale, 0.0)


def key_ext(info, clips, row, rows, piece):
    ids = lax.broadcasted_iota(jnp.int32, (rows, 128), 1)
    step = min(rows, piece)
    parts = []
    for k in range(rows // step):
        at = row + k * step
        first = info[1 + 4 * clips + at // piece] + lax.rem(at, piece)
        parts.append(first + lax.broadcasted_iota(jnp.int32, (step, 128), 0))
    place = parts[0] if len(parts) == 1 else jnp.concatenate(parts, axis=0)
    start, end = bounds(info, 1 + 2 * clips, clips, ids)
    inside = (place >= start) & (place < end)
    value = jnp.where(ids < clips, jnp.where(inside, 0.0, -1.0), jnp.where(ids < clips + 3, 1.0, 0.0))
    return value.astype(jnp.bfloat16)


def fill_ext(dst, h, src, tail):
    width = src.shape[1]
    half = h % 2
    zero = jnp.zeros((HD, width), jnp.bfloat16)
    dst[h, half * HD : half * HD + HD, :] = src[h * HD : h * HD + HD, :]
    dst[h, (1 - half) * HD : (1 - half) * HD + HD, :] = zero
    dst[h, 128:144, :] = tail.astype(jnp.bfloat16)
    dst[h, 144:256, :] = jnp.zeros((112, width), jnp.bfloat16)


def stack_rows(heads, rows, clips, width):
    ids = lax.broadcasted_iota(jnp.int32, (16, width), 0)
    total = jnp.zeros((16, width), jnp.float32)
    for k, row in enumerate(rows):
        total = jnp.where(ids == clips + k, jnp.broadcast_to(row, (16, width)), total)
    return total


def load_pieces(pieces, kv, sem):
    rows = pieces[0].shape[0]
    return [
        pltpu.make_async_copy(piece, kv.at[pl.ds(k * rows, rows), :], sem.at[k])
        for k, piece in enumerate(pieces)
    ]


def fwd_kernel(heads, clips, count, tile, again, info, qt, *rest):
    before, pieces, (out, qx, kv, sem) = rest[:again], rest[again : again + count], rest[again + count :]
    copies = load_pieces(pieces, kv, sem)
    for c in copies:
        c.start()
    width = qt.shape[1]
    wide = qt.shape[0]
    ext = query_ext(info, clips, width, MASK)
    for h in range(heads):
        fill_ext(qx, h, qt, ext)
        out[h] = before[0][h] if again else jnp.zeros((80, width), jnp.float32)
    for c in copies:
        c.wait()
    steps = count * pieces[0].shape[0] // tile
    ones = jnp.ones((16, tile), jnp.bfloat16)

    def step(t, carry):
        rows = pl.ds(pl.multiple_of(t * tile, tile), tile)
        extra = key_ext(info, clips, t * tile, tile, pieces[0].shape[0])
        for p in range((heads + 1) // 2):
            kx = jnp.concatenate([kv[rows, p * 128 : p * 128 + 128], extra], axis=1)
            vt = kv[rows, wide + p * 128 : wide + p * 128 + 128].T
            for h in range(2 * p, min(2 * p + 2, heads)):
                half = h % 2
                probs = jnp.exp(dot(kx, qx[h])).astype(jnp.bfloat16)
                vx = jnp.concatenate([vt[half * HD : half * HD + HD, :], ones], axis=0)
                out[h] += dot(vx, probs)
        return carry

    lax.fori_loop(0, steps, step, 0)


def attend(info, qt, pieces, heads, clips, before=None, tile=1024):
    count = len(pieces)
    before = [] if before is None else [before]
    wide, width = qt.shape
    rows = pieces[0].shape[0]
    tile = min(tile, rows * count)
    return pl.pallas_call(
        functools.partial(fwd_kernel, heads, clips, count, tile, len(before)),
        out_shape=jax.ShapeDtypeStruct((heads, 80, width), jnp.float32),
        in_specs=[pl.BlockSpec(memory_space=pltpu.SMEM)]
        + [pl.BlockSpec(memory_space=pltpu.VMEM)] * (1 + len(before))
        + [pl.BlockSpec(memory_space=pltpu.HBM)] * count,
        out_specs=pl.BlockSpec(memory_space=pltpu.VMEM),
        scratch_shapes=[
            pltpu.VMEM((heads, 256, width), jnp.bfloat16),
            pltpu.VMEM((count * rows, 2 * wide), jnp.bfloat16),
            pltpu.SemaphoreType.DMA((count,)),
        ],
        compiler_params=pltpu.CompilerParams(vmem_limit_bytes=ATTEND_MIB << 20),
        cost_estimate=CHEAP,
        name="attend",
    )(info, qt, *before, *pieces)


def bwd_kernel(heads, clips, count, tile, again, info, qt, dot_t, q_tok, do_tok, lse, delta, *rest):
    before, pieces, rest = rest[:again], rest[again : again + count], rest[again + count :]
    dqt, kdot, grads, (qx, dox, qpad, dopad, kv, sem) = rest[0], rest[1], rest[2:-6], rest[-6:]
    copies = load_pieces(pieces, kv, sem)
    for c in copies:
        c.start()
    wide, width = qt.shape
    ext = query_ext(info, clips, width, MASK)
    for h in range(heads):
        p, half = h // 2, h % 2
        fill_ext(qx, h, qt, ext - stack_rows(heads, split3(lse[h : h + 1, :]), clips, width))
        fill_ext(dox, h, dot_t, -stack_rows(heads, split3(delta[h : h + 1, :]), clips, width))
        lane = lax.broadcasted_iota(jnp.int32, (width, 128), 1) // HD
        zero = jnp.zeros((width, 128), jnp.bfloat16)
        qpad[h] = jnp.where(lane == half, q_tok[:, p * 128 : p * 128 + 128], zero)
        dopad[h] = jnp.where(lane == half, do_tok[:, p * 128 : p * 128 + 128], zero)
    kdot[...] = jnp.zeros((1, 128), jnp.float32)
    dqt[...] = before[0][...] if again else jnp.zeros((wide, width), jnp.float32)
    for c in copies:
        c.wait()
    steps = count * pieces[0].shape[0] // tile

    def step(t, carry):
        rows = pl.ds(pl.multiple_of(t * tile, tile), tile)
        extra = key_ext(info, clips, t * tile, tile, pieces[0].shape[0])
        for p in range((heads + 1) // 2):
            cols = slice(p * 128, p * 128 + 128)
            vcols = slice(wide + p * 128, wide + p * 128 + 128)
            k_tile = kv[rows, cols]
            kx = jnp.concatenate([k_tile, extra], axis=1)
            vx = jnp.concatenate([kv[rows, vcols], extra], axis=1)
            kt = k_tile.T
            dk = jnp.zeros((tile, 128), jnp.float32)
            dv = jnp.zeros((tile, 128), jnp.float32)
            for h in range(2 * p, min(2 * p + 2, heads)):
                half = h % 2
                probs = jnp.exp(dot(kx, qx[h]))
                ds = (probs * dot(vx, dox[h])).astype(jnp.bfloat16)
                dqt[h * HD : h * HD + HD, :] += dot(kt[half * HD : half * HD + HD, :], ds)
                dk = dk + dot(ds, qpad[h])
                dv = dv + dot(probs.astype(jnp.bfloat16), dopad[h])
            kdot[...] += jnp.sum(dk * k_tile.astype(jnp.float32), axis=0, keepdims=True)
            for g, grad in enumerate(grads):

                @pl.when(t // (steps // len(grads)) == g)
                def store(g=g, grad=grad, dk=dk, dv=dv, cols=cols, vcols=vcols):
                    start = (t - g * (steps // len(grads))) * tile
                    here = pl.ds(pl.multiple_of(start, tile), tile)
                    grad[here, cols] = dk.astype(grad.dtype)
                    grad[here, vcols] = dv.astype(grad.dtype)

        return carry

    lax.fori_loop(0, steps, step, 0)


def attend_back(info, qt, dot_t, q_tok, do_tok, lse, delta, pieces, heads, clips, kind, parts=1, before=None, tile=1024):
    count = len(pieces)
    before = [] if before is None else [before]
    wide, width = qt.shape
    rows = pieces[0].shape[0]
    tile = min(tile, rows * count // parts)
    return pl.pallas_call(
        functools.partial(bwd_kernel, heads, clips, count, tile, len(before)),
        out_shape=(
            jax.ShapeDtypeStruct((wide, width), jnp.float32),
            jax.ShapeDtypeStruct((1, 128), jnp.float32),
        )
        + (jax.ShapeDtypeStruct((count * rows // parts, 2 * wide), kind),) * parts,
        in_specs=[pl.BlockSpec(memory_space=pltpu.SMEM)]
        + [pl.BlockSpec(memory_space=pltpu.VMEM)] * (6 + len(before))
        + [pl.BlockSpec(memory_space=pltpu.HBM)] * count,
        out_specs=(pl.BlockSpec(memory_space=pltpu.VMEM),) * (2 + parts),
        scratch_shapes=[
            pltpu.VMEM((heads, 256, width), jnp.bfloat16),
            pltpu.VMEM((heads, 256, width), jnp.bfloat16),
            pltpu.VMEM((heads, width, 128), jnp.bfloat16),
            pltpu.VMEM((heads, width, 128), jnp.bfloat16),
            pltpu.VMEM((count * rows, 2 * wide), jnp.bfloat16),
            pltpu.SemaphoreType.DMA((count,)),
        ],
        compiler_params=pltpu.CompilerParams(vmem_limit_bytes=BACK_MIB << 20),
        cost_estimate=CHEAP,
        name="attend_back",
    )(info, qt, dot_t, q_tok, do_tok, lse, delta, *before, *pieces)


ROWS = (((1,), (1,)), ((), ()))
COLS = (((0,), (0,)), ((), ()))
f32 = jnp.float32
bf16 = jnp.bfloat16


def matmul(left, right, dims=None):
    if dims is None:
        return jnp.dot(left, right, preferred_element_type=f32)
    return lax.dot_general(left, right, dims, preferred_element_type=f32)


def first_way(i):
    return i ^ 2 if i % 2 == 0 else i ^ 4


def other_way(i):
    return i ^ 4 if i % 2 == 0 else i ^ 2


def swap(value, axis, count, to):
    return lax.ppermute(value, axis, [(i, to(i)) for i in range(count)])


def seq_roles(seq_index, seq_count):
    if seq_count != 8:
        return jnp.arange(seq_count, dtype=jnp.int32)
    peer = seq_index ^ 1

    def roles(i):
        even = i % 2 == 0
        return [i, jnp.where(even, i ^ 2, i ^ 4), jnp.where(even, i ^ 4, i ^ 2), i ^ 6]

    return jnp.stack(roles(seq_index) + roles(peer)).astype(jnp.int32)


def gather_pieces(block, seq_count):
    if seq_count != 8:
        whole = lax.all_gather(block, "seq", axis=0, tiled=False)
        return [whole[i] for i in range(seq_count)]
    near = swap(block, "seq", 8, first_way)
    next_ = swap(block, "seq", 8, other_way)
    far = swap(near, "seq", 8, other_way)
    mine = [block, near, next_, far]
    return mine + [swap(v, "seq", 8, lambda i: i ^ 1) for v in mine]


def place_kernel(count, rows, widths, roles, *rest):
    pieces, outs, sem = rest[:count], rest[count:-1], rest[-1]
    copies = []
    for k in range(count):
        to = pl.ds(pl.multiple_of(roles[k] * rows, rows), rows)
        first = 0
        for n, width in enumerate(widths):
            piece = pieces[k].at[:, first : first + width]
            copies.append(pltpu.make_async_copy(piece, outs[n].at[to, :], sem.at[k, n]))
            first += width
    for c in copies:
        c.start()
    for c in copies:
        c.wait()


def place(pieces, roles, widths=None, limit=SMALL_MIB):
    count = len(pieces)
    rows, width = pieces[0].shape
    outs = widths or (width,)
    placed = pl.pallas_call(
        functools.partial(place_kernel, count, rows, outs),
        out_shape=[jax.ShapeDtypeStruct((count * rows, w), pieces[0].dtype) for w in outs],
        in_specs=[pl.BlockSpec(memory_space=pltpu.SMEM)]
        + [pl.BlockSpec(memory_space=pltpu.HBM)] * count,
        out_specs=[pl.BlockSpec(memory_space=pltpu.VMEM)] * len(outs),
        scratch_shapes=[pltpu.SemaphoreType.DMA((count, len(outs)))],
        compiler_params=pltpu.CompilerParams(vmem_limit_bytes=limit << 20),
        cost_estimate=CHEAP,
        name="place",
    )(roles, *pieces)
    return placed if widths else placed[0]


def scatter_start(part, seq_index):
    blocks = part.reshape(4, 2, part.shape[0] // 8, part.shape[1])
    theirs = lax.dynamic_index_in_dim(blocks, 1 - seq_index % 2, 1, False)
    return part, swap(theirs, "seq", 8, lambda i: i ^ 1)


def scatter_first(pair, seq_index):
    part, got = pair
    blocks = part.reshape(4, 2, part.shape[0] // 8, part.shape[1])
    mine = add_low(lax.dynamic_index_in_dim(blocks, seq_index % 2, 1, False), got)
    chip = seq_index // 2
    next_ = jnp.where(seq_index % 2 == 0, chip ^ 2, chip ^ 1)
    pick = lambda c: lax.dynamic_index_in_dim(mine, c, 0, False)
    return mine, swap(jnp.stack([pick(chip ^ 3), pick(next_)]), "seq", 8, other_way)


def scatter_second(pair, seq_index):
    mine, got = pair
    chip = seq_index // 2
    near = jnp.where(seq_index % 2 == 0, chip ^ 1, chip ^ 2)
    pick = lambda c: lax.dynamic_index_in_dim(mine, c, 0, False)
    return add_low(pick(chip), got[1]), swap(add_low(pick(near), got[0]), "seq", 8, first_way)


def scatter_last(pair):
    return pair[0].astype(f32) + pair[1].astype(f32)


def scatter_sum(part, seq_index, seq_count):
    if seq_count != 8:
        return lax.psum_scatter(part, "seq", scatter_dimension=0, tiled=True).astype(f32)
    pair = scatter_first(scatter_start(part, seq_index), seq_index)
    return scatter_last(scatter_second(pair, seq_index))


def hops(axis, count):
    return [(axis, 1 << k) for k in range(count.bit_length() - 1)]


def sum_all(value, axes, order, beside=()):
    if any(count & (count - 1) for _, count in axes):
        return lax.psum(value, [axis for axis, _ in axes]), list(beside)
    counts, beside = dict(axes), list(beside)
    for k, (axis, bit) in enumerate(order):
        got = swap(value, axis, counts[axis], lambda i: i ^ bit)
        if k < len(beside):
            got, beside[k] = lax.optimization_barrier((got, beside[k]))
        value = value + got
    return value, beside


def add_low(a, b):
    return (a.astype(f32) + b.astype(f32)).astype(bf16)


def relay_kernel(names, end, *refs):
    ins = dict(zip(names, refs))
    outs = list(refs[len(names) :])
    add = lambda a, b: (ins[a][...].astype(f32) + ins[b][...].astype(f32)).astype(bf16)
    if "part" in ins:
        outs.pop(0)[...] = add("part", "part_got")
    if "total" in ins:
        total = add("total", "total_got")
        outs.pop(0)[...] = total
        if "own" in ins:
            send = outs.pop(0)
            rows, own_rows = total.shape[0], ins["own"].shape[0]
            both = min(rows, own_rows)
            send[:both, :] = jnp.where(end[0] == 1, ins["own"][:both, :], total[:both, :])
            if own_rows > both:
                send[both:, :] = ins["own"][both:, :]
            if rows > both:
                send[both:, :] = total[both:, :]


def relay(end, part, total, own):
    ins = {}
    shapes = []
    if part is not None:
        ins.update(part=part[0], part_got=part[1])
        shapes.append(part[0].shape)
    if total is not None:
        ins.update(total=total[0], total_got=total[1])
        shapes.append(total[0].shape)
        if own is not None:
            ins["own"] = own
            shapes.append((max(own.shape[0], total[0].shape[0]), own.shape[1]))
    if not shapes:
        return None, None, own
    outs = pl.pallas_call(
        functools.partial(relay_kernel, tuple(ins)),
        out_shape=[jax.ShapeDtypeStruct(shape, bf16) for shape in shapes],
        in_specs=[pl.BlockSpec(memory_space=pltpu.SMEM)] + [pl.BlockSpec(memory_space=pltpu.VMEM)] * len(ins),
        out_specs=[pl.BlockSpec(memory_space=pltpu.VMEM)] * len(shapes),
        compiler_params=pltpu.CompilerParams(vmem_limit_bytes=SMALL_MIB << 20),
        cost_estimate=CHEAP,
        name="relay",
    )(end, *ins.values())
    outs = list(outs)
    part = outs.pop(0) if part is not None else None
    total = outs.pop(0) if total is not None else None
    return part, total, outs.pop(0) if outs else own


def fused(kernel, outs, scalars, arrays, name, limit=40, **static):
    return pl.pallas_call(
        functools.partial(kernel, **static) if static else kernel,
        out_shape=[jax.ShapeDtypeStruct(shape, kind) for shape, kind in outs],
        in_specs=[pl.BlockSpec(memory_space=pltpu.SMEM)] * len(scalars)
        + [pl.BlockSpec() if limit == 60 else pl.BlockSpec(memory_space=pltpu.VMEM)] * len(arrays),
        out_specs=[pl.BlockSpec() if limit == 60 else pl.BlockSpec(memory_space=pltpu.VMEM)] * len(outs),
        compiler_params=pltpu.CompilerParams(vmem_limit_bytes=limit << 20),
        cost_estimate=CHEAP,
        name=name,
    )(*scalars, *arrays)


def rms(value):
    return lax.rsqrt(jnp.mean(value * value, axis=-1, keepdims=True) + 1e-06)


def rms_back(grad, normed, scale):
    return scale * (grad - normed * jnp.mean(grad * normed, axis=-1, keepdims=True))


def dot_rows(a, b):
    return lax.dot_general(a, b, ROWS, preferred_element_type=f32)


def picked(end, total, got):
    return jnp.where(end[0] == 1, got[...], total[...]).astype(f32)


def forward_kernel(
    end, total, got, x, gain_a, gain_in, gate_w, up_w, down_t, ra, na, mid, rm, act, gate, up, units, part
):
    attn = picked(end, total, got)
    scale = rms(attn)
    normed = attn * scale
    ra[...] = scale
    na[...] = normed
    middle = x[...].astype(f32) + normed * gain_a[...]
    mid[...] = middle
    scale = rms(middle)
    rm[...] = scale
    low = (middle * scale * gain_in[...]).astype(bf16)
    act[...] = low
    gated = dot(low, gate_w[...])
    upper = dot(low, up_w[...])
    gate[...] = gated
    up[...] = upper
    low = (gated * jax.nn.sigmoid(gated) * upper).astype(bf16)
    units[...] = low
    part[...] = dot_rows(low, down_t[...]).astype(bf16)


def backward_kernel(
    end, total, got, mid, cot, gate, up, gain_f, gate_w, up_w, down_t, out, uf, dffn, dgate, dup, part
):
    ffn = picked(end, total, got)
    scale = rms(ffn)
    normed = ffn * scale
    out[...] = (mid[...] + normed * gain_f[...]).astype(bf16)
    grad = cot[...].astype(f32)
    uf[...] = jnp.sum(grad * normed, axis=0, keepdims=True)
    low = rms_back(grad * gain_f[...], normed, scale).astype(bf16)
    dffn[...] = low
    grad_units = dot(low, down_t[...])
    gated = gate[...]
    sig = jax.nn.sigmoid(gated)
    low_gate = (grad_units * up[...] * sig * (1.0 + gated * (1.0 - sig))).astype(bf16)
    low_up = (grad_units * gated * sig).astype(bf16)
    dgate[...] = low_gate
    dup[...] = low_up
    part[...] = (dot_rows(low_gate, gate_w[...]) + dot_rows(low_up, up_w[...])).astype(bf16)


def attn_back_kernel(end, total, got, mid, rm, na, ra, cot, gain_in, gain_a, sf, ua, dmid, dattn):
    grad = picked(end, total, got)
    normed = mid[...] * rm[...]
    sf[...] = jnp.sum(grad * normed, axis=0, keepdims=True)
    middle = cot[...].astype(f32) + rms_back(grad * gain_in[...], normed, rm[...])
    dmid[...] = middle
    ua[...] = jnp.sum(middle * na[...], axis=0, keepdims=True)
    dattn[...] = rms_back(middle * gain_a[...], na[...], ra[...]).astype(bf16)


def weight_grad_kernel(*refs, count):
    left = jnp.concatenate([ref[...] for ref in refs[:count]], axis=0)
    right = jnp.concatenate([ref[...] for ref in refs[count : 2 * count]], axis=0)
    refs[2 * count][...] = lax.dot_general(left, right, COLS, preferred_element_type=f32).astype(bf16)


def weight_grad(left, right):
    shape = (left[0].shape[1], right[0].shape[1])
    return fused(weight_grad_kernel, [(shape, bf16)], [], [*left, *right], "weight_grad", 60, count=len(left))[0]


def run_ticks(parts, computes, head_index, head_count, fill):
    carry = []
    stages = 4 * len(computes)
    ticks = stages + len(parts) - 1
    if head_count != 4:
        for n, compute in enumerate(computes):
            sums = [lax.psum(part, "head") for part in parts]
            parts = [compute(k, jnp.zeros((1,), jnp.int32), part, part) for k, part in enumerate(sums)]
        for t in range(ticks):
            carry = fill[t](carry) if t in fill else carry
        return parts, carry
    end = jnp.where((head_index == 0) | (head_index == 3), 1, 0).astype(jnp.int32).reshape(1)
    states = [(part,) for part in parts]
    for t in range(ticks):
        at = {(t - k) % 4: k for k in range(len(parts)) if 0 <= t - k < stages}
        live = [k for k in range(len(parts)) if t - k < stages]
        own = states[at[0]][0] if 0 in at else None
        part, total, send = relay(
            end, states[at[1]] if 1 in at else None, states[at[2]] if 2 in at else None, own
        )
        if 1 in at:
            states[at[1]] = (part, lax.ppermute(part, "head", [(1, 2), (2, 1)]))
        if 0 in at and 2 in at:
            got = lax.ppermute(send, "head", [(0, 1), (3, 2), (1, 0), (2, 3)])
            states[at[0]] = (own, got[: own.shape[0]])
            states[at[2]] = (total, got[: total.shape[0]])
        elif 0 in at:
            states[at[0]] = (own, lax.ppermute(own, "head", [(0, 1), (3, 2)]))
        elif 2 in at:
            states[at[2]] = (total, lax.ppermute(total, "head", [(1, 0), (2, 3)]))
        if 3 in at:
            k = at[3]
            states[k] = (computes[(t - k) // 4](k, end, *states[k]),)
        if t in fill:
            carry = fill[t](carry)
        held, carry = lax.optimization_barrier(([states[k] for k in live], carry))
        for k, state in zip(live, held):
            states[k] = state
    return [state[0] for state in states], carry


def head_mean(value):
    row = lax.broadcasted_iota(jnp.int32, (128, 128), 0) // HD
    col = lax.broadcasted_iota(jnp.int32, (128, 128), 1) // HD
    ones = jnp.where(row == col, 1.0 / HD, 0.0).astype(bf16)
    hi, mid, lo = split3(value)
    return dot(hi.astype(bf16), ones) + dot(mid.astype(bf16), ones) + dot(lo.astype(bf16), ones)


def partner(value):
    lane = lax.broadcasted_iota(jnp.int32, value.shape, 1) % HD
    return jnp.where(lane < HD // 2, pltpu.roll(value, 128 - HD // 2, 1), pltpu.roll(value, HD // 2, 1))


def text_norm_kernel(pre, gain, out):
    wide = pre.shape[1] // 2
    for p in range(wide // 128):
        cols = slice(p * 128, p * 128 + 128)
        value = pre[:, cols]
        out[:, cols] = (value * lax.rsqrt(head_mean(value * value) + 1e-6) * gain[...]).astype(bf16)
    out[:, wide:] = pre[:, wide:].astype(bf16)


def text_norm(pre, gain):
    return pl.pallas_call(
        text_norm_kernel, out_shape=jax.ShapeDtypeStruct(pre.shape, bf16), name="text_norm", cost_estimate=CHEAP
    )(pre, gain)


def qkv_kernel(count, rows, wide, roles, x, gain, qgain, kgain, cos, sin, *rest):
    pieces, (act, scale, pre, kv, query, query_t, weight, sem) = rest[:count], rest[count:]
    copies = []
    for k in range(count):
        start = pl.multiple_of(roles[k] * rows, rows)
        copies.append(pltpu.make_async_copy(pieces[k], weight.at[pl.ds(start, rows), :], sem.at[k]))
    for c in copies:
        c.start()
    value = x[...].astype(f32)
    inverse = lax.rsqrt(jnp.mean(value * value, axis=-1, keepdims=True) + 1e-6)
    scale[...] = inverse
    act[...] = (value * inverse * gain[...]).astype(bf16)
    for c in copies:
        c.wait()
    pre[...] = dot(act[...], weight[:, : 2 * wide])
    kv[:, wide:] = dot(act[...], weight[:, 2 * wide :]).astype(bf16)
    for p in range(wide // 128):
        cols = slice(p * 128, p * 128 + 128)
        for which, out_gain in ((0, qgain), (1, kgain)):
            raw = pre[:, which * wide + p * 128 : which * wide + p * 128 + 128]
            raw = raw * lax.rsqrt(head_mean(raw * raw) + 1e-6) * out_gain[...]
            raw = raw * cos[...] + partner(raw) * sin[...]
            if which == 1:
                kv[:, cols] = raw.astype(bf16)
            else:
                raw = raw.astype(bf16).astype(f32) * HD**-0.5
                query[:, cols] = raw.astype(bf16)
                query_t[cols, :] = raw.T.astype(bf16)


def project(roles, x, gain, qgain, kgain, cos, sin, pieces, wide):
    count = len(pieces)
    rows = pieces[0].shape[0]
    tokens, width = x.shape
    shape = jax.ShapeDtypeStruct
    return pl.pallas_call(
        functools.partial(qkv_kernel, count, rows, wide),
        out_shape=(
            shape((tokens, width), bf16),
            shape((tokens, 1), f32),
            shape((tokens, 2 * wide), f32),
            shape((tokens, 2 * wide), bf16),
            shape((tokens, wide), bf16),
            shape((wide, tokens), bf16),
            shape((width, 3 * wide), bf16),
        ),
        in_specs=[pl.BlockSpec(memory_space=pltpu.SMEM)]
        + [pl.BlockSpec(memory_space=pltpu.VMEM)] * 6
        + [pl.BlockSpec(memory_space=pltpu.HBM)] * count,
        out_specs=(pl.BlockSpec(memory_space=pltpu.VMEM),) * 7,
        scratch_shapes=[pltpu.SemaphoreType.DMA((count,))],
        compiler_params=pltpu.CompilerParams(vmem_limit_bytes=24 << 20),
        cost_estimate=CHEAP,
        name="project",
    )(roles, x, gain, qgain, kgain, cos, sin, *pieces)


def mix_kernel(heads, gate, sums, cross, mixed, self_t, cross_t, lse, cross_lse):
    for p in range((heads + 1) // 2):
        both = []
        for h in range(2 * p, 2 * p + 2):
            if h >= heads:
                both.append(jnp.zeros_like(both[0]))
                continue
            rows = slice(h * HD, h * HD + HD)
            den, cross_den = sums[h, HD : HD + 1, :], cross[h, HD : HD + 1, :]
            lse[h : h + 1, :] = jnp.log(den)
            cross_lse[h : h + 1, :] = jnp.log(cross_den)
            own = sums[h, :HD, :] / den
            other = cross[h, :HD, :] / cross_den
            self_t[rows, :] = own
            cross_t[rows, :] = other
            both.append(own + gate[h] * other)
        mixed[:, p * 128 : p * 128 + 128] = jnp.concatenate(both, axis=0).T.astype(bf16)


def mix(gate, sums, cross, wide):
    heads, _, tokens = sums.shape
    shape = jax.ShapeDtypeStruct
    return pl.pallas_call(
        functools.partial(mix_kernel, heads),
        out_shape=(
            shape((tokens, wide), bf16),
            shape((heads * HD, tokens), f32),
            shape((heads * HD, tokens), f32),
            shape((heads, tokens), f32),
            shape((heads, tokens), f32),
        ),
        in_specs=[pl.BlockSpec(memory_space=pltpu.SMEM)] + [pl.BlockSpec(memory_space=pltpu.VMEM)] * 2,
        compiler_params=pltpu.CompilerParams(vmem_limit_bytes=SMALL_MIB << 20),
        name="mix",
        cost_estimate=CHEAP,
    )(gate, sums, cross)


def unmix_kernel(heads, count, gate, weight, self_t, cross_t, *rest):
    chunks, (tok, tok_t, ctok, ctok_t, delta, cdelta, cgate) = rest[:count], rest[count:]
    width = tok.shape[0]
    for p in range((heads + 1) // 2):
        cols = slice(p * 128, p * 128 + 128)
        value = jnp.concatenate([dot(grad[...], weight[:, cols]) for grad in chunks], axis=0)
        lane = lax.broadcasted_iota(jnp.int32, (width, 128), 1) // HD
        gates = jnp.where(lane == 0, gate[2 * p], gate[min(2 * p + 1, heads - 1)])
        tok[:, cols] = value.astype(bf16)
        ctok[:, cols] = (value * gates).astype(bf16)
        turned = value.T
        for h in range(2 * p, 2 * p + 2):
            rows = slice(h * HD, h * HD + HD)
            part = turned[(h % 2) * HD : (h % 2) * HD + HD, :]
            tok_t[rows, :] = part.astype(bf16)
            if h >= heads:
                ctok_t[rows, :] = part.astype(bf16)
                continue
            low = (part * gate[h]).astype(bf16)
            ctok_t[rows, :] = low
            delta[h : h + 1, :] = jnp.sum(part.astype(bf16).astype(f32) * self_t[rows, :], axis=0, keepdims=True)
            cdelta[h : h + 1, :] = jnp.sum(low.astype(f32) * cross_t[rows, :], axis=0, keepdims=True)
            cgate[h : h + 1, :] = jnp.sum(part * cross_t[rows, :], axis=0, keepdims=True)


def unmix(gate, chunks, weight, self_t, cross_t):
    tokens = self_t.shape[1]
    wide = weight.shape[1]
    heads = self_t.shape[0] // HD
    shape = jax.ShapeDtypeStruct
    return pl.pallas_call(
        functools.partial(unmix_kernel, heads, len(chunks)),
        out_shape=(shape((tokens, wide), bf16), shape((wide, tokens), bf16)) * 2 + (shape((heads, tokens), f32),) * 3,
        in_specs=[pl.BlockSpec(memory_space=pltpu.SMEM)]
        + [pl.BlockSpec(memory_space=pltpu.VMEM)] * (3 + len(chunks)),
        compiler_params=pltpu.CompilerParams(vmem_limit_bytes=SMALL_MIB << 20),
        name="unmix",
        cost_estimate=CHEAP,
    )(gate, weight, self_t, cross_t, *chunks)


def norm_back(raw, gain, grad, cos=None, sin=None):
    scale = lax.rsqrt(head_mean(raw * raw) + 1e-6)
    normed = raw * scale
    if cos is not None:
        grad = grad * cos - partner(grad) * sin
    gain_grad = jnp.sum(grad * normed, axis=0, keepdims=True)
    grad = grad * gain
    return scale * (grad - normed * head_mean(grad * normed)), gain_grad


def text_back_kernel(pre, gain, grad, out):
    wide = pre.shape[1] // 2
    for p in range(wide // 128):
        cols = slice(p * 128, p * 128 + 128)
        out[:, cols] = norm_back(pre[:, cols], gain[...], grad[:, cols])[0].astype(bf16)
    out[:, wide:] = grad[:, wide:].astype(bf16)


def text_back(pre, gain, grad):
    return pl.pallas_call(
        text_back_kernel,
        out_shape=jax.ShapeDtypeStruct(grad.shape, bf16),
        name="text_back",
        cost_estimate=CHEAP,
    )(pre, gain, grad)


def project_back_kernel(wide, starts, pre, qgain, kgain, cos, sin, dqt, *rest):
    kvs, (out, qgrad, kgrad) = rest[: len(starts)], rest[len(starts) :]
    tokens = pre.shape[0]
    total = [jnp.zeros((1, 128), f32), jnp.zeros((1, 128), f32)]
    summed = lambda cols: sum(kv[start : start + tokens, cols].astype(f32) for kv, start in zip(kvs, starts))
    for p in range(wide // 128):
        cols = slice(p * 128, p * 128 + 128)
        grads = (dqt[cols, :] * HD**-0.5).T, summed(cols)
        for which, gain in ((0, qgain), (1, kgain)):
            at = slice(which * wide + p * 128, which * wide + p * 128 + 128)
            value, extra = norm_back(pre[:, at], gain[...], grads[which], cos[...], sin[...])
            out[:, at] = value.astype(bf16)
            total[which] = total[which] + extra
    out[:, 2 * wide :] = summed(slice(wide, 2 * wide)).astype(bf16)
    qgrad[...] = total[0]
    kgrad[...] = total[1]


def project_back(pre, qgain, kgain, cos, sin, dqt, kvs, starts):
    tokens, wide = pre.shape[0], pre.shape[1] // 2
    shape = jax.ShapeDtypeStruct
    return pl.pallas_call(
        functools.partial(project_back_kernel, wide, tuple(starts)),
        out_shape=(shape((tokens, 3 * wide), bf16), shape((1, 128), f32), shape((1, 128), f32)),
        name="project_back",
        cost_estimate=CHEAP,
        compiler_params=pltpu.CompilerParams(vmem_limit_bytes=60 << 20),
    )(pre, qgain, kgain, cos, sin, dqt, *kvs)


def finish_kernel(count, x, scale, gain, *rest):
    grads, mids, out = rest[:count], rest[count : 2 * count], rest[2 * count]
    rows = grads[0].shape[0]
    for k in range(count):
        at = slice(k * rows, k * rows + rows)
        inverse = scale[at, :]
        normed = x[at, :].astype(f32) * inverse
        grad = grads[k][...].astype(f32) * gain[...]
        mean = jnp.mean(grad * normed, axis=-1, keepdims=True)
        out[at, :] = mids[k][...] + inverse * (grad - normed * mean)


def finish(grads, mids, x, scale, gain):
    return pl.pallas_call(
        functools.partial(finish_kernel, len(grads)),
        out_shape=jax.ShapeDtypeStruct(x.shape, f32),
        name="finish",
        cost_estimate=CHEAP,
        compiler_params=pltpu.CompilerParams(vmem_limit_bytes=60 << 20),
    )(x, scale, gain, *grads, *mids)


def per_device(
    seq_count,
    head_count,
    hidden_in,
    cond,
    captions,
    clip_lengths,
    ada_weight,
    norm_gains,
    qk_gains,
    w_query,
    w_key,
    w_value,
    w_out,
    cross_gate,
    w_text_key,
    w_text_value,
    w_gate,
    w_up,
    w_down,
    out_cotangent,
):
    local_rows, model_width = hidden_in.shape
    seq_index = lax.axis_index("seq")
    head_index = lax.axis_index("head")
    clips = clip_lengths.shape[0]
    cols = w_query.shape[1]
    heads = cols // HD
    wide = (cols + 127) // 128 * 128
    units = w_gate.shape[1]
    roles = seq_roles(seq_index, seq_count)
    pad = lambda v: jnp.pad(v, ((0, 0), (0, wide - cols))) if wide > cols else v
    cut = lambda v: v[:, :cols]

    spread = seq_count == 8
    core = lambda v: swap(v, "seq", 8, lambda i: i ^ 1)
    hold = lax.optimization_barrier
    axes = (("seq", seq_count), ("head", head_count))
    seq_hops, head_hops = hops("seq", seq_count), hops("head", head_count)
    finish_sum = lambda v: lax.psum_scatter(v, "seq", scatter_dimension=0, tiled=True)

    def hop(value, steps):
        for axis, bit in steps:
            value = value + swap(value, axis, dict(axes)[axis], lambda i: i ^ bit)
        return value

    clip_ends = jnp.cumsum(clip_lengths, dtype=jnp.int32)
    starts = clip_ends - clip_lengths
    text_rows = captions.reshape(-1, captions.shape[2])
    text_block = text_rows.shape[0] // seq_count
    text_ids = jnp.arange(clips, dtype=jnp.int32) * captions.shape[1]
    first_row = seq_index * local_rows
    place_info = jnp.concatenate([first_row[None], starts, clip_ends]).astype(jnp.int32)
    text_info = jnp.concatenate(
        [place_info, text_ids, text_ids + captions.shape[1], jnp.zeros((1,), jnp.int32)]
    )

    def self_info(which):
        return jnp.concatenate([place_info, starts, clip_ends, roles[which] * local_rows])

    places = first_row + jnp.arange(local_rows, dtype=jnp.int32)
    inside = (places[:, None] >= starts[None, :]) & (places[:, None] < clip_ends[None, :])
    position = places - jnp.sum(jnp.where(inside, starts[None, :], 0), axis=1, dtype=jnp.int32)
    lane = jnp.arange(128)
    frequency = 10000.0 ** (-(lane % (HD // 2)).astype(f32) / (HD // 2))
    angles = position.astype(f32)[:, None] * frequency[None, :]
    cos = jnp.cos(angles)
    sin = jnp.where(lane % HD < HD // 2, -1.0, 1.0)[None, :] * jnp.sin(angles)
    query_gain = jnp.tile(qk_gains[0], 2)[None, :]
    key_gain = jnp.tile(qk_gains[1], 2)[None, :]

    cond_act = jax.nn.silu(cond).astype(bf16)
    piece_width = ada_weight.shape[1]
    mod_piece = matmul(cond_act[None, :], ada_weight)
    mine = lax.broadcasted_iota(jnp.int32, (seq_count * head_count, 1), 0) == seq_index * head_count + head_index
    modulation = jnp.where(mine, mod_piece, 0.0)
    modulation, w_query = hold((modulation, w_query))
    qkv_block = jnp.concatenate([pad(w_query), pad(w_key), pad(w_value)], axis=1)
    out_block = pad(w_out.T)
    slab_width = text_rows.shape[1] // seq_count
    if spread:
        modulation = hop(modulation, seq_hops[:1])
        modulation, text_rows = hold((modulation, text_rows))
    own_text = lax.dynamic_slice_in_dim(text_rows, seq_index * slab_width, slab_width, 1)
    text_part = matmul(own_text, jnp.concatenate([pad(w_text_key), pad(w_text_value)], axis=1)).astype(bf16)

    def queries_keys(modulation, pieces):
        gain = norm_gains[0] * (1.0 + modulation.reshape(4, model_width)[0])
        return project(roles, hidden_in, gain[None, :], query_gain, key_gain, cos, sin, pieces, wide)

    def part_sums(group, blocks, before=None):
        return attend(self_info(jnp.array(group)), query_t, blocks, heads, clips, before)

    if spread:
        near = swap(qkv_block, "seq", 8, first_way)
        next_ = swap(qkv_block, "seq", 8, other_way)
        modulation = hop(modulation, head_hops[:1])
        text_pre = lax.psum(text_part, "seq")
        gate_w = lax.all_gather(w_gate, "seq", axis=0, tiled=True)
        near, next_, modulation = hold((near, next_, modulation))
        far = swap(near, "seq", 8, other_way)
        modulation = hop(modulation, head_hops[1:])
        modulation = hop(modulation, seq_hops[1:])
        qkv_pieces = [qkv_block, near, next_, far]
        qkv_pieces = qkv_pieces + [core(v) for v in qkv_pieces]
        modulation, qkv_pieces, out_block = hold((modulation, qkv_pieces, out_block))
        act_a, x_scale, pre, kv_own, queries, query_t, w_qkv = queries_keys(modulation, qkv_pieces)
        kv_own, modulation, out_block = hold((kv_own, modulation, out_block))
        near = swap(kv_own, "seq", 8, first_way)
        next_ = swap(kv_own, "seq", 8, other_way)
        kv_peer = core(kv_own)
        out_near = swap(out_block, "seq", 8, first_way)
        out_next = swap(out_block, "seq", 8, other_way)
        sums = part_sums((0, 4), [kv_own, kv_peer])
        near, next_, sums, out_near, out_next = hold((near, next_, sums, out_near, out_next))
        far = swap(near, "seq", 8, other_way)
        out_far = swap(out_near, "seq", 8, other_way)
        near_peer, next_peer = core(near), core(next_)
        out_peers = [core(out_block), core(out_near), core(out_next)]
        sums = part_sums((1, 2, 5, 6), [near, next_, near_peer, next_peer], sums)
        ud_block = jnp.concatenate([w_up, w_down.T], axis=1)
        far, sums, out_far, text_pre, ud_block = hold((far, sums, out_far, text_pre, ud_block))
        far_peer = core(far)
        ud_near = swap(ud_block, "seq", 8, first_way)
        ud_next = swap(ud_block, "seq", 8, other_way)
        out_t = place([out_block, out_near, out_next, out_far] + out_peers + [core(out_far)], roles)
        text_pre = text_pre.astype(f32)
        text_pieces = [text_norm(text_pre, key_gain)]
        cross_sums = attend(text_info, query_t, text_pieces, heads, clips)
        sums = part_sums((3, 7), [far, far_peer], sums)
        pieces = [kv_own, near, next_, far, kv_peer, near_peer, next_peer, far_peer]
    else:
        modulation = lax.psum(modulation, ("seq", "head"))
        text_pre = lax.psum(text_part, "seq").astype(f32)
        qkv_pieces = gather_pieces(qkv_block, seq_count)
        act_a, x_scale, pre, kv_own, queries, query_t, w_qkv = queries_keys(modulation, qkv_pieces)
        pieces = gather_pieces(kv_own, seq_count)
        text_pieces = [text_norm(text_pre, key_gain)]
        out_t = place(gather_pieces(out_block, seq_count), roles)
        sums = part_sums(tuple(range(seq_count)), pieces)
        cross_sums = attend(text_info, query_t, text_pieces, heads, clips)
        gate_w = lax.all_gather(w_gate, "seq", axis=0, tiled=True)
    scale_a, gate_a, scale_f, gate_f = jnp.split(modulation.reshape(-1), 4)
    gain_x = norm_gains[0] * (1.0 + scale_a)
    gate_local = jnp.tanh(cross_gate)
    mixed, self_t, cross_t, self_lse, cross_lse = mix(gate_local, sums, cross_sums, wide)
    attn_part = matmul(mixed, out_t, ROWS).astype(bf16)

    late = {}

    def split_weights(pieces):
        return place(pieces, roles, (units, units), 53)

    def fill_far(carry):
        far = swap(ud_near, "seq", 8, other_way)
        return [ud_near, ud_next, far, core(ud_block), core(ud_near), core(ud_next)]

    def fill_weights(carry):
        return [split_weights([ud_block] + carry + [core(carry[2])])]

    def fill_ready(carry):
        late["up"], late["down"] = carry[0]
        return []

    if not spread:
        weights = gather_pieces(jnp.concatenate([w_up, w_down.T], axis=1), seq_count)
        late["up"], late["down"] = split_weights(weights)
    chunk_count = 4
    chunk = local_rows // chunk_count
    rows_of = lambda v, k: v[k * chunk : (k + 1) * chunk]
    tanh_a, tanh_f = jnp.tanh(gate_a), jnp.tanh(gate_f)
    gain_a = tanh_a * norm_gains[1]
    gain_in = norm_gains[2] * (1.0 + scale_f)
    gain_f = tanh_f * norm_gains[3]
    kept = [{} for _ in range(chunk_count)]

    row = lambda v: v[None, :]

    def save(k, names, values):
        kept[k].update(zip(names, values))
        return values[-1]

    def feed_forward(k, end, total, got):
        tall, one, thin = (chunk, model_width), (chunk, 1), (chunk, units)
        outs = [(one, f32), (tall, f32), (tall, f32), (one, f32), (tall, bf16)]
        outs = outs + [(thin, f32), (thin, f32), (thin, bf16), (tall, bf16)]
        arrays = [total, got, rows_of(hidden_in, k), row(gain_a), row(gain_in), gate_w, late["up"], late["down"]]
        names = ["ra", "na", "mid", "rm", "act", "gate", "up", "units", "part"]
        return save(k, names, fused(forward_kernel, outs, [end], arrays, "feed_forward"))

    def feed_back(k, end, total, got):
        keep = kept[k]
        tall, thin = (chunk, model_width), (chunk, units)
        outs = [(tall, bf16), ((1, model_width), f32), (tall, bf16), (thin, bf16), (thin, bf16), (tall, bf16)]
        arrays = [total, got, keep["mid"], rows_of(out_cotangent, k), keep["gate"], keep["up"], row(gain_f)]
        arrays = arrays + [gate_w, late["up"], late["down"]]
        names = ["out", "uf", "dffn", "dgate", "dup", "part"]
        return save(k, names, fused(backward_kernel, outs, [end], arrays, "feed_back"))

    def attn_back(k, end, total, got):
        keep = kept[k]
        tall, line = (chunk, model_width), (1, model_width)
        outs = [(line, f32), (line, f32), (tall, f32), (tall, bf16)]
        arrays = [total, got, keep["mid"], keep["rm"], keep["na"], keep["ra"], rows_of(out_cotangent, k)]
        arrays = arrays + [row(gain_in), row(gain_a)]
        return save(k, ["sf", "ua", "dmid", "dattn"], fused(attn_back_kernel, outs, [end], arrays, "attn_back", 60))

    rows_all = lambda name: jnp.concatenate([keep[name] for keep in kept], axis=0)
    chunks_of = lambda name: [keep[name] for keep in kept]
    vec = lambda name: sum(keep[name][0] for keep in kept)
    def fill_down(carry):
        return [weight_grad(chunks_of("dffn"), chunks_of("units"))]

    def fill_gate(carry):
        low, carry = hold((chunks_of("dgate"), carry))
        down = scatter_start(carry[0], seq_index) if spread else carry[0]
        return [down, weight_grad(chunks_of("act"), low)]

    def fill_up(carry):
        late["gate_sum"] = finish_sum(carry[1])
        low, down = hold((chunks_of("dup"), carry[0]))
        down = scatter_first(down, seq_index) if spread else down
        return [down, weight_grad(chunks_of("act"), low)]

    def fill_last(carry):
        late["up_sum"] = finish_sum(carry[1])
        return [scatter_second(carry[0], seq_index) if spread else carry[0]]

    fills = {8 + chunk_count - 1: fill_down, 8 + chunk_count: fill_gate, 8 + chunk_count + 1: fill_up, 8 + chunk_count + 2: fill_last}
    first_parts = [rows_of(attn_part, k) for k in range(chunk_count)]
    if spread:
        fills.update({0: fill_far, 1: fill_weights, 2: fill_ready})
    grad_attn_chunks, (down_pair,) = run_ticks(
        first_parts, [feed_forward, feed_back, attn_back], head_index, head_count, fills
    )
    grad_attn_low = jnp.concatenate(grad_attn_chunks, axis=0)
    hidden_out = rows_all("out")
    down_grad = scatter_last(down_pair) if spread else finish_sum(down_pair).astype(f32)
    gate_grad, up_grad = late["gate_sum"], late["up_sum"]

    grad_self_tok, grad_self_t, grad_cross_tok, grad_cross_t, self_delta, cross_delta, gate_rows = unmix(
        gate_local, grad_attn_chunks, out_t, self_t, cross_t
    )
    cross_gate_part = jnp.sum(gate_rows, axis=1) * (1.0 - gate_local * gate_local)

    def back(group, parts, before=None):
        return attend_back(
            self_info(jnp.array(group)), query_t, grad_self_t, queries, grad_self_tok, self_lse, self_delta,
            [pieces[g] for g in group], heads, clips, bf16, parts, before,
        )

    def cross_back(before):
        return attend_back(
            text_info, query_t, grad_cross_t, queries, grad_cross_tok, cross_lse, cross_delta,
            text_pieces, heads, clips, f32, 1, before,
        )

    if spread:
        dq, _, kv_mine, kv_theirs = back((3, 2, 7, 6), 2)
        kv_got = core(kv_theirs)
        kv_mine, low = hold((kv_mine, grad_attn_low))
        out_part = matmul(low, mixed, COLS).astype(bf16)
        total = add_low(kv_mine, kv_got)
        total, dq = hold((total, dq))
        first = swap(total, "seq", 8, other_way)
        dq, text_dot, cross_kv = cross_back(dq)
        text_low = text_back(text_pre, key_gain, cross_kv)
        dq, text_low, gate_grad = hold((dq, text_low, gate_grad))
        dq, _, kv_mine, kv_theirs = back((1, 5), 2, dq)
        first, kv_mine, kv_theirs, up_grad = hold((first, kv_mine, kv_theirs, up_grad))
        total = kv_mine.astype(f32) + core(kv_theirs).astype(f32) + first[:local_rows].astype(f32)
        total = total.astype(bf16)
        second = swap(total, "seq", 8, first_way)
        dq, _, kv_mine, kv_theirs = back((0, 4), 2, dq)
        second, kv_mine, kv_theirs = hold((second, kv_mine, kv_theirs))
        kv_parts, kv_starts = [kv_mine, core(kv_theirs), first, second], (0, 0, local_rows, 0)
    else:
        dq, _, kv_all = back(tuple(range(seq_count)), 1)
        dq, text_dot, cross_kv = cross_back(dq)
        out_part = matmul(grad_attn_low, mixed, COLS).astype(bf16)
        text_low = text_back(text_pre, key_gain, cross_kv)
        kv_parts, kv_starts = [finish_sum(kv_all)], (0,)
    qkv_low, grad_query_gain, grad_key_gain = project_back(
        pre, query_gain, key_gain, cos, sin, dq, kv_parts, kv_starts
    )
    x_normed = hidden_in.astype(f32) * x_scale
    act_part = matmul(qkv_low, w_qkv, ROWS)
    sum_a = jnp.sum(act_part * x_normed, axis=0)
    act_low, qkv_low = hold((act_part.astype(bf16), qkv_low))
    fold = lambda v: v[0, :HD] + v[0, HD:]
    pair_gains = jnp.concatenate([fold(grad_query_gain), fold(grad_key_gain + text_dot / key_gain)])
    tail = jnp.stack([sum_a, jnp.pad(pair_gains, (0, model_width - 2 * HD))])
    tail = jnp.pad(tail, ((0, 14), (0, 0))).astype(bf16)
    small = jnp.concatenate([vec("ua"), vec("sf"), vec("uf"), cross_gate_part])

    def collect(k, end, total, got):
        total = jnp.where(end[0] == 1, got, total)
        if k == 0:
            late["tail"] = total[chunk:].astype(f32)
        return total[:chunk]

    def fill0(carry):
        part = matmul(act_a, qkv_low, COLS).astype(bf16)
        late["gate"] = gate_grad.astype(f32)
        late["qkv"] = scatter_start(part, seq_index) if spread else part
        if not spread:
            return [lax.psum(text_low, "seq")]
        return [scatter_start(text_low, seq_index)]

    def fill1(carry):
        if not spread:
            return carry
        return [scatter_first(carry[0], seq_index)]

    def fill2(carry):
        if not spread:
            return carry
        qkv, carry = hold((late["qkv"], carry))
        late["qkv"] = scatter_first(qkv, seq_index)
        return [scatter_second(carry[0], seq_index)]

    def fill3(carry):
        if not spread:
            late["down"] = down_grad.T
            return carry
        own = add_low(*carry[0])
        grad, own = hold((down_grad, own))
        late["down"] = grad.T
        return [[own, swap(own, "seq", 8, first_way), swap(own, "seq", 8, other_way)]]

    def fill4(carry):
        text = carry[0]
        values = jnp.concatenate([small, late["tail"][0], late["tail"][1, : 2 * HD]])
        values, text, up = hold((values, text, up_grad))
        late["up"] = up.astype(f32)
        if not spread:
            return [lax.psum(values, "seq"), text]
        qkv, text = hold((late["qkv"], text))
        late["qkv"] = scatter_second(qkv, seq_index)
        return [hop(values, seq_hops[:1]), text + [swap(text[1], "seq", 8, other_way)]]

    def fill5(carry):
        values, text = carry
        if not spread:
            return carry
        return [hop(values, seq_hops[1:]), text + [core(v) for v in text]]

    def fill6(carry):
        qkv = late["qkv"]
        qkv = scatter_last(qkv) if spread else finish_sum(qkv).astype(f32)
        text = place(carry[1], roles) if spread else carry[1]
        return [carry[0], matmul(own_text, text, COLS), qkv]

    parts = [rows_of(act_low, k) for k in range(chunk_count)]
    parts[0] = jnp.concatenate([parts[0], tail])
    fills = dict(enumerate([fill0, fill1, fill2, fill3, fill4, fill5, fill6]))
    act_chunks, (values, text_grad, own_qkv) = run_ticks(parts, [collect], head_index, head_count, fills)
    out_grad, act_chunks = hold((finish_sum(out_part), act_chunks))
    input_grad = finish(act_chunks, [keep["dmid"] for keep in kept], hidden_in, x_scale, gain_x[None, :])

    sum_ua, sum_sf, sum_uf = (values[k * model_width : (k + 1) * model_width] for k in range(3))
    values = values[3 * model_width :]
    cross_gate_grad, sum_sa, qk_sums = jnp.split(values, [heads, heads + model_width])
    qk_gains_grad = qk_sums.reshape(2, HD)
    norm_gains_grad = jnp.stack(
        [sum_sa * (1.0 + scale_a), sum_ua * tanh_a, sum_sf * (1.0 + scale_f), sum_uf * tanh_f]
    )
    mod_grad = jnp.concatenate(
        [
            sum_sa * norm_gains[0],
            sum_ua * norm_gains[1] * (1.0 - tanh_a * tanh_a),
            sum_sf * norm_gains[2],
            sum_uf * norm_gains[3] * (1.0 - tanh_f * tanh_f),
        ]
    )
    own_mod = lax.dynamic_slice_in_dim(
        mod_grad, (seq_index * head_count + head_index) * piece_width, piece_width
    )
    ada_grad = cond_act.astype(f32)[:, None] * own_mod[None, :]
    return (
        hidden_out,
        input_grad,
        ada_grad,
        norm_gains_grad,
        qk_gains_grad,
        cut(own_qkv[:, :wide]),
        cut(own_qkv[:, wide : 2 * wide]),
        cut(own_qkv[:, 2 * wide : 3 * wide]),
        cut(out_grad).astype(f32).T,
        cross_gate_grad,
        cut(text_grad[:, :wide]),
        cut(text_grad[:, wide:]),
        late["gate"],
        late["up"],
        late["down"],
    )


def solution(mesh):
    in_specs = (
        P("seq", None),
        P(),
        P(),
        P(),
        P(None, ("seq", "head")),
        P(),
        P(),
        P("seq", "head"),
        P("seq", "head"),
        P("seq", "head"),
        P("head", "seq"),
        P("head"),
        P("seq", "head"),
        P("seq", "head"),
        P("seq", "head"),
        P("seq", "head"),
        P("head", "seq"),
        P("seq", None),
    )
    out_specs = (
        P("seq", None),
        P("seq", None),
        P(None, ("seq", "head")),
        P(),
        P(),
        P("seq", "head"),
        P("seq", "head"),
        P("seq", "head"),
        P("head", "seq"),
        P("head"),
        P("seq", "head"),
        P("seq", "head"),
        P("seq", "head"),
        P("seq", "head"),
        P("head", "seq"),
    )
    body = functools.partial(per_device, mesh.shape["seq"], mesh.shape["head"])
    return jax.shard_map(body, mesh=mesh, in_specs=in_specs, out_specs=out_specs, check_vma=False)
```

```python
import functools
import jax
import jax.numpy as jnp
from jax import lax
from jax.experimental import pallas as pl
from jax.experimental.pallas import tpu as pltpu
from jax.sharding import PartitionSpec as P

HD = 64
MASK = 8192.0
CHEAP = pl.CostEstimate(flops=1, bytes_accessed=1, transcendentals=0)
ATTEND_MIB = 60
BACK_MIB = 60
SMALL_MIB = 16


def dot(a, b):
    return lax.dot_general(a, b, (((1,), (0,)), ((), ())), preferred_element_type=jnp.float32)


def split3(v):
    hi = v.astype(jnp.bfloat16).astype(jnp.float32)
    mid = (v - hi).astype(jnp.bfloat16).astype(jnp.float32)
    return hi, mid, v - hi - mid


def bounds(info, base, clips, ids):
    start = jnp.full(ids.shape, 1 << 30, jnp.int32)
    end = jnp.zeros(ids.shape, jnp.int32)
    for c in range(clips):
        start = jnp.where(ids == c, info[base + c], start)
        end = jnp.where(ids == c, info[base + clips + c], end)
    return start, end


def query_ext(info, clips, width, scale):
    ids = lax.broadcasted_iota(jnp.int32, (16, width), 0)
    place = info[0] + lax.broadcasted_iota(jnp.int32, (16, width), 1)
    start, end = bounds(info, 1, clips, ids)
    return jnp.where((place >= start) & (place < end), scale, 0.0)


def key_ext(info, clips, row, rows, piece):
    ids = lax.broadcasted_iota(jnp.int32, (rows, 128), 1)
    step = min(rows, piece)
    parts = []
    for k in range(rows // step):
        at = row + k * step
        first = info[1 + 4 * clips + at // piece] + lax.rem(at, piece)
        parts.append(first + lax.broadcasted_iota(jnp.int32, (step, 128), 0))
    place = parts[0] if len(parts) == 1 else jnp.concatenate(parts, axis=0)
    start, end = bounds(info, 1 + 2 * clips, clips, ids)
    inside = (place >= start) & (place < end)
    value = jnp.where(ids < clips, jnp.where(inside, 0.0, -1.0), jnp.where(ids < clips + 3, 1.0, 0.0))
    return value.astype(jnp.bfloat16)


def fill_ext(dst, h, src, tail):
    width = src.shape[1]
    half = h % 2
    zero = jnp.zeros((HD, width), jnp.bfloat16)
    dst[h, half * HD : half * HD + HD, :] = src[h * HD : h * HD + HD, :]
    dst[h, (1 - half) * HD : (1 - half) * HD + HD, :] = zero
    dst[h, 128:144, :] = tail.astype(jnp.bfloat16)
    dst[h, 144:256, :] = jnp.zeros((112, width), jnp.bfloat16)


def stack_rows(heads, rows, clips, width):
    ids = lax.broadcasted_iota(jnp.int32, (16, width), 0)
    total = jnp.zeros((16, width), jnp.float32)
    for k, row in enumerate(rows):
        total = jnp.where(ids == clips + k, jnp.broadcast_to(row, (16, width)), total)
    return total


def load_pieces(pieces, kv, sem):
    rows = pieces[0].shape[0]
    return [
        pltpu.make_async_copy(piece, kv.at[pl.ds(k * rows, rows), :], sem.at[k])
        for k, piece in enumerate(pieces)
    ]


def fwd_kernel(heads, clips, count, tile, again, info, qt, *rest):
    before, pieces, (out, qx, kv, sem) = rest[:again], rest[again : again + count], rest[again + count :]
    copies = load_pieces(pieces, kv, sem)
    for c in copies:
        c.start()
    width = qt.shape[1]
    wide = qt.shape[0]
    ext = query_ext(info, clips, width, MASK)
    for h in range(heads):
        fill_ext(qx, h, qt, ext)
        out[h] = before[0][h] if again else jnp.zeros((80, width), jnp.float32)
    for c in copies:
        c.wait()
    steps = count * pieces[0].shape[0] // tile
    ones = jnp.ones((16, tile), jnp.bfloat16)

    def step(t, carry):
        rows = pl.ds(pl.multiple_of(t * tile, tile), tile)
        extra = key_ext(info, clips, t * tile, tile, pieces[0].shape[0])
        for p in range((heads + 1) // 2):
            kx = jnp.concatenate([kv[rows, p * 128 : p * 128 + 128], extra], axis=1)
            vt = kv[rows, wide + p * 128 : wide + p * 128 + 128].T
            for h in range(2 * p, min(2 * p + 2, heads)):
                half = h % 2
                probs = jnp.exp(dot(kx, qx[h])).astype(jnp.bfloat16)
                vx = jnp.concatenate([vt[half * HD : half * HD + HD, :], ones], axis=0)
                out[h] += dot(vx, probs)
        return carry

    lax.fori_loop(0, steps, step, 0)


def attend(info, qt, pieces, heads, clips, before=None, tile=1024):
    count = len(pieces)
    before = [] if before is None else [before]
    wide, width = qt.shape
    rows = pieces[0].shape[0]
    tile = min(tile, rows * count)
    return pl.pallas_call(
        functools.partial(fwd_kernel, heads, clips, count, tile, len(before)),
        out_shape=jax.ShapeDtypeStruct((heads, 80, width), jnp.float32),
        in_specs=[pl.BlockSpec(memory_space=pltpu.SMEM)]
        + [pl.BlockSpec(memory_space=pltpu.VMEM)] * (1 + len(before))
        + [pl.BlockSpec(memory_space=pltpu.HBM)] * count,
        out_specs=pl.BlockSpec(memory_space=pltpu.VMEM),
        scratch_shapes=[
            pltpu.VMEM((heads, 256, width), jnp.bfloat16),
            pltpu.VMEM((count * rows, 2 * wide), jnp.bfloat16),
            pltpu.SemaphoreType.DMA((count,)),
        ],
        compiler_params=pltpu.CompilerParams(vmem_limit_bytes=ATTEND_MIB << 20),
        cost_estimate=CHEAP,
        name="attend",
    )(info, qt, *before, *pieces)


def bwd_kernel(heads, clips, count, tile, again, info, qt, dot_t, q_tok, do_tok, lse, delta, *rest):
    before, pieces, rest = rest[:again], rest[again : again + count], rest[again + count :]
    dqt, kdot, grads, (qx, dox, qpad, dopad, kv, sem) = rest[0], rest[1], rest[2:-6], rest[-6:]
    copies = load_pieces(pieces, kv, sem)
    for c in copies:
        c.start()
    wide, width = qt.shape
    ext = query_ext(info, clips, width, MASK)
    for h in range(heads):
        p, half = h // 2, h % 2
        fill_ext(qx, h, qt, ext - stack_rows(heads, split3(lse[h : h + 1, :]), clips, width))
        fill_ext(dox, h, dot_t, -stack_rows(heads, split3(delta[h : h + 1, :]), clips, width))
        lane = lax.broadcasted_iota(jnp.int32, (width, 128), 1) // HD
        zero = jnp.zeros((width, 128), jnp.bfloat16)
        qpad[h] = jnp.where(lane == half, q_tok[:, p * 128 : p * 128 + 128], zero)
        dopad[h] = jnp.where(lane == half, do_tok[:, p * 128 : p * 128 + 128], zero)
    kdot[...] = jnp.zeros((1, 128), jnp.float32)
    dqt[...] = before[0][...] if again else jnp.zeros((wide, width), jnp.float32)
    for c in copies:
        c.wait()
    steps = count * pieces[0].shape[0] // tile

    def step(t, carry):
        rows = pl.ds(pl.multiple_of(t * tile, tile), tile)
        extra = key_ext(info, clips, t * tile, tile, pieces[0].shape[0])
        for p in range((heads + 1) // 2):
            cols = slice(p * 128, p * 128 + 128)
            vcols = slice(wide + p * 128, wide + p * 128 + 128)
            k_tile = kv[rows, cols]
            kx = jnp.concatenate([k_tile, extra], axis=1)
            vx = jnp.concatenate([kv[rows, vcols], extra], axis=1)
            kt = k_tile.T
            dk = jnp.zeros((tile, 128), jnp.float32)
            dv = jnp.zeros((tile, 128), jnp.float32)
            for h in range(2 * p, min(2 * p + 2, heads)):
                half = h % 2
                probs = jnp.exp(dot(kx, qx[h]))
                ds = (probs * dot(vx, dox[h])).astype(jnp.bfloat16)
                dqt[h * HD : h * HD + HD, :] += dot(kt[half * HD : half * HD + HD, :], ds)
                dk = dk + dot(ds, qpad[h])
                dv = dv + dot(probs.astype(jnp.bfloat16), dopad[h])
            kdot[...] += jnp.sum(dk * k_tile.astype(jnp.float32), axis=0, keepdims=True)
            for g, grad in enumerate(grads):

                @pl.when(t // (steps // len(grads)) == g)
                def store(g=g, grad=grad, dk=dk, dv=dv, cols=cols, vcols=vcols):
                    start = (t - g * (steps // len(grads))) * tile
                    here = pl.ds(pl.multiple_of(start, tile), tile)
                    grad[here, cols] = dk.astype(grad.dtype)
                    grad[here, vcols] = dv.astype(grad.dtype)

        return carry

    lax.fori_loop(0, steps, step, 0)


def attend_back(info, qt, dot_t, q_tok, do_tok, lse, delta, pieces, heads, clips, kind, parts=1, before=None, tile=1024):
    count = len(pieces)
    before = [] if before is None else [before]
    wide, width = qt.shape
    rows = pieces[0].shape[0]
    tile = min(tile, rows * count // parts)
    return pl.pallas_call(
        functools.partial(bwd_kernel, heads, clips, count, tile, len(before)),
        out_shape=(
            jax.ShapeDtypeStruct((wide, width), jnp.float32),
            jax.ShapeDtypeStruct((1, 128), jnp.float32),
        )
        + (jax.ShapeDtypeStruct((count * rows // parts, 2 * wide), kind),) * parts,
        in_specs=[pl.BlockSpec(memory_space=pltpu.SMEM)]
        + [pl.BlockSpec(memory_space=pltpu.VMEM)] * (6 + len(before))
        + [pl.BlockSpec(memory_space=pltpu.HBM)] * count,
        out_specs=(pl.BlockSpec(memory_space=pltpu.VMEM),) * (2 + parts),
        scratch_shapes=[
            pltpu.VMEM((heads, 256, width), jnp.bfloat16),
            pltpu.VMEM((heads, 256, width), jnp.bfloat16),
            pltpu.VMEM((heads, width, 128), jnp.bfloat16),
            pltpu.VMEM((heads, width, 128), jnp.bfloat16),
            pltpu.VMEM((count * rows, 2 * wide), jnp.bfloat16),
            pltpu.SemaphoreType.DMA((count,)),
        ],
        compiler_params=pltpu.CompilerParams(vmem_limit_bytes=BACK_MIB << 20),
        cost_estimate=CHEAP,
        name="attend_back",
    )(info, qt, dot_t, q_tok, do_tok, lse, delta, *before, *pieces)


ROWS = (((1,), (1,)), ((), ()))
COLS = (((0,), (0,)), ((), ()))
f32 = jnp.float32
bf16 = jnp.bfloat16


def matmul(left, right, dims=None):
    if dims is None:
        return jnp.dot(left, right, preferred_element_type=f32)
    return lax.dot_general(left, right, dims, preferred_element_type=f32)


def first_way(i):
    return i ^ 2 if i % 2 == 0 else i ^ 4


def other_way(i):
    return i ^ 4 if i % 2 == 0 else i ^ 2


def swap(value, axis, count, to):
    return lax.ppermute(value, axis, [(i, to(i)) for i in range(count)])


def seq_roles(seq_index, seq_count):
    if seq_count != 8:
        return jnp.arange(seq_count, dtype=jnp.int32)
    peer = seq_index ^ 1

    def roles(i):
        even = i % 2 == 0
        return [i, jnp.where(even, i ^ 2, i ^ 4), jnp.where(even, i ^ 4, i ^ 2), i ^ 6]

    return jnp.stack(roles(seq_index) + roles(peer)).astype(jnp.int32)


def gather_pieces(block, seq_count):
    if seq_count != 8:
        whole = lax.all_gather(block, "seq", axis=0, tiled=False)
        return [whole[i] for i in range(seq_count)]
    near = swap(block, "seq", 8, first_way)
    next_ = swap(block, "seq", 8, other_way)
    far = swap(near, "seq", 8, other_way)
    mine = [block, near, next_, far]
    return mine + [swap(v, "seq", 8, lambda i: i ^ 1) for v in mine]


def place_kernel(count, rows, widths, roles, *rest):
    pieces, outs, sem = rest[:count], rest[count:-1], rest[-1]
    copies = []
    for k in range(count):
        to = pl.ds(pl.multiple_of(roles[k] * rows, rows), rows)
        first = 0
        for n, width in enumerate(widths):
            piece = pieces[k].at[:, first : first + width]
            copies.append(pltpu.make_async_copy(piece, outs[n].at[to, :], sem.at[k, n]))
            first += width
    for c in copies:
        c.start()
    for c in copies:
        c.wait()


def place(pieces, roles, widths=None, limit=SMALL_MIB):
    count = len(pieces)
    rows, width = pieces[0].shape
    outs = widths or (width,)
    placed = pl.pallas_call(
        functools.partial(place_kernel, count, rows, outs),
        out_shape=[jax.ShapeDtypeStruct((count * rows, w), pieces[0].dtype) for w in outs],
        in_specs=[pl.BlockSpec(memory_space=pltpu.SMEM)]
        + [pl.BlockSpec(memory_space=pltpu.HBM)] * count,
        out_specs=[pl.BlockSpec(memory_space=pltpu.VMEM)] * len(outs),
        scratch_shapes=[pltpu.SemaphoreType.DMA((count, len(outs)))],
        compiler_params=pltpu.CompilerParams(vmem_limit_bytes=limit << 20),
        cost_estimate=CHEAP,
        name="place",
    )(roles, *pieces)
    return placed if widths else placed[0]


def take_kernel(rows, core, part, out, sem):
    copies = []
    for chip in range(4):
        start = pl.multiple_of((2 * chip + core[0]) * rows, rows)
        to = out.at[pl.ds(chip * rows, rows), :]
        copies.append(pltpu.make_async_copy(part.at[pl.ds(start, rows), :], to, sem.at[chip]))
    for c in copies:
        c.start()
    for c in copies:
        c.wait()


def first_kernel(rows, where, part, got, mine, send, held, sem):
    copies = []
    for chip in range(4):
        start = pl.multiple_of((2 * chip + where[0]) * rows, rows)
        to = held.at[pl.ds(chip * rows, rows), :]
        copies.append(pltpu.make_async_copy(part.at[pl.ds(start, rows), :], to, sem.at[chip]))
    for c in copies:
        c.start()
    for c in copies:
        c.wait()
    mine[...] = (held[...].astype(f32) + got[...].astype(f32)).astype(bf16)
    for n in range(2):
        send[n * rows : n * rows + rows, :] = mine[pl.ds(pl.multiple_of(where[1 + n] * rows, rows), rows), :]


def second_kernel(rows, where, mine, got, own, send):
    block = lambda n: mine[pl.ds(pl.multiple_of(where[n] * rows, rows), rows), :].astype(f32)
    own[...] = (block(0) + got[rows:, :].astype(f32)).astype(bf16)
    send[...] = (block(1) + got[:rows, :].astype(f32)).astype(bf16)


def scatter_call(kernel, rows, where, arrays, outs, scratch, name, first=pltpu.VMEM):
    width = arrays[0].shape[1]
    vmem = pl.BlockSpec(memory_space=pltpu.VMEM)
    return pl.pallas_call(
        functools.partial(kernel, rows),
        out_shape=[jax.ShapeDtypeStruct((n * rows, width), bf16) for n in outs],
        in_specs=[pl.BlockSpec(memory_space=pltpu.SMEM), pl.BlockSpec(memory_space=first)]
        + [vmem] * (len(arrays) - 1),
        out_specs=[vmem] * len(outs),
        scratch_shapes=scratch,
        compiler_params=pltpu.CompilerParams(vmem_limit_bytes=SMALL_MIB << 20),
        cost_estimate=CHEAP,
        name=name,
    )(jnp.stack(where).astype(jnp.int32), *arrays)


def scatter_start(part, seq_index):
    rows = part.shape[0] // 8
    sems = [pltpu.SemaphoreType.DMA((4,))]
    theirs = scatter_call(take_kernel, rows, [1 - seq_index % 2], [part], [4], sems, "scatter_take", pl.ANY)[0]
    return part, swap(theirs, "seq", 8, lambda i: i ^ 1)


def scatter_first(pair, seq_index):
    part, got = pair
    rows = part.shape[0] // 8
    core, chip = seq_index % 2, seq_index // 2
    where = [core, chip ^ 3, jnp.where(core == 0, chip ^ 2, chip ^ 1)]
    scratch = [pltpu.VMEM(got.shape, bf16), pltpu.SemaphoreType.DMA((4,))]
    mine, send = scatter_call(first_kernel, rows, where, [part, got], [4, 2], scratch, "scatter_first", pl.ANY)
    return mine, swap(send, "seq", 8, other_way)


def scatter_second(pair, seq_index):
    mine, got = pair
    core, chip = seq_index % 2, seq_index // 2
    where = [chip, jnp.where(core == 0, chip ^ 1, chip ^ 2)]
    own, send = scatter_call(second_kernel, mine.shape[0] // 4, where, [mine, got], [1, 1], [], "scatter_second")
    return own, swap(send, "seq", 8, first_way)


def widen_kernel(count, turn, *refs):
    total = refs[0][...].astype(f32)
    for ref in refs[1:count]:
        total = total + ref[...].astype(f32)
    refs[count][...] = total.T if turn else total


def widen(parts, turn=False):
    rows, width = parts[0].shape
    return pl.pallas_call(
        functools.partial(widen_kernel, len(parts), turn),
        out_shape=jax.ShapeDtypeStruct((width, rows) if turn else (rows, width), f32),
        compiler_params=pltpu.CompilerParams(vmem_limit_bytes=SMALL_MIB << 20),
        cost_estimate=CHEAP,
        name="widen",
    )(*parts)


def scatter_sum(part, seq_index, seq_count):
    if seq_count != 8:
        return lax.psum_scatter(part, "seq", scatter_dimension=0, tiled=True)
    pair = scatter_first(scatter_start(part, seq_index), seq_index)
    return widen(list(scatter_second(pair, seq_index)))


def hops(axis, count):
    return [(axis, 1 << k) for k in range(count.bit_length() - 1)]


def sum_all(value, axes, order, beside=()):
    if any(count & (count - 1) for _, count in axes):
        return lax.psum(value, [axis for axis, _ in axes]), list(beside)
    counts, beside = dict(axes), list(beside)
    for k, (axis, bit) in enumerate(order):
        got = swap(value, axis, counts[axis], lambda i: i ^ bit)
        if k < len(beside):
            got, beside[k] = lax.optimization_barrier((got, beside[k]))
        value = value + got
    return value, beside


def add_low(a, b):
    return (a.astype(f32) + b.astype(f32)).astype(bf16)


def relay_kernel(names, end, *refs):
    ins = dict(zip(names, refs))
    outs = list(refs[len(names) :])
    add = lambda a, b: (ins[a][...].astype(f32) + ins[b][...].astype(f32)).astype(bf16)
    if "part" in ins:
        outs.pop(0)[...] = add("part", "part_got")
    if "total" in ins:
        total = add("total", "total_got")
        outs.pop(0)[...] = total
        if "own" in ins:
            send = outs.pop(0)
            rows, own_rows = total.shape[0], ins["own"].shape[0]
            both = min(rows, own_rows)
            send[:both, :] = jnp.where(end[0] == 1, ins["own"][:both, :], total[:both, :])
            if own_rows > both:
                send[both:, :] = ins["own"][both:, :]
            if rows > both:
                send[both:, :] = total[both:, :]


def relay(end, part, total, own):
    ins = {}
    shapes = []
    if part is not None:
        ins.update(part=part[0], part_got=part[1])
        shapes.append(part[0].shape)
    if total is not None:
        ins.update(total=total[0], total_got=total[1])
        shapes.append(total[0].shape)
        if own is not None:
            ins["own"] = own
            shapes.append((max(own.shape[0], total[0].shape[0]), own.shape[1]))
    if not shapes:
        return None, None, own
    outs = pl.pallas_call(
        functools.partial(relay_kernel, tuple(ins)),
        out_shape=[jax.ShapeDtypeStruct(shape, bf16) for shape in shapes],
        in_specs=[pl.BlockSpec(memory_space=pltpu.SMEM)] + [pl.BlockSpec(memory_space=pltpu.VMEM)] * len(ins),
        out_specs=[pl.BlockSpec(memory_space=pltpu.VMEM)] * len(shapes),
        compiler_params=pltpu.CompilerParams(vmem_limit_bytes=SMALL_MIB << 20),
        cost_estimate=CHEAP,
        name="relay",
    )(end, *ins.values())
    outs = list(outs)
    part = outs.pop(0) if part is not None else None
    total = outs.pop(0) if total is not None else None
    return part, total, outs.pop(0) if outs else own


def staged(kernel, k, outs, wholes, scalars, arrays, before, name, limit=SMALL_MIB):
    before = before or []
    vmem = pl.BlockSpec() if limit == 60 else pl.BlockSpec(memory_space=pltpu.VMEM)
    anywhere = pl.BlockSpec(memory_space=pl.ANY)
    given = len(scalars) + len(arrays)
    return pl.pallas_call(
        functools.partial(kernel, k, len(before)),
        out_shape=[jax.ShapeDtypeStruct(shape, kind) for shape, kind in outs]
        + [jax.ShapeDtypeStruct((tokens, width), kind) for tokens, rows, width, kind in wholes],
        in_specs=[pl.BlockSpec(memory_space=pltpu.SMEM)] * len(scalars)
        + [vmem] * len(arrays)
        + [anywhere] * len(before),
        out_specs=[vmem] * len(outs) + [anywhere] * len(wholes),
        scratch_shapes=[pltpu.VMEM((rows, width), kind) for tokens, rows, width, kind in wholes]
        + [pltpu.SemaphoreType.DMA(())] * len(wholes),
        input_output_aliases={given + n: len(outs) + n for n in range(len(before))},
        compiler_params=pltpu.CompilerParams(vmem_limit_bytes=limit << 20),
        cost_estimate=CHEAP,
        name=name,
    )(*scalars, *arrays, *before)


def put_rows(k, value, whole, sem):
    rows = value.shape[0]
    copy = pltpu.make_async_copy(value, whole.at[pl.ds(k * rows, rows), :], sem)
    copy.start()
    return copy


def rms(value):
    return lax.rsqrt(jnp.mean(value * value, axis=-1, keepdims=True) + 1e-06)


def rms_back(grad, normed, scale):
    return scale * (grad - normed * jnp.mean(grad * normed, axis=-1, keepdims=True))


def dot_rows(a, b):
    return lax.dot_general(a, b, ROWS, preferred_element_type=f32)


def picked(end, total, got):
    return jnp.where(end[0] == 1, got[...], total[...]).astype(f32)


def forward_kernel(k, again, end, total, got, x, gains, gate_w, up_w, down_t, *rest):
    norms, stats, pre, part, low, pack, sem = rest[again:]
    width, units = x.shape[1], gate_w.shape[1]
    attn = picked(end, total, got)
    scale = rms(attn)
    normed = attn * scale
    norms[:, :width] = normed
    middle = x[...].astype(f32) + normed * gains[1:2, :]
    norms[:, width:] = middle
    middle_scale = rms(middle)
    lane = lax.broadcasted_iota(jnp.int32, stats.shape, 1)
    stats[...] = jnp.where(lane == 0, scale, middle_scale)
    act = (middle * middle_scale * gains[2:3, :]).astype(bf16)
    pack[:, units:] = act
    gated = dot(act, gate_w[...])
    upper = dot(act, up_w[...])
    pre[:, :units] = gated
    pre[:, units:] = upper
    unit = (gated * jax.nn.sigmoid(gated) * upper).astype(bf16)
    pack[:, :units] = unit
    copy = put_rows(k, pack, low, sem)
    part[...] = dot_rows(unit, down_t[...]).astype(bf16)
    copy.wait()


def backward_kernel(k, again, end, total, got, norms, pre, cot, gains, gate_w, up_w, down_t, *rest):
    sums, part, low, out, pack, done, sem, out_sem = rest[again:]
    width, units = cot.shape[1], gate_w.shape[1]
    ffn = picked(end, total, got)
    scale = rms(ffn)
    normed = ffn * scale
    done[...] = (norms[:, width:] + normed * gains[3:4, :]).astype(bf16)
    out_copy = put_rows(k, done, out, out_sem)
    grad = cot[...].astype(f32)
    sums[...] = jnp.sum(grad * normed, axis=0, keepdims=True)
    grad_ffn = rms_back(grad * gains[3:4, :], normed, scale).astype(bf16)
    pack[:, 2 * units :] = grad_ffn
    grad_units = dot(grad_ffn, down_t[...])
    gated = pre[:, :units]
    sig = jax.nn.sigmoid(gated)
    low_gate = (grad_units * pre[:, units:] * sig * (1.0 + gated * (1.0 - sig))).astype(bf16)
    low_up = (grad_units * gated * sig).astype(bf16)
    pack[:, :units] = low_gate
    pack[:, units : 2 * units] = low_up
    copy = put_rows(k, pack, low, sem)
    part[...] = (dot_rows(low_gate, gate_w[...]) + dot_rows(low_up, up_w[...])).astype(bf16)
    copy.wait()
    out_copy.wait()


def attn_back_kernel(k, again, end, total, got, norms, stats, cot, gains, *rest):
    sums, dmid, dattn, pack, sem = rest[again:]
    width = cot.shape[1]
    grad = picked(end, total, got)
    scale, middle_scale = stats[:, 0:1], stats[:, 1:2]
    normed = norms[:, width:] * middle_scale
    sums[0:1, :] = jnp.sum(grad * normed, axis=0, keepdims=True)
    middle = cot[...].astype(f32) + rms_back(grad * gains[2:3, :], normed, middle_scale)
    dmid[...] = middle
    normed = norms[:, :width]
    sums[1:2, :] = jnp.sum(middle * normed, axis=0, keepdims=True)
    pack[...] = rms_back(middle * gains[1:2, :], normed, scale).astype(bf16)
    put_rows(k, pack, dattn, sem).wait()


def weight_grad_kernel(left, right, out):
    out[...] = lax.dot_general(left[...], right[...], COLS, preferred_element_type=f32).astype(bf16)


def weight_grad(left, first, width, right, place, right_width):
    tokens = left.shape[0]
    step = 512
    return pl.pallas_call(
        weight_grad_kernel,
        out_shape=jax.ShapeDtypeStruct((width, right_width), bf16),
        grid=(width // step,),
        in_specs=[
            pl.BlockSpec((tokens, step), lambda i: (0, first // step + i)),
            pl.BlockSpec((tokens, right_width), lambda i: (0, place)),
        ],
        out_specs=pl.BlockSpec((step, right_width), lambda i: (i, 0)),
        compiler_params=pltpu.CompilerParams(vmem_limit_bytes=60 << 20),
        cost_estimate=CHEAP,
        name="weight_grad",
    )(left, right)


def run_ticks(parts, computes, head_index, head_count, fill):
    carry = []
    stages = 4 * len(computes)
    ticks = stages + len(parts) - 1
    if head_count != 4:
        for n, compute in enumerate(computes):
            sums = [lax.psum(part, "head") for part in parts]
            parts = []
            for k, part in enumerate(sums):
                before = parts[k - 1] if k else None
                parts.append(compute(k, jnp.zeros((1,), jnp.int32), part, part, before))
        for t in range(ticks):
            carry = fill[t](carry) if t in fill else carry
        return parts, carry
    end = jnp.where((head_index == 0) | (head_index == 3), 1, 0).astype(jnp.int32).reshape(1)
    states = [(part,) for part in parts]
    for t in range(ticks):
        at = {(t - k) % 4: k for k in range(len(parts)) if 0 <= t - k < stages}
        live = [k for k in range(len(parts)) if t - k < stages + 1]
        own = states[at[0]][0] if 0 in at else None
        part, total, send = relay(
            end, states[at[1]] if 1 in at else None, states[at[2]] if 2 in at else None, own
        )
        late = states[at[3]] if 3 in at else ()
        if part is not None or total is not None:
            part, total, send, late, carry = lax.optimization_barrier((part, total, send, late, carry))
        if 3 in at:
            states[at[3]] = late
        if 1 in at:
            states[at[1]] = (part, lax.ppermute(part, "head", [(1, 2), (2, 1)]))
        if 0 in at and 2 in at:
            got = lax.ppermute(send, "head", [(0, 1), (3, 2), (1, 0), (2, 3)])
            states[at[0]] = (own, got[: own.shape[0]])
            states[at[2]] = (total, got[: total.shape[0]])
        elif 0 in at:
            states[at[0]] = (own, lax.ppermute(own, "head", [(0, 1), (3, 2)]))
        elif 2 in at:
            states[at[2]] = (total, lax.ppermute(total, "head", [(1, 0), (2, 3)]))
        if 3 in at:
            k = at[3]
            before = states[k - 1][0] if k else None
            states[k] = (computes[(t - k) // 4](k, end, *states[k], before),)
        if t in fill:
            carry = fill[t](carry)
        held, carry = lax.optimization_barrier(([states[k] for k in live], carry))
        for k, state in zip(live, held):
            states[k] = state
    return [state[0] for state in states], carry


def head_mean(value):
    row = lax.broadcasted_iota(jnp.int32, (128, 128), 0) // HD
    col = lax.broadcasted_iota(jnp.int32, (128, 128), 1) // HD
    ones = jnp.where(row == col, 1.0 / HD, 0.0).astype(bf16)
    hi, mid, lo = split3(value)
    return dot(hi.astype(bf16), ones) + dot(mid.astype(bf16), ones) + dot(lo.astype(bf16), ones)


def partner(value):
    lane = lax.broadcasted_iota(jnp.int32, value.shape, 1) % HD
    return jnp.where(lane < HD // 2, pltpu.roll(value, 128 - HD // 2, 1), pltpu.roll(value, HD // 2, 1))


def text_norm_kernel(pre, gain, out):
    wide = pre.shape[1] // 2
    for p in range(wide // 128):
        cols = slice(p * 128, p * 128 + 128)
        value = pre[:, cols].astype(f32)
        out[:, cols] = (value * lax.rsqrt(head_mean(value * value) + 1e-6) * gain[...]).astype(bf16)
    out[:, wide:] = pre[:, wide:]


def text_norm(pre, gain):
    return pl.pallas_call(
        text_norm_kernel, out_shape=jax.ShapeDtypeStruct(pre.shape, bf16), name="text_norm", cost_estimate=CHEAP
    )(pre, gain)


def qkv_kernel(count, rows, wide, roles, x, gain, qgain, kgain, cos, sin, *rest):
    pieces, (act, scale, pre, kv, query, query_t, weight, sem) = rest[:count], rest[count:]
    copies = []
    for k in range(count):
        start = pl.multiple_of(roles[k] * rows, rows)
        copies.append(pltpu.make_async_copy(pieces[k], weight.at[pl.ds(start, rows), :], sem.at[k]))
    for c in copies:
        c.start()
    value = x[...].astype(f32)
    inverse = lax.rsqrt(jnp.mean(value * value, axis=-1, keepdims=True) + 1e-6)
    scale[...] = inverse
    act[...] = (value * inverse * gain[0:1, :]).astype(bf16)
    for c in copies:
        c.wait()
    pre[...] = dot(act[...], weight[:, : 2 * wide])
    kv[:, wide:] = dot(act[...], weight[:, 2 * wide :]).astype(bf16)
    for p in range(wide // 128):
        cols = slice(p * 128, p * 128 + 128)
        for which, out_gain in ((0, qgain), (1, kgain)):
            raw = pre[:, which * wide + p * 128 : which * wide + p * 128 + 128]
            raw = raw * lax.rsqrt(head_mean(raw * raw) + 1e-6) * out_gain[...]
            raw = raw * cos[...] + partner(raw) * sin[...]
            if which == 1:
                kv[:, cols] = raw.astype(bf16)
            else:
                raw = raw.astype(bf16).astype(f32) * HD**-0.5
                query[:, cols] = raw.astype(bf16)
                query_t[cols, :] = raw.T.astype(bf16)


def project(roles, x, gain, qgain, kgain, cos, sin, pieces, wide):
    count = len(pieces)
    rows = pieces[0].shape[0]
    tokens, width = x.shape
    shape = jax.ShapeDtypeStruct
    return pl.pallas_call(
        functools.partial(qkv_kernel, count, rows, wide),
        out_shape=(
            shape((tokens, width), bf16),
            shape((tokens, 1), f32),
            shape((tokens, 2 * wide), f32),
            shape((tokens, 2 * wide), bf16),
            shape((tokens, wide), bf16),
            shape((wide, tokens), bf16),
            shape((width, 3 * wide), bf16),
        ),
        in_specs=[pl.BlockSpec(memory_space=pltpu.SMEM)]
        + [pl.BlockSpec(memory_space=pltpu.VMEM)] * 6
        + [pl.BlockSpec(memory_space=pltpu.HBM)] * count,
        out_specs=(pl.BlockSpec(memory_space=pltpu.VMEM),) * 7,
        scratch_shapes=[pltpu.SemaphoreType.DMA((count,))],
        compiler_params=pltpu.CompilerParams(vmem_limit_bytes=60 << 20),
        cost_estimate=CHEAP,
        name="project",
    )(roles, x, gain, qgain, kgain, cos, sin, *pieces)


def mix_kernel(heads, gate, sums, cross, mixed, self_t, cross_t, lse, cross_lse):
    for p in range((heads + 1) // 2):
        both = []
        for h in range(2 * p, 2 * p + 2):
            if h >= heads:
                both.append(jnp.zeros_like(both[0]))
                continue
            rows = slice(h * HD, h * HD + HD)
            den, cross_den = sums[h, HD : HD + 1, :], cross[h, HD : HD + 1, :]
            lse[h : h + 1, :] = jnp.log(den)
            cross_lse[h : h + 1, :] = jnp.log(cross_den)
            own = sums[h, :HD, :] / den
            other = cross[h, :HD, :] / cross_den
            self_t[rows, :] = own
            cross_t[rows, :] = other
            both.append(own + gate[h] * other)
        mixed[:, p * 128 : p * 128 + 128] = jnp.concatenate(both, axis=0).T.astype(bf16)


def mix(gate, sums, cross, wide):
    heads, _, tokens = sums.shape
    shape = jax.ShapeDtypeStruct
    return pl.pallas_call(
        functools.partial(mix_kernel, heads),
        out_shape=(
            shape((tokens, wide), bf16),
            shape((heads * HD, tokens), f32),
            shape((heads * HD, tokens), f32),
            shape((heads, tokens), f32),
            shape((heads, tokens), f32),
        ),
        in_specs=[pl.BlockSpec(memory_space=pltpu.SMEM)] + [pl.BlockSpec(memory_space=pltpu.VMEM)] * 2,
        compiler_params=pltpu.CompilerParams(vmem_limit_bytes=SMALL_MIB << 20),
        name="mix",
        cost_estimate=CHEAP,
    )(gate, sums, cross)


def unmix_kernel(heads, gate, weight, self_t, cross_t, grad, tok, tok_t, ctok, ctok_t, delta, cdelta, cgate):
    width = tok.shape[0]
    for p in range((heads + 1) // 2):
        cols = slice(p * 128, p * 128 + 128)
        value = dot(grad[...], weight[:, cols])
        lane = lax.broadcasted_iota(jnp.int32, (width, 128), 1) // HD
        gates = jnp.where(lane == 0, gate[2 * p], gate[min(2 * p + 1, heads - 1)])
        tok[:, cols] = value.astype(bf16)
        ctok[:, cols] = (value * gates).astype(bf16)
        turned = value.T
        for h in range(2 * p, 2 * p + 2):
            rows = slice(h * HD, h * HD + HD)
            part = turned[(h % 2) * HD : (h % 2) * HD + HD, :]
            tok_t[rows, :] = part.astype(bf16)
            if h >= heads:
                ctok_t[rows, :] = part.astype(bf16)
                continue
            low = (part * gate[h]).astype(bf16)
            ctok_t[rows, :] = low
            delta[h : h + 1, :] = jnp.sum(part.astype(bf16).astype(f32) * self_t[rows, :], axis=0, keepdims=True)
            cdelta[h : h + 1, :] = jnp.sum(low.astype(f32) * cross_t[rows, :], axis=0, keepdims=True)
            cgate[h : h + 1, :] = jnp.sum(part * cross_t[rows, :], axis=0, keepdims=True)


def unmix(gate, grad, weight, self_t, cross_t):
    tokens = self_t.shape[1]
    wide = weight.shape[1]
    heads = self_t.shape[0] // HD
    shape = jax.ShapeDtypeStruct
    return pl.pallas_call(
        functools.partial(unmix_kernel, heads),
        out_shape=(shape((tokens, wide), bf16), shape((wide, tokens), bf16)) * 2 + (shape((heads, tokens), f32),) * 3,
        in_specs=[pl.BlockSpec(memory_space=pltpu.SMEM)]
        + [pl.BlockSpec(memory_space=pltpu.VMEM)] * 4,
        compiler_params=pltpu.CompilerParams(vmem_limit_bytes=SMALL_MIB << 20),
        name="unmix",
        cost_estimate=CHEAP,
    )(gate, weight, self_t, cross_t, grad)


def norm_back(raw, gain, grad, cos=None, sin=None):
    scale = lax.rsqrt(head_mean(raw * raw) + 1e-6)
    normed = raw * scale
    if cos is not None:
        grad = grad * cos - partner(grad) * sin
    gain_grad = jnp.sum(grad * normed, axis=0, keepdims=True)
    grad = grad * gain
    return scale * (grad - normed * head_mean(grad * normed)), gain_grad


def text_back_kernel(pre, gain, grad, out):
    wide = pre.shape[1] // 2
    for p in range(wide // 128):
        cols = slice(p * 128, p * 128 + 128)
        out[:, cols] = norm_back(pre[:, cols].astype(f32), gain[...], grad[:, cols])[0].astype(bf16)
    out[:, wide:] = grad[:, wide:].astype(bf16)


def text_back(pre, gain, grad):
    return pl.pallas_call(
        text_back_kernel,
        out_shape=jax.ShapeDtypeStruct(grad.shape, bf16),
        name="text_back",
        cost_estimate=CHEAP,
    )(pre, gain, grad)


def project_back_kernel(wide, starts, pre, qgain, kgain, cos, sin, dqt, *rest):
    kvs, (out, qgrad, kgrad) = rest[: len(starts)], rest[len(starts) :]
    tokens = pre.shape[0]
    total = [jnp.zeros((1, 128), f32), jnp.zeros((1, 128), f32)]
    summed = lambda cols: sum(kv[start : start + tokens, cols].astype(f32) for kv, start in zip(kvs, starts))
    for p in range(wide // 128):
        cols = slice(p * 128, p * 128 + 128)
        grads = (dqt[cols, :] * HD**-0.5).T, summed(cols)
        for which, gain in ((0, qgain), (1, kgain)):
            at = slice(which * wide + p * 128, which * wide + p * 128 + 128)
            value, extra = norm_back(pre[:, at], gain[...], grads[which], cos[...], sin[...])
            out[:, at] = value.astype(bf16)
            total[which] = total[which] + extra
    out[:, 2 * wide :] = summed(slice(wide, 2 * wide)).astype(bf16)
    qgrad[...] = total[0]
    kgrad[...] = total[1]


def project_back(pre, qgain, kgain, cos, sin, dqt, kvs, starts):
    tokens, wide = pre.shape[0], pre.shape[1] // 2
    shape = jax.ShapeDtypeStruct
    return pl.pallas_call(
        functools.partial(project_back_kernel, wide, tuple(starts)),
        out_shape=(shape((tokens, 3 * wide), bf16), shape((1, 128), f32), shape((1, 128), f32)),
        name="project_back",
        cost_estimate=CHEAP,
        compiler_params=pltpu.CompilerParams(vmem_limit_bytes=60 << 20),
    )(pre, qgain, kgain, cos, sin, dqt, *kvs)


def finish_kernel(k, end, total, got, x, scale, gain, mid, mark, *rest):
    out, done, value, sem = rest[-4:]
    rows = mid.shape[0]
    inverse = scale[...]
    normed = x[...].astype(f32) * inverse
    grad = picked(end, total, got)[:rows] * gain[0:1, :]
    mean = jnp.mean(grad * normed, axis=-1, keepdims=True)
    value[...] = mid[...] + inverse * (grad - normed * mean)
    copy = pltpu.make_async_copy(value, out.at[pl.ds(k * rows, rows), :], sem)
    copy.start()
    done[...] = mark[...]
    copy.wait()


def finish(k, end, total, got, x, scale, gain, mid, mark, tokens, before):
    before = [] if before is None else [before]
    vmem = pl.BlockSpec(memory_space=pltpu.VMEM)
    return pl.pallas_call(
        functools.partial(finish_kernel, k),
        out_shape=[jax.ShapeDtypeStruct((tokens, mid.shape[1]), f32), jax.ShapeDtypeStruct(mark.shape, f32)],
        in_specs=[pl.BlockSpec(memory_space=pltpu.SMEM)] + [vmem] * 7 + [pl.BlockSpec(memory_space=pl.ANY)] * len(before),
        out_specs=[pl.BlockSpec(memory_space=pl.ANY), vmem],
        scratch_shapes=[pltpu.VMEM(mid.shape, f32), pltpu.SemaphoreType.DMA(())],
        input_output_aliases={8: 0} if before else {},
        name="finish",
        cost_estimate=CHEAP,
        compiler_params=pltpu.CompilerParams(vmem_limit_bytes=SMALL_MIB << 20),
    )(end, total, got, x, scale, gain, mid, mark, *before)


def touch_kernel(*refs):
    refs[-1][...] = refs[0][...]


def touch(value, arrays):
    return pl.pallas_call(
        touch_kernel,
        out_shape=jax.ShapeDtypeStruct(value.shape, value.dtype),
        in_specs=[pl.BlockSpec(memory_space=pltpu.VMEM)] * (1 + len(arrays)),
        cost_estimate=CHEAP,
        compiler_params=pltpu.CompilerParams(vmem_limit_bytes=SMALL_MIB << 20),
        name="touch",
    )(value, *arrays)


def gains_back_kernel(sums, mods, gains, gain_grad, mod_grad):
    for n in range(4):
        row = slice(n, n + 1)
        if n % 2 == 0:
            gain_grad[row, :] = sums[row, :] * (1.0 + mods[row, :])
            mod_grad[row, :] = sums[row, :] * gains[row, :]
        else:
            gate = jnp.tanh(mods[row, :])
            gain_grad[row, :] = sums[row, :] * gate
            mod_grad[row, :] = sums[row, :] * gains[row, :] * (1.0 - gate * gate)


def gains_back(sums, mods, gains):
    return pl.pallas_call(
        gains_back_kernel,
        out_shape=[jax.ShapeDtypeStruct(gains.shape, f32)] * 2,
        cost_estimate=CHEAP,
        name="gains_back",
    )(sums, mods, gains)


def vectors_kernel(mods, gains, out):
    out[0:1, :] = gains[0:1, :] * (1.0 + mods[0:1, :])
    out[1:2, :] = jnp.tanh(mods[1:2, :]) * gains[1:2, :]
    out[2:3, :] = gains[2:3, :] * (1.0 + mods[2:3, :])
    out[3:4, :] = jnp.tanh(mods[3:4, :]) * gains[3:4, :]


def vectors(mods, gains):
    return pl.pallas_call(
        vectors_kernel,
        out_shape=jax.ShapeDtypeStruct(gains.shape, f32),
        cost_estimate=CHEAP,
        name="vectors",
    )(mods, gains)


def per_device(
    seq_count,
    head_count,
    hidden_in,
    cond,
    captions,
    clip_lengths,
    ada_weight,
    norm_gains,
    qk_gains,
    w_query,
    w_key,
    w_value,
    w_out,
    cross_gate,
    w_text_key,
    w_text_value,
    w_gate,
    w_up,
    w_down,
    out_cotangent,
):
    local_rows, model_width = hidden_in.shape
    seq_index = lax.axis_index("seq")
    head_index = lax.axis_index("head")
    clips = clip_lengths.shape[0]
    cols = w_query.shape[1]
    heads = cols // HD
    wide = (cols + 127) // 128 * 128
    units = w_gate.shape[1]
    roles = seq_roles(seq_index, seq_count)
    pad = lambda v: jnp.pad(v, ((0, 0), (0, wide - cols))) if wide > cols else v
    cut = lambda v: v[:, :cols]

    spread = seq_count == 8
    core = lambda v: swap(v, "seq", 8, lambda i: i ^ 1)
    hold = lax.optimization_barrier
    axes = (("seq", seq_count), ("head", head_count))
    seq_hops, head_hops = hops("seq", seq_count), hops("head", head_count)
    finish_sum = lambda v: lax.psum_scatter(v, "seq", scatter_dimension=0, tiled=True)

    def hop(value, steps):
        for axis, bit in steps:
            value = value + swap(value, axis, dict(axes)[axis], lambda i: i ^ bit)
        return value

    clip_ends = jnp.cumsum(clip_lengths, dtype=jnp.int32)
    starts = clip_ends - clip_lengths
    text_rows = captions.reshape(-1, captions.shape[2])
    text_block = text_rows.shape[0] // seq_count
    text_ids = jnp.arange(clips, dtype=jnp.int32) * captions.shape[1]
    first_row = seq_index * local_rows
    place_info = jnp.concatenate([first_row[None], starts, clip_ends]).astype(jnp.int32)
    text_info = jnp.concatenate(
        [place_info, text_ids, text_ids + captions.shape[1], jnp.zeros((1,), jnp.int32)]
    )

    def self_info(which):
        return jnp.concatenate([place_info, starts, clip_ends, roles[which] * local_rows])

    places = first_row + jnp.arange(local_rows, dtype=jnp.int32)
    inside = (places[:, None] >= starts[None, :]) & (places[:, None] < clip_ends[None, :])
    position = places - jnp.sum(jnp.where(inside, starts[None, :], 0), axis=1, dtype=jnp.int32)
    lane = jnp.arange(128)
    frequency = 10000.0 ** (-(lane % (HD // 2)).astype(f32) / (HD // 2))
    angles = position.astype(f32)[:, None] * frequency[None, :]
    cos = jnp.cos(angles)
    sin = jnp.where(lane % HD < HD // 2, -1.0, 1.0)[None, :] * jnp.sin(angles)
    query_gain = jnp.tile(qk_gains[0], 2)[None, :]
    key_gain = jnp.tile(qk_gains[1], 2)[None, :]

    cond_act = jax.nn.silu(cond).astype(bf16)
    piece_width = ada_weight.shape[1]
    mod_piece = matmul(cond_act[None, :], ada_weight)
    mine = lax.broadcasted_iota(jnp.int32, (seq_count * head_count, 1), 0) == seq_index * head_count + head_index
    modulation = jnp.where(mine, mod_piece, 0.0)
    modulation, w_query = hold((modulation, w_query))
    qkv_block = jnp.concatenate([pad(w_query), pad(w_key), pad(w_value)], axis=1)
    out_block = pad(w_out.T)
    slab_width = text_rows.shape[1] // seq_count
    if spread:
        modulation = hop(modulation, seq_hops[:1])
        modulation, text_rows = hold((modulation, text_rows))
    own_text = lax.dynamic_slice_in_dim(text_rows, seq_index * slab_width, slab_width, 1)
    text_part = matmul(own_text, jnp.concatenate([pad(w_text_key), pad(w_text_value)], axis=1)).astype(bf16)

    def queries_keys(pieces):
        return project(roles, hidden_in, rows, query_gain, key_gain, cos, sin, pieces, wide)

    def part_sums(group, blocks, before=None):
        return attend(self_info(jnp.array(group)), query_t, blocks, heads, clips, before)

    if spread:
        near = swap(qkv_block, "seq", 8, first_way)
        next_ = swap(qkv_block, "seq", 8, other_way)
        modulation = hop(modulation, head_hops[:1])
        text_pre = lax.psum(text_part, "seq")
        gate_w = lax.all_gather(w_gate, "seq", axis=0, tiled=True)
        near, next_, modulation = hold((near, next_, modulation))
        far = swap(near, "seq", 8, other_way)
        modulation = hop(modulation, head_hops[1:])
        modulation = hop(modulation, seq_hops[1:])
        qkv_pieces = [qkv_block, near, next_, far]
        qkv_pieces = qkv_pieces + [core(v) for v in qkv_pieces]
        modulation, qkv_pieces, out_block = hold((modulation, qkv_pieces, out_block))
        modulation = modulation.reshape(4, model_width)
        rows = vectors(modulation, norm_gains)
        act_a, x_scale, pre, kv_own, queries, query_t, w_qkv = queries_keys(qkv_pieces)
        kv_own, modulation, out_block = hold((kv_own, modulation, out_block))
        near = swap(kv_own, "seq", 8, first_way)
        next_ = swap(kv_own, "seq", 8, other_way)
        kv_peer = core(kv_own)
        out_near = swap(out_block, "seq", 8, first_way)
        out_next = swap(out_block, "seq", 8, other_way)
        sums = part_sums((0, 4), [kv_own, kv_peer])
        near, next_, sums, out_near, out_next = hold((near, next_, sums, out_near, out_next))
        far = swap(near, "seq", 8, other_way)
        out_far = swap(out_near, "seq", 8, other_way)
        near_peer, next_peer = core(near), core(next_)
        out_peers = [core(out_block), core(out_near), core(out_next)]
        sums = part_sums((1, 2, 5, 6), [near, next_, near_peer, next_peer], sums)
        ud_block = jnp.concatenate([w_up, w_down.T], axis=1)
        far, sums, out_far, text_pre, ud_block = hold((far, sums, out_far, text_pre, ud_block))
        far_peer = core(far)
        ud_near = swap(ud_block, "seq", 8, first_way)
        ud_next = swap(ud_block, "seq", 8, other_way)
        out_t = place([out_block, out_near, out_next, out_far] + out_peers + [core(out_far)], roles)
        text_pieces = [text_norm(text_pre, key_gain)]
        cross_sums = attend(text_info, query_t, text_pieces, heads, clips)
        sums = part_sums((3, 7), [far, far_peer], sums)
        pieces = [kv_own, near, next_, far, kv_peer, near_peer, next_peer, far_peer]
    else:
        modulation = lax.psum(modulation, ("seq", "head"))
        text_pre = lax.psum(text_part, "seq")
        qkv_pieces = gather_pieces(qkv_block, seq_count)
        modulation = modulation.reshape(4, model_width)
        rows = vectors(modulation, norm_gains)
        act_a, x_scale, pre, kv_own, queries, query_t, w_qkv = queries_keys(qkv_pieces)
        pieces = gather_pieces(kv_own, seq_count)
        text_pieces = [text_norm(text_pre, key_gain)]
        out_t = place(gather_pieces(out_block, seq_count), roles)
        sums = part_sums(tuple(range(seq_count)), pieces)
        cross_sums = attend(text_info, query_t, text_pieces, heads, clips)
        gate_w = lax.all_gather(w_gate, "seq", axis=0, tiled=True)
    gate_local = jnp.tanh(cross_gate)
    mixed, self_t, cross_t, self_lse, cross_lse = mix(gate_local, sums, cross_sums, wide)
    attn_part = matmul(mixed, out_t, ROWS).astype(bf16)

    late = {}

    def split_weights(pieces):
        return place(pieces, roles, (units, units), 53)

    def fill_near(carry):
        return [ud_near, ud_next]

    def fill_far(carry):
        near, next_ = carry
        return [near, next_, swap(near, "seq", 8, other_way), core(ud_block), core(near), core(next_)]

    def fill_weights(carry):
        late["up"], late["down"] = split_weights([ud_block] + carry + [core(carry[2])])
        late["rows"] = touch(rows, [gate_w, late["up"], late["down"]])
        return [late["rows"]]

    if not spread:
        weights = gather_pieces(jnp.concatenate([w_up, w_down.T], axis=1), seq_count)
        late["up"], late["down"] = split_weights(weights)
        late["rows"] = rows
    chunk_count = 4
    chunk = local_rows // chunk_count
    rows_of = lambda v, k: v[k * chunk : (k + 1) * chunk]
    kept = [{} for _ in range(chunk_count)]


    tall, thin = (chunk, model_width), (chunk, units)
    whole = lambda width: (local_rows, chunk, width, bf16)

    def feed_forward(k, end, total, got, before):
        keep = kept[k]
        outs = [((chunk, 2 * model_width), f32), ((chunk, 128), f32), ((chunk, 2 * units), f32), (tall, bf16)]
        arrays = [total, got, rows_of(hidden_in, k), late["rows"], gate_w, late["up"], late["down"]]
        keep["norms"], keep["stats"], keep["pre"], part, late["first"] = staged(
            forward_kernel, k, outs, [whole(units + model_width)], [end], arrays,
            [late["first"]] if k else None, "feed_forward",
        )
        return part

    def feed_back(k, end, total, got, before):
        keep = kept[k]
        arrays = [total, got, keep["norms"], keep["pre"], rows_of(out_cotangent, k), late["rows"]]
        keep["uf"], part, late["second"], late["hidden"] = staged(
            backward_kernel, k, [((1, model_width), f32), (tall, bf16)],
            [whole(2 * units + model_width), whole(model_width)], [end], arrays + [gate_w, late["up"], late["down"]],
            [late["second"], late["hidden"]] if k else None, "feed_back",
        )
        return part

    def attn_back(k, end, total, got, before):
        keep = kept[k]
        arrays = [total, got, keep["norms"], keep["stats"], rows_of(out_cotangent, k), rows]
        keep["sums"], keep["dmid"], late["dattn"] = staged(
            attn_back_kernel, k, [((2, model_width), f32), (tall, f32)], [whole(model_width)], [end], arrays,
            [late["dattn"]] if k else None, "attn_back", 60,
        )
        return keep["sums"]

    total_of = lambda name, n: sum(keep[name][n] for keep in kept)

    def fill_down(carry):
        return [weight_grad(late["second"], 2 * units, model_width, late["first"], 0, units)]

    def fill_gate(carry):
        late["down_sum"] = finish_sum(carry[0])
        (first, second), carry = hold(((late["first"], late["second"]), carry))
        late["first"], late["second"] = first, second
        return [weight_grad(first, units, model_width, second, 0, units)]

    def fill_up(carry):
        late["gate_sum"] = finish_sum(carry[0])
        (first, second), carry = hold(((late["first"], late["second"]), carry))
        return [weight_grad(first, units, model_width, second, 1, units)]

    def fill_last(carry):
        late["up_sum"] = finish_sum(carry[0])
        return []

    fills = {8 + chunk_count - 1: fill_down, 8 + chunk_count: fill_gate, 8 + chunk_count + 1: fill_up, 8 + chunk_count + 2: fill_last}
    first_parts = [rows_of(attn_part, k) for k in range(chunk_count)]
    if spread:
        fills.update({0: fill_near, 1: fill_far, 2: fill_weights})
    run_ticks(
        first_parts, [feed_forward, feed_back, attn_back], head_index, head_count, fills
    )
    grad_attn_low, hidden_out = late["dattn"], late["hidden"]
    down_grad, gate_grad, up_grad = late["down_sum"], late["gate_sum"], late["up_sum"]

    grad_self_tok, grad_self_t, grad_cross_tok, grad_cross_t, self_delta, cross_delta, gate_rows = unmix(
        gate_local, grad_attn_low, out_t, self_t, cross_t
    )
    cross_gate_part = jnp.sum(gate_rows, axis=1) * (1.0 - gate_local * gate_local)

    def back(group, parts, before=None):
        return attend_back(
            self_info(jnp.array(group)), query_t, grad_self_t, queries, grad_self_tok, self_lse, self_delta,
            [pieces[g] for g in group], heads, clips, bf16, parts, before,
        )

    def cross_back(before):
        return attend_back(
            text_info, query_t, grad_cross_t, queries, grad_cross_tok, cross_lse, cross_delta,
            text_pieces, heads, clips, f32, 1, before,
        )

    if spread:
        dq, _, kv_mine, kv_theirs = back((3, 2, 7, 6), 2)
        kv_got = core(kv_theirs)
        kv_mine, low = hold((kv_mine, grad_attn_low))
        out_part = matmul(low, mixed, COLS).astype(bf16)
        total = add_low(kv_mine, kv_got)
        total, dq, out_part = hold((total, dq, out_part))
        first = swap(total, "seq", 8, other_way)
        dq, text_dot, cross_kv = cross_back(dq)
        dq, cross_kv, down_grad = hold((dq, cross_kv, down_grad))
        dq, _, kv_mine, kv_theirs = back((1, 5), 2, dq)
        first, kv_mine, kv_theirs = hold((first, kv_mine, kv_theirs))
        total = kv_mine.astype(f32) + core(kv_theirs).astype(f32) + first[:local_rows].astype(f32)
        total = total.astype(bf16)
        second = swap(total, "seq", 8, first_way)
        dq, _, kv_mine, kv_theirs = back((0, 4), 2, dq)
        second, kv_mine, kv_theirs, gate_grad = hold((second, kv_mine, kv_theirs, gate_grad))
        kv_parts, kv_starts = [kv_mine, core(kv_theirs), first, second], (0, 0, local_rows, 0)
    else:
        dq, _, kv_all = back(tuple(range(seq_count)), 1)
        dq, text_dot, cross_kv = cross_back(dq)
        out_part = weight_grad(grad_attn_low, 0, model_width, mixed, 0, wide)
        kv_parts, kv_starts = [finish_sum(kv_all)], (0,)
    qkv_low, grad_query_gain, grad_key_gain = project_back(
        pre, query_gain, key_gain, cos, sin, dq, kv_parts, kv_starts
    )
    x_normed = hidden_in.astype(f32) * x_scale
    act_part = matmul(qkv_low, w_qkv, ROWS)
    sum_a = jnp.sum(act_part * x_normed, axis=0)
    act_low, qkv_low, cross_kv, gate_grad = hold((act_part.astype(bf16), qkv_low, cross_kv, gate_grad))
    fold = lambda v: v[0, :HD] + v[0, HD:]
    pair_gains = jnp.concatenate([fold(grad_query_gain), fold(grad_key_gain + text_dot / key_gain)])
    tail = jnp.stack([sum_a, jnp.pad(pair_gains, (0, model_width - 2 * HD))])
    tail = jnp.pad(tail, ((0, 14), (0, 0))).astype(bf16)
    small = [total_of("sums", 1), total_of("sums", 0), total_of("uf", 0)]
    cross_row = jnp.pad(cross_gate_part, (2 * HD, model_width - 2 * HD - heads))

    def collect(k, end, total, got, before):
        if k == 0:
            late["tail"] = jnp.where(end[0] == 1, got, total)[chunk:].astype(f32)
        arrays = rows_of(hidden_in, k), rows_of(x_scale, k), rows, kept[k]["dmid"]
        mark = jnp.zeros((8, 128), f32) if before is None else before
        late["input"], mark = finish(k, end, total, got, *arrays, mark, local_rows, late.get("input"))
        return mark

    late["out_sum"] = finish_sum(out_part)

    def fill0(carry):
        return [text_back(text_pre, key_gain, cross_kv)]

    def fill1(carry):
        low, carry = hold((qkv_low, carry))
        part = weight_grad(act_a, 0, model_width, low, 0, 3 * wide)
        if not spread:
            return [lax.psum(carry[0], "seq"), part]
        return [scatter_first(scatter_start(carry[0], seq_index), seq_index), part]

    def fill2(carry):
        late["qkv"] = finish_sum(carry[1])
        down, up, text = hold((down_grad, up_grad, carry[0]))
        late["down"] = widen([down], True)
        if not spread:
            return [text, late["down"], up]
        own = add_low(*scatter_second(text, seq_index))
        text = [own, swap(own, "seq", 8, first_way), swap(own, "seq", 8, other_way)]
        return [text, late["down"], up]

    def fill3(carry):
        late["down"] = carry[1]
        gate, text = hold((gate_grad, carry[0]))
        late["up"], late["gate"] = widen([carry[2]]), widen([gate])
        tail_rows = [late["tail"][0]] + small + [jnp.pad(late["tail"][1, : 2 * HD], (0, model_width - 2 * HD)) + cross_row]
        values = jnp.pad(jnp.stack(tail_rows), ((0, 3), (0, 0)))
        if not spread:
            return [text, late["up"], late["gate"], lax.psum(values, "seq")]
        text = text + [swap(text[1], "seq", 8, other_way)]
        text = text + [core(v) for v in text[:3]]
        return [text, late["up"], late["gate"], hop(values, seq_hops[:2])]

    def fill4(carry):
        text, late["up"], late["gate"], values = carry
        out, text = hold((late["out_sum"], text))
        late["out"] = widen([out], True)
        if spread:
            text = text + [core(text[3])]
            values = hop(values, seq_hops[2:])
        return [values, text, late["out"]]

    def fill5(carry):
        values, text, late["out"] = carry
        gain_grad, mod_grad = gains_back(values[:4], modulation, norm_gains)
        own_mod = lax.dynamic_slice_in_dim(
            mod_grad.reshape(-1), (seq_index * head_count + head_index) * piece_width, piece_width
        )
        text = place(text, roles) if spread else text
        text_grad = matmul(own_text, text, COLS)
        return [gain_grad, values[4], text_grad, cond_act.astype(f32)[:, None] * own_mod[None, :]]

    parts = [rows_of(act_low, k) for k in range(chunk_count)]
    parts[0] = jnp.concatenate([parts[0], tail])
    fills = dict(enumerate([fill0, fill1, fill2, fill3, fill4, fill5]))
    _, (norm_gains_grad, values, text_grad, ada_grad) = run_ticks(parts, [collect], head_index, head_count, fills)
    input_grad = late["input"]
    own_qkv = widen([late["qkv"]])

    qk_gains_grad = values[: 2 * HD].reshape(2, HD)
    cross_gate_grad = values[2 * HD : 2 * HD + heads]
    return (
        hidden_out,
        input_grad,
        ada_grad,
        norm_gains_grad,
        qk_gains_grad,
        cut(own_qkv[:, :wide]),
        cut(own_qkv[:, wide : 2 * wide]),
        cut(own_qkv[:, 2 * wide : 3 * wide]),
        late["out"][:cols],
        cross_gate_grad,
        cut(text_grad[:, :wide]),
        cut(text_grad[:, wide:]),
        late["gate"],
        late["up"],
        late["down"],
    )


def solution(mesh):
    in_specs = (
        P("seq", None),
        P(),
        P(),
        P(),
        P(None, ("seq", "head")),
        P(),
        P(),
        P("seq", "head"),
        P("seq", "head"),
        P("seq", "head"),
        P("head", "seq"),
        P("head"),
        P("seq", "head"),
        P("seq", "head"),
        P("seq", "head"),
        P("seq", "head"),
        P("head", "seq"),
        P("seq", None),
    )
    out_specs = (
        P("seq", None),
        P("seq", None),
        P(None, ("seq", "head")),
        P(),
        P(),
        P("seq", "head"),
        P("seq", "head"),
        P("seq", "head"),
        P("head", "seq"),
        P("head"),
        P("seq", "head"),
        P("seq", "head"),
        P("seq", "head"),
        P("seq", "head"),
        P("head", "seq"),
    )
    body = functools.partial(per_device, mesh.shape["seq"], mesh.shape["head"])
    return jax.shard_map(body, mesh=mesh, in_specs=in_specs, out_specs=out_specs, check_vma=False)
```

```python
import functools
import jax
import jax.numpy as jnp
from jax import lax
from jax.experimental import pallas as pl
from jax.experimental.pallas import tpu as pltpu
from jax.sharding import PartitionSpec as P

HD = 64
MASK = 8192.0
CHEAP = pl.CostEstimate(flops=1, bytes_accessed=1, transcendentals=0)
ATTEND_MIB = 60
BACK_MIB = 60
SMALL_MIB = 16


def dot(a, b):
    return lax.dot_general(a, b, (((1,), (0,)), ((), ())), preferred_element_type=jnp.float32)


def split3(v):
    hi = v.astype(jnp.bfloat16).astype(jnp.float32)
    mid = (v - hi).astype(jnp.bfloat16).astype(jnp.float32)
    return hi, mid, v - hi - mid


def bounds(info, base, clips, ids):
    start = jnp.full(ids.shape, 1 << 30, jnp.int32)
    end = jnp.zeros(ids.shape, jnp.int32)
    for c in range(clips):
        start = jnp.where(ids == c, info[base + c], start)
        end = jnp.where(ids == c, info[base + clips + c], end)
    return start, end


def query_ext(info, clips, width, scale):
    ids = lax.broadcasted_iota(jnp.int32, (16, width), 0)
    place = info[0] + lax.broadcasted_iota(jnp.int32, (16, width), 1)
    start, end = bounds(info, 1, clips, ids)
    return jnp.where((place >= start) & (place < end), scale, 0.0)


def key_ext(info, clips, row, rows, piece):
    ids = lax.broadcasted_iota(jnp.int32, (rows, 128), 1)
    step = min(rows, piece)
    parts = []
    for k in range(rows // step):
        at = row + k * step
        first = info[1 + 4 * clips + at // piece] + lax.rem(at, piece)
        parts.append(first + lax.broadcasted_iota(jnp.int32, (step, 128), 0))
    place = parts[0] if len(parts) == 1 else jnp.concatenate(parts, axis=0)
    start, end = bounds(info, 1 + 2 * clips, clips, ids)
    inside = (place >= start) & (place < end)
    value = jnp.where(ids < clips, jnp.where(inside, 0.0, -1.0), jnp.where(ids < clips + 3, 1.0, 0.0))
    return value.astype(jnp.bfloat16)


def fill_ext(dst, h, src, tail):
    width = src.shape[1]
    half = h % 2
    zero = jnp.zeros((HD, width), jnp.bfloat16)
    dst[h, half * HD : half * HD + HD, :] = src[h * HD : h * HD + HD, :]
    dst[h, (1 - half) * HD : (1 - half) * HD + HD, :] = zero
    dst[h, 128:144, :] = tail.astype(jnp.bfloat16)
    dst[h, 144:256, :] = jnp.zeros((112, width), jnp.bfloat16)


def stack_rows(heads, rows, clips, width):
    ids = lax.broadcasted_iota(jnp.int32, (16, width), 0)
    total = jnp.zeros((16, width), jnp.float32)
    for k, row in enumerate(rows):
        total = jnp.where(ids == clips + k, jnp.broadcast_to(row, (16, width)), total)
    return total


def load_pieces(pieces, kv, sem):
    rows = pieces[0].shape[0]
    return [
        pltpu.make_async_copy(piece, kv.at[pl.ds(k * rows, rows), :], sem.at[k])
        for k, piece in enumerate(pieces)
    ]


def fwd_kernel(heads, clips, count, tile, again, info, qt, *rest):
    before, pieces, (out, qx, kv, sem) = rest[:again], rest[again : again + count], rest[again + count :]
    copies = load_pieces(pieces, kv, sem)
    for c in copies:
        c.start()
    width = qt.shape[1]
    wide = qt.shape[0]
    ext = query_ext(info, clips, width, MASK)
    for h in range(heads):
        fill_ext(qx, h, qt, ext)
        out[h] = before[0][h] if again else jnp.zeros((80, width), jnp.float32)
    for c in copies:
        c.wait()
    steps = count * pieces[0].shape[0] // tile
    ones = jnp.ones((16, tile), jnp.bfloat16)

    def step(t, carry):
        rows = pl.ds(pl.multiple_of(t * tile, tile), tile)
        extra = key_ext(info, clips, t * tile, tile, pieces[0].shape[0])
        for p in range((heads + 1) // 2):
            kx = jnp.concatenate([kv[rows, p * 128 : p * 128 + 128], extra], axis=1)
            vt = kv[rows, wide + p * 128 : wide + p * 128 + 128].T
            for h in range(2 * p, min(2 * p + 2, heads)):
                half = h % 2
                probs = jnp.exp(dot(kx, qx[h])).astype(jnp.bfloat16)
                vx = jnp.concatenate([vt[half * HD : half * HD + HD, :], ones], axis=0)
                out[h] += dot(vx, probs)
        return carry

    lax.fori_loop(0, steps, step, 0)


def attend(info, qt, pieces, heads, clips, before=None, tile=1024):
    count = len(pieces)
    before = [] if before is None else [before]
    wide, width = qt.shape
    rows = pieces[0].shape[0]
    tile = min(tile, rows * count)
    return pl.pallas_call(
        functools.partial(fwd_kernel, heads, clips, count, tile, len(before)),
        out_shape=jax.ShapeDtypeStruct((heads, 80, width), jnp.float32),
        in_specs=[pl.BlockSpec(memory_space=pltpu.SMEM)]
        + [pl.BlockSpec(memory_space=pltpu.VMEM)] * (1 + len(before))
        + [pl.BlockSpec(memory_space=pltpu.HBM)] * count,
        out_specs=pl.BlockSpec(memory_space=pltpu.VMEM),
        scratch_shapes=[
            pltpu.VMEM((heads, 256, width), jnp.bfloat16),
            pltpu.VMEM((count * rows, 2 * wide), jnp.bfloat16),
            pltpu.SemaphoreType.DMA((count,)),
        ],
        compiler_params=pltpu.CompilerParams(vmem_limit_bytes=ATTEND_MIB << 20),
        cost_estimate=CHEAP,
        name="attend",
    )(info, qt, *before, *pieces)


def bwd_kernel(heads, clips, count, tile, again, info, qt, dot_t, q_tok, do_tok, lse, delta, *rest):
    before, pieces, rest = rest[:again], rest[again : again + count], rest[again + count :]
    dqt, kdot, grads, (qx, dox, qpad, dopad, kv, sem) = rest[0], rest[1], rest[2:-6], rest[-6:]
    copies = load_pieces(pieces, kv, sem)
    for c in copies:
        c.start()
    wide, width = qt.shape
    ext = query_ext(info, clips, width, MASK)
    for h in range(heads):
        p, half = h // 2, h % 2
        fill_ext(qx, h, qt, ext - stack_rows(heads, split3(lse[h : h + 1, :]), clips, width))
        fill_ext(dox, h, dot_t, -stack_rows(heads, split3(delta[h : h + 1, :]), clips, width))
        lane = lax.broadcasted_iota(jnp.int32, (width, 128), 1) // HD
        zero = jnp.zeros((width, 128), jnp.bfloat16)
        qpad[h] = jnp.where(lane == half, q_tok[:, p * 128 : p * 128 + 128], zero)
        dopad[h] = jnp.where(lane == half, do_tok[:, p * 128 : p * 128 + 128], zero)
    kdot[...] = jnp.zeros((1, 128), jnp.float32)
    dqt[...] = before[0][...] if again else jnp.zeros((wide, width), jnp.float32)
    for c in copies:
        c.wait()
    steps = count * pieces[0].shape[0] // tile

    def step(t, carry):
        rows = pl.ds(pl.multiple_of(t * tile, tile), tile)
        extra = key_ext(info, clips, t * tile, tile, pieces[0].shape[0])
        for p in range((heads + 1) // 2):
            cols = slice(p * 128, p * 128 + 128)
            vcols = slice(wide + p * 128, wide + p * 128 + 128)
            k_tile = kv[rows, cols]
            kx = jnp.concatenate([k_tile, extra], axis=1)
            vx = jnp.concatenate([kv[rows, vcols], extra], axis=1)
            kt = k_tile.T
            dk = jnp.zeros((tile, 128), jnp.float32)
            dv = jnp.zeros((tile, 128), jnp.float32)
            for h in range(2 * p, min(2 * p + 2, heads)):
                half = h % 2
                probs = jnp.exp(dot(kx, qx[h]))
                ds = (probs * dot(vx, dox[h])).astype(jnp.bfloat16)
                dqt[h * HD : h * HD + HD, :] += dot(kt[half * HD : half * HD + HD, :], ds)
                dk = dk + dot(ds, qpad[h])
                dv = dv + dot(probs.astype(jnp.bfloat16), dopad[h])
            kdot[...] += jnp.sum(dk * k_tile.astype(jnp.float32), axis=0, keepdims=True)
            part = grads[0].shape[0]
            if tile > part:
                for g, grad in enumerate(grads):
                    grad[:, cols] = dk[g * part : g * part + part, :].astype(grad.dtype)
                    grad[:, vcols] = dv[g * part : g * part + part, :].astype(grad.dtype)
                continue
            for g, grad in enumerate(grads):

                @pl.when(t // (steps // len(grads)) == g)
                def store(g=g, grad=grad, dk=dk, dv=dv, cols=cols, vcols=vcols):
                    start = (t - g * (steps // len(grads))) * tile
                    here = pl.ds(pl.multiple_of(start, tile), tile)
                    grad[here, cols] = dk.astype(grad.dtype)
                    grad[here, vcols] = dv.astype(grad.dtype)

        return carry

    lax.fori_loop(0, steps, step, 0)


def attend_back(info, qt, dot_t, q_tok, do_tok, lse, delta, pieces, heads, clips, kind, parts=1, before=None, tile=2048):
    count = len(pieces)
    before = [] if before is None else [before]
    wide, width = qt.shape
    rows = pieces[0].shape[0]
    tile = rows * count if rows * count <= tile else min(tile, rows * count // parts)
    return pl.pallas_call(
        functools.partial(bwd_kernel, heads, clips, count, tile, len(before)),
        out_shape=(
            jax.ShapeDtypeStruct((wide, width), jnp.float32),
            jax.ShapeDtypeStruct((1, 128), jnp.float32),
        )
        + (jax.ShapeDtypeStruct((count * rows // parts, 2 * wide), kind),) * parts,
        in_specs=[pl.BlockSpec(memory_space=pltpu.SMEM)]
        + [pl.BlockSpec(memory_space=pltpu.VMEM)] * (6 + len(before))
        + [pl.BlockSpec(memory_space=pltpu.HBM)] * count,
        out_specs=(pl.BlockSpec(memory_space=pltpu.VMEM),) * (2 + parts),
        scratch_shapes=[
            pltpu.VMEM((heads, 256, width), jnp.bfloat16),
            pltpu.VMEM((heads, 256, width), jnp.bfloat16),
            pltpu.VMEM((heads, width, 128), jnp.bfloat16),
            pltpu.VMEM((heads, width, 128), jnp.bfloat16),
            pltpu.VMEM((count * rows, 2 * wide), jnp.bfloat16),
            pltpu.SemaphoreType.DMA((count,)),
        ],
        compiler_params=pltpu.CompilerParams(vmem_limit_bytes=BACK_MIB << 20),
        cost_estimate=CHEAP,
        name="attend_back",
    )(info, qt, dot_t, q_tok, do_tok, lse, delta, *before, *pieces)


ROWS = (((1,), (1,)), ((), ()))
COLS = (((0,), (0,)), ((), ()))
f32 = jnp.float32
bf16 = jnp.bfloat16


def matmul(left, right, dims=None):
    if dims is None:
        return jnp.dot(left, right, preferred_element_type=f32)
    return lax.dot_general(left, right, dims, preferred_element_type=f32)


def first_way(i):
    return i ^ 2 if i % 2 == 0 else i ^ 4


def other_way(i):
    return i ^ 4 if i % 2 == 0 else i ^ 2


def swap(value, axis, count, to):
    return lax.ppermute(value, axis, [(i, to(i)) for i in range(count)])


def seq_roles(seq_index, seq_count):
    if seq_count != 8:
        return jnp.arange(seq_count, dtype=jnp.int32)
    peer = seq_index ^ 1

    def roles(i):
        even = i % 2 == 0
        return [i, jnp.where(even, i ^ 2, i ^ 4), jnp.where(even, i ^ 4, i ^ 2), i ^ 6]

    return jnp.stack(roles(seq_index) + roles(peer)).astype(jnp.int32)


def gather_pieces(block, seq_count):
    if seq_count != 8:
        whole = lax.all_gather(block, "seq", axis=0, tiled=False)
        return [whole[i] for i in range(seq_count)]
    near = swap(block, "seq", 8, first_way)
    next_ = swap(block, "seq", 8, other_way)
    far = swap(near, "seq", 8, other_way)
    mine = [block, near, next_, far]
    return mine + [swap(v, "seq", 8, lambda i: i ^ 1) for v in mine]


def place_kernel(count, rows, widths, roles, *rest):
    pieces, outs, sem = rest[:count], rest[count:-1], rest[-1]
    copies = []
    for k in range(count):
        to = pl.ds(pl.multiple_of(roles[k] * rows, rows), rows)
        first = 0
        for n, width in enumerate(widths):
            piece = pieces[k].at[:, first : first + width]
            copies.append(pltpu.make_async_copy(piece, outs[n].at[to, :], sem.at[k, n]))
            first += width
    for c in copies:
        c.start()
    for c in copies:
        c.wait()


def place(pieces, roles, widths=None, limit=SMALL_MIB):
    count = len(pieces)
    rows, width = pieces[0].shape
    outs = widths or (width,)
    placed = pl.pallas_call(
        functools.partial(place_kernel, count, rows, outs),
        out_shape=[jax.ShapeDtypeStruct((count * rows, w), pieces[0].dtype) for w in outs],
        in_specs=[pl.BlockSpec(memory_space=pltpu.SMEM)]
        + [pl.BlockSpec(memory_space=pltpu.HBM)] * count,
        out_specs=[pl.BlockSpec(memory_space=pltpu.VMEM)] * len(outs),
        scratch_shapes=[pltpu.SemaphoreType.DMA((count, len(outs)))],
        compiler_params=pltpu.CompilerParams(vmem_limit_bytes=limit << 20),
        cost_estimate=CHEAP,
        name="place",
    )(roles, *pieces)
    return placed if widths else placed[0]


def take_kernel(rows, core, part, out, sem):
    copies = []
    for chip in range(4):
        start = pl.multiple_of((2 * chip + core[0]) * rows, rows)
        to = out.at[pl.ds(chip * rows, rows), :]
        copies.append(pltpu.make_async_copy(part.at[pl.ds(start, rows), :], to, sem.at[chip]))
    for c in copies:
        c.start()
    for c in copies:
        c.wait()


def first_kernel(rows, where, part, got, mine, send, held, sem):
    copies = []
    for chip in range(4):
        start = pl.multiple_of((2 * chip + where[0]) * rows, rows)
        to = held.at[pl.ds(chip * rows, rows), :]
        copies.append(pltpu.make_async_copy(part.at[pl.ds(start, rows), :], to, sem.at[chip]))
    for c in copies:
        c.start()
    for c in copies:
        c.wait()
    mine[...] = (held[...].astype(f32) + got[...].astype(f32)).astype(bf16)
    for n in range(2):
        send[n * rows : n * rows + rows, :] = mine[pl.ds(pl.multiple_of(where[1 + n] * rows, rows), rows), :]


def second_kernel(rows, where, mine, got, own, send):
    block = lambda n: mine[pl.ds(pl.multiple_of(where[n] * rows, rows), rows), :].astype(f32)
    own[...] = (block(0) + got[rows:, :].astype(f32)).astype(bf16)
    send[...] = (block(1) + got[:rows, :].astype(f32)).astype(bf16)


def scatter_call(kernel, rows, where, arrays, outs, scratch, name, first=pltpu.VMEM):
    width = arrays[0].shape[1]
    vmem = pl.BlockSpec(memory_space=pltpu.VMEM)
    return pl.pallas_call(
        functools.partial(kernel, rows),
        out_shape=[jax.ShapeDtypeStruct((n * rows, width), bf16) for n in outs],
        in_specs=[pl.BlockSpec(memory_space=pltpu.SMEM), pl.BlockSpec(memory_space=first)]
        + [vmem] * (len(arrays) - 1),
        out_specs=[vmem] * len(outs),
        scratch_shapes=scratch,
        compiler_params=pltpu.CompilerParams(vmem_limit_bytes=SMALL_MIB << 20),
        cost_estimate=CHEAP,
        name=name,
    )(jnp.stack(where).astype(jnp.int32), *arrays)


def scatter_start(part, seq_index):
    rows = part.shape[0] // 8
    sems = [pltpu.SemaphoreType.DMA((4,))]
    theirs = scatter_call(take_kernel, rows, [1 - seq_index % 2], [part], [4], sems, "scatter_take", pl.ANY)[0]
    return part, swap(theirs, "seq", 8, lambda i: i ^ 1)


def scatter_first(pair, seq_index):
    part, got = pair
    rows = part.shape[0] // 8
    core, chip = seq_index % 2, seq_index // 2
    where = [core, chip ^ 3, jnp.where(core == 0, chip ^ 2, chip ^ 1)]
    scratch = [pltpu.VMEM(got.shape, bf16), pltpu.SemaphoreType.DMA((4,))]
    mine, send = scatter_call(first_kernel, rows, where, [part, got], [4, 2], scratch, "scatter_first", pl.ANY)
    return mine, swap(send, "seq", 8, other_way)


def scatter_second(pair, seq_index):
    mine, got = pair
    core, chip = seq_index % 2, seq_index // 2
    where = [chip, jnp.where(core == 0, chip ^ 1, chip ^ 2)]
    own, send = scatter_call(second_kernel, mine.shape[0] // 4, where, [mine, got], [1, 1], [], "scatter_second")
    return own, swap(send, "seq", 8, first_way)


def widen_kernel(count, turn, *refs):
    total = refs[0][...].astype(f32)
    for ref in refs[1:count]:
        total = total + ref[...].astype(f32)
    refs[count][...] = total.T if turn else total


def widen(parts, turn=False):
    rows, width = parts[0].shape
    return pl.pallas_call(
        functools.partial(widen_kernel, len(parts), turn),
        out_shape=jax.ShapeDtypeStruct((width, rows) if turn else (rows, width), f32),
        compiler_params=pltpu.CompilerParams(vmem_limit_bytes=SMALL_MIB << 20),
        cost_estimate=CHEAP,
        name="widen",
    )(*parts)


def scatter_sum(part, seq_index, seq_count):
    if seq_count != 8:
        return lax.psum_scatter(part, "seq", scatter_dimension=0, tiled=True)
    pair = scatter_first(scatter_start(part, seq_index), seq_index)
    return widen(list(scatter_second(pair, seq_index)))


def hops(axis, count):
    return [(axis, 1 << k) for k in range(count.bit_length() - 1)]


def sum_all(value, axes, order, beside=()):
    if any(count & (count - 1) for _, count in axes):
        return lax.psum(value, [axis for axis, _ in axes]), list(beside)
    counts, beside = dict(axes), list(beside)
    for k, (axis, bit) in enumerate(order):
        got = swap(value, axis, counts[axis], lambda i: i ^ bit)
        if k < len(beside):
            got, beside[k] = lax.optimization_barrier((got, beside[k]))
        value = value + got
    return value, beside


def add_low(a, b):
    return (a.astype(f32) + b.astype(f32)).astype(bf16)


def relay_kernel(names, end, *refs):
    ins = dict(zip(names, refs))
    outs = list(refs[len(names) :])
    add = lambda a, b: (ins[a][...].astype(f32) + ins[b][...].astype(f32)).astype(bf16)
    if "part" in ins:
        outs.pop(0)[...] = add("part", "part_got")
    if "total" in ins:
        total = add("total", "total_got")
        outs.pop(0)[...] = total
        if "own" in ins:
            send = outs.pop(0)
            rows, own_rows = total.shape[0], ins["own"].shape[0]
            both = min(rows, own_rows)
            send[:both, :] = jnp.where(end[0] == 1, ins["own"][:both, :], total[:both, :])
            if own_rows > both:
                send[both:, :] = ins["own"][both:, :]
            if rows > both:
                send[both:, :] = total[both:, :]


def relay(end, part, total, own):
    ins = {}
    shapes = []
    if part is not None:
        ins.update(part=part[0], part_got=part[1])
        shapes.append(part[0].shape)
    if total is not None:
        ins.update(total=total[0], total_got=total[1])
        shapes.append(total[0].shape)
        if own is not None:
            ins["own"] = own
            shapes.append((max(own.shape[0], total[0].shape[0]), own.shape[1]))
    if not shapes:
        return None, None, own
    outs = pl.pallas_call(
        functools.partial(relay_kernel, tuple(ins)),
        out_shape=[jax.ShapeDtypeStruct(shape, bf16) for shape in shapes],
        in_specs=[pl.BlockSpec(memory_space=pltpu.SMEM)] + [pl.BlockSpec(memory_space=pltpu.VMEM)] * len(ins),
        out_specs=[pl.BlockSpec(memory_space=pltpu.VMEM)] * len(shapes),
        compiler_params=pltpu.CompilerParams(vmem_limit_bytes=SMALL_MIB << 20),
        cost_estimate=CHEAP,
        name="relay",
    )(end, *ins.values())
    outs = list(outs)
    part = outs.pop(0) if part is not None else None
    total = outs.pop(0) if total is not None else None
    return part, total, outs.pop(0) if outs else own


def staged(kernel, k, outs, wholes, scalars, arrays, before, name, limit=SMALL_MIB):
    before = before or []
    vmem = pl.BlockSpec() if limit == 60 else pl.BlockSpec(memory_space=pltpu.VMEM)
    anywhere = pl.BlockSpec(memory_space=pl.ANY)
    given = len(scalars) + len(arrays)
    return pl.pallas_call(
        functools.partial(kernel, k, len(before)),
        out_shape=[jax.ShapeDtypeStruct(shape, kind) for shape, kind in outs]
        + [jax.ShapeDtypeStruct((tokens, width), kind) for tokens, rows, width, kind in wholes],
        in_specs=[pl.BlockSpec(memory_space=pltpu.SMEM)] * len(scalars)
        + [vmem] * len(arrays)
        + [anywhere] * len(before),
        out_specs=[vmem] * len(outs) + [anywhere] * len(wholes),
        scratch_shapes=[pltpu.VMEM((rows, width), kind) for tokens, rows, width, kind in wholes]
        + [pltpu.SemaphoreType.DMA(())] * len(wholes),
        input_output_aliases={given + n: len(outs) + n for n in range(len(before))},
        compiler_params=pltpu.CompilerParams(vmem_limit_bytes=limit << 20),
        cost_estimate=CHEAP,
        name=name,
    )(*scalars, *arrays, *before)


def put_rows(k, value, whole, sem):
    rows = value.shape[0]
    copy = pltpu.make_async_copy(value, whole.at[pl.ds(k * rows, rows), :], sem)
    copy.start()
    return copy


def rms(value):
    return lax.rsqrt(jnp.mean(value * value, axis=-1, keepdims=True) + 1e-06)


def rms_back(grad, normed, scale):
    return scale * (grad - normed * jnp.mean(grad * normed, axis=-1, keepdims=True))


def dot_rows(a, b):
    return lax.dot_general(a, b, ROWS, preferred_element_type=f32)


def picked(end, total, got):
    return jnp.where(end[0] == 1, got[...], total[...]).astype(f32)


def forward_kernel(k, again, end, total, got, x, gains, gate_w, up_w, down_t, *rest):
    norms, stats, pre, part, low, pack, sem = rest[again:]
    width, units = x.shape[1], gate_w.shape[1]
    attn = picked(end, total, got)
    scale = rms(attn)
    normed = attn * scale
    norms[:, :width] = normed
    middle = x[...].astype(f32) + normed * gains[1:2, :]
    norms[:, width:] = middle
    middle_scale = rms(middle)
    lane = lax.broadcasted_iota(jnp.int32, stats.shape, 1)
    stats[...] = jnp.where(lane == 0, scale, middle_scale)
    act = (middle * middle_scale * gains[2:3, :]).astype(bf16)
    pack[:, units:] = act
    gated = dot(act, gate_w[...])
    upper = dot(act, up_w[...])
    pre[:, :units] = gated
    pre[:, units:] = upper
    unit = (gated * jax.nn.sigmoid(gated) * upper).astype(bf16)
    pack[:, :units] = unit
    copy = put_rows(k, pack, low, sem)
    part[...] = dot_rows(unit, down_t[...]).astype(bf16)
    copy.wait()


def backward_kernel(k, again, end, total, got, norms, pre, cot, gains, gate_w, up_w, down_t, *rest):
    sums, part, low, out, pack, done, sem, out_sem = rest[again:]
    width, units = cot.shape[1], gate_w.shape[1]
    ffn = picked(end, total, got)
    scale = rms(ffn)
    normed = ffn * scale
    done[...] = (norms[:, width:] + normed * gains[3:4, :]).astype(bf16)
    out_copy = put_rows(k, done, out, out_sem)
    grad = cot[...].astype(f32)
    sums[...] = jnp.sum(grad * normed, axis=0, keepdims=True)
    grad_ffn = rms_back(grad * gains[3:4, :], normed, scale).astype(bf16)
    pack[:, 2 * units :] = grad_ffn
    grad_units = dot(grad_ffn, down_t[...])
    gated = pre[:, :units]
    sig = jax.nn.sigmoid(gated)
    low_gate = (grad_units * pre[:, units:] * sig * (1.0 + gated * (1.0 - sig))).astype(bf16)
    low_up = (grad_units * gated * sig).astype(bf16)
    pack[:, :units] = low_gate
    pack[:, units : 2 * units] = low_up
    copy = put_rows(k, pack, low, sem)
    part[...] = (dot_rows(low_gate, gate_w[...]) + dot_rows(low_up, up_w[...])).astype(bf16)
    copy.wait()
    out_copy.wait()


def attn_back_kernel(k, again, end, total, got, norms, stats, cot, gains, *rest):
    sums, dmid, dattn, pack, sem = rest[again:]
    width = cot.shape[1]
    grad = picked(end, total, got)
    scale, middle_scale = stats[:, 0:1], stats[:, 1:2]
    normed = norms[:, width:] * middle_scale
    sums[0:1, :] = jnp.sum(grad * normed, axis=0, keepdims=True)
    middle = cot[...].astype(f32) + rms_back(grad * gains[2:3, :], normed, middle_scale)
    dmid[...] = middle
    normed = norms[:, :width]
    sums[1:2, :] = jnp.sum(middle * normed, axis=0, keepdims=True)
    pack[...] = rms_back(middle * gains[1:2, :], normed, scale).astype(bf16)
    put_rows(k, pack, dattn, sem).wait()


def weight_grad_kernel(left, right, out):
    out[...] = lax.dot_general(left[...], right[...], COLS, preferred_element_type=f32).astype(bf16)


def weight_grad(left, first, width, right, place, right_width):
    tokens = left.shape[0]
    step = 512
    return pl.pallas_call(
        weight_grad_kernel,
        out_shape=jax.ShapeDtypeStruct((width, right_width), bf16),
        grid=(width // step,),
        in_specs=[
            pl.BlockSpec((tokens, step), lambda i: (0, first // step + i)),
            pl.BlockSpec((tokens, right_width), lambda i: (0, place)),
        ],
        out_specs=pl.BlockSpec((step, right_width), lambda i: (i, 0)),
        compiler_params=pltpu.CompilerParams(vmem_limit_bytes=60 << 20),
        cost_estimate=CHEAP,
        name="weight_grad",
    )(left, right)


def run_ticks(parts, computes, head_index, head_count, fill):
    carry = []
    stages = 4 * len(computes)
    ticks = stages + len(parts) - 1
    if head_count != 4:
        for n, compute in enumerate(computes):
            sums = [lax.psum(part, "head") for part in parts]
            parts = []
            for k, part in enumerate(sums):
                before = parts[k - 1] if k else None
                parts.append(compute(k, jnp.zeros((1,), jnp.int32), part, part, before))
        for t in range(ticks):
            carry = fill[t](carry) if t in fill else carry
        return parts, carry
    end = jnp.where((head_index == 0) | (head_index == 3), 1, 0).astype(jnp.int32).reshape(1)
    states = [(part,) for part in parts]
    for t in range(ticks):
        at = {(t - k) % 4: k for k in range(len(parts)) if 0 <= t - k < stages}
        live = [k for k in range(len(parts)) if t - k < stages + 1]
        own = states[at[0]][0] if 0 in at else None
        part, total, send = relay(
            end, states[at[1]] if 1 in at else None, states[at[2]] if 2 in at else None, own
        )
        late = states[at[3]] if 3 in at else ()
        if part is not None or total is not None:
            part, total, send, late, carry = lax.optimization_barrier((part, total, send, late, carry))
        if 3 in at:
            states[at[3]] = late
        if 1 in at:
            states[at[1]] = (part, lax.ppermute(part, "head", [(1, 2), (2, 1)]))
        if 0 in at and 2 in at:
            got = lax.ppermute(send, "head", [(0, 1), (3, 2), (1, 0), (2, 3)])
            states[at[0]] = (own, got[: own.shape[0]])
            states[at[2]] = (total, got[: total.shape[0]])
        elif 0 in at:
            states[at[0]] = (own, lax.ppermute(own, "head", [(0, 1), (3, 2)]))
        elif 2 in at:
            states[at[2]] = (total, lax.ppermute(total, "head", [(1, 0), (2, 3)]))
        if 3 in at:
            k = at[3]
            before = states[k - 1][0] if k else None
            states[k] = (computes[(t - k) // 4](k, end, *states[k], before),)
        if t in fill:
            carry = fill[t](carry)
        held, carry = lax.optimization_barrier(([states[k] for k in live], carry))
        for k, state in zip(live, held):
            states[k] = state
    return [state[0] for state in states], carry


def head_mean(value):
    row = lax.broadcasted_iota(jnp.int32, (128, 128), 0) // HD
    col = lax.broadcasted_iota(jnp.int32, (128, 128), 1) // HD
    ones = jnp.where(row == col, 1.0 / HD, 0.0).astype(bf16)
    hi, mid, lo = split3(value)
    return dot(hi.astype(bf16), ones) + dot(mid.astype(bf16), ones) + dot(lo.astype(bf16), ones)


def partner(value):
    lane = lax.broadcasted_iota(jnp.int32, value.shape, 1) % HD
    return jnp.where(lane < HD // 2, pltpu.roll(value, 128 - HD // 2, 1), pltpu.roll(value, HD // 2, 1))


def text_norm_kernel(pre, gain, out):
    wide = pre.shape[1] // 2
    for p in range(wide // 128):
        cols = slice(p * 128, p * 128 + 128)
        value = pre[:, cols].astype(f32)
        out[:, cols] = (value * lax.rsqrt(head_mean(value * value) + 1e-6) * gain[...]).astype(bf16)
    out[:, wide:] = pre[:, wide:]


def text_norm(pre, gain):
    return pl.pallas_call(
        text_norm_kernel, out_shape=jax.ShapeDtypeStruct(pre.shape, bf16), name="text_norm", cost_estimate=CHEAP
    )(pre, gain)


def qkv_kernel(count, rows, wide, roles, x, gain, qgain, kgain, cos, sin, *rest):
    pieces, (act, scale, pre, kv, query, query_t, weight, sem) = rest[:count], rest[count:]
    copies = []
    for k in range(count):
        start = pl.multiple_of(roles[k] * rows, rows)
        copies.append(pltpu.make_async_copy(pieces[k], weight.at[pl.ds(start, rows), :], sem.at[k]))
    for c in copies:
        c.start()
    value = x[...].astype(f32)
    inverse = lax.rsqrt(jnp.mean(value * value, axis=-1, keepdims=True) + 1e-6)
    scale[...] = inverse
    act[...] = (value * inverse * gain[0:1, :]).astype(bf16)
    for c in copies:
        c.wait()
    pre[...] = dot(act[...], weight[:, : 2 * wide])
    kv[:, wide:] = dot(act[...], weight[:, 2 * wide :]).astype(bf16)
    for p in range(wide // 128):
        cols = slice(p * 128, p * 128 + 128)
        for which, out_gain in ((0, qgain), (1, kgain)):
            raw = pre[:, which * wide + p * 128 : which * wide + p * 128 + 128]
            raw = raw * lax.rsqrt(head_mean(raw * raw) + 1e-6) * out_gain[...]
            raw = raw * cos[...] + partner(raw) * sin[...]
            if which == 1:
                kv[:, cols] = raw.astype(bf16)
            else:
                raw = raw.astype(bf16).astype(f32) * HD**-0.5
                query[:, cols] = raw.astype(bf16)
                query_t[cols, :] = raw.T.astype(bf16)


def project(roles, x, gain, qgain, kgain, cos, sin, pieces, wide):
    count = len(pieces)
    rows = pieces[0].shape[0]
    tokens, width = x.shape
    shape = jax.ShapeDtypeStruct
    return pl.pallas_call(
        functools.partial(qkv_kernel, count, rows, wide),
        out_shape=(
            shape((tokens, width), bf16),
            shape((tokens, 1), f32),
            shape((tokens, 2 * wide), f32),
            shape((tokens, 2 * wide), bf16),
            shape((tokens, wide), bf16),
            shape((wide, tokens), bf16),
            shape((width, 3 * wide), bf16),
        ),
        in_specs=[pl.BlockSpec(memory_space=pltpu.SMEM)]
        + [pl.BlockSpec(memory_space=pltpu.VMEM)] * 6
        + [pl.BlockSpec(memory_space=pltpu.HBM)] * count,
        out_specs=(pl.BlockSpec(memory_space=pltpu.VMEM),) * 7,
        scratch_shapes=[pltpu.SemaphoreType.DMA((count,))],
        compiler_params=pltpu.CompilerParams(vmem_limit_bytes=60 << 20),
        cost_estimate=CHEAP,
        name="project",
    )(roles, x, gain, qgain, kgain, cos, sin, *pieces)


def mix_kernel(heads, gate, sums, cross, mixed, self_t, cross_t, lse, cross_lse):
    for p in range((heads + 1) // 2):
        both = []
        for h in range(2 * p, 2 * p + 2):
            if h >= heads:
                both.append(jnp.zeros_like(both[0]))
                continue
            rows = slice(h * HD, h * HD + HD)
            den, cross_den = sums[h, HD : HD + 1, :], cross[h, HD : HD + 1, :]
            lse[h : h + 1, :] = jnp.log(den)
            cross_lse[h : h + 1, :] = jnp.log(cross_den)
            own = sums[h, :HD, :] / den
            other = cross[h, :HD, :] / cross_den
            self_t[rows, :] = own
            cross_t[rows, :] = other
            both.append(own + gate[h] * other)
        mixed[:, p * 128 : p * 128 + 128] = jnp.concatenate(both, axis=0).T.astype(bf16)


def mix(gate, sums, cross, wide):
    heads, _, tokens = sums.shape
    shape = jax.ShapeDtypeStruct
    return pl.pallas_call(
        functools.partial(mix_kernel, heads),
        out_shape=(
            shape((tokens, wide), bf16),
            shape((heads * HD, tokens), f32),
            shape((heads * HD, tokens), f32),
            shape((heads, tokens), f32),
            shape((heads, tokens), f32),
        ),
        in_specs=[pl.BlockSpec(memory_space=pltpu.SMEM)] + [pl.BlockSpec(memory_space=pltpu.VMEM)] * 2,
        compiler_params=pltpu.CompilerParams(vmem_limit_bytes=SMALL_MIB << 20),
        name="mix",
        cost_estimate=CHEAP,
    )(gate, sums, cross)


def unmix_kernel(heads, gate, weight, self_t, cross_t, grad, tok, tok_t, ctok, ctok_t, delta, cdelta, cgate):
    width = tok.shape[0]
    for p in range((heads + 1) // 2):
        cols = slice(p * 128, p * 128 + 128)
        value = dot(grad[...], weight[:, cols])
        lane = lax.broadcasted_iota(jnp.int32, (width, 128), 1) // HD
        gates = jnp.where(lane == 0, gate[2 * p], gate[min(2 * p + 1, heads - 1)])
        tok[:, cols] = value.astype(bf16)
        ctok[:, cols] = (value * gates).astype(bf16)
        turned = value.T
        for h in range(2 * p, 2 * p + 2):
            rows = slice(h * HD, h * HD + HD)
            part = turned[(h % 2) * HD : (h % 2) * HD + HD, :]
            tok_t[rows, :] = part.astype(bf16)
            if h >= heads:
                ctok_t[rows, :] = part.astype(bf16)
                continue
            low = (part * gate[h]).astype(bf16)
            ctok_t[rows, :] = low
            delta[h : h + 1, :] = jnp.sum(part.astype(bf16).astype(f32) * self_t[rows, :], axis=0, keepdims=True)
            cdelta[h : h + 1, :] = jnp.sum(low.astype(f32) * cross_t[rows, :], axis=0, keepdims=True)
            cgate[h : h + 1, :] = jnp.sum(part * cross_t[rows, :], axis=0, keepdims=True)


def unmix(gate, grad, weight, self_t, cross_t):
    tokens = self_t.shape[1]
    wide = weight.shape[1]
    heads = self_t.shape[0] // HD
    shape = jax.ShapeDtypeStruct
    return pl.pallas_call(
        functools.partial(unmix_kernel, heads),
        out_shape=(shape((tokens, wide), bf16), shape((wide, tokens), bf16)) * 2 + (shape((heads, tokens), f32),) * 3,
        in_specs=[pl.BlockSpec(memory_space=pltpu.SMEM)]
        + [pl.BlockSpec(memory_space=pltpu.VMEM)] * 4,
        compiler_params=pltpu.CompilerParams(vmem_limit_bytes=SMALL_MIB << 20),
        name="unmix",
        cost_estimate=CHEAP,
    )(gate, weight, self_t, cross_t, grad)


def norm_back(raw, gain, grad, cos=None, sin=None):
    scale = lax.rsqrt(head_mean(raw * raw) + 1e-6)
    normed = raw * scale
    if cos is not None:
        grad = grad * cos - partner(grad) * sin
    gain_grad = jnp.sum(grad * normed, axis=0, keepdims=True)
    grad = grad * gain
    return scale * (grad - normed * head_mean(grad * normed)), gain_grad


def text_back_kernel(pre, gain, grad, out):
    wide = pre.shape[1] // 2
    for p in range(wide // 128):
        cols = slice(p * 128, p * 128 + 128)
        out[:, cols] = norm_back(pre[:, cols].astype(f32), gain[...], grad[:, cols])[0].astype(bf16)
    out[:, wide:] = grad[:, wide:].astype(bf16)


def text_back(pre, gain, grad):
    return pl.pallas_call(
        text_back_kernel,
        out_shape=jax.ShapeDtypeStruct(grad.shape, bf16),
        name="text_back",
        cost_estimate=CHEAP,
    )(pre, gain, grad)


def project_back_kernel(wide, starts, pre, qgain, kgain, cos, sin, dqt, x, scale, weight, *rest):
    kvs, (out, qgrad, kgrad, act, sums) = rest[: len(starts)], rest[len(starts) :]
    tokens = pre.shape[0]
    total = [jnp.zeros((1, 128), f32), jnp.zeros((1, 128), f32)]
    summed = lambda cols: sum(kv[start : start + tokens, cols].astype(f32) for kv, start in zip(kvs, starts))
    for p in range(wide // 128):
        cols = slice(p * 128, p * 128 + 128)
        grads = (dqt[cols, :] * HD**-0.5).T, summed(cols)
        for which, gain in ((0, qgain), (1, kgain)):
            at = slice(which * wide + p * 128, which * wide + p * 128 + 128)
            value, extra = norm_back(pre[:, at], gain[...], grads[which], cos[...], sin[...])
            out[:, at] = value.astype(bf16)
            total[which] = total[which] + extra
    out[:, 2 * wide :] = summed(slice(wide, 2 * wide)).astype(bf16)
    qgrad[...] = total[0]
    kgrad[...] = total[1]
    value = dot_rows(out[...], weight[...])
    act[...] = value.astype(bf16)
    sums[...] = jnp.sum(value * (x[...].astype(f32) * scale[...]), axis=0, keepdims=True)


def project_back(pre, qgain, kgain, cos, sin, dqt, x, scale, weight, kvs, starts):
    tokens, wide = pre.shape[0], pre.shape[1] // 2
    shape = jax.ShapeDtypeStruct
    return pl.pallas_call(
        functools.partial(project_back_kernel, wide, tuple(starts)),
        out_shape=(
            shape((tokens, 3 * wide), bf16),
            shape((1, 128), f32),
            shape((1, 128), f32),
            shape(x.shape, bf16),
            shape((1, x.shape[1]), f32),
        ),
        name="project_back",
        cost_estimate=CHEAP,
        compiler_params=pltpu.CompilerParams(vmem_limit_bytes=60 << 20),
    )(pre, qgain, kgain, cos, sin, dqt, x, scale, weight, *kvs)


def finish_kernel(k, end, total, got, x, scale, gain, mid, mark, *rest):
    out, done, value, sem = rest[-4:]
    rows = mid.shape[0]
    inverse = scale[...]
    normed = x[...].astype(f32) * inverse
    grad = picked(end, total, got)[:rows] * gain[0:1, :]
    mean = jnp.mean(grad * normed, axis=-1, keepdims=True)
    value[...] = mid[...] + inverse * (grad - normed * mean)
    copy = pltpu.make_async_copy(value, out.at[pl.ds(k * rows, rows), :], sem)
    copy.start()
    done[...] = mark[...]
    copy.wait()


def finish(k, end, total, got, x, scale, gain, mid, mark, tokens, before):
    before = [] if before is None else [before]
    vmem = pl.BlockSpec(memory_space=pltpu.VMEM)
    return pl.pallas_call(
        functools.partial(finish_kernel, k),
        out_shape=[jax.ShapeDtypeStruct((tokens, mid.shape[1]), f32), jax.ShapeDtypeStruct(mark.shape, f32)],
        in_specs=[pl.BlockSpec(memory_space=pltpu.SMEM)] + [vmem] * 7 + [pl.BlockSpec(memory_space=pl.ANY)] * len(before),
        out_specs=[pl.BlockSpec(memory_space=pl.ANY), vmem],
        scratch_shapes=[pltpu.VMEM(mid.shape, f32), pltpu.SemaphoreType.DMA(())],
        input_output_aliases={8: 0} if before else {},
        name="finish",
        cost_estimate=CHEAP,
        compiler_params=pltpu.CompilerParams(vmem_limit_bytes=SMALL_MIB << 20),
    )(end, total, got, x, scale, gain, mid, mark, *before)


def touch_kernel(*refs):
    refs[-1][...] = refs[0][...]


def touch(value, arrays):
    return pl.pallas_call(
        touch_kernel,
        out_shape=jax.ShapeDtypeStruct(value.shape, value.dtype),
        in_specs=[pl.BlockSpec(memory_space=pltpu.VMEM)] * (1 + len(arrays)),
        cost_estimate=CHEAP,
        compiler_params=pltpu.CompilerParams(vmem_limit_bytes=SMALL_MIB << 20),
        name="touch",
    )(value, *arrays)


def gains_back_kernel(sums, mods, gains, gain_grad, mod_grad):
    for n in range(4):
        row = slice(n, n + 1)
        if n % 2 == 0:
            gain_grad[row, :] = sums[row, :] * (1.0 + mods[row, :])
            mod_grad[row, :] = sums[row, :] * gains[row, :]
        else:
            gate = jnp.tanh(mods[row, :])
            gain_grad[row, :] = sums[row, :] * gate
            mod_grad[row, :] = sums[row, :] * gains[row, :] * (1.0 - gate * gate)


def gains_back(sums, mods, gains):
    return pl.pallas_call(
        gains_back_kernel,
        out_shape=[jax.ShapeDtypeStruct(gains.shape, f32)] * 2,
        cost_estimate=CHEAP,
        name="gains_back",
    )(sums, mods, gains)


def vectors_kernel(mods, gains, out):
    out[0:1, :] = gains[0:1, :] * (1.0 + mods[0:1, :])
    out[1:2, :] = jnp.tanh(mods[1:2, :]) * gains[1:2, :]
    out[2:3, :] = gains[2:3, :] * (1.0 + mods[2:3, :])
    out[3:4, :] = jnp.tanh(mods[3:4, :]) * gains[3:4, :]


def vectors(mods, gains):
    return pl.pallas_call(
        vectors_kernel,
        out_shape=jax.ShapeDtypeStruct(gains.shape, f32),
        cost_estimate=CHEAP,
        name="vectors",
    )(mods, gains)


def per_device(
    seq_count,
    head_count,
    hidden_in,
    cond,
    captions,
    clip_lengths,
    ada_weight,
    norm_gains,
    qk_gains,
    w_query,
    w_key,
    w_value,
    w_out,
    cross_gate,
    w_text_key,
    w_text_value,
    w_gate,
    w_up,
    w_down,
    out_cotangent,
):
    local_rows, model_width = hidden_in.shape
    seq_index = lax.axis_index("seq")
    head_index = lax.axis_index("head")
    clips = clip_lengths.shape[0]
    cols = w_query.shape[1]
    heads = cols // HD
    wide = (cols + 127) // 128 * 128
    units = w_gate.shape[1]
    roles = seq_roles(seq_index, seq_count)
    pad = lambda v: jnp.pad(v, ((0, 0), (0, wide - cols))) if wide > cols else v
    cut = lambda v: v[:, :cols]

    spread = seq_count == 8
    core = lambda v: swap(v, "seq", 8, lambda i: i ^ 1)
    hold = lax.optimization_barrier
    axes = (("seq", seq_count), ("head", head_count))
    seq_hops, head_hops = hops("seq", seq_count), hops("head", head_count)
    finish_sum = lambda v: lax.psum_scatter(v, "seq", scatter_dimension=0, tiled=True)

    def hop(value, steps):
        for axis, bit in steps:
            value = value + swap(value, axis, dict(axes)[axis], lambda i: i ^ bit)
        return value

    clip_ends = jnp.cumsum(clip_lengths, dtype=jnp.int32)
    starts = clip_ends - clip_lengths
    text_rows = captions.reshape(-1, captions.shape[2])
    text_block = text_rows.shape[0] // seq_count
    text_ids = jnp.arange(clips, dtype=jnp.int32) * captions.shape[1]
    first_row = seq_index * local_rows
    place_info = jnp.concatenate([first_row[None], starts, clip_ends]).astype(jnp.int32)
    text_info = jnp.concatenate(
        [place_info, text_ids, text_ids + captions.shape[1], jnp.zeros((1,), jnp.int32)]
    )

    def self_info(which):
        return jnp.concatenate([place_info, starts, clip_ends, roles[which] * local_rows])

    places = first_row + jnp.arange(local_rows, dtype=jnp.int32)
    inside = (places[:, None] >= starts[None, :]) & (places[:, None] < clip_ends[None, :])
    position = places - jnp.sum(jnp.where(inside, starts[None, :], 0), axis=1, dtype=jnp.int32)
    lane = jnp.arange(128)
    frequency = 10000.0 ** (-(lane % (HD // 2)).astype(f32) / (HD // 2))
    angles = position.astype(f32)[:, None] * frequency[None, :]
    cos = jnp.cos(angles)
    sin = jnp.where(lane % HD < HD // 2, -1.0, 1.0)[None, :] * jnp.sin(angles)
    query_gain = jnp.tile(qk_gains[0], 2)[None, :]
    key_gain = jnp.tile(qk_gains[1], 2)[None, :]

    cond_act = jax.nn.silu(cond).astype(bf16)
    piece_width = ada_weight.shape[1]
    mod_piece = matmul(cond_act[None, :], ada_weight)
    mine = lax.broadcasted_iota(jnp.int32, (seq_count * head_count, 1), 0) == seq_index * head_count + head_index
    modulation = jnp.where(mine, mod_piece, 0.0)
    modulation, w_query = hold((modulation, w_query))
    qkv_block = jnp.concatenate([pad(w_query), pad(w_key), pad(w_value)], axis=1)
    out_block = pad(w_out.T)
    slab_width = text_rows.shape[1] // seq_count
    if spread:
        modulation = hop(modulation, seq_hops[:1])
        modulation, text_rows = hold((modulation, text_rows))
    own_text = lax.dynamic_slice_in_dim(text_rows, seq_index * slab_width, slab_width, 1)
    text_part = matmul(own_text, jnp.concatenate([pad(w_text_key), pad(w_text_value)], axis=1)).astype(bf16)

    def queries_keys(pieces):
        return project(roles, hidden_in, rows, query_gain, key_gain, cos, sin, pieces, wide)

    def part_sums(group, blocks, before=None):
        return attend(self_info(jnp.array(group)), query_t, blocks, heads, clips, before)

    if spread:
        near = swap(qkv_block, "seq", 8, first_way)
        next_ = swap(qkv_block, "seq", 8, other_way)
        modulation = hop(modulation, head_hops[:1])
        text_pre = lax.psum(text_part, "seq")
        gate_w = lax.all_gather(w_gate, "seq", axis=0, tiled=True)
        near, next_, modulation = hold((near, next_, modulation))
        far = swap(near, "seq", 8, other_way)
        modulation = hop(modulation, head_hops[1:])
        modulation = hop(modulation, seq_hops[1:])
        qkv_pieces = [qkv_block, near, next_, far]
        qkv_pieces = qkv_pieces + [core(v) for v in qkv_pieces]
        modulation, qkv_pieces, out_block = hold((modulation, qkv_pieces, out_block))
        modulation = modulation.reshape(4, model_width)
        rows = vectors(modulation, norm_gains)
        act_a, x_scale, pre, kv_own, queries, query_t, w_qkv = queries_keys(qkv_pieces)
        kv_own, modulation, out_block = hold((kv_own, modulation, out_block))
        near = swap(kv_own, "seq", 8, first_way)
        next_ = swap(kv_own, "seq", 8, other_way)
        kv_peer = core(kv_own)
        out_near = swap(out_block, "seq", 8, first_way)
        out_next = swap(out_block, "seq", 8, other_way)
        sums = part_sums((0, 4), [kv_own, kv_peer])
        near, next_, sums, out_near, out_next = hold((near, next_, sums, out_near, out_next))
        far = swap(near, "seq", 8, other_way)
        out_far = swap(out_near, "seq", 8, other_way)
        near_peer, next_peer = core(near), core(next_)
        out_peers = [core(out_block), core(out_near), core(out_next)]
        sums = part_sums((1, 2, 5, 6), [near, next_, near_peer, next_peer], sums)
        ud_block = jnp.concatenate([w_up, w_down.T], axis=1)
        far, sums, out_far, text_pre, ud_block = hold((far, sums, out_far, text_pre, ud_block))
        far_peer = core(far)
        ud_near = swap(ud_block, "seq", 8, first_way)
        ud_next = swap(ud_block, "seq", 8, other_way)
        out_t = place([out_block, out_near, out_next, out_far] + out_peers + [core(out_far)], roles)
        text_pieces = [text_norm(text_pre, key_gain)]
        cross_sums = attend(text_info, query_t, text_pieces, heads, clips)
        sums = part_sums((3, 7), [far, far_peer], sums)
        pieces = [kv_own, near, next_, far, kv_peer, near_peer, next_peer, far_peer]
    else:
        modulation = lax.psum(modulation, ("seq", "head"))
        text_pre = lax.psum(text_part, "seq")
        qkv_pieces = gather_pieces(qkv_block, seq_count)
        modulation = modulation.reshape(4, model_width)
        rows = vectors(modulation, norm_gains)
        act_a, x_scale, pre, kv_own, queries, query_t, w_qkv = queries_keys(qkv_pieces)
        pieces = gather_pieces(kv_own, seq_count)
        text_pieces = [text_norm(text_pre, key_gain)]
        out_t = place(gather_pieces(out_block, seq_count), roles)
        sums = part_sums(tuple(range(seq_count)), pieces)
        cross_sums = attend(text_info, query_t, text_pieces, heads, clips)
        gate_w = lax.all_gather(w_gate, "seq", axis=0, tiled=True)
    gate_local = jnp.tanh(cross_gate)
    mixed, self_t, cross_t, self_lse, cross_lse = mix(gate_local, sums, cross_sums, wide)
    attn_part = matmul(mixed, out_t, ROWS).astype(bf16)

    late = {}

    def split_weights(pieces):
        return place(pieces, roles, (units, units), 40)

    def fill_near(carry):
        return [ud_near, ud_next]

    def fill_far(carry):
        near, next_ = carry
        return [near, next_, swap(near, "seq", 8, other_way), core(ud_block), core(near), core(next_)]

    def fill_weights(carry):
        late["up"], late["down"] = split_weights([ud_block] + carry + [core(carry[2])])
        late["rows"] = touch(rows, [gate_w, late["up"], late["down"]])
        return [late["rows"]]

    if not spread:
        weights = gather_pieces(jnp.concatenate([w_up, w_down.T], axis=1), seq_count)
        late["up"], late["down"] = split_weights(weights)
        late["rows"] = rows
    chunk_count = 4
    chunk = local_rows // chunk_count
    rows_of = lambda v, k: v[k * chunk : (k + 1) * chunk]
    kept = [{} for _ in range(chunk_count)]


    tall, thin = (chunk, model_width), (chunk, units)
    whole = lambda width: (local_rows, chunk, width, bf16)

    def feed_forward(k, end, total, got, before):
        keep = kept[k]
        outs = [((chunk, 2 * model_width), f32), ((chunk, 128), f32), ((chunk, 2 * units), f32), (tall, bf16)]
        arrays = [total, got, rows_of(hidden_in, k), late["rows"], gate_w, late["up"], late["down"]]
        keep["norms"], keep["stats"], keep["pre"], part, late["first"] = staged(
            forward_kernel, k, outs, [whole(units + model_width)], [end], arrays,
            [late["first"]] if k else None, "feed_forward",
        )
        return part

    def feed_back(k, end, total, got, before):
        keep = kept[k]
        arrays = [total, got, keep["norms"], keep["pre"], rows_of(out_cotangent, k), late["rows"]]
        keep["uf"], part, late["second"], late["hidden"] = staged(
            backward_kernel, k, [((1, model_width), f32), (tall, bf16)],
            [whole(2 * units + model_width), whole(model_width)], [end], arrays + [gate_w, late["up"], late["down"]],
            [late["second"], late["hidden"]] if k else None, "feed_back",
        )
        return part

    def attn_back(k, end, total, got, before):
        keep = kept[k]
        arrays = [total, got, keep["norms"], keep["stats"], rows_of(out_cotangent, k), rows]
        keep["sums"], keep["dmid"], late["dattn"] = staged(
            attn_back_kernel, k, [((2, model_width), f32), (tall, f32)], [whole(model_width)], [end], arrays,
            [late["dattn"]] if k else None, "attn_back", 60,
        )
        return keep["sums"]

    total_of = lambda name, n: sum(keep[name][n] for keep in kept)

    def fill_down(carry):
        return [weight_grad(late["second"], 2 * units, model_width, late["first"], 0, units)]

    def fill_gate(carry):
        late["down_sum"] = finish_sum(carry[0])
        (first, second), carry = hold(((late["first"], late["second"]), carry))
        late["first"], late["second"] = first, second
        return [weight_grad(first, units, model_width, second, 0, units)]

    def fill_up(carry):
        late["gate_sum"] = finish_sum(carry[0])
        (first, second), carry = hold(((late["first"], late["second"]), carry))
        return [weight_grad(first, units, model_width, second, 1, units)]

    def fill_last(carry):
        late["up_sum"] = finish_sum(carry[0])
        return []

    fills = {8 + chunk_count - 1: fill_down, 8 + chunk_count: fill_gate, 8 + chunk_count + 1: fill_up, 8 + chunk_count + 2: fill_last}
    first_parts = [rows_of(attn_part, k) for k in range(chunk_count)]
    if spread:
        fills.update({0: fill_near, 1: fill_far, 2: fill_weights})
    run_ticks(
        first_parts, [feed_forward, feed_back, attn_back], head_index, head_count, fills
    )
    grad_attn_low, hidden_out = late["dattn"], late["hidden"]
    down_grad, gate_grad, up_grad = late["down_sum"], late["gate_sum"], late["up_sum"]

    grad_self_tok, grad_self_t, grad_cross_tok, grad_cross_t, self_delta, cross_delta, gate_rows = unmix(
        gate_local, grad_attn_low, out_t, self_t, cross_t
    )
    cross_gate_part = jnp.sum(gate_rows, axis=1) * (1.0 - gate_local * gate_local)

    def back(group, parts, before=None):
        return attend_back(
            self_info(jnp.array(group)), query_t, grad_self_t, queries, grad_self_tok, self_lse, self_delta,
            [pieces[g] for g in group], heads, clips, bf16, parts, before,
        )

    def cross_back(before):
        return attend_back(
            text_info, query_t, grad_cross_t, queries, grad_cross_tok, cross_lse, cross_delta,
            text_pieces, heads, clips, f32, 1, before,
        )

    if spread:
        dq, _, kv_mine, kv_theirs = back((3, 2, 7, 6), 2)
        kv_got = core(kv_theirs)
        kv_mine, low = hold((kv_mine, grad_attn_low))
        out_part = matmul(low, mixed, COLS).astype(bf16)
        total = add_low(kv_mine, kv_got)
        total, dq, out_part = hold((total, dq, out_part))
        first = swap(total[:local_rows], "seq", 8, other_way)
        dq, text_dot, cross_kv = cross_back(dq)
        dq, cross_kv, down_grad, total = hold((dq, cross_kv, down_grad, total))
        own_first = swap(total[local_rows:], "seq", 8, other_way)
        dq, _, kv_mine, kv_theirs = back((1, 5), 2, dq)
        first, kv_mine, kv_theirs = hold((first, kv_mine, kv_theirs))
        total = kv_mine.astype(f32) + core(kv_theirs).astype(f32) + first.astype(f32)
        total = total.astype(bf16)
        second = swap(total, "seq", 8, first_way)
        dq, _, kv_mine, kv_theirs = back((0, 4), 2, dq)
        second, kv_mine, kv_theirs, gate_grad, own_first = hold((second, kv_mine, kv_theirs, gate_grad, own_first))
        kv_parts, kv_starts = [kv_mine, core(kv_theirs), own_first, second], (0, 0, 0, 0)
    else:
        dq, _, kv_all = back(tuple(range(seq_count)), 1)
        dq, text_dot, cross_kv = cross_back(dq)
        out_part = weight_grad(grad_attn_low, 0, model_width, mixed, 0, wide)
        kv_parts, kv_starts = [finish_sum(kv_all)], (0,)
    qkv_low, grad_query_gain, grad_key_gain, act_low, sum_a = project_back(
        pre, query_gain, key_gain, cos, sin, dq, hidden_in, x_scale, w_qkv, kv_parts, kv_starts
    )
    act_low, qkv_low, cross_kv, gate_grad = hold((act_low, qkv_low, cross_kv, gate_grad))
    fold = lambda v: v[0, :HD] + v[0, HD:]
    pair_gains = jnp.concatenate([fold(grad_query_gain), fold(grad_key_gain + text_dot / key_gain)])
    tail = jnp.stack([sum_a[0], jnp.pad(pair_gains, (0, model_width - 2 * HD))])
    tail = jnp.pad(tail, ((0, 14), (0, 0))).astype(bf16)
    small = [total_of("sums", 1), total_of("sums", 0), total_of("uf", 0)]
    cross_row = jnp.pad(cross_gate_part, (2 * HD, model_width - 2 * HD - heads))

    def collect(k, end, total, got, before):
        if k == 0:
            late["tail"] = jnp.where(end[0] == 1, got, total)[chunk:].astype(f32)
        arrays = rows_of(hidden_in, k), rows_of(x_scale, k), rows, kept[k]["dmid"]
        mark = jnp.zeros((8, 128), f32) if before is None else before
        late["input"], mark = finish(k, end, total, got, *arrays, mark, local_rows, late.get("input"))
        return mark

    late["out_sum"] = finish_sum(out_part)

    def fill0(carry):
        part = weight_grad(act_a, 0, model_width, qkv_low, 0, 3 * wide)
        return [text_back(text_pre, key_gain, cross_kv), part]

    def fill1(carry):
        late["qkv"] = finish_sum(carry[1])
        gate, down, text = hold((gate_grad, down_grad, carry[0]))
        late["gate"], late["down"] = widen([gate]), widen([down], True)
        if not spread:
            return [lax.psum(text, "seq"), late["gate"], late["down"]]
        return [scatter_first(scatter_start(text, seq_index), seq_index), late["gate"], late["down"]]

    def fill2(carry):
        text, late["gate"], late["down"] = carry
        up, text = hold((up_grad, text))
        late["up"] = widen([up])
        if not spread:
            return [text, late["up"]]
        own = add_low(*scatter_second(text, seq_index))
        return [[own, swap(own, "seq", 8, first_way), swap(own, "seq", 8, other_way)], late["up"]]

    def fill3(carry):
        text, late["up"] = carry
        tail_rows = [late["tail"][0]] + small + [jnp.pad(late["tail"][1, : 2 * HD], (0, model_width - 2 * HD)) + cross_row]
        values = jnp.pad(jnp.stack(tail_rows), ((0, 3), (0, 0)))
        if not spread:
            return [text, lax.psum(values, "seq")]
        text = text + [swap(text[1], "seq", 8, other_way)]
        text = text + [core(v) for v in text[:3]]
        return [text, hop(values, seq_hops[:2])]

    def fill4(carry):
        text, values = carry
        out, text = hold((late["out_sum"], text))
        late["out"] = widen([out], True)
        if spread:
            text = text + [core(text[3])]
            values = hop(values, seq_hops[2:])
        return [values, text, late["out"]]

    def fill5(carry):
        values, text, late["out"] = carry
        gain_grad, mod_grad = gains_back(values[:4], modulation, norm_gains)
        own_mod = lax.dynamic_slice_in_dim(
            mod_grad.reshape(-1), (seq_index * head_count + head_index) * piece_width, piece_width
        )
        text = place(text, roles) if spread else text
        text_grad = matmul(own_text, text, COLS)
        return [gain_grad, values[4], text_grad, cond_act.astype(f32)[:, None] * own_mod[None, :]]

    parts = [rows_of(act_low, k) for k in range(chunk_count)]
    parts[0] = jnp.concatenate([parts[0], tail])
    fills = dict(enumerate([fill0, fill1, fill2, fill3, fill4, fill5]))
    _, (norm_gains_grad, values, text_grad, ada_grad) = run_ticks(parts, [collect], head_index, head_count, fills)
    input_grad = late["input"]
    own_qkv = widen([late["qkv"]])

    qk_gains_grad = values[: 2 * HD].reshape(2, HD)
    cross_gate_grad = values[2 * HD : 2 * HD + heads]
    return (
        hidden_out,
        input_grad,
        ada_grad,
        norm_gains_grad,
        qk_gains_grad,
        cut(own_qkv[:, :wide]),
        cut(own_qkv[:, wide : 2 * wide]),
        cut(own_qkv[:, 2 * wide : 3 * wide]),
        late["out"][:cols],
        cross_gate_grad,
        cut(text_grad[:, :wide]),
        cut(text_grad[:, wide:]),
        late["gate"],
        late["up"],
        late["down"],
    )


def solution(mesh):
    in_specs = (
        P("seq", None),
        P(),
        P(),
        P(),
        P(None, ("seq", "head")),
        P(),
        P(),
        P("seq", "head"),
        P("seq", "head"),
        P("seq", "head"),
        P("head", "seq"),
        P("head"),
        P("seq", "head"),
        P("seq", "head"),
        P("seq", "head"),
        P("seq", "head"),
        P("head", "seq"),
        P("seq", None),
    )
    out_specs = (
        P("seq", None),
        P("seq", None),
        P(None, ("seq", "head")),
        P(),
        P(),
        P("seq", "head"),
        P("seq", "head"),
        P("seq", "head"),
        P("head", "seq"),
        P("head"),
        P("seq", "head"),
        P("seq", "head"),
        P("seq", "head"),
        P("seq", "head"),
        P("head", "seq"),
    )
    body = functools.partial(per_device, mesh.shape["seq"], mesh.shape["head"])
    return jax.shard_map(body, mesh=mesh, in_specs=in_specs, out_specs=out_specs, check_vma=False)
```

```python
import functools
import jax
import jax.numpy as jnp
from jax import lax
from jax.experimental import pallas as pl
from jax.experimental.pallas import tpu as pltpu
from jax.sharding import PartitionSpec as P

HD = 64
MASK = 8192.0
CHEAP = pl.CostEstimate(flops=1, bytes_accessed=1, transcendentals=0)
ATTEND_MIB = 60
BACK_MIB = 60
SMALL_MIB = 16


def dot(a, b):
    return lax.dot_general(a, b, (((1,), (0,)), ((), ())), preferred_element_type=jnp.float32)


def split3(v):
    hi = v.astype(jnp.bfloat16).astype(jnp.float32)
    mid = (v - hi).astype(jnp.bfloat16).astype(jnp.float32)
    return hi, mid, v - hi - mid


def bounds(info, base, clips, ids):
    start = jnp.full(ids.shape, 1 << 30, jnp.int32)
    end = jnp.zeros(ids.shape, jnp.int32)
    for c in range(clips):
        start = jnp.where(ids == c, info[base + c], start)
        end = jnp.where(ids == c, info[base + clips + c], end)
    return start, end


def query_ext(info, clips, width, scale):
    ids = lax.broadcasted_iota(jnp.int32, (16, width), 0)
    place = info[0] + lax.broadcasted_iota(jnp.int32, (16, width), 1)
    start, end = bounds(info, 1, clips, ids)
    return jnp.where((place >= start) & (place < end), scale, 0.0)


def key_ext(info, clips, row, rows, piece):
    ids = lax.broadcasted_iota(jnp.int32, (rows, 128), 1)
    step = min(rows, piece)
    parts = []
    for k in range(rows // step):
        at = row + k * step
        first = info[1 + 4 * clips + at // piece] + lax.rem(at, piece)
        parts.append(first + lax.broadcasted_iota(jnp.int32, (step, 128), 0))
    place = parts[0] if len(parts) == 1 else jnp.concatenate(parts, axis=0)
    start, end = bounds(info, 1 + 2 * clips, clips, ids)
    inside = (place >= start) & (place < end)
    value = jnp.where(ids < clips, jnp.where(inside, 0.0, -1.0), jnp.where(ids < clips + 3, 1.0, 0.0))
    return value.astype(jnp.bfloat16)


def fill_ext(dst, h, src, tail):
    width = src.shape[1]
    half = h % 2
    zero = jnp.zeros((HD, width), jnp.bfloat16)
    dst[h, half * HD : half * HD + HD, :] = src[h * HD : h * HD + HD, :]
    dst[h, (1 - half) * HD : (1 - half) * HD + HD, :] = zero
    dst[h, 128:144, :] = tail.astype(jnp.bfloat16)
    dst[h, 144:256, :] = jnp.zeros((112, width), jnp.bfloat16)


def stack_rows(heads, rows, clips, width):
    ids = lax.broadcasted_iota(jnp.int32, (16, width), 0)
    total = jnp.zeros((16, width), jnp.float32)
    for k, row in enumerate(rows):
        total = jnp.where(ids == clips + k, jnp.broadcast_to(row, (16, width)), total)
    return total


def load_pieces(pieces, kv, sem):
    rows = pieces[0].shape[0]
    return [
        pltpu.make_async_copy(piece, kv.at[pl.ds(k * rows, rows), :], sem.at[k])
        for k, piece in enumerate(pieces)
    ]


def fwd_kernel(heads, clips, count, tile, again, info, qt, *rest):
    before, pieces, (out, qx, kv, sem) = rest[:again], rest[again : again + count], rest[again + count :]
    copies = load_pieces(pieces, kv, sem)
    for c in copies:
        c.start()
    width = qt.shape[1]
    wide = qt.shape[0]
    ext = query_ext(info, clips, width, MASK)
    for h in range(heads):
        fill_ext(qx, h, qt, ext)
        out[h] = before[0][h] if again else jnp.zeros((80, width), jnp.float32)
    for c in copies:
        c.wait()
    steps = count * pieces[0].shape[0] // tile
    ones = jnp.ones((16, tile), jnp.bfloat16)

    def step(t, carry):
        rows = pl.ds(pl.multiple_of(t * tile, tile), tile)
        extra = key_ext(info, clips, t * tile, tile, pieces[0].shape[0])
        for p in range((heads + 1) // 2):
            kx = jnp.concatenate([kv[rows, p * 128 : p * 128 + 128], extra], axis=1)
            vt = kv[rows, wide + p * 128 : wide + p * 128 + 128].T
            for h in range(2 * p, min(2 * p + 2, heads)):
                half = h % 2
                probs = jnp.exp(dot(kx, qx[h])).astype(jnp.bfloat16)
                vx = jnp.concatenate([vt[half * HD : half * HD + HD, :], ones], axis=0)
                out[h] += dot(vx, probs)
        return carry

    lax.fori_loop(0, steps, step, 0)


def attend(info, qt, pieces, heads, clips, before=None, tile=1024):
    count = len(pieces)
    before = [] if before is None else [before]
    wide, width = qt.shape
    rows = pieces[0].shape[0]
    tile = min(tile, rows * count)
    return pl.pallas_call(
        functools.partial(fwd_kernel, heads, clips, count, tile, len(before)),
        out_shape=jax.ShapeDtypeStruct((heads, 80, width), jnp.float32),
        in_specs=[pl.BlockSpec(memory_space=pltpu.SMEM)]
        + [pl.BlockSpec(memory_space=pltpu.VMEM)] * (1 + len(before))
        + [pl.BlockSpec(memory_space=pltpu.HBM)] * count,
        out_specs=pl.BlockSpec(memory_space=pltpu.VMEM),
        scratch_shapes=[
            pltpu.VMEM((heads, 256, width), jnp.bfloat16),
            pltpu.VMEM((count * rows, 2 * wide), jnp.bfloat16),
            pltpu.SemaphoreType.DMA((count,)),
        ],
        compiler_params=pltpu.CompilerParams(vmem_limit_bytes=ATTEND_MIB << 20),
        cost_estimate=CHEAP,
        name="attend",
    )(info, qt, *before, *pieces)


def bwd_kernel(heads, clips, count, tile, again, info, qt, dot_t, q_tok, do_tok, lse, delta, *rest):
    before, pieces, rest = rest[:again], rest[again : again + count], rest[again + count :]
    dqt, kdot, grads, (qx, dox, qpad, dopad, kv, sem) = rest[0], rest[1], rest[2:-6], rest[-6:]
    copies = load_pieces(pieces, kv, sem)
    for c in copies:
        c.start()
    wide, width = qt.shape
    ext = query_ext(info, clips, width, MASK)
    for h in range(heads):
        p, half = h // 2, h % 2
        fill_ext(qx, h, qt, ext - stack_rows(heads, split3(lse[h : h + 1, :]), clips, width))
        fill_ext(dox, h, dot_t, -stack_rows(heads, split3(delta[h : h + 1, :]), clips, width))
        lane = lax.broadcasted_iota(jnp.int32, (width, 128), 1) // HD
        zero = jnp.zeros((width, 128), jnp.bfloat16)
        qpad[h] = jnp.where(lane == half, q_tok[:, p * 128 : p * 128 + 128], zero)
        dopad[h] = jnp.where(lane == half, do_tok[:, p * 128 : p * 128 + 128], zero)
    kdot[...] = jnp.zeros((1, 128), jnp.float32)
    dqt[...] = before[0][...] if again else jnp.zeros((wide, width), jnp.float32)
    for c in copies:
        c.wait()
    steps = count * pieces[0].shape[0] // tile

    def step(t, carry):
        rows = pl.ds(pl.multiple_of(t * tile, tile), tile)
        extra = key_ext(info, clips, t * tile, tile, pieces[0].shape[0])
        for p in range((heads + 1) // 2):
            cols = slice(p * 128, p * 128 + 128)
            vcols = slice(wide + p * 128, wide + p * 128 + 128)
            k_tile = kv[rows, cols]
            kx = jnp.concatenate([k_tile, extra], axis=1)
            vx = jnp.concatenate([kv[rows, vcols], extra], axis=1)
            kt = k_tile.T
            dk = jnp.zeros((tile, 128), jnp.float32)
            dv = jnp.zeros((tile, 128), jnp.float32)
            for h in range(2 * p, min(2 * p + 2, heads)):
                half = h % 2
                probs = jnp.exp(dot(kx, qx[h]))
                ds = (probs * dot(vx, dox[h])).astype(jnp.bfloat16)
                dqt[h * HD : h * HD + HD, :] += dot(kt[half * HD : half * HD + HD, :], ds)
                dk = dk + dot(ds, qpad[h])
                dv = dv + dot(probs.astype(jnp.bfloat16), dopad[h])
            kdot[...] += jnp.sum(dk * k_tile.astype(jnp.float32), axis=0, keepdims=True)
            part = grads[0].shape[0]
            if tile > part:
                for g, grad in enumerate(grads):
                    grad[:, cols] = dk[g * part : g * part + part, :].astype(grad.dtype)
                    grad[:, vcols] = dv[g * part : g * part + part, :].astype(grad.dtype)
                continue
            for g, grad in enumerate(grads):

                @pl.when(t // (steps // len(grads)) == g)
                def store(g=g, grad=grad, dk=dk, dv=dv, cols=cols, vcols=vcols):
                    start = (t - g * (steps // len(grads))) * tile
                    here = pl.ds(pl.multiple_of(start, tile), tile)
                    grad[here, cols] = dk.astype(grad.dtype)
                    grad[here, vcols] = dv.astype(grad.dtype)

        return carry

    lax.fori_loop(0, steps, step, 0)


def attend_back(info, qt, dot_t, q_tok, do_tok, lse, delta, pieces, heads, clips, kind, parts=1, before=None, tile=2048):
    count = len(pieces)
    before = [] if before is None else [before]
    wide, width = qt.shape
    rows = pieces[0].shape[0]
    tile = rows * count if rows * count <= tile else min(tile, rows * count // parts)
    return pl.pallas_call(
        functools.partial(bwd_kernel, heads, clips, count, tile, len(before)),
        out_shape=(
            jax.ShapeDtypeStruct((wide, width), jnp.float32),
            jax.ShapeDtypeStruct((1, 128), jnp.float32),
        )
        + (jax.ShapeDtypeStruct((count * rows // parts, 2 * wide), kind),) * parts,
        in_specs=[pl.BlockSpec(memory_space=pltpu.SMEM)]
        + [pl.BlockSpec()] * (6 + len(before))
        + [pl.BlockSpec(memory_space=pltpu.HBM)] * count,
        out_specs=(pl.BlockSpec(),) * (2 + parts),
        scratch_shapes=[
            pltpu.VMEM((heads, 256, width), jnp.bfloat16),
            pltpu.VMEM((heads, 256, width), jnp.bfloat16),
            pltpu.VMEM((heads, width, 128), jnp.bfloat16),
            pltpu.VMEM((heads, width, 128), jnp.bfloat16),
            pltpu.VMEM((count * rows, 2 * wide), jnp.bfloat16),
            pltpu.SemaphoreType.DMA((count,)),
        ],
        compiler_params=pltpu.CompilerParams(vmem_limit_bytes=BACK_MIB << 20),
        cost_estimate=CHEAP,
        name="attend_back",
    )(info, qt, dot_t, q_tok, do_tok, lse, delta, *before, *pieces)


ROWS = (((1,), (1,)), ((), ()))
COLS = (((0,), (0,)), ((), ()))
f32 = jnp.float32
bf16 = jnp.bfloat16


def matmul(left, right, dims=None):
    if dims is None:
        return jnp.dot(left, right, preferred_element_type=f32)
    return lax.dot_general(left, right, dims, preferred_element_type=f32)


def first_way(i):
    return i ^ 2 if i % 2 == 0 else i ^ 4


def other_way(i):
    return i ^ 4 if i % 2 == 0 else i ^ 2


def swap(value, axis, count, to):
    return lax.ppermute(value, axis, [(i, to(i)) for i in range(count)])


def seq_roles(seq_index, seq_count):
    if seq_count != 8:
        return jnp.arange(seq_count, dtype=jnp.int32)
    peer = seq_index ^ 1

    def roles(i):
        even = i % 2 == 0
        return [i, jnp.where(even, i ^ 2, i ^ 4), jnp.where(even, i ^ 4, i ^ 2), i ^ 6]

    return jnp.stack(roles(seq_index) + roles(peer)).astype(jnp.int32)


def gather_pieces(block, seq_count):
    if seq_count != 8:
        whole = lax.all_gather(block, "seq", axis=0, tiled=False)
        return [whole[i] for i in range(seq_count)]
    near = swap(block, "seq", 8, first_way)
    next_ = swap(block, "seq", 8, other_way)
    far = swap(near, "seq", 8, other_way)
    mine = [block, near, next_, far]
    return mine + [swap(v, "seq", 8, lambda i: i ^ 1) for v in mine]


def place_kernel(count, rows, widths, roles, *rest):
    pieces, outs, sem = rest[:count], rest[count:-1], rest[-1]
    copies = []
    for k in range(count):
        to = pl.ds(pl.multiple_of(roles[k] * rows, rows), rows)
        first = 0
        for n, width in enumerate(widths):
            piece = pieces[k].at[:, first : first + width]
            copies.append(pltpu.make_async_copy(piece, outs[n].at[to, :], sem.at[k, n]))
            first += width
    for c in copies:
        c.start()
    for c in copies:
        c.wait()


def place(pieces, roles, widths=None, limit=SMALL_MIB):
    count = len(pieces)
    rows, width = pieces[0].shape
    outs = widths or (width,)
    placed = pl.pallas_call(
        functools.partial(place_kernel, count, rows, outs),
        out_shape=[jax.ShapeDtypeStruct((count * rows, w), pieces[0].dtype) for w in outs],
        in_specs=[pl.BlockSpec(memory_space=pltpu.SMEM)]
        + [pl.BlockSpec(memory_space=pltpu.HBM)] * count,
        out_specs=[pl.BlockSpec(memory_space=pltpu.VMEM)] * len(outs),
        scratch_shapes=[pltpu.SemaphoreType.DMA((count, len(outs)))],
        compiler_params=pltpu.CompilerParams(vmem_limit_bytes=limit << 20),
        cost_estimate=CHEAP,
        name="place",
    )(roles, *pieces)
    return placed if widths else placed[0]


def take_kernel(rows, core, part, out, sem):
    copies = []
    for chip in range(4):
        start = pl.multiple_of((2 * chip + core[0]) * rows, rows)
        to = out.at[pl.ds(chip * rows, rows), :]
        copies.append(pltpu.make_async_copy(part.at[pl.ds(start, rows), :], to, sem.at[chip]))
    for c in copies:
        c.start()
    for c in copies:
        c.wait()


def first_kernel(rows, where, part, got, mine, send, held, sem):
    copies = []
    for chip in range(4):
        start = pl.multiple_of((2 * chip + where[0]) * rows, rows)
        to = held.at[pl.ds(chip * rows, rows), :]
        copies.append(pltpu.make_async_copy(part.at[pl.ds(start, rows), :], to, sem.at[chip]))
    for c in copies:
        c.start()
    for c in copies:
        c.wait()
    mine[...] = (held[...].astype(f32) + got[...].astype(f32)).astype(bf16)
    for n in range(2):
        send[n * rows : n * rows + rows, :] = mine[pl.ds(pl.multiple_of(where[1 + n] * rows, rows), rows), :]


def second_kernel(rows, where, mine, got, own, send):
    block = lambda n: mine[pl.ds(pl.multiple_of(where[n] * rows, rows), rows), :].astype(f32)
    own[...] = (block(0) + got[rows:, :].astype(f32)).astype(bf16)
    send[...] = (block(1) + got[:rows, :].astype(f32)).astype(bf16)


def scatter_call(kernel, rows, where, arrays, outs, scratch, name, first=pltpu.VMEM):
    width = arrays[0].shape[1]
    vmem = pl.BlockSpec(memory_space=pltpu.VMEM)
    return pl.pallas_call(
        functools.partial(kernel, rows),
        out_shape=[jax.ShapeDtypeStruct((n * rows, width), bf16) for n in outs],
        in_specs=[pl.BlockSpec(memory_space=pltpu.SMEM), pl.BlockSpec(memory_space=first)]
        + [vmem] * (len(arrays) - 1),
        out_specs=[vmem] * len(outs),
        scratch_shapes=scratch,
        compiler_params=pltpu.CompilerParams(vmem_limit_bytes=SMALL_MIB << 20),
        cost_estimate=CHEAP,
        name=name,
    )(where, *arrays)


def scatter_start(part, where):
    rows = part.shape[0] // 8
    sems = [pltpu.SemaphoreType.DMA((4,))]
    theirs = scatter_call(take_kernel, rows, where, [part], [4], sems, "scatter_take", pl.ANY)[0]
    return part, swap(theirs, "seq", 8, lambda i: i ^ 1)


def scatter_first(pair, where):
    part, got = pair
    rows = part.shape[0] // 8
    scratch = [pltpu.VMEM(got.shape, bf16), pltpu.SemaphoreType.DMA((4,))]
    mine, send = scatter_call(first_kernel, rows, where, [part, got], [4, 2], scratch, "scatter_first", pl.ANY)
    return mine, swap(send, "seq", 8, other_way)


def scatter_second(pair, where):
    mine, got = pair
    own, send = scatter_call(second_kernel, mine.shape[0] // 4, where, [mine, got], [1, 1], [], "scatter_second")
    return own, swap(send, "seq", 8, first_way)


def widen_kernel(count, turn, *refs):
    total = refs[0][...].astype(f32)
    for ref in refs[1:count]:
        total = total + ref[...].astype(f32)
    refs[count][...] = total.T if turn else total


def widen(parts, turn=False):
    rows, width = parts[0].shape
    return pl.pallas_call(
        functools.partial(widen_kernel, len(parts), turn),
        out_shape=jax.ShapeDtypeStruct((width, rows) if turn else (rows, width), f32),
        compiler_params=pltpu.CompilerParams(vmem_limit_bytes=SMALL_MIB << 20),
        cost_estimate=CHEAP,
        name="widen",
    )(*parts)


def hops(axis, count):
    return [(axis, 1 << k) for k in range(count.bit_length() - 1)]


def sum_all(value, axes, order, beside=()):
    if any(count & (count - 1) for _, count in axes):
        return lax.psum(value, [axis for axis, _ in axes]), list(beside)
    counts, beside = dict(axes), list(beside)
    for k, (axis, bit) in enumerate(order):
        got = swap(value, axis, counts[axis], lambda i: i ^ bit)
        if k < len(beside):
            got, beside[k] = lax.optimization_barrier((got, beside[k]))
        value = value + got
    return value, beside


def add_low(a, b):
    return (a.astype(f32) + b.astype(f32)).astype(bf16)


def relay_kernel(names, end, *refs):
    ins = dict(zip(names, refs))
    outs = list(refs[len(names) :])
    add = lambda a, b: (ins[a][...].astype(f32) + ins[b][...].astype(f32)).astype(bf16)
    if "part" in ins:
        outs.pop(0)[...] = add("part", "part_got")
    if "total" in ins:
        total = add("total", "total_got")
        outs.pop(0)[...] = total
        if "own" in ins:
            send = outs.pop(0)
            rows, own_rows = total.shape[0], ins["own"].shape[0]
            both = min(rows, own_rows)
            send[:both, :] = jnp.where(end[0] == 1, ins["own"][:both, :], total[:both, :])
            if own_rows > both:
                send[both:, :] = ins["own"][both:, :]
            if rows > both:
                send[both:, :] = total[both:, :]


def relay(end, part, total, own):
    ins = {}
    shapes = []
    if part is not None:
        ins.update(part=part[0], part_got=part[1])
        shapes.append(part[0].shape)
    if total is not None:
        ins.update(total=total[0], total_got=total[1])
        shapes.append(total[0].shape)
        if own is not None:
            ins["own"] = own
            shapes.append((max(own.shape[0], total[0].shape[0]), own.shape[1]))
    if not shapes:
        return None, None, own
    outs = pl.pallas_call(
        functools.partial(relay_kernel, tuple(ins)),
        out_shape=[jax.ShapeDtypeStruct(shape, bf16) for shape in shapes],
        in_specs=[pl.BlockSpec(memory_space=pltpu.SMEM)] + [pl.BlockSpec(memory_space=pltpu.VMEM)] * len(ins),
        out_specs=[pl.BlockSpec(memory_space=pltpu.VMEM)] * len(shapes),
        compiler_params=pltpu.CompilerParams(vmem_limit_bytes=SMALL_MIB << 20),
        cost_estimate=CHEAP,
        name="relay",
    )(end, *ins.values())
    outs = list(outs)
    part = outs.pop(0) if part is not None else None
    total = outs.pop(0) if total is not None else None
    return part, total, outs.pop(0) if outs else own


def staged(kernel, k, outs, wholes, scalars, arrays, before, name, limit=SMALL_MIB):
    before = before or []
    vmem = pl.BlockSpec() if limit == 60 else pl.BlockSpec(memory_space=pltpu.VMEM)
    anywhere = pl.BlockSpec(memory_space=pl.ANY)
    given = len(scalars) + len(arrays)
    return pl.pallas_call(
        functools.partial(kernel, k, len(before)),
        out_shape=[jax.ShapeDtypeStruct(shape, kind) for shape, kind in outs]
        + [jax.ShapeDtypeStruct((tokens, width), kind) for tokens, rows, width, kind in wholes],
        in_specs=[pl.BlockSpec(memory_space=pltpu.SMEM)] * len(scalars)
        + [vmem] * len(arrays)
        + [anywhere] * len(before),
        out_specs=[vmem] * len(outs) + [anywhere] * len(wholes),
        scratch_shapes=[pltpu.VMEM((rows, width), kind) for tokens, rows, width, kind in wholes]
        + [pltpu.SemaphoreType.DMA(())] * len(wholes),
        input_output_aliases={given + n: len(outs) + n for n in range(len(before))},
        compiler_params=pltpu.CompilerParams(vmem_limit_bytes=limit << 20),
        cost_estimate=CHEAP,
        name=name,
    )(*scalars, *arrays, *before)


def put_rows(k, value, whole, sem):
    rows = value.shape[0]
    copy = pltpu.make_async_copy(value, whole.at[pl.ds(k * rows, rows), :], sem)
    copy.start()
    return copy


def rms(value):
    return lax.rsqrt(jnp.mean(value * value, axis=-1, keepdims=True) + 1e-06)


def rms_back(grad, normed, scale):
    return scale * (grad - normed * jnp.mean(grad * normed, axis=-1, keepdims=True))


def dot_rows(a, b):
    return lax.dot_general(a, b, ROWS, preferred_element_type=f32)


def picked(end, total, got):
    return jnp.where(end[0] == 1, got[...], total[...]).astype(f32)


def forward_kernel(k, again, end, total, got, x, gains, gate_w, up_w, down_t, *rest):
    norms, stats, pre, part, low, pack, sem = rest[again:]
    width, units = x.shape[1], gate_w.shape[1]
    attn = picked(end, total, got)
    scale = rms(attn)
    normed = attn * scale
    norms[:, :width] = normed
    middle = x[...].astype(f32) + normed * gains[1:2, :]
    norms[:, width:] = middle
    middle_scale = rms(middle)
    lane = lax.broadcasted_iota(jnp.int32, stats.shape, 1)
    stats[...] = jnp.where(lane == 0, scale, middle_scale)
    act = (middle * middle_scale * gains[2:3, :]).astype(bf16)
    pack[:, units:] = act
    gated = dot(act, gate_w[...])
    upper = dot(act, up_w[...])
    pre[:, :units] = gated
    pre[:, units:] = upper
    unit = (gated * jax.nn.sigmoid(gated) * upper).astype(bf16)
    pack[:, :units] = unit
    copy = put_rows(k, pack, low, sem)
    part[...] = dot_rows(unit, down_t[...]).astype(bf16)
    copy.wait()


def backward_kernel(k, again, end, total, got, norms, pre, cot, gains, gate_w, up_w, down_t, *rest):
    sums, part, low, out, pack, done, sem, out_sem = rest[again:]
    width, units = cot.shape[1], gate_w.shape[1]
    ffn = picked(end, total, got)
    scale = rms(ffn)
    normed = ffn * scale
    done[...] = (norms[:, width:] + normed * gains[3:4, :]).astype(bf16)
    out_copy = put_rows(k, done, out, out_sem)
    grad = cot[...].astype(f32)
    sums[...] = jnp.sum(grad * normed, axis=0, keepdims=True)
    grad_ffn = rms_back(grad * gains[3:4, :], normed, scale).astype(bf16)
    pack[:, 2 * units :] = grad_ffn
    grad_units = dot(grad_ffn, down_t[...])
    gated = pre[:, :units]
    sig = jax.nn.sigmoid(gated)
    low_gate = (grad_units * pre[:, units:] * sig * (1.0 + gated * (1.0 - sig))).astype(bf16)
    low_up = (grad_units * gated * sig).astype(bf16)
    pack[:, :units] = low_gate
    pack[:, units : 2 * units] = low_up
    copy = put_rows(k, pack, low, sem)
    part[...] = (dot_rows(low_gate, gate_w[...]) + dot_rows(low_up, up_w[...])).astype(bf16)
    copy.wait()
    out_copy.wait()


def attn_back_kernel(k, again, end, total, got, norms, stats, cot, gains, *rest):
    sums, dmid, dattn, pack, sem = rest[again:]
    width = cot.shape[1]
    grad = picked(end, total, got)
    scale, middle_scale = stats[:, 0:1], stats[:, 1:2]
    normed = norms[:, width:] * middle_scale
    sums[0:1, :] = jnp.sum(grad * normed, axis=0, keepdims=True)
    middle = cot[...].astype(f32) + rms_back(grad * gains[2:3, :], normed, middle_scale)
    dmid[...] = middle
    normed = norms[:, :width]
    sums[1:2, :] = jnp.sum(middle * normed, axis=0, keepdims=True)
    pack[...] = rms_back(middle * gains[1:2, :], normed, scale).astype(bf16)
    put_rows(k, pack, dattn, sem).wait()


def weight_grad_kernel(left, right, out):
    out[...] = lax.dot_general(left[...], right[...], COLS, preferred_element_type=f32).astype(bf16)


def weight_grad(left, first, width, right, place, right_width):
    tokens = left.shape[0]
    step = 512
    return pl.pallas_call(
        weight_grad_kernel,
        out_shape=jax.ShapeDtypeStruct((width, right_width), bf16),
        grid=(width // step,),
        in_specs=[
            pl.BlockSpec((tokens, step), lambda i: (0, first // step + i)),
            pl.BlockSpec((tokens, right_width), lambda i: (0, place)),
        ],
        out_specs=pl.BlockSpec((step, right_width), lambda i: (i, 0)),
        compiler_params=pltpu.CompilerParams(vmem_limit_bytes=60 << 20),
        cost_estimate=CHEAP,
        name="weight_grad",
    )(left, right)


def run_ticks(parts, computes, head_index, head_count, fill):
    carry = []
    stages = 4 * len(computes)
    ticks = stages + len(parts) - 1
    if head_count != 4:
        for n, compute in enumerate(computes):
            sums = [lax.psum(part, "head") for part in parts]
            parts = []
            for k, part in enumerate(sums):
                before = parts[k - 1] if k else None
                parts.append(compute(k, jnp.zeros((1,), jnp.int32), part, part, before))
        for t in range(ticks):
            carry = fill[t](carry) if t in fill else carry
        return parts, carry
    end = jnp.where((head_index == 0) | (head_index == 3), 1, 0).astype(jnp.int32).reshape(1)
    states = [(part,) for part in parts]
    for t in range(ticks):
        at = {(t - k) % 4: k for k in range(len(parts)) if 0 <= t - k < stages}
        live = [k for k in range(len(parts)) if t - k < stages + 1]
        own = states[at[0]][0] if 0 in at else None
        part, total, send = relay(
            end, states[at[1]] if 1 in at else None, states[at[2]] if 2 in at else None, own
        )
        late = states[at[3]] if 3 in at else ()
        if part is not None or total is not None:
            part, total, send, late, carry = lax.optimization_barrier((part, total, send, late, carry))
        if 3 in at:
            states[at[3]] = late
        if 1 in at:
            states[at[1]] = (part, lax.ppermute(part, "head", [(1, 2), (2, 1)]))
        if 0 in at and 2 in at:
            got = lax.ppermute(send, "head", [(0, 1), (3, 2), (1, 0), (2, 3)])
            states[at[0]] = (own, got[: own.shape[0]])
            states[at[2]] = (total, got[: total.shape[0]])
        elif 0 in at:
            states[at[0]] = (own, lax.ppermute(own, "head", [(0, 1), (3, 2)]))
        elif 2 in at:
            states[at[2]] = (total, lax.ppermute(total, "head", [(1, 0), (2, 3)]))
        if 3 in at:
            k = at[3]
            before = states[k - 1][0] if k else None
            states[k] = (computes[(t - k) // 4](k, end, *states[k], before),)
        if t in fill:
            carry = fill[t](carry)
        held, carry = lax.optimization_barrier(([states[k] for k in live], carry))
        for k, state in zip(live, held):
            states[k] = state
    return [state[0] for state in states], carry


def head_mean(value):
    row = lax.broadcasted_iota(jnp.int32, (128, 128), 0) // HD
    col = lax.broadcasted_iota(jnp.int32, (128, 128), 1) // HD
    ones = jnp.where(row == col, 1.0 / HD, 0.0).astype(bf16)
    hi, mid, lo = split3(value)
    return dot(hi.astype(bf16), ones) + dot(mid.astype(bf16), ones) + dot(lo.astype(bf16), ones)


def partner(value):
    lane = lax.broadcasted_iota(jnp.int32, value.shape, 1) % HD
    return jnp.where(lane < HD // 2, pltpu.roll(value, 128 - HD // 2, 1), pltpu.roll(value, HD // 2, 1))


def text_norm_kernel(pre, gain, out):
    wide = pre.shape[1] // 2
    for p in range(wide // 128):
        cols = slice(p * 128, p * 128 + 128)
        value = pre[:, cols].astype(f32)
        out[:, cols] = (value * lax.rsqrt(head_mean(value * value) + 1e-6) * gain[...]).astype(bf16)
    out[:, wide:] = pre[:, wide:]


def text_norm(pre, gain):
    return pl.pallas_call(
        text_norm_kernel, out_shape=jax.ShapeDtypeStruct(pre.shape, bf16), name="text_norm", cost_estimate=CHEAP
    )(pre, gain)


def qkv_kernel(count, rows, wide, roles, x, gain, qgain, kgain, cos, sin, *rest):
    pieces, (act, scale, pre, kv, query, query_t, weight, sem) = rest[:count], rest[count:]
    copies = []
    for k in range(count):
        start = pl.multiple_of(roles[k] * rows, rows)
        copies.append(pltpu.make_async_copy(pieces[k], weight.at[pl.ds(start, rows), :], sem.at[k]))
    for c in copies:
        c.start()
    value = x[...].astype(f32)
    inverse = lax.rsqrt(jnp.mean(value * value, axis=-1, keepdims=True) + 1e-6)
    scale[...] = inverse
    act[...] = (value * inverse * gain[0:1, :]).astype(bf16)
    for c in copies:
        c.wait()
    pre[...] = dot(act[...], weight[:, : 2 * wide])
    kv[:, wide:] = dot(act[...], weight[:, 2 * wide :]).astype(bf16)
    for p in range(wide // 128):
        cols = slice(p * 128, p * 128 + 128)
        for which, out_gain in ((0, qgain), (1, kgain)):
            raw = pre[:, which * wide + p * 128 : which * wide + p * 128 + 128]
            raw = raw * lax.rsqrt(head_mean(raw * raw) + 1e-6) * out_gain[...]
            raw = raw * cos[...] + partner(raw) * sin[...]
            if which == 1:
                kv[:, cols] = raw.astype(bf16)
            else:
                raw = raw.astype(bf16).astype(f32) * HD**-0.5
                query[:, cols] = raw.astype(bf16)
                query_t[cols, :] = raw.T.astype(bf16)


def project(roles, x, gain, qgain, kgain, cos, sin, pieces, wide):
    count = len(pieces)
    rows = pieces[0].shape[0]
    tokens, width = x.shape
    shape = jax.ShapeDtypeStruct
    return pl.pallas_call(
        functools.partial(qkv_kernel, count, rows, wide),
        out_shape=(
            shape((tokens, width), bf16),
            shape((tokens, 1), f32),
            shape((tokens, 2 * wide), f32),
            shape((tokens, 2 * wide), bf16),
            shape((tokens, wide), bf16),
            shape((wide, tokens), bf16),
            shape((width, 3 * wide), bf16),
        ),
        in_specs=[pl.BlockSpec(memory_space=pltpu.SMEM)]
        + [pl.BlockSpec(memory_space=pltpu.VMEM)] * 6
        + [pl.BlockSpec(memory_space=pltpu.HBM)] * count,
        out_specs=(pl.BlockSpec(memory_space=pltpu.VMEM),) * 7,
        scratch_shapes=[pltpu.SemaphoreType.DMA((count,))],
        compiler_params=pltpu.CompilerParams(vmem_limit_bytes=60 << 20),
        cost_estimate=CHEAP,
        name="project",
    )(roles, x, gain, qgain, kgain, cos, sin, *pieces)


def mix_kernel(heads, gate, sums, cross, mixed, self_t, cross_t, lse, cross_lse):
    for p in range((heads + 1) // 2):
        both = []
        for h in range(2 * p, 2 * p + 2):
            if h >= heads:
                both.append(jnp.zeros_like(both[0]))
                continue
            rows = slice(h * HD, h * HD + HD)
            den, cross_den = sums[h, HD : HD + 1, :], cross[h, HD : HD + 1, :]
            lse[h : h + 1, :] = jnp.log(den)
            cross_lse[h : h + 1, :] = jnp.log(cross_den)
            own = sums[h, :HD, :] / den
            other = cross[h, :HD, :] / cross_den
            self_t[rows, :] = own
            cross_t[rows, :] = other
            both.append(own + gate[h] * other)
        mixed[:, p * 128 : p * 128 + 128] = jnp.concatenate(both, axis=0).T.astype(bf16)


def mix(gate, sums, cross, wide):
    heads, _, tokens = sums.shape
    shape = jax.ShapeDtypeStruct
    return pl.pallas_call(
        functools.partial(mix_kernel, heads),
        out_shape=(
            shape((tokens, wide), bf16),
            shape((heads * HD, tokens), f32),
            shape((heads * HD, tokens), f32),
            shape((heads, tokens), f32),
            shape((heads, tokens), f32),
        ),
        in_specs=[pl.BlockSpec(memory_space=pltpu.SMEM)] + [pl.BlockSpec(memory_space=pltpu.VMEM)] * 2,
        compiler_params=pltpu.CompilerParams(vmem_limit_bytes=SMALL_MIB << 20),
        name="mix",
        cost_estimate=CHEAP,
    )(gate, sums, cross)


def unmix_kernel(heads, gate, weight, self_t, cross_t, grad, tok, tok_t, ctok, ctok_t, delta, cdelta, cgate):
    width = tok.shape[0]
    for p in range((heads + 1) // 2):
        cols = slice(p * 128, p * 128 + 128)
        value = dot(grad[...], weight[:, cols])
        lane = lax.broadcasted_iota(jnp.int32, (width, 128), 1) // HD
        gates = jnp.where(lane == 0, gate[2 * p], gate[min(2 * p + 1, heads - 1)])
        tok[:, cols] = value.astype(bf16)
        ctok[:, cols] = (value * gates).astype(bf16)
        turned = value.T
        for h in range(2 * p, 2 * p + 2):
            rows = slice(h * HD, h * HD + HD)
            part = turned[(h % 2) * HD : (h % 2) * HD + HD, :]
            tok_t[rows, :] = part.astype(bf16)
            if h >= heads:
                ctok_t[rows, :] = part.astype(bf16)
                continue
            low = (part * gate[h]).astype(bf16)
            ctok_t[rows, :] = low
            delta[h : h + 1, :] = jnp.sum(part.astype(bf16).astype(f32) * self_t[rows, :], axis=0, keepdims=True)
            cdelta[h : h + 1, :] = jnp.sum(low.astype(f32) * cross_t[rows, :], axis=0, keepdims=True)
            cgate[h : h + 1, :] = jnp.sum(part * cross_t[rows, :], axis=0, keepdims=True)


def unmix(gate, grad, weight, self_t, cross_t):
    tokens = self_t.shape[1]
    wide = weight.shape[1]
    heads = self_t.shape[0] // HD
    shape = jax.ShapeDtypeStruct
    return pl.pallas_call(
        functools.partial(unmix_kernel, heads),
        out_shape=(shape((tokens, wide), bf16), shape((wide, tokens), bf16)) * 2 + (shape((heads, tokens), f32),) * 3,
        in_specs=[pl.BlockSpec(memory_space=pltpu.SMEM)]
        + [pl.BlockSpec(memory_space=pltpu.VMEM)] * 4,
        compiler_params=pltpu.CompilerParams(vmem_limit_bytes=SMALL_MIB << 20),
        name="unmix",
        cost_estimate=CHEAP,
    )(gate, weight, self_t, cross_t, grad)


def norm_back(raw, gain, grad, cos=None, sin=None):
    scale = lax.rsqrt(head_mean(raw * raw) + 1e-6)
    normed = raw * scale
    if cos is not None:
        grad = grad * cos - partner(grad) * sin
    gain_grad = jnp.sum(grad * normed, axis=0, keepdims=True)
    grad = grad * gain
    return scale * (grad - normed * head_mean(grad * normed)), gain_grad


def text_back_kernel(pre, gain, grad, out):
    wide = pre.shape[1] // 2
    for p in range(wide // 128):
        cols = slice(p * 128, p * 128 + 128)
        out[:, cols] = norm_back(pre[:, cols].astype(f32), gain[...], grad[:, cols])[0].astype(bf16)
    out[:, wide:] = grad[:, wide:].astype(bf16)


def text_back(pre, gain, grad):
    return pl.pallas_call(
        text_back_kernel,
        out_shape=jax.ShapeDtypeStruct(grad.shape, bf16),
        name="text_back",
        cost_estimate=CHEAP,
    )(pre, gain, grad)


def project_back_kernel(wide, starts, pre, qgain, kgain, cos, sin, dqt, x, scale, weight, *rest):
    kvs, (out, qgrad, kgrad, sums, *acts) = rest[: len(starts)], rest[len(starts) :]
    tokens = pre.shape[0]
    total = [jnp.zeros((1, 128), f32), jnp.zeros((1, 128), f32)]
    summed = lambda cols: sum(kv[start : start + tokens, cols].astype(f32) for kv, start in zip(kvs, starts))
    for p in range(wide // 128):
        cols = slice(p * 128, p * 128 + 128)
        grads = (dqt[cols, :] * HD**-0.5).T, summed(cols)
        for which, gain in ((0, qgain), (1, kgain)):
            at = slice(which * wide + p * 128, which * wide + p * 128 + 128)
            value, extra = norm_back(pre[:, at], gain[...], grads[which], cos[...], sin[...])
            out[:, at] = value.astype(bf16)
            total[which] = total[which] + extra
    out[:, 2 * wide :] = summed(slice(wide, 2 * wide)).astype(bf16)
    qgrad[...] = total[0]
    kgrad[...] = total[1]
    value = dot_rows(out[...], weight[...])
    rows = acts[0].shape[0]
    for n, act in enumerate(acts):
        act[...] = value[n * rows : n * rows + rows, :].astype(bf16)
    sums[...] = jnp.sum(value * (x[...].astype(f32) * scale[...]), axis=0, keepdims=True)


def project_back(pre, qgain, kgain, cos, sin, dqt, x, scale, weight, kvs, starts):
    tokens, wide = pre.shape[0], pre.shape[1] // 2
    shape = jax.ShapeDtypeStruct
    return pl.pallas_call(
        functools.partial(project_back_kernel, wide, tuple(starts)),
        out_shape=(
            shape((tokens, 3 * wide), bf16),
            shape((1, 128), f32),
            shape((1, 128), f32),
            shape((1, x.shape[1]), f32),
        )
        + (shape((tokens // 4, x.shape[1]), bf16),) * 4,
        name="project_back",
        cost_estimate=CHEAP,
        compiler_params=pltpu.CompilerParams(vmem_limit_bytes=60 << 20),
    )(pre, qgain, kgain, cos, sin, dqt, x, scale, weight, *kvs)


def finish_kernel(k, end, total, got, x, gain, mid, mark, *rest):
    out, done, value, sem = rest[-4:]
    rows = mid.shape[0]
    value_x = x[...].astype(f32)
    inverse = rms(value_x)
    normed = value_x * inverse
    grad = picked(end, total, got)[:rows] * gain[0:1, :]
    mean = jnp.mean(grad * normed, axis=-1, keepdims=True)
    value[...] = mid[...] + inverse * (grad - normed * mean)
    copy = pltpu.make_async_copy(value, out.at[pl.ds(k * rows, rows), :], sem)
    copy.start()
    done[...] = mark[...]
    copy.wait()


def finish(k, end, total, got, x, gain, mid, mark, tokens, before):
    before = [] if before is None else [before]
    vmem = pl.BlockSpec(memory_space=pltpu.VMEM)
    return pl.pallas_call(
        functools.partial(finish_kernel, k),
        out_shape=[jax.ShapeDtypeStruct((tokens, mid.shape[1]), f32), jax.ShapeDtypeStruct(mark.shape, f32)],
        in_specs=[pl.BlockSpec(memory_space=pltpu.SMEM)] + [vmem] * 6 + [pl.BlockSpec(memory_space=pl.ANY)] * len(before),
        out_specs=[pl.BlockSpec(memory_space=pl.ANY), vmem],
        scratch_shapes=[pltpu.VMEM(mid.shape, f32), pltpu.SemaphoreType.DMA(())],
        input_output_aliases={7: 0} if before else {},
        name="finish",
        cost_estimate=CHEAP,
        compiler_params=pltpu.CompilerParams(vmem_limit_bytes=SMALL_MIB << 20),
    )(end, total, got, x, gain, mid, mark, *before)


def text_weights_kernel(count, rows, roles, *rest):
    pieces, (own, key_grad, value_grad, held, sem) = rest[:count], rest[count:]
    copies = []
    for k in range(count):
        to = pl.ds(pl.multiple_of(roles[k] * rows, rows), rows)
        copies.append(pltpu.make_async_copy(pieces[k], held.at[to, :], sem.at[k]))
    for c in copies:
        c.start()
    for c in copies:
        c.wait()
    wide = key_grad.shape[1]
    key_grad[...] = lax.dot_general(own[...], held[:, :wide], COLS, preferred_element_type=f32)
    value_grad[...] = lax.dot_general(own[...], held[:, wide:], COLS, preferred_element_type=f32)


def text_weight_grads(pieces, roles, own):
    count = len(pieces)
    rows, width = pieces[0].shape
    vmem = pl.BlockSpec(memory_space=pltpu.VMEM)
    return pl.pallas_call(
        functools.partial(text_weights_kernel, count, rows),
        out_shape=[jax.ShapeDtypeStruct((own.shape[1], width // 2), f32)] * 2,
        in_specs=[pl.BlockSpec(memory_space=pltpu.SMEM)] + [pl.BlockSpec(memory_space=pl.ANY)] * count + [vmem],
        out_specs=[vmem] * 2,
        scratch_shapes=[pltpu.VMEM((count * rows, width), bf16), pltpu.SemaphoreType.DMA((count,))],
        compiler_params=pltpu.CompilerParams(vmem_limit_bytes=60 << 20),
        cost_estimate=CHEAP,
        name="text_weight_grads",
    )(roles, *pieces, own)


def touch_kernel(*refs):
    refs[-1][...] = refs[0][...]


def touch(value, arrays):
    return pl.pallas_call(
        touch_kernel,
        out_shape=jax.ShapeDtypeStruct(value.shape, value.dtype),
        in_specs=[pl.BlockSpec(memory_space=pltpu.VMEM)] * (1 + len(arrays)),
        cost_estimate=CHEAP,
        compiler_params=pltpu.CompilerParams(vmem_limit_bytes=SMALL_MIB << 20),
        name="touch",
    )(value, *arrays)


def gains_back_kernel(sums, mods, gains, gain_grad, mod_grad):
    for n in range(4):
        row = slice(n, n + 1)
        if n % 2 == 0:
            gain_grad[row, :] = sums[row, :] * (1.0 + mods[row, :])
            mod_grad[row, :] = sums[row, :] * gains[row, :]
        else:
            gate = jnp.tanh(mods[row, :])
            gain_grad[row, :] = sums[row, :] * gate
            mod_grad[row, :] = sums[row, :] * gains[row, :] * (1.0 - gate * gate)


def gains_back(sums, mods, gains):
    return pl.pallas_call(
        gains_back_kernel,
        out_shape=[jax.ShapeDtypeStruct(gains.shape, f32)] * 2,
        cost_estimate=CHEAP,
        name="gains_back",
    )(sums, mods, gains)


def vectors_kernel(mods, gains, out):
    out[0:1, :] = gains[0:1, :] * (1.0 + mods[0:1, :])
    out[1:2, :] = jnp.tanh(mods[1:2, :]) * gains[1:2, :]
    out[2:3, :] = gains[2:3, :] * (1.0 + mods[2:3, :])
    out[3:4, :] = jnp.tanh(mods[3:4, :]) * gains[3:4, :]


def vectors(mods, gains):
    return pl.pallas_call(
        vectors_kernel,
        out_shape=jax.ShapeDtypeStruct(gains.shape, f32),
        cost_estimate=CHEAP,
        name="vectors",
    )(mods, gains)


def per_device(
    seq_count,
    head_count,
    hidden_in,
    cond,
    captions,
    clip_lengths,
    ada_weight,
    norm_gains,
    qk_gains,
    w_query,
    w_key,
    w_value,
    w_out,
    cross_gate,
    w_text_key,
    w_text_value,
    w_gate,
    w_up,
    w_down,
    out_cotangent,
):
    local_rows, model_width = hidden_in.shape
    seq_index = lax.axis_index("seq")
    head_index = lax.axis_index("head")
    clips = clip_lengths.shape[0]
    cols = w_query.shape[1]
    heads = cols // HD
    wide = (cols + 127) // 128 * 128
    units = w_gate.shape[1]
    roles = seq_roles(seq_index, seq_count)
    pad = lambda v: jnp.pad(v, ((0, 0), (0, wide - cols))) if wide > cols else v
    cut = lambda v: v[:, :cols]

    spread = seq_count == 8
    core = lambda v: swap(v, "seq", 8, lambda i: i ^ 1)
    hold = lax.optimization_barrier
    axes = (("seq", seq_count), ("head", head_count))
    seq_hops, head_hops = hops("seq", seq_count), hops("head", head_count)
    finish_sum = lambda v: lax.psum_scatter(v, "seq", scatter_dimension=0, tiled=True)

    def hop(value, steps):
        for axis, bit in steps:
            value = value + swap(value, axis, dict(axes)[axis], lambda i: i ^ bit)
        return value

    clip_ends = jnp.cumsum(clip_lengths, dtype=jnp.int32)
    starts = clip_ends - clip_lengths
    text_rows = captions.reshape(-1, captions.shape[2])
    text_block = text_rows.shape[0] // seq_count
    text_ids = jnp.arange(clips, dtype=jnp.int32) * captions.shape[1]
    first_row = seq_index * local_rows
    place_info = jnp.concatenate([first_row[None], starts, clip_ends]).astype(jnp.int32)
    text_info = jnp.concatenate(
        [place_info, text_ids, text_ids + captions.shape[1], jnp.zeros((1,), jnp.int32)]
    )

    infos = {}

    def self_info(which):
        which = tuple(which)
        if which not in infos:
            infos[which] = jnp.concatenate([place_info, starts, clip_ends, roles[jnp.array(which)] * local_rows])
        return infos[which]

    places = first_row + jnp.arange(local_rows, dtype=jnp.int32)
    inside = (places[:, None] >= starts[None, :]) & (places[:, None] < clip_ends[None, :])
    position = places - jnp.sum(jnp.where(inside, starts[None, :], 0), axis=1, dtype=jnp.int32)
    lane = jnp.arange(128)
    frequency = 10000.0 ** (-(lane % (HD // 2)).astype(f32) / (HD // 2))
    angles = position.astype(f32)[:, None] * frequency[None, :]
    cos = jnp.cos(angles)
    sin = jnp.where(lane % HD < HD // 2, -1.0, 1.0)[None, :] * jnp.sin(angles)
    query_gain = jnp.tile(qk_gains[0], 2)[None, :]
    key_gain = jnp.tile(qk_gains[1], 2)[None, :]

    cond_act = jax.nn.silu(cond).astype(bf16)
    piece_width = ada_weight.shape[1]
    mod_piece = matmul(cond_act[None, :], ada_weight)
    mine = lax.broadcasted_iota(jnp.int32, (seq_count * head_count, 1), 0) == seq_index * head_count + head_index
    modulation = jnp.where(mine, mod_piece, 0.0)
    modulation, w_query = hold((modulation, w_query))
    qkv_block = jnp.concatenate([pad(w_query), pad(w_key), pad(w_value)], axis=1)
    out_block = pad(w_out.T)
    slab_width = text_rows.shape[1] // seq_count
    if spread:
        modulation = hop(modulation, seq_hops[:1])
        modulation, text_rows = hold((modulation, text_rows))
    own_text = lax.dynamic_slice_in_dim(text_rows, seq_index * slab_width, slab_width, 1)
    text_part = matmul(own_text, jnp.concatenate([pad(w_text_key), pad(w_text_value)], axis=1)).astype(bf16)

    def queries_keys(pieces):
        return project(roles, hidden_in, rows, query_gain, key_gain, cos, sin, pieces, wide)

    def part_sums(group, blocks, before=None):
        return attend(self_info(group), query_t, blocks, heads, clips, before)

    if spread:
        near = swap(qkv_block, "seq", 8, first_way)
        next_ = swap(qkv_block, "seq", 8, other_way)
        modulation = hop(modulation, head_hops[:1])
        text_pre = lax.psum(text_part, "seq")
        gate_w = lax.all_gather(w_gate, "seq", axis=0, tiled=True)
        near, next_, modulation = hold((near, next_, modulation))
        far = swap(near, "seq", 8, other_way)
        modulation = hop(modulation, head_hops[1:])
        modulation = hop(modulation, seq_hops[1:])
        qkv_pieces = [qkv_block, near, next_, far]
        qkv_pieces = qkv_pieces + [core(v) for v in qkv_pieces]
        modulation, qkv_pieces, out_block = hold((modulation, qkv_pieces, out_block))
        modulation = modulation.reshape(4, model_width)
        rows = vectors(modulation, norm_gains)
        act_a, x_scale, pre, kv_own, queries, query_t, w_qkv = queries_keys(qkv_pieces)
        kv_own, modulation, out_block = hold((kv_own, modulation, out_block))
        near = swap(kv_own, "seq", 8, first_way)
        next_ = swap(kv_own, "seq", 8, other_way)
        kv_peer = core(kv_own)
        out_near = swap(out_block, "seq", 8, first_way)
        out_next = swap(out_block, "seq", 8, other_way)
        sums = part_sums((0, 4), [kv_own, kv_peer])
        for group in ((1, 2, 5, 6), (3, 7), (3, 2, 7, 6), (1, 5)):
            self_info(group)
        chip = seq_index // 2
        near_chip = jnp.where(seq_index % 2 == 0, chip ^ 1, chip ^ 2)
        next_chip = jnp.where(seq_index % 2 == 0, chip ^ 2, chip ^ 1)
        wheres = [[1 - seq_index % 2], [seq_index % 2, chip ^ 3, next_chip], [chip, near_chip]]
        wheres = [jnp.stack(where).astype(jnp.int32) for where in wheres]
        ready = (near, next_, sums, out_near, out_next, infos, text_info, wheres)
        near, next_, sums, out_near, out_next, infos_held, text_info, wheres = hold(ready)
        infos.update(infos_held)
        far = swap(near, "seq", 8, other_way)
        out_far = swap(out_near, "seq", 8, other_way)
        near_peer, next_peer = core(near), core(next_)
        out_peers = [core(out_block), core(out_near), core(out_next)]
        sums = part_sums((1, 2, 5, 6), [near, next_, near_peer, next_peer], sums)
        ud_block = jnp.concatenate([w_up, w_down.T], axis=1)
        far, sums, out_far, text_pre, ud_block = hold((far, sums, out_far, text_pre, ud_block))
        far_peer = core(far)
        ud_near = swap(ud_block, "seq", 8, first_way)
        ud_next = swap(ud_block, "seq", 8, other_way)
        out_t = place([out_block, out_near, out_next, out_far] + out_peers + [core(out_far)], roles)
        text_pieces = [text_norm(text_pre, key_gain)]
        cross_sums = attend(text_info, query_t, text_pieces, heads, clips)
        sums = part_sums((3, 7), [far, far_peer], sums)
        pieces = [kv_own, near, next_, far, kv_peer, near_peer, next_peer, far_peer]
    else:
        modulation = lax.psum(modulation, ("seq", "head"))
        text_pre = lax.psum(text_part, "seq")
        qkv_pieces = gather_pieces(qkv_block, seq_count)
        modulation = modulation.reshape(4, model_width)
        rows = vectors(modulation, norm_gains)
        act_a, x_scale, pre, kv_own, queries, query_t, w_qkv = queries_keys(qkv_pieces)
        pieces = gather_pieces(kv_own, seq_count)
        text_pieces = [text_norm(text_pre, key_gain)]
        out_t = place(gather_pieces(out_block, seq_count), roles)
        sums = part_sums(tuple(range(seq_count)), pieces)
        cross_sums = attend(text_info, query_t, text_pieces, heads, clips)
        gate_w = lax.all_gather(w_gate, "seq", axis=0, tiled=True)
    gate_local = jnp.tanh(cross_gate)
    mixed, self_t, cross_t, self_lse, cross_lse = mix(gate_local, sums, cross_sums, wide)
    attn_part = matmul(mixed, out_t, ROWS).astype(bf16)

    late = {}

    def split_weights(pieces):
        return place(pieces, roles, (units, units), 40)

    def fill_near(carry):
        return [ud_near, ud_next]

    def fill_far(carry):
        near, next_ = carry
        return [near, next_, swap(near, "seq", 8, other_way), core(ud_block), core(near), core(next_)]

    def fill_weights(carry):
        late["up"], late["down"] = split_weights([ud_block] + carry + [core(carry[2])])
        late["rows"] = touch(rows, [gate_w, late["up"], late["down"]])
        return [late["rows"]]

    if not spread:
        weights = gather_pieces(jnp.concatenate([w_up, w_down.T], axis=1), seq_count)
        late["up"], late["down"] = split_weights(weights)
        late["rows"] = rows
    chunk_count = 4
    chunk = local_rows // chunk_count
    rows_of = lambda v, k: v[k * chunk : (k + 1) * chunk]
    kept = [{} for _ in range(chunk_count)]


    tall, thin = (chunk, model_width), (chunk, units)
    whole = lambda width: (local_rows, chunk, width, bf16)

    def feed_forward(k, end, total, got, before):
        keep = kept[k]
        outs = [((chunk, 2 * model_width), f32), ((chunk, 128), f32), ((chunk, 2 * units), f32), (tall, bf16)]
        arrays = [total, got, rows_of(hidden_in, k), late["rows"], gate_w, late["up"], late["down"]]
        keep["norms"], keep["stats"], keep["pre"], part, late["first"] = staged(
            forward_kernel, k, outs, [whole(units + model_width)], [end], arrays,
            [late["first"]] if k else None, "feed_forward",
        )
        return part

    def feed_back(k, end, total, got, before):
        keep = kept[k]
        arrays = [total, got, keep["norms"], keep["pre"], rows_of(out_cotangent, k), late["rows"]]
        keep["uf"], part, late["second"], late["hidden"] = staged(
            backward_kernel, k, [((1, model_width), f32), (tall, bf16)],
            [whole(2 * units + model_width), whole(model_width)], [end], arrays + [gate_w, late["up"], late["down"]],
            [late["second"], late["hidden"]] if k else None, "feed_back",
        )
        return part

    def attn_back(k, end, total, got, before):
        keep = kept[k]
        arrays = [total, got, keep["norms"], keep["stats"], rows_of(out_cotangent, k), rows]
        keep["sums"], keep["dmid"], late["dattn"] = staged(
            attn_back_kernel, k, [((2, model_width), f32), (tall, f32)], [whole(model_width)], [end], arrays,
            [late["dattn"]] if k else None, "attn_back", 60,
        )
        return keep["sums"]

    total_of = lambda name, n: sum(keep[name][n] for keep in kept)

    def fill_down(carry):
        return [weight_grad(late["second"], 2 * units, model_width, late["first"], 0, units)]

    def fill_gate(carry):
        late["down_sum"] = finish_sum(carry[0])
        (first, second), carry = hold(((late["first"], late["second"]), carry))
        late["first"], late["second"] = first, second
        return [weight_grad(first, units, model_width, second, 0, units)]

    def fill_up(carry):
        late["gate_sum"] = finish_sum(carry[0])
        (first, second), carry = hold(((late["first"], late["second"]), carry))
        return [weight_grad(first, units, model_width, second, 1, units)]

    def fill_last(carry):
        late["up_sum"] = finish_sum(carry[0])
        return []

    fills = {8 + chunk_count - 1: fill_down, 8 + chunk_count: fill_gate, 8 + chunk_count + 1: fill_up, 8 + chunk_count + 2: fill_last}
    first_parts = [rows_of(attn_part, k) for k in range(chunk_count)]
    if spread:
        fills.update({0: fill_near, 1: fill_far, 2: fill_weights})
    run_ticks(
        first_parts, [feed_forward, feed_back, attn_back], head_index, head_count, fills
    )
    grad_attn_low, hidden_out = late["dattn"], late["hidden"]
    down_grad, gate_grad, up_grad = late["down_sum"], late["gate_sum"], late["up_sum"]

    grad_self_tok, grad_self_t, grad_cross_tok, grad_cross_t, self_delta, cross_delta, gate_rows = unmix(
        gate_local, grad_attn_low, out_t, self_t, cross_t
    )
    cross_gate_part = jnp.sum(gate_rows, axis=1) * (1.0 - gate_local * gate_local)

    def back(group, parts, before=None):
        return attend_back(
            self_info(group), query_t, grad_self_t, queries, grad_self_tok, self_lse, self_delta,
            [pieces[g] for g in group], heads, clips, bf16, parts, before,
        )

    def cross_back(before):
        return attend_back(
            text_info, query_t, grad_cross_t, queries, grad_cross_tok, cross_lse, cross_delta,
            text_pieces, heads, clips, f32, 1, before,
        )

    if spread:
        dq, _, kv_mine, kv_theirs = back((3, 2, 7, 6), 2)
        kv_got = core(kv_theirs)
        kv_mine, low = hold((kv_mine, grad_attn_low))
        out_part = matmul(low, mixed, COLS).astype(bf16)
        total = add_low(kv_mine, kv_got)
        total, dq, out_part = hold((total, dq, out_part))
        first = swap(total[:local_rows], "seq", 8, other_way)
        dq, text_dot, cross_kv = cross_back(dq)
        dq, cross_kv, down_grad, total = hold((dq, cross_kv, down_grad, total))
        own_first = swap(total[local_rows:], "seq", 8, other_way)
        dq, _, kv_mine, kv_theirs = back((1, 5), 2, dq)
        first, kv_mine, kv_theirs = hold((first, kv_mine, kv_theirs))
        total = kv_mine.astype(f32) + core(kv_theirs).astype(f32) + first.astype(f32)
        total = total.astype(bf16)
        second = swap(total, "seq", 8, first_way)
        dq, _, kv_mine, kv_theirs = back((0, 4), 2, dq)
        second, kv_mine, kv_theirs, gate_grad, own_first = hold((second, kv_mine, kv_theirs, gate_grad, own_first))
        kv_parts, kv_starts = [kv_mine, core(kv_theirs), own_first, second], (0, 0, 0, 0)
    else:
        dq, _, kv_all = back(tuple(range(seq_count)), 1)
        dq, text_dot, cross_kv = cross_back(dq)
        out_part = weight_grad(grad_attn_low, 0, model_width, mixed, 0, wide)
        kv_parts, kv_starts = [finish_sum(kv_all)], (0,)
    qkv_low, grad_query_gain, grad_key_gain, sum_a, *act_low = project_back(
        pre, query_gain, key_gain, cos, sin, dq, hidden_in, x_scale, w_qkv, kv_parts, kv_starts
    )
    act_low, qkv_low, cross_kv, gate_grad, out_part = hold((act_low, qkv_low, cross_kv, gate_grad, out_part))
    fold = lambda v: v[0, :HD] + v[0, HD:]
    pair_gains = jnp.concatenate([fold(grad_query_gain), fold(grad_key_gain + text_dot / key_gain)])
    tail = jnp.stack([sum_a[0], jnp.pad(pair_gains, (0, model_width - 2 * HD))])
    tail = jnp.pad(tail, ((0, 14), (0, 0))).astype(bf16)
    small = [total_of("sums", 1), total_of("sums", 0), total_of("uf", 0)]
    cross_row = jnp.pad(cross_gate_part, (2 * HD, model_width - 2 * HD - heads))

    def collect(k, end, total, got, before):
        if k == 1:
            late["tail"] = jnp.where(end[0] == 1, got, total)[chunk:].astype(f32)
        arrays = rows_of(hidden_in, k), rows, kept[k]["dmid"]
        mark = jnp.zeros((8, 128), f32) if before is None else before
        late["input"], mark = finish(k, end, total, got, *arrays, mark, local_rows, late.get("input"))
        return mark


    def fill0(carry):
        text_low = text_back(text_pre, key_gain, cross_kv)
        out = scatter_start(out_part, wheres[0]) if spread else out_part
        return [text_low, weight_grad(act_a, 0, model_width, qkv_low, 0, 3 * wide), out]

    def fill1(carry):
        late["qkv"] = finish_sum(carry[1])
        late["out"] = scatter_first(carry[2], wheres[1]) if spread else carry[2]
        gate, down, text = hold((gate_grad, down_grad, carry[0]))
        late["gate"], late["down"] = widen([gate]), widen([down]).T
        if not spread:
            return [lax.psum(text, "seq"), late["gate"], late["down"]]
        return [scatter_first(scatter_start(text, wheres[0]), wheres[1]), late["gate"], late["down"]]

    def fill2(carry):
        text, late["gate"], late["down"] = carry
        up, text = hold((up_grad, text))
        late["up"] = widen([up])
        if not spread:
            return [text, late["up"]]
        own = add_low(*scatter_second(text, wheres[2]))
        return [[own, swap(own, "seq", 8, first_way), swap(own, "seq", 8, other_way)], late["up"]]

    def fill3(carry):
        text, late["up"] = carry
        if not spread:
            return [text]
        text = text + [swap(text[1], "seq", 8, other_way)]
        out, text = hold((late["out"], text))
        late["out"] = scatter_second(out, wheres[2])
        return [text + [core(v) for v in text[:3]]]

    def fill4(carry):
        (text,) = carry
        tail_rows = [late["tail"][0]] + small + [jnp.pad(late["tail"][1, : 2 * HD], (0, model_width - 2 * HD)) + cross_row]
        values = jnp.pad(jnp.stack(tail_rows), ((0, 3), (0, 0)))
        out, text = hold((late["out"], text))
        late["out"] = widen(list(out)).T if spread else finish_sum(out).astype(f32).T
        if not spread:
            return [lax.psum(values, "seq"), text, late["out"]]
        return [hop(values, seq_hops[:2]), text + [core(text[3])], late["out"]]

    def fill5(carry):
        values, text, late["out"] = carry
        values = hop(values, seq_hops[2:]) if spread else values
        gain_grad, mod_grad = gains_back(values[:4], modulation, norm_gains)
        own_mod = lax.dynamic_slice_in_dim(
            mod_grad.reshape(-1), (seq_index * head_count + head_index) * piece_width, piece_width
        )
        text_grads = text_weight_grads(text if spread else [text], roles if spread else jnp.zeros((1,), jnp.int32), own_text)
        return [gain_grad, values[4], text_grads, cond_act.astype(f32)[:, None] * own_mod[None, :]]

    parts = list(act_low)
    parts[1] = jnp.concatenate([parts[1], tail])
    fills = dict(enumerate([fill0, fill1, fill2, fill3, fill4, fill5]))
    _, (norm_gains_grad, values, text_grad, ada_grad) = run_ticks(parts, [collect], head_index, head_count, fills)
    input_grad = late["input"]
    own_qkv = widen([late["qkv"]])

    qk_gains_grad = values[: 2 * HD].reshape(2, HD)
    cross_gate_grad = values[2 * HD : 2 * HD + heads]
    return (
        hidden_out,
        input_grad,
        ada_grad,
        norm_gains_grad,
        qk_gains_grad,
        cut(own_qkv[:, :wide]),
        cut(own_qkv[:, wide : 2 * wide]),
        cut(own_qkv[:, 2 * wide : 3 * wide]),
        late["out"][:cols],
        cross_gate_grad,
        cut(text_grad[0]),
        cut(text_grad[1]),
        late["gate"],
        late["up"],
        late["down"],
    )


def solution(mesh):
    in_specs = (
        P("seq", None),
        P(),
        P(),
        P(),
        P(None, ("seq", "head")),
        P(),
        P(),
        P("seq", "head"),
        P("seq", "head"),
        P("seq", "head"),
        P("head", "seq"),
        P("head"),
        P("seq", "head"),
        P("seq", "head"),
        P("seq", "head"),
        P("seq", "head"),
        P("head", "seq"),
        P("seq", None),
    )
    out_specs = (
        P("seq", None),
        P("seq", None),
        P(None, ("seq", "head")),
        P(),
        P(),
        P("seq", "head"),
        P("seq", "head"),
        P("seq", "head"),
        P("head", "seq"),
        P("head"),
        P("seq", "head"),
        P("seq", "head"),
        P("seq", "head"),
        P("seq", "head"),
        P("head", "seq"),
    )
    body = functools.partial(per_device, mesh.shape["seq"], mesh.shape["head"])
    return jax.shard_map(body, mesh=mesh, in_specs=in_specs, out_specs=out_specs, check_vma=False)
```

```python
import functools
import jax
import jax.numpy as jnp
from jax import lax
from jax.experimental import pallas as pl
from jax.experimental.pallas import tpu as pltpu
from jax.sharding import PartitionSpec as P

HD = 64
MASK = 8192.0
CHEAP = pl.CostEstimate(flops=1, bytes_accessed=1, transcendentals=0)
ATTEND_MIB = 60
BACK_MIB = 60
SMALL_MIB = 16


def dot(a, b):
    return lax.dot_general(a, b, (((1,), (0,)), ((), ())), preferred_element_type=jnp.float32)


def split3(v):
    hi = v.astype(jnp.bfloat16).astype(jnp.float32)
    mid = (v - hi).astype(jnp.bfloat16).astype(jnp.float32)
    return hi, mid, v - hi - mid


def bounds(info, base, clips, ids):
    start = jnp.full(ids.shape, 1 << 30, jnp.int32)
    end = jnp.zeros(ids.shape, jnp.int32)
    for c in range(clips):
        start = jnp.where(ids == c, info[base + c], start)
        end = jnp.where(ids == c, info[base + clips + c], end)
    return start, end


def query_ext(info, clips, width, scale):
    ids = lax.broadcasted_iota(jnp.int32, (16, width), 0)
    place = info[0] + lax.broadcasted_iota(jnp.int32, (16, width), 1)
    start, end = bounds(info, 1, clips, ids)
    return jnp.where((place >= start) & (place < end), scale, 0.0)


def key_ext(info, clips, row, rows, piece):
    ids = lax.broadcasted_iota(jnp.int32, (rows, 128), 1)
    step = min(rows, piece)
    parts = []
    for k in range(rows // step):
        at = row + k * step
        first = info[1 + 4 * clips + at // piece] + lax.rem(at, piece)
        parts.append(first + lax.broadcasted_iota(jnp.int32, (step, 128), 0))
    place = parts[0] if len(parts) == 1 else jnp.concatenate(parts, axis=0)
    start, end = bounds(info, 1 + 2 * clips, clips, ids)
    inside = (place >= start) & (place < end)
    value = jnp.where(ids < clips, jnp.where(inside, 0.0, -1.0), jnp.where(ids < clips + 3, 1.0, 0.0))
    return value.astype(jnp.bfloat16)


def fill_ext(dst, h, src, tail):
    width = src.shape[1]
    half = h % 2
    zero = jnp.zeros((HD, width), jnp.bfloat16)
    dst[h, half * HD : half * HD + HD, :] = src[h * HD : h * HD + HD, :]
    dst[h, (1 - half) * HD : (1 - half) * HD + HD, :] = zero
    dst[h, 128:144, :] = tail.astype(jnp.bfloat16)
    dst[h, 144:256, :] = jnp.zeros((112, width), jnp.bfloat16)


def stack_rows(heads, rows, clips, width):
    ids = lax.broadcasted_iota(jnp.int32, (16, width), 0)
    total = jnp.zeros((16, width), jnp.float32)
    for k, row in enumerate(rows):
        total = jnp.where(ids == clips + k, jnp.broadcast_to(row, (16, width)), total)
    return total


def load_pieces(pieces, kv, sem):
    rows = pieces[0].shape[0]
    return [
        pltpu.make_async_copy(piece, kv.at[pl.ds(k * rows, rows), :], sem.at[k])
        for k, piece in enumerate(pieces)
    ]


def fwd_kernel(heads, clips, count, tile, again, info, qt, *rest):
    before, pieces, (out, qx, kv, sem) = rest[:again], rest[again : again + count], rest[again + count :]
    copies = load_pieces(pieces, kv, sem)
    for c in copies:
        c.start()
    width = qt.shape[1]
    wide = qt.shape[0]
    ext = query_ext(info, clips, width, MASK)
    for h in range(heads):
        fill_ext(qx, h, qt, ext)
        out[h] = before[0][h] if again else jnp.zeros((80, width), jnp.float32)
    for c in copies:
        c.wait()
    steps = count * pieces[0].shape[0] // tile
    ones = jnp.ones((16, tile), jnp.bfloat16)

    def step(t, carry):
        rows = pl.ds(pl.multiple_of(t * tile, tile), tile)
        extra = key_ext(info, clips, t * tile, tile, pieces[0].shape[0])
        for p in range((heads + 1) // 2):
            kx = jnp.concatenate([kv[rows, p * 128 : p * 128 + 128], extra], axis=1)
            vt = kv[rows, wide + p * 128 : wide + p * 128 + 128].T
            for h in range(2 * p, min(2 * p + 2, heads)):
                half = h % 2
                probs = jnp.exp(dot(kx, qx[h])).astype(jnp.bfloat16)
                vx = jnp.concatenate([vt[half * HD : half * HD + HD, :], ones], axis=0)
                out[h] += dot(vx, probs)
        return carry

    lax.fori_loop(0, steps, step, 0)


def attend(info, qt, pieces, heads, clips, before=None, tile=1024):
    count = len(pieces)
    before = [] if before is None else [before]
    wide, width = qt.shape
    rows = pieces[0].shape[0]
    tile = min(tile, rows * count)
    return pl.pallas_call(
        functools.partial(fwd_kernel, heads, clips, count, tile, len(before)),
        out_shape=jax.ShapeDtypeStruct((heads, 80, width), jnp.float32),
        in_specs=[pl.BlockSpec(memory_space=pltpu.SMEM)]
        + [pl.BlockSpec()] * (1 + len(before))
        + [pl.BlockSpec(memory_space=pltpu.HBM)] * count,
        out_specs=pl.BlockSpec(),
        scratch_shapes=[
            pltpu.VMEM((heads, 256, width), jnp.bfloat16),
            pltpu.VMEM((count * rows, 2 * wide), jnp.bfloat16),
            pltpu.SemaphoreType.DMA((count,)),
        ],
        compiler_params=pltpu.CompilerParams(vmem_limit_bytes=ATTEND_MIB << 20),
        cost_estimate=CHEAP,
        name="attend",
    )(info, qt, *before, *pieces)


def bwd_kernel(heads, clips, count, tile, again, info, qt, dot_t, q_tok, do_tok, lse, delta, *rest):
    before, pieces, rest = rest[:again], rest[again : again + count], rest[again + count :]
    dqt, kdot, grads, (qx, dox, qpad, dopad, kv, sem) = rest[0], rest[1], rest[2:-6], rest[-6:]
    copies = load_pieces(pieces, kv, sem)
    for c in copies:
        c.start()
    wide, width = qt.shape
    ext = query_ext(info, clips, width, MASK)
    for h in range(heads):
        p, half = h // 2, h % 2
        fill_ext(qx, h, qt, ext - stack_rows(heads, split3(lse[h : h + 1, :]), clips, width))
        fill_ext(dox, h, dot_t, -stack_rows(heads, split3(delta[h : h + 1, :]), clips, width))
        lane = lax.broadcasted_iota(jnp.int32, (width, 128), 1) // HD
        zero = jnp.zeros((width, 128), jnp.bfloat16)
        qpad[h] = jnp.where(lane == half, q_tok[:, p * 128 : p * 128 + 128], zero)
        dopad[h] = jnp.where(lane == half, do_tok[:, p * 128 : p * 128 + 128], zero)
    kdot[...] = jnp.zeros((1, 128), jnp.float32)
    dqt[...] = before[0][...] if again else jnp.zeros((wide, width), jnp.float32)
    for c in copies:
        c.wait()
    steps = count * pieces[0].shape[0] // tile

    def step(t, carry):
        rows = pl.ds(pl.multiple_of(t * tile, tile), tile)
        extra = key_ext(info, clips, t * tile, tile, pieces[0].shape[0])
        for p in range((heads + 1) // 2):
            cols = slice(p * 128, p * 128 + 128)
            vcols = slice(wide + p * 128, wide + p * 128 + 128)
            k_tile = kv[rows, cols]
            kx = jnp.concatenate([k_tile, extra], axis=1)
            vx = jnp.concatenate([kv[rows, vcols], extra], axis=1)
            kt = k_tile.T
            dk = jnp.zeros((tile, 128), jnp.float32)
            dv = jnp.zeros((tile, 128), jnp.float32)
            for h in range(2 * p, min(2 * p + 2, heads)):
                half = h % 2
                probs = jnp.exp(dot(kx, qx[h]))
                ds = (probs * dot(vx, dox[h])).astype(jnp.bfloat16)
                dqt[h * HD : h * HD + HD, :] += dot(kt[half * HD : half * HD + HD, :], ds)
                dk = dk + dot(ds, qpad[h])
                dv = dv + dot(probs.astype(jnp.bfloat16), dopad[h])
            kdot[...] += jnp.sum(dk * k_tile.astype(jnp.float32), axis=0, keepdims=True)
            part = grads[0].shape[0]
            if tile > part:
                for g, grad in enumerate(grads):
                    grad[:, cols] = dk[g * part : g * part + part, :].astype(grad.dtype)
                    grad[:, vcols] = dv[g * part : g * part + part, :].astype(grad.dtype)
                continue
            for g, grad in enumerate(grads):

                @pl.when(t // (steps // len(grads)) == g)
                def store(g=g, grad=grad, dk=dk, dv=dv, cols=cols, vcols=vcols):
                    start = (t - g * (steps // len(grads))) * tile
                    here = pl.ds(pl.multiple_of(start, tile), tile)
                    grad[here, cols] = dk.astype(grad.dtype)
                    grad[here, vcols] = dv.astype(grad.dtype)

        return carry

    lax.fori_loop(0, steps, step, 0)


def attend_back(info, qt, dot_t, q_tok, do_tok, lse, delta, pieces, heads, clips, kind, parts=1, before=None, tile=2048):
    count = len(pieces)
    before = [] if before is None else [before]
    wide, width = qt.shape
    rows = pieces[0].shape[0]
    tile = rows * count if rows * count <= tile else min(tile, rows * count // parts)
    return pl.pallas_call(
        functools.partial(bwd_kernel, heads, clips, count, tile, len(before)),
        out_shape=(
            jax.ShapeDtypeStruct((wide, width), jnp.float32),
            jax.ShapeDtypeStruct((1, 128), jnp.float32),
        )
        + (jax.ShapeDtypeStruct((count * rows // parts, 2 * wide), kind),) * parts,
        in_specs=[pl.BlockSpec(memory_space=pltpu.SMEM)]
        + [pl.BlockSpec()] * (6 + len(before))
        + [pl.BlockSpec(memory_space=pltpu.HBM)] * count,
        out_specs=(pl.BlockSpec(),) * (2 + parts),
        scratch_shapes=[
            pltpu.VMEM((heads, 256, width), jnp.bfloat16),
            pltpu.VMEM((heads, 256, width), jnp.bfloat16),
            pltpu.VMEM((heads, width, 128), jnp.bfloat16),
            pltpu.VMEM((heads, width, 128), jnp.bfloat16),
            pltpu.VMEM((count * rows, 2 * wide), jnp.bfloat16),
            pltpu.SemaphoreType.DMA((count,)),
        ],
        compiler_params=pltpu.CompilerParams(vmem_limit_bytes=BACK_MIB << 20),
        cost_estimate=CHEAP,
        name="attend_back",
    )(info, qt, dot_t, q_tok, do_tok, lse, delta, *before, *pieces)


ROWS = (((1,), (1,)), ((), ()))
COLS = (((0,), (0,)), ((), ()))
f32 = jnp.float32
bf16 = jnp.bfloat16


def matmul(left, right, dims=None):
    if dims is None:
        return jnp.dot(left, right, preferred_element_type=f32)
    return lax.dot_general(left, right, dims, preferred_element_type=f32)


def first_way(i):
    return i ^ 2 if i % 2 == 0 else i ^ 4


def other_way(i):
    return i ^ 4 if i % 2 == 0 else i ^ 2


def swap(value, axis, count, to):
    return lax.ppermute(value, axis, [(i, to(i)) for i in range(count)])


def seq_roles(seq_index, seq_count):
    if seq_count != 8:
        return jnp.arange(seq_count, dtype=jnp.int32)
    peer = seq_index ^ 1

    def roles(i):
        even = i % 2 == 0
        return [i, jnp.where(even, i ^ 2, i ^ 4), jnp.where(even, i ^ 4, i ^ 2), i ^ 6]

    return jnp.stack(roles(seq_index) + roles(peer)).astype(jnp.int32)


def gather_pieces(block, seq_count):
    if seq_count != 8:
        whole = lax.all_gather(block, "seq", axis=0, tiled=False)
        return [whole[i] for i in range(seq_count)]
    near = swap(block, "seq", 8, first_way)
    next_ = swap(block, "seq", 8, other_way)
    far = swap(near, "seq", 8, other_way)
    mine = [block, near, next_, far]
    return mine + [swap(v, "seq", 8, lambda i: i ^ 1) for v in mine]


def place_kernel(count, rows, widths, roles, *rest):
    pieces, outs, sem = rest[:count], rest[count:-1], rest[-1]
    copies = []
    for k in range(count):
        to = pl.ds(pl.multiple_of(roles[k] * rows, rows), rows)
        first = 0
        for n, width in enumerate(widths):
            piece = pieces[k].at[:, first : first + width]
            copies.append(pltpu.make_async_copy(piece, outs[n].at[to, :], sem.at[k, n]))
            first += width
    for c in copies:
        c.start()
    for c in copies:
        c.wait()


def place(pieces, roles, widths=None, limit=SMALL_MIB):
    count = len(pieces)
    rows, width = pieces[0].shape
    outs = widths or (width,)
    placed = pl.pallas_call(
        functools.partial(place_kernel, count, rows, outs),
        out_shape=[jax.ShapeDtypeStruct((count * rows, w), pieces[0].dtype) for w in outs],
        in_specs=[pl.BlockSpec(memory_space=pltpu.SMEM)]
        + [pl.BlockSpec(memory_space=pltpu.HBM)] * count,
        out_specs=[pl.BlockSpec(memory_space=pltpu.VMEM)] * len(outs),
        scratch_shapes=[pltpu.SemaphoreType.DMA((count, len(outs)))],
        compiler_params=pltpu.CompilerParams(vmem_limit_bytes=limit << 20),
        cost_estimate=CHEAP,
        name="place",
    )(roles, *pieces)
    return placed if widths else placed[0]


def take_kernel(rows, core, part, out, sem):
    copies = []
    for chip in range(4):
        start = pl.multiple_of((2 * chip + core[0]) * rows, rows)
        to = out.at[pl.ds(chip * rows, rows), :]
        copies.append(pltpu.make_async_copy(part.at[pl.ds(start, rows), :], to, sem.at[chip]))
    for c in copies:
        c.start()
    for c in copies:
        c.wait()


def first_kernel(rows, where, part, got, mine, send, held, sem):
    copies = []
    for chip in range(4):
        start = pl.multiple_of((2 * chip + where[0]) * rows, rows)
        to = held.at[pl.ds(chip * rows, rows), :]
        copies.append(pltpu.make_async_copy(part.at[pl.ds(start, rows), :], to, sem.at[chip]))
    for c in copies:
        c.start()
    for c in copies:
        c.wait()
    mine[...] = (held[...].astype(f32) + got[...].astype(f32)).astype(bf16)
    for n in range(2):
        send[n * rows : n * rows + rows, :] = mine[pl.ds(pl.multiple_of(where[1 + n] * rows, rows), rows), :]


def second_kernel(rows, where, mine, got, own, send):
    block = lambda n: mine[pl.ds(pl.multiple_of(where[n] * rows, rows), rows), :].astype(f32)
    own[...] = (block(0) + got[rows:, :].astype(f32)).astype(bf16)
    send[...] = (block(1) + got[:rows, :].astype(f32)).astype(bf16)


def scatter_call(kernel, rows, where, arrays, outs, scratch, name, first=pltpu.VMEM):
    width = arrays[0].shape[1]
    vmem = pl.BlockSpec(memory_space=pltpu.VMEM)
    return pl.pallas_call(
        functools.partial(kernel, rows),
        out_shape=[jax.ShapeDtypeStruct((n * rows, width), bf16) for n in outs],
        in_specs=[pl.BlockSpec(memory_space=pltpu.SMEM), pl.BlockSpec(memory_space=first)]
        + [vmem] * (len(arrays) - 1),
        out_specs=[vmem] * len(outs),
        scratch_shapes=scratch,
        compiler_params=pltpu.CompilerParams(vmem_limit_bytes=SMALL_MIB << 20),
        cost_estimate=CHEAP,
        name=name,
    )(where, *arrays)


def scatter_start(part, where):
    rows = part.shape[0] // 8
    sems = [pltpu.SemaphoreType.DMA((4,))]
    theirs = scatter_call(take_kernel, rows, where, [part], [4], sems, "scatter_take", pl.ANY)[0]
    return part, swap(theirs, "seq", 8, lambda i: i ^ 1)


def scatter_first(pair, where):
    part, got = pair
    rows = part.shape[0] // 8
    scratch = [pltpu.VMEM(got.shape, bf16), pltpu.SemaphoreType.DMA((4,))]
    mine, send = scatter_call(first_kernel, rows, where, [part, got], [4, 2], scratch, "scatter_first", pl.ANY)
    return mine, swap(send, "seq", 8, other_way)


def scatter_second(pair, where):
    mine, got = pair
    own, send = scatter_call(second_kernel, mine.shape[0] // 4, where, [mine, got], [1, 1], [], "scatter_second")
    return own, swap(send, "seq", 8, first_way)


def widen_kernel(count, turn, *refs):
    total = refs[0][...].astype(f32)
    for ref in refs[1:count]:
        total = total + ref[...].astype(f32)
    refs[count][...] = total.T if turn else total


def widen(parts, turn=False):
    rows, width = parts[0].shape
    return pl.pallas_call(
        functools.partial(widen_kernel, len(parts), turn),
        out_shape=jax.ShapeDtypeStruct((width, rows) if turn else (rows, width), f32),
        compiler_params=pltpu.CompilerParams(vmem_limit_bytes=SMALL_MIB << 20),
        cost_estimate=CHEAP,
        name="widen",
    )(*parts)


def hops(axis, count):
    return [(axis, 1 << k) for k in range(count.bit_length() - 1)]


def sum_all(value, axes, order, beside=()):
    if any(count & (count - 1) for _, count in axes):
        return lax.psum(value, [axis for axis, _ in axes]), list(beside)
    counts, beside = dict(axes), list(beside)
    for k, (axis, bit) in enumerate(order):
        got = swap(value, axis, counts[axis], lambda i: i ^ bit)
        if k < len(beside):
            got, beside[k] = lax.optimization_barrier((got, beside[k]))
        value = value + got
    return value, beside


def add_low(a, b):
    return (a.astype(f32) + b.astype(f32)).astype(bf16)


def relay_kernel(names, end, *refs):
    ins = dict(zip(names, refs))
    outs = list(refs[len(names) :])
    add = lambda a, b: (ins[a][...].astype(f32) + ins[b][...].astype(f32)).astype(bf16)
    if "part" in ins:
        outs.pop(0)[...] = add("part", "part_got")
    if "total" in ins:
        total = add("total", "total_got")
        outs.pop(0)[...] = total
        if "own" in ins:
            send = outs.pop(0)
            rows, own_rows = total.shape[0], ins["own"].shape[0]
            both = min(rows, own_rows)
            send[:both, :] = jnp.where(end[0] == 1, ins["own"][:both, :], total[:both, :])
            if own_rows > both:
                send[both:, :] = ins["own"][both:, :]
            if rows > both:
                send[both:, :] = total[both:, :]


def relay(end, part, total, own):
    ins = {}
    shapes = []
    if part is not None:
        ins.update(part=part[0], part_got=part[1])
        shapes.append(part[0].shape)
    if total is not None:
        ins.update(total=total[0], total_got=total[1])
        shapes.append(total[0].shape)
        if own is not None:
            ins["own"] = own
            shapes.append((max(own.shape[0], total[0].shape[0]), own.shape[1]))
    if not shapes:
        return None, None, own
    outs = pl.pallas_call(
        functools.partial(relay_kernel, tuple(ins)),
        out_shape=[jax.ShapeDtypeStruct(shape, bf16) for shape in shapes],
        in_specs=[pl.BlockSpec(memory_space=pltpu.SMEM)] + [pl.BlockSpec(memory_space=pltpu.VMEM)] * len(ins),
        out_specs=[pl.BlockSpec(memory_space=pltpu.VMEM)] * len(shapes),
        compiler_params=pltpu.CompilerParams(vmem_limit_bytes=SMALL_MIB << 20),
        cost_estimate=CHEAP,
        name="relay",
    )(end, *ins.values())
    outs = list(outs)
    part = outs.pop(0) if part is not None else None
    total = outs.pop(0) if total is not None else None
    return part, total, outs.pop(0) if outs else own


def staged(kernel, k, outs, wholes, scalars, arrays, before, name, limit=SMALL_MIB):
    before = before or []
    vmem = pl.BlockSpec() if limit == 60 else pl.BlockSpec(memory_space=pltpu.VMEM)
    anywhere = pl.BlockSpec(memory_space=pl.ANY)
    given = len(scalars) + len(arrays)
    return pl.pallas_call(
        functools.partial(kernel, k, len(before)),
        out_shape=[jax.ShapeDtypeStruct(shape, kind) for shape, kind in outs]
        + [jax.ShapeDtypeStruct((tokens, width), kind) for tokens, rows, width, kind in wholes],
        in_specs=[pl.BlockSpec(memory_space=pltpu.SMEM)] * len(scalars)
        + [vmem] * len(arrays)
        + [anywhere] * len(before),
        out_specs=[vmem] * len(outs) + [anywhere] * len(wholes),
        scratch_shapes=[pltpu.VMEM((rows, width), kind) for tokens, rows, width, kind in wholes]
        + [pltpu.SemaphoreType.DMA(())] * len(wholes),
        input_output_aliases={given + n: len(outs) + n for n in range(len(before))},
        compiler_params=pltpu.CompilerParams(vmem_limit_bytes=limit << 20),
        cost_estimate=CHEAP,
        name=name,
    )(*scalars, *arrays, *before)


def put_rows(k, value, whole, sem):
    rows = value.shape[0]
    copy = pltpu.make_async_copy(value, whole.at[pl.ds(k * rows, rows), :], sem)
    copy.start()
    return copy


def rms(value):
    return lax.rsqrt(jnp.mean(value * value, axis=-1, keepdims=True) + 1e-06)


def rms_back(grad, normed, scale):
    return scale * (grad - normed * jnp.mean(grad * normed, axis=-1, keepdims=True))


def dot_rows(a, b):
    return lax.dot_general(a, b, ROWS, preferred_element_type=f32)


def picked(end, total, got):
    return jnp.where(end[0] == 1, got[...], total[...]).astype(f32)


def forward_kernel(k, again, end, total, got, x, gains, gate_w, up_w, down_t, *rest):
    norms, stats, pre, part, low, pack, sem = rest[again:]
    width, units = x.shape[1], gate_w.shape[1]
    attn = picked(end, total, got)
    scale = rms(attn)
    normed = attn * scale
    norms[:, :width] = normed
    middle = x[...].astype(f32) + normed * gains[1:2, :]
    norms[:, width:] = middle
    middle_scale = rms(middle)
    lane = lax.broadcasted_iota(jnp.int32, stats.shape, 1)
    stats[...] = jnp.where(lane == 0, scale, middle_scale)
    act = (middle * middle_scale * gains[2:3, :]).astype(bf16)
    pack[:, units:] = act
    gated = dot(act, gate_w[...])
    upper = dot(act, up_w[...])
    pre[:, :units] = gated
    pre[:, units:] = upper
    unit = (gated * jax.nn.sigmoid(gated) * upper).astype(bf16)
    pack[:, :units] = unit
    copy = put_rows(k, pack, low, sem)
    part[...] = dot_rows(unit, down_t[...]).astype(bf16)
    copy.wait()


def backward_kernel(k, again, end, total, got, norms, pre, cot, gains, gate_w, up_w, down_t, *rest):
    sums, part, low, out, pack, done, sem, out_sem = rest[again:]
    width, units = cot.shape[1], gate_w.shape[1]
    ffn = picked(end, total, got)
    scale = rms(ffn)
    normed = ffn * scale
    done[...] = (norms[:, width:] + normed * gains[3:4, :]).astype(bf16)
    out_copy = put_rows(k, done, out, out_sem)
    grad = cot[...].astype(f32)
    sums[...] = jnp.sum(grad * normed, axis=0, keepdims=True)
    grad_ffn = rms_back(grad * gains[3:4, :], normed, scale).astype(bf16)
    pack[:, 2 * units :] = grad_ffn
    grad_units = dot(grad_ffn, down_t[...])
    gated = pre[:, :units]
    sig = jax.nn.sigmoid(gated)
    low_gate = (grad_units * pre[:, units:] * sig * (1.0 + gated * (1.0 - sig))).astype(bf16)
    low_up = (grad_units * gated * sig).astype(bf16)
    pack[:, :units] = low_gate
    pack[:, units : 2 * units] = low_up
    copy = put_rows(k, pack, low, sem)
    part[...] = (dot_rows(low_gate, gate_w[...]) + dot_rows(low_up, up_w[...])).astype(bf16)
    copy.wait()
    out_copy.wait()


def attn_back_kernel(k, again, end, total, got, norms, stats, cot, gains, *rest):
    sums, dmid, dattn, pack, sem = rest[again:]
    width = cot.shape[1]
    grad = picked(end, total, got)
    scale, middle_scale = stats[:, 0:1], stats[:, 1:2]
    normed = norms[:, width:] * middle_scale
    sums[0:1, :] = jnp.sum(grad * normed, axis=0, keepdims=True)
    middle = cot[...].astype(f32) + rms_back(grad * gains[2:3, :], normed, middle_scale)
    dmid[...] = middle
    normed = norms[:, :width]
    sums[1:2, :] = jnp.sum(middle * normed, axis=0, keepdims=True)
    pack[...] = rms_back(middle * gains[1:2, :], normed, scale).astype(bf16)
    put_rows(k, pack, dattn, sem).wait()


def weight_grad_kernel(left, right, out):
    out[...] = lax.dot_general(left[...], right[...], COLS, preferred_element_type=f32).astype(bf16)


def weight_grad(left, first, width, right, place, right_width):
    tokens = left.shape[0]
    step = 512
    return pl.pallas_call(
        weight_grad_kernel,
        out_shape=jax.ShapeDtypeStruct((width, right_width), bf16),
        grid=(width // step,),
        in_specs=[
            pl.BlockSpec((tokens, step), lambda i: (0, first // step + i)),
            pl.BlockSpec((tokens, right_width), lambda i: (0, place)),
        ],
        out_specs=pl.BlockSpec((step, right_width), lambda i: (i, 0)),
        compiler_params=pltpu.CompilerParams(vmem_limit_bytes=60 << 20),
        cost_estimate=CHEAP,
        name="weight_grad",
    )(left, right)


def run_ticks(parts, computes, head_index, head_count, fill):
    carry = []
    stages = 4 * len(computes)
    ticks = stages + len(parts) - 1
    if head_count != 4:
        for n, compute in enumerate(computes):
            sums = [lax.psum(part, "head") for part in parts]
            parts = []
            for k, part in enumerate(sums):
                before = parts[k - 1] if k else None
                parts.append(compute(k, jnp.zeros((1,), jnp.int32), part, part, before))
        for t in range(ticks):
            carry = fill[t](carry) if t in fill else carry
        return parts, carry
    end = jnp.where((head_index == 0) | (head_index == 3), 1, 0).astype(jnp.int32).reshape(1)
    states = [(part,) for part in parts]
    for t in range(ticks):
        at = {(t - k) % 4: k for k in range(len(parts)) if 0 <= t - k < stages}
        live = [k for k in range(len(parts)) if t - k < stages + 1]
        own = states[at[0]][0] if 0 in at else None
        part, total, send = relay(
            end, states[at[1]] if 1 in at else None, states[at[2]] if 2 in at else None, own
        )
        late = states[at[3]] if 3 in at else ()
        if part is not None or total is not None:
            part, total, send, late, carry = lax.optimization_barrier((part, total, send, late, carry))
        if 3 in at:
            states[at[3]] = late
        if 1 in at:
            states[at[1]] = (part, lax.ppermute(part, "head", [(1, 2), (2, 1)]))
        if 0 in at and 2 in at:
            got = lax.ppermute(send, "head", [(0, 1), (3, 2), (1, 0), (2, 3)])
            states[at[0]] = (own, got[: own.shape[0]])
            states[at[2]] = (total, got[: total.shape[0]])
        elif 0 in at:
            states[at[0]] = (own, lax.ppermute(own, "head", [(0, 1), (3, 2)]))
        elif 2 in at:
            states[at[2]] = (total, lax.ppermute(total, "head", [(1, 0), (2, 3)]))
        if 3 in at:
            k = at[3]
            before = states[k - 1][0] if k else None
            states[k] = (computes[(t - k) // 4](k, end, *states[k], before),)
        if t in fill:
            carry = fill[t](carry)
        held, carry = lax.optimization_barrier(([states[k] for k in live], carry))
        for k, state in zip(live, held):
            states[k] = state
    return [state[0] for state in states], carry


def head_mean(value):
    row = lax.broadcasted_iota(jnp.int32, (128, 128), 0) // HD
    col = lax.broadcasted_iota(jnp.int32, (128, 128), 1) // HD
    ones = jnp.where(row == col, 1.0 / HD, 0.0).astype(bf16)
    hi, mid, lo = split3(value)
    return dot(hi.astype(bf16), ones) + dot(mid.astype(bf16), ones) + dot(lo.astype(bf16), ones)


def partner(value):
    lane = lax.broadcasted_iota(jnp.int32, value.shape, 1) % HD
    return jnp.where(lane < HD // 2, pltpu.roll(value, 128 - HD // 2, 1), pltpu.roll(value, HD // 2, 1))


def text_norm_kernel(pre, gain, out):
    wide = pre.shape[1] // 2
    for p in range(wide // 128):
        cols = slice(p * 128, p * 128 + 128)
        value = pre[:, cols].astype(f32)
        out[:, cols] = (value * lax.rsqrt(head_mean(value * value) + 1e-6) * gain[...]).astype(bf16)
    out[:, wide:] = pre[:, wide:]


def text_norm(pre, gain):
    return pl.pallas_call(
        text_norm_kernel, out_shape=jax.ShapeDtypeStruct(pre.shape, bf16), name="text_norm", cost_estimate=CHEAP
    )(pre, gain)


def qkv_kernel(count, rows, wide, roles, x, gain, qgain, kgain, cos, sin, *rest):
    pieces, (act, scale, pre, kv, query, query_t, weight, sem) = rest[:count], rest[count:]
    copies = []
    for k in range(count):
        start = pl.multiple_of(roles[k] * rows, rows)
        copies.append(pltpu.make_async_copy(pieces[k], weight.at[pl.ds(start, rows), :], sem.at[k]))
    for c in copies:
        c.start()
    value = x[...].astype(f32)
    inverse = lax.rsqrt(jnp.mean(value * value, axis=-1, keepdims=True) + 1e-6)
    scale[...] = inverse
    act[...] = (value * inverse * gain[0:1, :]).astype(bf16)
    for c in copies:
        c.wait()
    pre[...] = dot(act[...], weight[:, : 2 * wide])
    kv[:, wide:] = dot(act[...], weight[:, 2 * wide :]).astype(bf16)
    for p in range(wide // 128):
        cols = slice(p * 128, p * 128 + 128)
        for which, out_gain in ((0, qgain), (1, kgain)):
            raw = pre[:, which * wide + p * 128 : which * wide + p * 128 + 128]
            raw = raw * lax.rsqrt(head_mean(raw * raw) + 1e-6) * out_gain[...]
            raw = raw * cos[...] + partner(raw) * sin[...]
            if which == 1:
                kv[:, cols] = raw.astype(bf16)
            else:
                raw = raw.astype(bf16).astype(f32) * HD**-0.5
                query[:, cols] = raw.astype(bf16)
                query_t[cols, :] = raw.T.astype(bf16)


def project(roles, x, gain, qgain, kgain, cos, sin, pieces, wide):
    count = len(pieces)
    rows = pieces[0].shape[0]
    tokens, width = x.shape
    shape = jax.ShapeDtypeStruct
    return pl.pallas_call(
        functools.partial(qkv_kernel, count, rows, wide),
        out_shape=(
            shape((tokens, width), bf16),
            shape((tokens, 1), f32),
            shape((tokens, 2 * wide), f32),
            shape((tokens, 2 * wide), bf16),
            shape((tokens, wide), bf16),
            shape((wide, tokens), bf16),
            shape((width, 3 * wide), bf16),
        ),
        in_specs=[pl.BlockSpec(memory_space=pltpu.SMEM)]
        + [pl.BlockSpec(memory_space=pltpu.VMEM)] * 6
        + [pl.BlockSpec(memory_space=pltpu.HBM)] * count,
        out_specs=(pl.BlockSpec(memory_space=pltpu.VMEM),) * 7,
        scratch_shapes=[pltpu.SemaphoreType.DMA((count,))],
        compiler_params=pltpu.CompilerParams(vmem_limit_bytes=60 << 20),
        cost_estimate=CHEAP,
        name="project",
    )(roles, x, gain, qgain, kgain, cos, sin, *pieces)


def mix_kernel(heads, gate, sums, cross, mixed, self_t, cross_t, lse, cross_lse):
    for p in range((heads + 1) // 2):
        both = []
        for h in range(2 * p, 2 * p + 2):
            if h >= heads:
                both.append(jnp.zeros_like(both[0]))
                continue
            rows = slice(h * HD, h * HD + HD)
            den, cross_den = sums[h, HD : HD + 1, :], cross[h, HD : HD + 1, :]
            lse[h : h + 1, :] = jnp.log(den)
            cross_lse[h : h + 1, :] = jnp.log(cross_den)
            own = sums[h, :HD, :] / den
            other = cross[h, :HD, :] / cross_den
            self_t[rows, :] = own
            cross_t[rows, :] = other
            both.append(own + gate[h] * other)
        mixed[:, p * 128 : p * 128 + 128] = jnp.concatenate(both, axis=0).T.astype(bf16)


def mix(gate, sums, cross, wide):
    heads, _, tokens = sums.shape
    shape = jax.ShapeDtypeStruct
    return pl.pallas_call(
        functools.partial(mix_kernel, heads),
        out_shape=(
            shape((tokens, wide), bf16),
            shape((heads * HD, tokens), f32),
            shape((heads * HD, tokens), f32),
            shape((heads, tokens), f32),
            shape((heads, tokens), f32),
        ),
        in_specs=[pl.BlockSpec(memory_space=pltpu.SMEM)] + [pl.BlockSpec(memory_space=pltpu.VMEM)] * 2,
        compiler_params=pltpu.CompilerParams(vmem_limit_bytes=SMALL_MIB << 20),
        name="mix",
        cost_estimate=CHEAP,
    )(gate, sums, cross)


def unmix_kernel(heads, gate, weight, self_t, cross_t, grad, tok, tok_t, ctok, ctok_t, delta, cdelta, cgate):
    width = tok.shape[0]
    for p in range((heads + 1) // 2):
        cols = slice(p * 128, p * 128 + 128)
        value = dot(grad[...], weight[:, cols])
        lane = lax.broadcasted_iota(jnp.int32, (width, 128), 1) // HD
        gates = jnp.where(lane == 0, gate[2 * p], gate[min(2 * p + 1, heads - 1)])
        tok[:, cols] = value.astype(bf16)
        ctok[:, cols] = (value * gates).astype(bf16)
        turned = value.T
        for h in range(2 * p, 2 * p + 2):
            rows = slice(h * HD, h * HD + HD)
            part = turned[(h % 2) * HD : (h % 2) * HD + HD, :]
            tok_t[rows, :] = part.astype(bf16)
            if h >= heads:
                ctok_t[rows, :] = part.astype(bf16)
                continue
            low = (part * gate[h]).astype(bf16)
            ctok_t[rows, :] = low
            delta[h : h + 1, :] = jnp.sum(part.astype(bf16).astype(f32) * self_t[rows, :], axis=0, keepdims=True)
            cdelta[h : h + 1, :] = jnp.sum(low.astype(f32) * cross_t[rows, :], axis=0, keepdims=True)
            cgate[h : h + 1, :] = jnp.sum(part * cross_t[rows, :], axis=0, keepdims=True)


def unmix(gate, grad, weight, self_t, cross_t):
    tokens = self_t.shape[1]
    wide = weight.shape[1]
    heads = self_t.shape[0] // HD
    shape = jax.ShapeDtypeStruct
    return pl.pallas_call(
        functools.partial(unmix_kernel, heads),
        out_shape=(shape((tokens, wide), bf16), shape((wide, tokens), bf16)) * 2 + (shape((heads, tokens), f32),) * 3,
        in_specs=[pl.BlockSpec(memory_space=pltpu.SMEM)]
        + [pl.BlockSpec()] * 4,
        compiler_params=pltpu.CompilerParams(vmem_limit_bytes=60 << 20),
        name="unmix",
        cost_estimate=CHEAP,
    )(gate, weight, self_t, cross_t, grad)


def norm_back(raw, gain, grad, cos=None, sin=None):
    scale = lax.rsqrt(head_mean(raw * raw) + 1e-6)
    normed = raw * scale
    if cos is not None:
        grad = grad * cos - partner(grad) * sin
    gain_grad = jnp.sum(grad * normed, axis=0, keepdims=True)
    grad = grad * gain
    return scale * (grad - normed * head_mean(grad * normed)), gain_grad


def text_back_kernel(pre, gain, grad, out):
    wide = pre.shape[1] // 2
    for p in range(wide // 128):
        cols = slice(p * 128, p * 128 + 128)
        out[:, cols] = norm_back(pre[:, cols].astype(f32), gain[...], grad[:, cols])[0].astype(bf16)
    out[:, wide:] = grad[:, wide:].astype(bf16)


def text_back(pre, gain, grad):
    return pl.pallas_call(
        text_back_kernel,
        out_shape=jax.ShapeDtypeStruct(grad.shape, bf16),
        name="text_back",
        cost_estimate=CHEAP,
    )(pre, gain, grad)


def project_back_kernel(wide, starts, pre, qgain, kgain, cos, sin, dqt, x, scale, weight, *rest):
    kvs, (out, qgrad, kgrad, sums, *acts) = rest[: len(starts)], rest[len(starts) :]
    tokens = pre.shape[0]
    total = [jnp.zeros((1, 128), f32), jnp.zeros((1, 128), f32)]
    summed = lambda cols: sum(kv[start : start + tokens, cols].astype(f32) for kv, start in zip(kvs, starts))
    for p in range(wide // 128):
        cols = slice(p * 128, p * 128 + 128)
        grads = (dqt[cols, :] * HD**-0.5).T, summed(cols)
        for which, gain in ((0, qgain), (1, kgain)):
            at = slice(which * wide + p * 128, which * wide + p * 128 + 128)
            value, extra = norm_back(pre[:, at], gain[...], grads[which], cos[...], sin[...])
            out[:, at] = value.astype(bf16)
            total[which] = total[which] + extra
    out[:, 2 * wide :] = summed(slice(wide, 2 * wide)).astype(bf16)
    qgrad[...] = total[0]
    kgrad[...] = total[1]
    value = dot_rows(out[...], weight[...])
    rows = acts[0].shape[0]
    for n, act in enumerate(acts):
        act[...] = value[n * rows : n * rows + rows, :].astype(bf16)
    sums[...] = jnp.sum(value * (x[...].astype(f32) * scale[...]), axis=0, keepdims=True)


def project_back(pre, qgain, kgain, cos, sin, dqt, x, scale, weight, kvs, starts):
    tokens, wide = pre.shape[0], pre.shape[1] // 2
    shape = jax.ShapeDtypeStruct
    return pl.pallas_call(
        functools.partial(project_back_kernel, wide, tuple(starts)),
        out_shape=(
            shape((tokens, 3 * wide), bf16),
            shape((1, 128), f32),
            shape((1, 128), f32),
            shape((1, x.shape[1]), f32),
        )
        + (shape((tokens // 4, x.shape[1]), bf16),) * 4,
        name="project_back",
        cost_estimate=CHEAP,
        compiler_params=pltpu.CompilerParams(vmem_limit_bytes=60 << 20),
    )(pre, qgain, kgain, cos, sin, dqt, x, scale, weight, *kvs)


def finish_kernel(k, end, total, got, x, gain, mid, mark, *rest):
    out, done, value, sem = rest[-4:]
    rows = mid.shape[0]
    value_x = x[...].astype(f32)
    inverse = rms(value_x)
    normed = value_x * inverse
    grad = picked(end, total, got)[:rows] * gain[0:1, :]
    mean = jnp.mean(grad * normed, axis=-1, keepdims=True)
    value[...] = mid[...] + inverse * (grad - normed * mean)
    copy = pltpu.make_async_copy(value, out.at[pl.ds(k * rows, rows), :], sem)
    copy.start()
    done[...] = mark[...]
    copy.wait()


def finish(k, end, total, got, x, gain, mid, mark, tokens, before):
    before = [] if before is None else [before]
    vmem = pl.BlockSpec(memory_space=pltpu.VMEM)
    return pl.pallas_call(
        functools.partial(finish_kernel, k),
        out_shape=[jax.ShapeDtypeStruct((tokens, mid.shape[1]), f32), jax.ShapeDtypeStruct(mark.shape, f32)],
        in_specs=[pl.BlockSpec(memory_space=pltpu.SMEM)] + [vmem] * 6 + [pl.BlockSpec(memory_space=pl.ANY)] * len(before),
        out_specs=[pl.BlockSpec(memory_space=pl.ANY), vmem],
        scratch_shapes=[pltpu.VMEM(mid.shape, f32), pltpu.SemaphoreType.DMA(())],
        input_output_aliases={7: 0} if before else {},
        name="finish",
        cost_estimate=CHEAP,
        compiler_params=pltpu.CompilerParams(vmem_limit_bytes=SMALL_MIB << 20),
    )(end, total, got, x, gain, mid, mark, *before)


def text_weights_kernel(count, rows, roles, *rest):
    pieces, (own, key_grad, value_grad, held, sem) = rest[:count], rest[count:]
    copies = []
    for k in range(count):
        to = pl.ds(pl.multiple_of(roles[k] * rows, rows), rows)
        copies.append(pltpu.make_async_copy(pieces[k], held.at[to, :], sem.at[k]))
    for c in copies:
        c.start()
    for c in copies:
        c.wait()
    wide = key_grad.shape[1]
    key_grad[...] = lax.dot_general(own[...], held[:, :wide], COLS, preferred_element_type=f32)
    value_grad[...] = lax.dot_general(own[...], held[:, wide:], COLS, preferred_element_type=f32)


def text_weight_grads(pieces, roles, own):
    count = len(pieces)
    rows, width = pieces[0].shape
    vmem = pl.BlockSpec(memory_space=pltpu.VMEM)
    return pl.pallas_call(
        functools.partial(text_weights_kernel, count, rows),
        out_shape=[jax.ShapeDtypeStruct((own.shape[1], width // 2), f32)] * 2,
        in_specs=[pl.BlockSpec(memory_space=pltpu.SMEM)] + [pl.BlockSpec(memory_space=pl.ANY)] * count + [vmem],
        out_specs=[vmem] * 2,
        scratch_shapes=[pltpu.VMEM((count * rows, width), bf16), pltpu.SemaphoreType.DMA((count,))],
        compiler_params=pltpu.CompilerParams(vmem_limit_bytes=60 << 20),
        cost_estimate=CHEAP,
        name="text_weight_grads",
    )(roles, *pieces, own)


def touch_kernel(*refs):
    refs[-1][...] = refs[0][...]


def touch(value, arrays):
    return pl.pallas_call(
        touch_kernel,
        out_shape=jax.ShapeDtypeStruct(value.shape, value.dtype),
        in_specs=[pl.BlockSpec(memory_space=pltpu.VMEM)] * (1 + len(arrays)),
        cost_estimate=CHEAP,
        compiler_params=pltpu.CompilerParams(vmem_limit_bytes=SMALL_MIB << 20),
        name="touch",
    )(value, *arrays)


def gains_back_kernel(sums, mods, gains, gain_grad, mod_grad):
    for n in range(4):
        row = slice(n, n + 1)
        if n % 2 == 0:
            gain_grad[row, :] = sums[row, :] * (1.0 + mods[row, :])
            mod_grad[row, :] = sums[row, :] * gains[row, :]
        else:
            gate = jnp.tanh(mods[row, :])
            gain_grad[row, :] = sums[row, :] * gate
            mod_grad[row, :] = sums[row, :] * gains[row, :] * (1.0 - gate * gate)


def gains_back(sums, mods, gains):
    return pl.pallas_call(
        gains_back_kernel,
        out_shape=[jax.ShapeDtypeStruct(gains.shape, f32)] * 2,
        cost_estimate=CHEAP,
        name="gains_back",
    )(sums, mods, gains)


def vectors_kernel(mods, gains, out):
    out[0:1, :] = gains[0:1, :] * (1.0 + mods[0:1, :])
    out[1:2, :] = jnp.tanh(mods[1:2, :]) * gains[1:2, :]
    out[2:3, :] = gains[2:3, :] * (1.0 + mods[2:3, :])
    out[3:4, :] = jnp.tanh(mods[3:4, :]) * gains[3:4, :]


def vectors(mods, gains):
    return pl.pallas_call(
        vectors_kernel,
        out_shape=jax.ShapeDtypeStruct(gains.shape, f32),
        cost_estimate=CHEAP,
        name="vectors",
    )(mods, gains)


def per_device(
    seq_count,
    head_count,
    hidden_in,
    cond,
    captions,
    clip_lengths,
    ada_weight,
    norm_gains,
    qk_gains,
    w_query,
    w_key,
    w_value,
    w_out,
    cross_gate,
    w_text_key,
    w_text_value,
    w_gate,
    w_up,
    w_down,
    out_cotangent,
):
    local_rows, model_width = hidden_in.shape
    seq_index = lax.axis_index("seq")
    head_index = lax.axis_index("head")
    clips = clip_lengths.shape[0]
    cols = w_query.shape[1]
    heads = cols // HD
    wide = (cols + 127) // 128 * 128
    units = w_gate.shape[1]
    roles = seq_roles(seq_index, seq_count)
    pad = lambda v: jnp.pad(v, ((0, 0), (0, wide - cols))) if wide > cols else v
    cut = lambda v: v[:, :cols]

    spread = seq_count == 8
    core = lambda v: swap(v, "seq", 8, lambda i: i ^ 1)
    hold = lax.optimization_barrier
    axes = (("seq", seq_count), ("head", head_count))
    seq_hops, head_hops = hops("seq", seq_count), hops("head", head_count)
    finish_sum = lambda v: lax.psum_scatter(v, "seq", scatter_dimension=0, tiled=True)

    def hop(value, steps):
        for axis, bit in steps:
            value = value + swap(value, axis, dict(axes)[axis], lambda i: i ^ bit)
        return value

    clip_ends = jnp.cumsum(clip_lengths, dtype=jnp.int32)
    starts = clip_ends - clip_lengths
    text_rows = captions.reshape(-1, captions.shape[2])
    text_block = text_rows.shape[0] // seq_count
    text_ids = jnp.arange(clips, dtype=jnp.int32) * captions.shape[1]
    first_row = seq_index * local_rows
    place_info = jnp.concatenate([first_row[None], starts, clip_ends]).astype(jnp.int32)
    text_info = jnp.concatenate(
        [place_info, text_ids, text_ids + captions.shape[1], jnp.zeros((1,), jnp.int32)]
    )

    infos = {}

    def self_info(which):
        which = tuple(which)
        if which not in infos:
            infos[which] = jnp.concatenate([place_info, starts, clip_ends, roles[jnp.array(which)] * local_rows])
        return infos[which]

    places = first_row + jnp.arange(local_rows, dtype=jnp.int32)
    inside = (places[:, None] >= starts[None, :]) & (places[:, None] < clip_ends[None, :])
    position = places - jnp.sum(jnp.where(inside, starts[None, :], 0), axis=1, dtype=jnp.int32)
    lane = jnp.arange(128)
    frequency = 10000.0 ** (-(lane % (HD // 2)).astype(f32) / (HD // 2))
    angles = position.astype(f32)[:, None] * frequency[None, :]
    cos = jnp.cos(angles)
    sin = jnp.where(lane % HD < HD // 2, -1.0, 1.0)[None, :] * jnp.sin(angles)
    query_gain = jnp.tile(qk_gains[0], 2)[None, :]
    key_gain = jnp.tile(qk_gains[1], 2)[None, :]

    cond_act = jax.nn.silu(cond).astype(bf16)
    piece_width = ada_weight.shape[1]
    mod_piece = matmul(cond_act[None, :], ada_weight)
    mine = lax.broadcasted_iota(jnp.int32, (seq_count * head_count, 1), 0) == seq_index * head_count + head_index
    modulation = jnp.where(mine, mod_piece, 0.0)
    modulation, w_query = hold((modulation, w_query))
    qkv_block = jnp.concatenate([pad(w_query), pad(w_key), pad(w_value)], axis=1)
    out_block = pad(w_out.T)
    slab_width = text_rows.shape[1] // seq_count
    if spread:
        modulation = hop(modulation, seq_hops[:1])
        modulation, text_rows = hold((modulation, text_rows))
    own_text = lax.dynamic_slice_in_dim(text_rows, seq_index * slab_width, slab_width, 1)
    text_part = matmul(own_text, jnp.concatenate([pad(w_text_key), pad(w_text_value)], axis=1)).astype(bf16)

    def queries_keys(pieces):
        return project(roles, hidden_in, rows, query_gain, key_gain, cos, sin, pieces, wide)

    def part_sums(group, blocks, before=None):
        return attend(self_info(group), query_t, blocks, heads, clips, before)

    if spread:
        near = swap(qkv_block, "seq", 8, first_way)
        next_ = swap(qkv_block, "seq", 8, other_way)
        modulation = hop(modulation, head_hops[:1])
        text_pre = lax.psum(text_part, "seq")
        gate_w = lax.all_gather(w_gate, "seq", axis=0, tiled=True)
        near, next_, modulation = hold((near, next_, modulation))
        far = swap(near, "seq", 8, other_way)
        modulation = hop(modulation, head_hops[1:])
        modulation = hop(modulation, seq_hops[1:])
        qkv_pieces = [qkv_block, near, next_, far]
        qkv_pieces = qkv_pieces + [core(v) for v in qkv_pieces]
        modulation, qkv_pieces, out_block = hold((modulation, qkv_pieces, out_block))
        modulation = modulation.reshape(4, model_width)
        rows = vectors(modulation, norm_gains)
        act_a, x_scale, pre, kv_own, queries, query_t, w_qkv = queries_keys(qkv_pieces)
        kv_own, modulation, out_block = hold((kv_own, modulation, out_block))
        near = swap(kv_own, "seq", 8, first_way)
        next_ = swap(kv_own, "seq", 8, other_way)
        kv_peer = core(kv_own)
        out_near = swap(out_block, "seq", 8, first_way)
        out_next = swap(out_block, "seq", 8, other_way)
        sums = part_sums((0, 4), [kv_own, kv_peer])
        for group in ((1, 2, 5, 6), (3, 7), (3, 2, 7, 6), (1, 5)):
            self_info(group)
        chip = seq_index // 2
        near_chip = jnp.where(seq_index % 2 == 0, chip ^ 1, chip ^ 2)
        next_chip = jnp.where(seq_index % 2 == 0, chip ^ 2, chip ^ 1)
        wheres = [[1 - seq_index % 2], [seq_index % 2, chip ^ 3, next_chip], [chip, near_chip]]
        wheres = [jnp.stack(where).astype(jnp.int32) for where in wheres]
        ready = (near, next_, sums, out_near, out_next, infos, text_info, wheres)
        near, next_, sums, out_near, out_next, infos_held, text_info, wheres = hold(ready)
        infos.update(infos_held)
        far = swap(near, "seq", 8, other_way)
        out_far = swap(out_near, "seq", 8, other_way)
        near_peer, next_peer = core(near), core(next_)
        out_peers = [core(out_block), core(out_near), core(out_next)]
        sums = part_sums((1, 2, 5, 6), [near, next_, near_peer, next_peer], sums)
        ud_block = jnp.concatenate([w_up, w_down.T], axis=1)
        far, sums, out_far, text_pre, ud_block = hold((far, sums, out_far, text_pre, ud_block))
        far_peer = core(far)
        ud_near = swap(ud_block, "seq", 8, first_way)
        ud_next = swap(ud_block, "seq", 8, other_way)
        out_t = place([out_block, out_near, out_next, out_far] + out_peers + [core(out_far)], roles)
        text_pieces = [text_norm(text_pre, key_gain)]
        cross_sums = attend(text_info, query_t, text_pieces, heads, clips)
        sums = part_sums((3, 7), [far, far_peer], sums)
        pieces = [kv_own, near, next_, far, kv_peer, near_peer, next_peer, far_peer]
    else:
        modulation = lax.psum(modulation, ("seq", "head"))
        text_pre = lax.psum(text_part, "seq")
        qkv_pieces = gather_pieces(qkv_block, seq_count)
        modulation = modulation.reshape(4, model_width)
        rows = vectors(modulation, norm_gains)
        act_a, x_scale, pre, kv_own, queries, query_t, w_qkv = queries_keys(qkv_pieces)
        pieces = gather_pieces(kv_own, seq_count)
        text_pieces = [text_norm(text_pre, key_gain)]
        out_t = place(gather_pieces(out_block, seq_count), roles)
        sums = part_sums(tuple(range(seq_count)), pieces)
        cross_sums = attend(text_info, query_t, text_pieces, heads, clips)
        gate_w = lax.all_gather(w_gate, "seq", axis=0, tiled=True)
    gate_local = jnp.tanh(cross_gate)
    mixed, self_t, cross_t, self_lse, cross_lse = mix(gate_local, sums, cross_sums, wide)
    attn_part = matmul(mixed, out_t, ROWS).astype(bf16)

    late = {}

    def split_weights(pieces):
        return place(pieces, roles, (units, units), 40)

    def fill_near(carry):
        return [ud_near, ud_next]

    def fill_far(carry):
        near, next_ = carry
        return [near, next_, swap(near, "seq", 8, other_way), core(ud_block), core(near), core(next_)]

    def fill_weights(carry):
        late["up"], late["down"] = split_weights([ud_block] + carry + [core(carry[2])])
        late["rows"] = touch(rows, [gate_w, late["up"], late["down"]])
        return [late["rows"]]

    if not spread:
        weights = gather_pieces(jnp.concatenate([w_up, w_down.T], axis=1), seq_count)
        late["up"], late["down"] = split_weights(weights)
        late["rows"] = rows
    chunk_count = 4
    chunk = local_rows // chunk_count
    rows_of = lambda v, k: v[k * chunk : (k + 1) * chunk]
    kept = [{} for _ in range(chunk_count)]


    tall, thin = (chunk, model_width), (chunk, units)
    whole = lambda width: (local_rows, chunk, width, bf16)

    def feed_forward(k, end, total, got, before):
        keep = kept[k]
        outs = [((chunk, 2 * model_width), f32), ((chunk, 128), f32), ((chunk, 2 * units), f32), (tall, bf16)]
        arrays = [total, got, rows_of(hidden_in, k), late["rows"], gate_w, late["up"], late["down"]]
        keep["norms"], keep["stats"], keep["pre"], part, late["first"] = staged(
            forward_kernel, k, outs, [whole(units + model_width)], [end], arrays,
            [late["first"]] if k else None, "feed_forward",
        )
        return part

    def feed_back(k, end, total, got, before):
        keep = kept[k]
        arrays = [total, got, keep["norms"], keep["pre"], rows_of(out_cotangent, k), late["rows"]]
        keep["uf"], part, late["second"], late["hidden"] = staged(
            backward_kernel, k, [((1, model_width), f32), (tall, bf16)],
            [whole(2 * units + model_width), whole(model_width)], [end], arrays + [gate_w, late["up"], late["down"]],
            [late["second"], late["hidden"]] if k else None, "feed_back",
        )
        return part

    def attn_back(k, end, total, got, before):
        keep = kept[k]
        arrays = [total, got, keep["norms"], keep["stats"], rows_of(out_cotangent, k), rows]
        keep["sums"], keep["dmid"], late["dattn"] = staged(
            attn_back_kernel, k, [((2, model_width), f32), (tall, f32)], [whole(model_width)], [end], arrays,
            [late["dattn"]] if k else None, "attn_back", 60,
        )
        return keep["sums"]

    total_of = lambda name, n: sum(keep[name][n] for keep in kept)

    def fill_down(carry):
        return [weight_grad(late["second"], 2 * units, model_width, late["first"], 0, units)]

    def fill_gate(carry):
        late["down_sum"] = finish_sum(carry[0])
        (first, second), carry = hold(((late["first"], late["second"]), carry))
        late["first"], late["second"] = first, second
        return [weight_grad(first, units, model_width, second, 0, units)]

    def fill_up(carry):
        late["gate_sum"] = finish_sum(carry[0])
        (first, second), carry = hold(((late["first"], late["second"]), carry))
        return [weight_grad(first, units, model_width, second, 1, units)]

    def fill_last(carry):
        late["up_sum"] = finish_sum(carry[0])
        return []

    fills = {8 + chunk_count - 1: fill_down, 8 + chunk_count: fill_gate, 8 + chunk_count + 1: fill_up, 8 + chunk_count + 2: fill_last}
    first_parts = [rows_of(attn_part, k) for k in range(chunk_count)]
    if spread:
        fills.update({0: fill_near, 1: fill_far, 2: fill_weights})
    run_ticks(
        first_parts, [feed_forward, feed_back, attn_back], head_index, head_count, fills
    )
    grad_attn_low, hidden_out = late["dattn"], late["hidden"]
    down_grad, gate_grad, up_grad = late["down_sum"], late["gate_sum"], late["up_sum"]

    grad_self_tok, grad_self_t, grad_cross_tok, grad_cross_t, self_delta, cross_delta, gate_rows = unmix(
        gate_local, grad_attn_low, out_t, self_t, cross_t
    )
    cross_gate_part = jnp.sum(gate_rows, axis=1) * (1.0 - gate_local * gate_local)

    def back(group, parts, before=None):
        return attend_back(
            self_info(group), query_t, grad_self_t, queries, grad_self_tok, self_lse, self_delta,
            [pieces[g] for g in group], heads, clips, bf16, parts, before,
        )

    def cross_back(before):
        return attend_back(
            text_info, query_t, grad_cross_t, queries, grad_cross_tok, cross_lse, cross_delta,
            text_pieces, heads, clips, f32, 1, before,
        )

    if spread:
        dq, _, kv_mine, kv_theirs = back((3, 2, 7, 6), 2)
        kv_got = core(kv_theirs)
        kv_mine, low = hold((kv_mine, grad_attn_low))
        out_part = matmul(low, mixed, COLS).astype(bf16)
        total = [add_low(kv_mine[:local_rows], kv_got[:local_rows]), add_low(kv_mine[local_rows:], kv_got[local_rows:])]
        total, dq, out_part = hold((total, dq, out_part))
        first = swap(total[0], "seq", 8, other_way)
        dq, text_dot, cross_kv = cross_back(dq)
        dq, cross_kv, down_grad, total = hold((dq, cross_kv, down_grad, total))
        own_first = swap(total[1], "seq", 8, other_way)
        dq, _, kv_mine, kv_theirs = back((1, 5), 2, dq)
        first, kv_mine, kv_theirs = hold((first, kv_mine, kv_theirs))
        total = kv_mine.astype(f32) + core(kv_theirs).astype(f32) + first.astype(f32)
        total = total.astype(bf16)
        second = swap(total, "seq", 8, first_way)
        dq, _, kv_mine, kv_theirs = back((0, 4), 2, dq)
        second, kv_mine, kv_theirs, gate_grad, own_first = hold((second, kv_mine, kv_theirs, gate_grad, own_first))
        kv_parts, kv_starts = [kv_mine, core(kv_theirs), own_first, second], (0, 0, 0, 0)
    else:
        dq, _, kv_all = back(tuple(range(seq_count)), 1)
        dq, text_dot, cross_kv = cross_back(dq)
        out_part = weight_grad(grad_attn_low, 0, model_width, mixed, 0, wide)
        kv_parts, kv_starts = [finish_sum(kv_all)], (0,)
    qkv_low, grad_query_gain, grad_key_gain, sum_a, *act_low = project_back(
        pre, query_gain, key_gain, cos, sin, dq, hidden_in, x_scale, w_qkv, kv_parts, kv_starts
    )
    act_low, qkv_low, cross_kv, gate_grad, out_part = hold((act_low, qkv_low, cross_kv, gate_grad, out_part))
    fold = lambda v: v[0, :HD] + v[0, HD:]
    pair_gains = jnp.concatenate([fold(grad_query_gain), fold(grad_key_gain + text_dot / key_gain)])
    tail = jnp.stack([sum_a[0], jnp.pad(pair_gains, (0, model_width - 2 * HD))])
    tail = jnp.pad(tail, ((0, 14), (0, 0))).astype(bf16)
    small = [total_of("sums", 1), total_of("sums", 0), total_of("uf", 0)]
    cross_row = jnp.pad(cross_gate_part, (2 * HD, model_width - 2 * HD - heads))

    def collect(k, end, total, got, before):
        if k == 1:
            late["tail"] = jnp.where(end[0] == 1, got, total)[chunk:].astype(f32)
        arrays = rows_of(hidden_in, k), rows, kept[k]["dmid"]
        mark = jnp.zeros((8, 128), f32) if before is None else before
        late["input"], mark = finish(k, end, total, got, *arrays, mark, local_rows, late.get("input"))
        return mark


    def fill0(carry):
        text_low = text_back(text_pre, key_gain, cross_kv)
        out = scatter_start(out_part, wheres[0]) if spread else out_part
        return [text_low, weight_grad(act_a, 0, model_width, qkv_low, 0, 3 * wide), out]

    def fill1(carry):
        late["qkv"] = finish_sum(carry[1])
        late["out"] = scatter_first(carry[2], wheres[1]) if spread else carry[2]
        gate, down, text = hold((gate_grad, down_grad, carry[0]))
        late["gate"], late["down"] = widen([gate]), widen([down]).T
        if not spread:
            return [lax.psum(text, "seq"), late["gate"], late["down"]]
        return [scatter_first(scatter_start(text, wheres[0]), wheres[1]), late["gate"], late["down"]]

    def fill2(carry):
        text, late["gate"], late["down"] = carry
        up, text = hold((up_grad, text))
        late["up"] = widen([up])
        if not spread:
            return [text, late["up"]]
        own = add_low(*scatter_second(text, wheres[2]))
        return [[own, swap(own, "seq", 8, first_way), swap(own, "seq", 8, other_way)], late["up"]]

    def fill3(carry):
        text, late["up"] = carry
        if not spread:
            return [text]
        text = text + [swap(text[1], "seq", 8, other_way)]
        out, text = hold((late["out"], text))
        late["out"] = scatter_second(out, wheres[2])
        return [text + [core(v) for v in text[:3]]]

    def fill4(carry):
        (text,) = carry
        tail_rows = [late["tail"][0]] + small + [jnp.pad(late["tail"][1, : 2 * HD], (0, model_width - 2 * HD)) + cross_row]
        values = jnp.pad(jnp.stack(tail_rows), ((0, 3), (0, 0)))
        out, text = hold((late["out"], text))
        late["out"] = widen(list(out)).T if spread else finish_sum(out).astype(f32).T
        if not spread:
            return [lax.psum(values, "seq"), text, late["out"]]
        return [hop(values, seq_hops[:2]), text + [core(text[3])], late["out"]]

    def fill5(carry):
        values, text, late["out"] = carry
        values = hop(values, seq_hops[2:]) if spread else values
        gain_grad, mod_grad = gains_back(values[:4], modulation, norm_gains)
        own_mod = lax.dynamic_slice_in_dim(
            mod_grad.reshape(-1), (seq_index * head_count + head_index) * piece_width, piece_width
        )
        text_grads = text_weight_grads(text if spread else [text], roles if spread else jnp.zeros((1,), jnp.int32), own_text)
        return [gain_grad, values[4], text_grads, cond_act.astype(f32)[:, None] * own_mod[None, :]]

    parts = list(act_low)
    parts[1] = jnp.concatenate([parts[1], tail])
    fills = dict(enumerate([fill0, fill1, fill2, fill3, fill4, fill5]))
    _, (norm_gains_grad, values, text_grad, ada_grad) = run_ticks(parts, [collect], head_index, head_count, fills)
    input_grad = late["input"]
    own_qkv = widen([late["qkv"]])

    qk_gains_grad = values[: 2 * HD].reshape(2, HD)
    cross_gate_grad = values[2 * HD : 2 * HD + heads]
    return (
        hidden_out,
        input_grad,
        ada_grad,
        norm_gains_grad,
        qk_gains_grad,
        cut(own_qkv[:, :wide]),
        cut(own_qkv[:, wide : 2 * wide]),
        cut(own_qkv[:, 2 * wide : 3 * wide]),
        late["out"][:cols],
        cross_gate_grad,
        cut(text_grad[0]),
        cut(text_grad[1]),
        late["gate"],
        late["up"],
        late["down"],
    )


def solution(mesh):
    in_specs = (
        P("seq", None),
        P(),
        P(),
        P(),
        P(None, ("seq", "head")),
        P(),
        P(),
        P("seq", "head"),
        P("seq", "head"),
        P("seq", "head"),
        P("head", "seq"),
        P("head"),
        P("seq", "head"),
        P("seq", "head"),
        P("seq", "head"),
        P("seq", "head"),
        P("head", "seq"),
        P("seq", None),
    )
    out_specs = (
        P("seq", None),
        P("seq", None),
        P(None, ("seq", "head")),
        P(),
        P(),
        P("seq", "head"),
        P("seq", "head"),
        P("seq", "head"),
        P("head", "seq"),
        P("head"),
        P("seq", "head"),
        P("seq", "head"),
        P("seq", "head"),
        P("seq", "head"),
        P("head", "seq"),
    )
    body = functools.partial(per_device, mesh.shape["seq"], mesh.shape["head"])
    return jax.shard_map(body, mesh=mesh, in_specs=in_specs, out_specs=out_specs, check_vma=False)
```

```python
import functools
import jax
import jax.numpy as jnp
from jax import lax
from jax.experimental import pallas as pl
from jax.experimental.pallas import tpu as pltpu
from jax.sharding import PartitionSpec as P

HD = 64
MASK = 8192.0
CHEAP = pl.CostEstimate(flops=1, bytes_accessed=1, transcendentals=0)
ATTEND_MIB = 60
BACK_MIB = 60
SMALL_MIB = 16


def dot(a, b):
    return lax.dot_general(a, b, (((1,), (0,)), ((), ())), preferred_element_type=jnp.float32)


def split3(v):
    hi = v.astype(jnp.bfloat16).astype(jnp.float32)
    mid = (v - hi).astype(jnp.bfloat16).astype(jnp.float32)
    return hi, mid, v - hi - mid


def bounds(info, base, clips, ids):
    start = jnp.full(ids.shape, 1 << 30, jnp.int32)
    end = jnp.zeros(ids.shape, jnp.int32)
    for c in range(clips):
        start = jnp.where(ids == c, info[base + c], start)
        end = jnp.where(ids == c, info[base + clips + c], end)
    return start, end


def query_ext(info, clips, width, scale):
    ids = lax.broadcasted_iota(jnp.int32, (16, width), 0)
    place = info[0] + lax.broadcasted_iota(jnp.int32, (16, width), 1)
    start, end = bounds(info, 1, clips, ids)
    return jnp.where((place >= start) & (place < end), scale, 0.0)


def key_ext(info, clips, row, rows, piece):
    ids = lax.broadcasted_iota(jnp.int32, (rows, 128), 1)
    step = min(rows, piece)
    parts = []
    for k in range(rows // step):
        at = row + k * step
        first = info[1 + 4 * clips + at // piece] + lax.rem(at, piece)
        parts.append(first + lax.broadcasted_iota(jnp.int32, (step, 128), 0))
    place = parts[0] if len(parts) == 1 else jnp.concatenate(parts, axis=0)
    start, end = bounds(info, 1 + 2 * clips, clips, ids)
    inside = (place >= start) & (place < end)
    value = jnp.where(ids < clips, jnp.where(inside, 0.0, -1.0), jnp.where(ids < clips + 3, 1.0, 0.0))
    return value.astype(jnp.bfloat16)


def fill_ext(dst, h, src, tail):
    width = src.shape[1]
    half = h % 2
    zero = jnp.zeros((HD, width), jnp.bfloat16)
    dst[h, half * HD : half * HD + HD, :] = src[h * HD : h * HD + HD, :]
    dst[h, (1 - half) * HD : (1 - half) * HD + HD, :] = zero
    dst[h, 128:144, :] = tail.astype(jnp.bfloat16)
    dst[h, 144:256, :] = jnp.zeros((112, width), jnp.bfloat16)


def stack_rows(heads, rows, clips, width):
    ids = lax.broadcasted_iota(jnp.int32, (16, width), 0)
    total = jnp.zeros((16, width), jnp.float32)
    for k, row in enumerate(rows):
        total = jnp.where(ids == clips + k, jnp.broadcast_to(row, (16, width)), total)
    return total


def load_pieces(pieces, kv, sem):
    rows = pieces[0].shape[0]
    return [
        pltpu.make_async_copy(piece, kv.at[pl.ds(k * rows, rows), :], sem.at[k])
        for k, piece in enumerate(pieces)
    ]


def fwd_kernel(heads, clips, count, tile, again, info, qt, *rest):
    before, pieces, (out, qx, kv, sem) = rest[:again], rest[again : again + count], rest[again + count :]
    copies = load_pieces(pieces, kv, sem)
    for c in copies:
        c.start()
    width = qt.shape[1]
    wide = qt.shape[0]
    ext = query_ext(info, clips, width, MASK)
    for h in range(heads):
        fill_ext(qx, h, qt, ext)
        out[h] = before[0][h] if again else jnp.zeros((80, width), jnp.float32)
    for c in copies:
        c.wait()
    steps = count * pieces[0].shape[0] // tile
    ones = jnp.ones((16, tile), jnp.bfloat16)

    def step(t, carry):
        rows = pl.ds(pl.multiple_of(t * tile, tile), tile)
        extra = key_ext(info, clips, t * tile, tile, pieces[0].shape[0])
        for p in range((heads + 1) // 2):
            kx = jnp.concatenate([kv[rows, p * 128 : p * 128 + 128], extra], axis=1)
            vt = kv[rows, wide + p * 128 : wide + p * 128 + 128].T
            for h in range(2 * p, min(2 * p + 2, heads)):
                half = h % 2
                probs = jnp.exp(dot(kx, qx[h])).astype(jnp.bfloat16)
                vx = jnp.concatenate([vt[half * HD : half * HD + HD, :], ones], axis=0)
                out[h] += dot(vx, probs)
        return carry

    lax.fori_loop(0, steps, step, 0)


def attend(info, qt, pieces, heads, clips, before=None, tile=1024):
    count = len(pieces)
    before = [] if before is None else [before]
    wide, width = qt.shape
    rows = pieces[0].shape[0]
    tile = min(tile, rows * count)
    return pl.pallas_call(
        functools.partial(fwd_kernel, heads, clips, count, tile, len(before)),
        out_shape=jax.ShapeDtypeStruct((heads, 80, width), jnp.float32),
        in_specs=[pl.BlockSpec(memory_space=pltpu.SMEM)]
        + [pl.BlockSpec()] * (1 + len(before))
        + [pl.BlockSpec(memory_space=pltpu.HBM)] * count,
        out_specs=pl.BlockSpec(),
        scratch_shapes=[
            pltpu.VMEM((heads, 256, width), jnp.bfloat16),
            pltpu.VMEM((count * rows, 2 * wide), jnp.bfloat16),
            pltpu.SemaphoreType.DMA((count,)),
        ],
        compiler_params=pltpu.CompilerParams(vmem_limit_bytes=ATTEND_MIB << 20),
        cost_estimate=CHEAP,
        name="attend",
    )(info, qt, *before, *pieces)


def bwd_kernel(heads, clips, count, tile, again, info, qt, dot_t, q_tok, do_tok, lse, delta, *rest):
    before, pieces, rest = rest[:again], rest[again : again + count], rest[again + count :]
    dqt, kdot, grads, (qx, dox, qpad, dopad, kv, sem) = rest[0], rest[1], rest[2:-6], rest[-6:]
    copies = load_pieces(pieces, kv, sem)
    for c in copies:
        c.start()
    wide, width = qt.shape
    ext = query_ext(info, clips, width, MASK)
    for h in range(heads):
        p, half = h // 2, h % 2
        fill_ext(qx, h, qt, ext - stack_rows(heads, split3(lse[h : h + 1, :]), clips, width))
        fill_ext(dox, h, dot_t, -stack_rows(heads, split3(delta[h : h + 1, :]), clips, width))
        lane = lax.broadcasted_iota(jnp.int32, (width, 128), 1) // HD
        zero = jnp.zeros((width, 128), jnp.bfloat16)
        qpad[h] = jnp.where(lane == half, q_tok[:, p * 128 : p * 128 + 128], zero)
        dopad[h] = jnp.where(lane == half, do_tok[:, p * 128 : p * 128 + 128], zero)
    kdot[...] = jnp.zeros((1, 128), jnp.float32)
    dqt[...] = before[0][...] if again else jnp.zeros((wide, width), jnp.float32)
    for c in copies:
        c.wait()
    steps = count * pieces[0].shape[0] // tile

    def step(t, carry):
        rows = pl.ds(pl.multiple_of(t * tile, tile), tile)
        extra = key_ext(info, clips, t * tile, tile, pieces[0].shape[0])
        for p in range((heads + 1) // 2):
            cols = slice(p * 128, p * 128 + 128)
            vcols = slice(wide + p * 128, wide + p * 128 + 128)
            k_tile = kv[rows, cols]
            kx = jnp.concatenate([k_tile, extra], axis=1)
            vx = jnp.concatenate([kv[rows, vcols], extra], axis=1)
            kt = k_tile.T
            dk = jnp.zeros((tile, 128), jnp.float32)
            dv = jnp.zeros((tile, 128), jnp.float32)
            for h in range(2 * p, min(2 * p + 2, heads)):
                half = h % 2
                probs = jnp.exp(dot(kx, qx[h]))
                ds = (probs * dot(vx, dox[h])).astype(jnp.bfloat16)
                dqt[h * HD : h * HD + HD, :] += dot(kt[half * HD : half * HD + HD, :], ds)
                dk = dk + dot(ds, qpad[h])
                dv = dv + dot(probs.astype(jnp.bfloat16), dopad[h])
            kdot[...] += jnp.sum(dk * k_tile.astype(jnp.float32), axis=0, keepdims=True)
            part = grads[0].shape[0]
            if tile > part:
                for g, grad in enumerate(grads):
                    grad[:, cols] = dk[g * part : g * part + part, :].astype(grad.dtype)
                    grad[:, vcols] = dv[g * part : g * part + part, :].astype(grad.dtype)
                continue
            for g, grad in enumerate(grads):

                @pl.when(t // (steps // len(grads)) == g)
                def store(g=g, grad=grad, dk=dk, dv=dv, cols=cols, vcols=vcols):
                    start = (t - g * (steps // len(grads))) * tile
                    here = pl.ds(pl.multiple_of(start, tile), tile)
                    grad[here, cols] = dk.astype(grad.dtype)
                    grad[here, vcols] = dv.astype(grad.dtype)

        return carry

    lax.fori_loop(0, steps, step, 0)


def attend_back(info, qt, dot_t, q_tok, do_tok, lse, delta, pieces, heads, clips, kind, parts=1, before=None, tile=2048):
    count = len(pieces)
    before = [] if before is None else [before]
    wide, width = qt.shape
    rows = pieces[0].shape[0]
    tile = rows * count if rows * count <= tile else min(tile, rows * count // parts)
    return pl.pallas_call(
        functools.partial(bwd_kernel, heads, clips, count, tile, len(before)),
        out_shape=(
            jax.ShapeDtypeStruct((wide, width), jnp.float32),
            jax.ShapeDtypeStruct((1, 128), jnp.float32),
        )
        + (jax.ShapeDtypeStruct((count * rows // parts, 2 * wide), kind),) * parts,
        in_specs=[pl.BlockSpec(memory_space=pltpu.SMEM)]
        + [pl.BlockSpec()] * (6 + len(before))
        + [pl.BlockSpec(memory_space=pltpu.HBM)] * count,
        out_specs=(pl.BlockSpec(),) * (2 + parts),
        scratch_shapes=[
            pltpu.VMEM((heads, 256, width), jnp.bfloat16),
            pltpu.VMEM((heads, 256, width), jnp.bfloat16),
            pltpu.VMEM((heads, width, 128), jnp.bfloat16),
            pltpu.VMEM((heads, width, 128), jnp.bfloat16),
            pltpu.VMEM((count * rows, 2 * wide), jnp.bfloat16),
            pltpu.SemaphoreType.DMA((count,)),
        ],
        compiler_params=pltpu.CompilerParams(vmem_limit_bytes=BACK_MIB << 20),
        cost_estimate=CHEAP,
        name="attend_back",
    )(info, qt, dot_t, q_tok, do_tok, lse, delta, *before, *pieces)


ROWS = (((1,), (1,)), ((), ()))
COLS = (((0,), (0,)), ((), ()))
f32 = jnp.float32
bf16 = jnp.bfloat16


def matmul(left, right, dims=None):
    if dims is None:
        return jnp.dot(left, right, preferred_element_type=f32)
    return lax.dot_general(left, right, dims, preferred_element_type=f32)


def first_way(i):
    return i ^ 2 if i % 2 == 0 else i ^ 4


def other_way(i):
    return i ^ 4 if i % 2 == 0 else i ^ 2


def swap(value, axis, count, to):
    return lax.ppermute(value, axis, [(i, to(i)) for i in range(count)])


def seq_roles(seq_index, seq_count):
    if seq_count != 8:
        return jnp.arange(seq_count, dtype=jnp.int32)
    peer = seq_index ^ 1

    def roles(i):
        even = i % 2 == 0
        return [i, jnp.where(even, i ^ 2, i ^ 4), jnp.where(even, i ^ 4, i ^ 2), i ^ 6]

    return jnp.stack(roles(seq_index) + roles(peer)).astype(jnp.int32)


def gather_pieces(block, seq_count):
    if seq_count != 8:
        whole = lax.all_gather(block, "seq", axis=0, tiled=False)
        return [whole[i] for i in range(seq_count)]
    near = swap(block, "seq", 8, first_way)
    next_ = swap(block, "seq", 8, other_way)
    far = swap(near, "seq", 8, other_way)
    mine = [block, near, next_, far]
    return mine + [swap(v, "seq", 8, lambda i: i ^ 1) for v in mine]


def place_kernel(count, rows, widths, roles, *rest):
    pieces, outs, sem = rest[:count], rest[count:-1], rest[-1]
    copies = []
    for k in range(count):
        to = pl.ds(pl.multiple_of(roles[k] * rows, rows), rows)
        first = 0
        for n, width in enumerate(widths):
            piece = pieces[k].at[:, first : first + width]
            copies.append(pltpu.make_async_copy(piece, outs[n].at[to, :], sem.at[k, n]))
            first += width
    for c in copies:
        c.start()
    for c in copies:
        c.wait()


def place(pieces, roles, widths=None, limit=SMALL_MIB):
    count = len(pieces)
    rows, width = pieces[0].shape
    outs = widths or (width,)
    placed = pl.pallas_call(
        functools.partial(place_kernel, count, rows, outs),
        out_shape=[jax.ShapeDtypeStruct((count * rows, w), pieces[0].dtype) for w in outs],
        in_specs=[pl.BlockSpec(memory_space=pltpu.SMEM)]
        + [pl.BlockSpec(memory_space=pltpu.HBM)] * count,
        out_specs=[pl.BlockSpec(memory_space=pltpu.VMEM)] * len(outs),
        scratch_shapes=[pltpu.SemaphoreType.DMA((count, len(outs)))],
        compiler_params=pltpu.CompilerParams(vmem_limit_bytes=limit << 20),
        cost_estimate=CHEAP,
        name="place",
    )(roles, *pieces)
    return placed if widths else placed[0]


def take_kernel(rows, core, part, out, sem):
    copies = []
    for chip in range(4):
        start = pl.multiple_of((2 * chip + core[0]) * rows, rows)
        to = out.at[pl.ds(chip * rows, rows), :]
        copies.append(pltpu.make_async_copy(part.at[pl.ds(start, rows), :], to, sem.at[chip]))
    for c in copies:
        c.start()
    for c in copies:
        c.wait()


def first_kernel(rows, where, part, got, mine, send, held, sem):
    copies = []
    for chip in range(4):
        start = pl.multiple_of((2 * chip + where[0]) * rows, rows)
        to = held.at[pl.ds(chip * rows, rows), :]
        copies.append(pltpu.make_async_copy(part.at[pl.ds(start, rows), :], to, sem.at[chip]))
    for c in copies:
        c.start()
    for c in copies:
        c.wait()
    mine[...] = (held[...].astype(f32) + got[...].astype(f32)).astype(bf16)
    for n in range(2):
        send[n * rows : n * rows + rows, :] = mine[pl.ds(pl.multiple_of(where[1 + n] * rows, rows), rows), :]


def second_kernel(rows, where, mine, got, own, send):
    block = lambda n: mine[pl.ds(pl.multiple_of(where[n] * rows, rows), rows), :].astype(f32)
    own[...] = (block(0) + got[rows:, :].astype(f32)).astype(bf16)
    send[...] = (block(1) + got[:rows, :].astype(f32)).astype(bf16)


def scatter_call(kernel, rows, where, arrays, outs, scratch, name, first=pltpu.VMEM):
    width = arrays[0].shape[1]
    vmem = pl.BlockSpec(memory_space=pltpu.VMEM)
    return pl.pallas_call(
        functools.partial(kernel, rows),
        out_shape=[jax.ShapeDtypeStruct((n * rows, width), bf16) for n in outs],
        in_specs=[pl.BlockSpec(memory_space=pltpu.SMEM), pl.BlockSpec(memory_space=first)]
        + [vmem] * (len(arrays) - 1),
        out_specs=[vmem] * len(outs),
        scratch_shapes=scratch,
        compiler_params=pltpu.CompilerParams(vmem_limit_bytes=SMALL_MIB << 20),
        cost_estimate=CHEAP,
        name=name,
    )(where, *arrays)


def scatter_start(part, where):
    rows = part.shape[0] // 8
    sems = [pltpu.SemaphoreType.DMA((4,))]
    theirs = scatter_call(take_kernel, rows, where, [part], [4], sems, "scatter_take", pl.ANY)[0]
    return part, swap(theirs, "seq", 8, lambda i: i ^ 1)


def scatter_first(pair, where):
    part, got = pair
    rows = part.shape[0] // 8
    scratch = [pltpu.VMEM(got.shape, bf16), pltpu.SemaphoreType.DMA((4,))]
    mine, send = scatter_call(first_kernel, rows, where, [part, got], [4, 2], scratch, "scatter_first", pl.ANY)
    return mine, swap(send, "seq", 8, other_way)


def scatter_second(pair, where):
    mine, got = pair
    own, send = scatter_call(second_kernel, mine.shape[0] // 4, where, [mine, got], [1, 1], [], "scatter_second")
    return own, swap(send, "seq", 8, first_way)


def widen_kernel(count, turn, *refs):
    total = refs[0][...].astype(f32)
    for ref in refs[1:count]:
        total = total + ref[...].astype(f32)
    refs[count][...] = total.T if turn else total


def widen(parts, turn=False):
    rows, width = parts[0].shape
    return pl.pallas_call(
        functools.partial(widen_kernel, len(parts), turn),
        out_shape=jax.ShapeDtypeStruct((width, rows) if turn else (rows, width), f32),
        compiler_params=pltpu.CompilerParams(vmem_limit_bytes=SMALL_MIB << 20),
        cost_estimate=CHEAP,
        name="widen",
    )(*parts)


def hops(axis, count):
    return [(axis, 1 << k) for k in range(count.bit_length() - 1)]


def sum_all(value, axes, order, beside=()):
    if any(count & (count - 1) for _, count in axes):
        return lax.psum(value, [axis for axis, _ in axes]), list(beside)
    counts, beside = dict(axes), list(beside)
    for k, (axis, bit) in enumerate(order):
        got = swap(value, axis, counts[axis], lambda i: i ^ bit)
        if k < len(beside):
            got, beside[k] = lax.optimization_barrier((got, beside[k]))
        value = value + got
    return value, beside


def add_low(a, b):
    return (a.astype(f32) + b.astype(f32)).astype(bf16)


def relay_kernel(names, end, *refs):
    ins = dict(zip(names, refs))
    outs = list(refs[len(names) :])
    add = lambda a, b: (ins[a][...].astype(f32) + ins[b][...].astype(f32)).astype(bf16)
    if "part" in ins:
        outs.pop(0)[...] = add("part", "part_got")
    if "total" in ins:
        total = add("total", "total_got")
        outs.pop(0)[...] = total
        if "own" in ins:
            send = outs.pop(0)
            rows, own_rows = total.shape[0], ins["own"].shape[0]
            both = min(rows, own_rows)
            send[:both, :] = jnp.where(end[0] == 1, ins["own"][:both, :], total[:both, :])
            if own_rows > both:
                send[both:, :] = ins["own"][both:, :]
            if rows > both:
                send[both:, :] = total[both:, :]


def relay(end, part, total, own):
    ins = {}
    shapes = []
    if part is not None:
        ins.update(part=part[0], part_got=part[1])
        shapes.append(part[0].shape)
    if total is not None:
        ins.update(total=total[0], total_got=total[1])
        shapes.append(total[0].shape)
        if own is not None:
            ins["own"] = own
            shapes.append((max(own.shape[0], total[0].shape[0]), own.shape[1]))
    if not shapes:
        return None, None, own
    outs = pl.pallas_call(
        functools.partial(relay_kernel, tuple(ins)),
        out_shape=[jax.ShapeDtypeStruct(shape, bf16) for shape in shapes],
        in_specs=[pl.BlockSpec(memory_space=pltpu.SMEM)] + [pl.BlockSpec(memory_space=pltpu.VMEM)] * len(ins),
        out_specs=[pl.BlockSpec(memory_space=pltpu.VMEM)] * len(shapes),
        compiler_params=pltpu.CompilerParams(vmem_limit_bytes=SMALL_MIB << 20),
        cost_estimate=CHEAP,
        name="relay",
    )(end, *ins.values())
    outs = list(outs)
    part = outs.pop(0) if part is not None else None
    total = outs.pop(0) if total is not None else None
    return part, total, outs.pop(0) if outs else own


def staged(kernel, k, outs, wholes, scalars, arrays, before, name, limit=SMALL_MIB):
    before = before or []
    vmem = pl.BlockSpec() if limit == 60 else pl.BlockSpec(memory_space=pltpu.VMEM)
    anywhere = pl.BlockSpec(memory_space=pl.ANY)
    given = len(scalars) + len(arrays)
    return pl.pallas_call(
        functools.partial(kernel, k, len(before)),
        out_shape=[jax.ShapeDtypeStruct(shape, kind) for shape, kind in outs]
        + [jax.ShapeDtypeStruct((tokens, width), kind) for tokens, rows, width, kind in wholes],
        in_specs=[pl.BlockSpec(memory_space=pltpu.SMEM)] * len(scalars)
        + [vmem] * len(arrays)
        + [anywhere] * len(before),
        out_specs=[vmem] * len(outs) + [anywhere] * len(wholes),
        scratch_shapes=[pltpu.VMEM((rows, width), kind) for tokens, rows, width, kind in wholes]
        + [pltpu.SemaphoreType.DMA(())] * len(wholes),
        input_output_aliases={given + n: len(outs) + n for n in range(len(before))},
        compiler_params=pltpu.CompilerParams(vmem_limit_bytes=limit << 20),
        cost_estimate=CHEAP,
        name=name,
    )(*scalars, *arrays, *before)


def put_rows(k, value, whole, sem):
    rows = value.shape[0]
    copy = pltpu.make_async_copy(value, whole.at[pl.ds(k * rows, rows), :], sem)
    copy.start()
    return copy


def rms(value):
    return lax.rsqrt(jnp.mean(value * value, axis=-1, keepdims=True) + 1e-06)


def rms_back(grad, normed, scale):
    return scale * (grad - normed * jnp.mean(grad * normed, axis=-1, keepdims=True))


def dot_rows(a, b):
    return lax.dot_general(a, b, ROWS, preferred_element_type=f32)


def picked(end, total, got):
    return jnp.where(end[0] == 1, got[...], total[...]).astype(f32)


def forward_kernel(k, again, end, total, got, x, gains, gate_w, up_w, down_t, *rest):
    norms, stats, pre, part, low, pack, sem = rest[again:]
    width, units = x.shape[1], gate_w.shape[1]
    attn = picked(end, total, got)
    scale = rms(attn)
    normed = attn * scale
    norms[:, :width] = normed
    middle = x[...].astype(f32) + normed * gains[1:2, :]
    norms[:, width:] = middle
    middle_scale = rms(middle)
    lane = lax.broadcasted_iota(jnp.int32, stats.shape, 1)
    stats[...] = jnp.where(lane == 0, scale, middle_scale)
    act = (middle * middle_scale * gains[2:3, :]).astype(bf16)
    pack[:, units:] = act
    gated = dot(act, gate_w[...])
    upper = dot(act, up_w[...])
    pre[:, :units] = gated
    pre[:, units:] = upper
    unit = (gated * jax.nn.sigmoid(gated) * upper).astype(bf16)
    pack[:, :units] = unit
    copy = put_rows(k, pack, low, sem)
    part[...] = dot_rows(unit, down_t[...]).astype(bf16)
    copy.wait()


def backward_kernel(k, again, end, total, got, norms, pre, cot, gains, gate_w, up_w, down_t, *rest):
    sums, part, low, out, pack, done, sem, out_sem = rest[again:]
    width, units = cot.shape[1], gate_w.shape[1]
    ffn = picked(end, total, got)
    scale = rms(ffn)
    normed = ffn * scale
    done[...] = (norms[:, width:] + normed * gains[3:4, :]).astype(bf16)
    out_copy = put_rows(k, done, out, out_sem)
    grad = cot[...].astype(f32)
    sums[...] = jnp.sum(grad * normed, axis=0, keepdims=True)
    grad_ffn = rms_back(grad * gains[3:4, :], normed, scale).astype(bf16)
    pack[:, 2 * units :] = grad_ffn
    grad_units = dot(grad_ffn, down_t[...])
    gated = pre[:, :units]
    sig = jax.nn.sigmoid(gated)
    low_gate = (grad_units * pre[:, units:] * sig * (1.0 + gated * (1.0 - sig))).astype(bf16)
    low_up = (grad_units * gated * sig).astype(bf16)
    pack[:, :units] = low_gate
    pack[:, units : 2 * units] = low_up
    copy = put_rows(k, pack, low, sem)
    part[...] = (dot_rows(low_gate, gate_w[...]) + dot_rows(low_up, up_w[...])).astype(bf16)
    copy.wait()
    out_copy.wait()


def attn_back_kernel(k, again, end, total, got, norms, stats, cot, gains, *rest):
    sums, dmid, dattn, pack, sem = rest[again:]
    width = cot.shape[1]
    grad = picked(end, total, got)
    scale, middle_scale = stats[:, 0:1], stats[:, 1:2]
    normed = norms[:, width:] * middle_scale
    sums[0:1, :] = jnp.sum(grad * normed, axis=0, keepdims=True)
    middle = cot[...].astype(f32) + rms_back(grad * gains[2:3, :], normed, middle_scale)
    dmid[...] = middle
    normed = norms[:, :width]
    sums[1:2, :] = jnp.sum(middle * normed, axis=0, keepdims=True)
    pack[...] = rms_back(middle * gains[1:2, :], normed, scale).astype(bf16)
    put_rows(k, pack, dattn, sem).wait()


def weight_grad_kernel(left, right, out):
    out[...] = lax.dot_general(left[...], right[...], COLS, preferred_element_type=f32).astype(bf16)


def weight_grad(left, first, width, right, place, right_width):
    tokens = left.shape[0]
    step = 512
    return pl.pallas_call(
        weight_grad_kernel,
        out_shape=jax.ShapeDtypeStruct((width, right_width), bf16),
        grid=(width // step,),
        in_specs=[
            pl.BlockSpec((tokens, step), lambda i: (0, first // step + i)),
            pl.BlockSpec((tokens, right_width), lambda i: (0, place)),
        ],
        out_specs=pl.BlockSpec((step, right_width), lambda i: (i, 0)),
        compiler_params=pltpu.CompilerParams(vmem_limit_bytes=60 << 20),
        cost_estimate=CHEAP,
        name="weight_grad",
    )(left, right)


def run_ticks(parts, computes, head_index, head_count, fill):
    carry = []
    stages = 4 * len(computes)
    ticks = stages + len(parts) - 1
    if head_count != 4:
        for n, compute in enumerate(computes):
            sums = [lax.psum(part, "head") for part in parts]
            parts = []
            for k, part in enumerate(sums):
                before = parts[k - 1] if k else None
                parts.append(compute(k, jnp.zeros((1,), jnp.int32), part, part, before))
        for t in range(ticks):
            carry = fill[t](carry) if t in fill else carry
        return parts, carry
    end = jnp.where((head_index == 0) | (head_index == 3), 1, 0).astype(jnp.int32).reshape(1)
    states = [(part,) for part in parts]
    for t in range(ticks):
        at = {(t - k) % 4: k for k in range(len(parts)) if 0 <= t - k < stages}
        live = [k for k in range(len(parts)) if t - k < stages + 1]
        own = states[at[0]][0] if 0 in at else None
        part, total, send = relay(
            end, states[at[1]] if 1 in at else None, states[at[2]] if 2 in at else None, own
        )
        late = states[at[3]] if 3 in at else ()
        if part is not None or total is not None:
            part, total, send, late, carry = lax.optimization_barrier((part, total, send, late, carry))
        if 3 in at:
            states[at[3]] = late
        if 1 in at:
            states[at[1]] = (part, lax.ppermute(part, "head", [(1, 2), (2, 1)]))
        if 0 in at and 2 in at:
            got = lax.ppermute(send, "head", [(0, 1), (3, 2), (1, 0), (2, 3)])
            states[at[0]] = (own, got[: own.shape[0]])
            states[at[2]] = (total, got[: total.shape[0]])
        elif 0 in at:
            states[at[0]] = (own, lax.ppermute(own, "head", [(0, 1), (3, 2)]))
        elif 2 in at:
            states[at[2]] = (total, lax.ppermute(total, "head", [(1, 0), (2, 3)]))
        if 3 in at:
            k = at[3]
            before = states[k - 1][0] if k else None
            states[k] = (computes[(t - k) // 4](k, end, *states[k], before),)
        if t in fill:
            carry = fill[t](carry)
        held, carry = lax.optimization_barrier(([states[k] for k in live], carry))
        for k, state in zip(live, held):
            states[k] = state
    return [state[0] for state in states], carry


def head_mean(value):
    row = lax.broadcasted_iota(jnp.int32, (128, 128), 0) // HD
    col = lax.broadcasted_iota(jnp.int32, (128, 128), 1) // HD
    ones = jnp.where(row == col, 1.0 / HD, 0.0).astype(bf16)
    hi, mid, lo = split3(value)
    return dot(hi.astype(bf16), ones) + dot(mid.astype(bf16), ones) + dot(lo.astype(bf16), ones)


def partner(value):
    lane = lax.broadcasted_iota(jnp.int32, value.shape, 1) % HD
    return jnp.where(lane < HD // 2, pltpu.roll(value, 128 - HD // 2, 1), pltpu.roll(value, HD // 2, 1))


def text_norm_kernel(pre, gain, out):
    wide = pre.shape[1] // 2
    for p in range(wide // 128):
        cols = slice(p * 128, p * 128 + 128)
        value = pre[:, cols].astype(f32)
        out[:, cols] = (value * lax.rsqrt(head_mean(value * value) + 1e-6) * gain[...]).astype(bf16)
    out[:, wide:] = pre[:, wide:]


def text_norm(pre, gain):
    return pl.pallas_call(
        text_norm_kernel, out_shape=jax.ShapeDtypeStruct(pre.shape, bf16), name="text_norm", cost_estimate=CHEAP
    )(pre, gain)


def qkv_kernel(count, rows, wide, roles, x, gain, qgain, kgain, cos, sin, *rest):
    pieces, (act, scale, pre, kv, query, query_t, weight, sem) = rest[:count], rest[count:]
    copies = []
    for k in range(count):
        start = pl.multiple_of(roles[k] * rows, rows)
        copies.append(pltpu.make_async_copy(pieces[k], weight.at[pl.ds(start, rows), :], sem.at[k]))
    for c in copies:
        c.start()
    value = x[...].astype(f32)
    inverse = lax.rsqrt(jnp.mean(value * value, axis=-1, keepdims=True) + 1e-6)
    scale[...] = inverse
    act[...] = (value * inverse * gain[0:1, :]).astype(bf16)
    for c in copies:
        c.wait()
    pre[...] = dot(act[...], weight[:, : 2 * wide])
    kv[:, wide:] = dot(act[...], weight[:, 2 * wide :]).astype(bf16)
    for p in range(wide // 128):
        cols = slice(p * 128, p * 128 + 128)
        for which, out_gain in ((0, qgain), (1, kgain)):
            raw = pre[:, which * wide + p * 128 : which * wide + p * 128 + 128]
            raw = raw * lax.rsqrt(head_mean(raw * raw) + 1e-6) * out_gain[...]
            raw = raw * cos[...] + partner(raw) * sin[...]
            if which == 1:
                kv[:, cols] = raw.astype(bf16)
            else:
                raw = raw.astype(bf16).astype(f32) * HD**-0.5
                query[:, cols] = raw.astype(bf16)
                query_t[cols, :] = raw.T.astype(bf16)


def project(roles, x, gain, qgain, kgain, cos, sin, pieces, wide):
    count = len(pieces)
    rows = pieces[0].shape[0]
    tokens, width = x.shape
    shape = jax.ShapeDtypeStruct
    return pl.pallas_call(
        functools.partial(qkv_kernel, count, rows, wide),
        out_shape=(
            shape((tokens, width), bf16),
            shape((tokens, 1), f32),
            shape((tokens, 2 * wide), f32),
            shape((tokens, 2 * wide), bf16),
            shape((tokens, wide), bf16),
            shape((wide, tokens), bf16),
            shape((width, 3 * wide), bf16),
        ),
        in_specs=[pl.BlockSpec(memory_space=pltpu.SMEM)]
        + [pl.BlockSpec(memory_space=pltpu.VMEM)] * 6
        + [pl.BlockSpec(memory_space=pltpu.HBM)] * count,
        out_specs=(pl.BlockSpec(memory_space=pltpu.VMEM),) * 7,
        scratch_shapes=[pltpu.SemaphoreType.DMA((count,))],
        compiler_params=pltpu.CompilerParams(vmem_limit_bytes=60 << 20),
        cost_estimate=CHEAP,
        name="project",
    )(roles, x, gain, qgain, kgain, cos, sin, *pieces)


def mix_kernel(heads, gate, sums, cross, mixed, self_t, cross_t, lse, cross_lse):
    for p in range((heads + 1) // 2):
        both = []
        for h in range(2 * p, 2 * p + 2):
            if h >= heads:
                both.append(jnp.zeros_like(both[0]))
                continue
            rows = slice(h * HD, h * HD + HD)
            den, cross_den = sums[h, HD : HD + 1, :], cross[h, HD : HD + 1, :]
            lse[h : h + 1, :] = jnp.log(den)
            cross_lse[h : h + 1, :] = jnp.log(cross_den)
            own = sums[h, :HD, :] / den
            other = cross[h, :HD, :] / cross_den
            self_t[rows, :] = own
            cross_t[rows, :] = other
            both.append(own + gate[h] * other)
        mixed[:, p * 128 : p * 128 + 128] = jnp.concatenate(both, axis=0).T.astype(bf16)


def mix(gate, sums, cross, wide):
    heads, _, tokens = sums.shape
    shape = jax.ShapeDtypeStruct
    return pl.pallas_call(
        functools.partial(mix_kernel, heads),
        out_shape=(
            shape((tokens, wide), bf16),
            shape((heads * HD, tokens), f32),
            shape((heads * HD, tokens), f32),
            shape((heads, tokens), f32),
            shape((heads, tokens), f32),
        ),
        in_specs=[pl.BlockSpec(memory_space=pltpu.SMEM)] + [pl.BlockSpec(memory_space=pltpu.VMEM)] * 2,
        compiler_params=pltpu.CompilerParams(vmem_limit_bytes=SMALL_MIB << 20),
        name="mix",
        cost_estimate=CHEAP,
    )(gate, sums, cross)


def unmix_kernel(heads, gate, weight, self_t, cross_t, grad, tok, tok_t, ctok, ctok_t, delta, cdelta, cgate):
    width = tok.shape[0]
    for p in range((heads + 1) // 2):
        cols = slice(p * 128, p * 128 + 128)
        value = dot(grad[...], weight[:, cols])
        lane = lax.broadcasted_iota(jnp.int32, (width, 128), 1) // HD
        gates = jnp.where(lane == 0, gate[2 * p], gate[min(2 * p + 1, heads - 1)])
        tok[:, cols] = value.astype(bf16)
        ctok[:, cols] = (value * gates).astype(bf16)
        turned = value.T
        for h in range(2 * p, 2 * p + 2):
            rows = slice(h * HD, h * HD + HD)
            part = turned[(h % 2) * HD : (h % 2) * HD + HD, :]
            tok_t[rows, :] = part.astype(bf16)
            if h >= heads:
                ctok_t[rows, :] = part.astype(bf16)
                continue
            low = (part * gate[h]).astype(bf16)
            ctok_t[rows, :] = low
            delta[h : h + 1, :] = jnp.sum(part.astype(bf16).astype(f32) * self_t[rows, :], axis=0, keepdims=True)
            cdelta[h : h + 1, :] = jnp.sum(low.astype(f32) * cross_t[rows, :], axis=0, keepdims=True)
            cgate[h : h + 1, :] = jnp.sum(part * cross_t[rows, :], axis=0, keepdims=True)


def unmix(gate, grad, weight, self_t, cross_t):
    tokens = self_t.shape[1]
    wide = weight.shape[1]
    heads = self_t.shape[0] // HD
    shape = jax.ShapeDtypeStruct
    return pl.pallas_call(
        functools.partial(unmix_kernel, heads),
        out_shape=(shape((tokens, wide), bf16), shape((wide, tokens), bf16)) * 2 + (shape((heads, tokens), f32),) * 3,
        in_specs=[pl.BlockSpec(memory_space=pltpu.SMEM)]
        + [pl.BlockSpec()] * 4,
        compiler_params=pltpu.CompilerParams(vmem_limit_bytes=60 << 20),
        name="unmix",
        cost_estimate=CHEAP,
    )(gate, weight, self_t, cross_t, grad)


def norm_back(raw, gain, grad, cos=None, sin=None):
    scale = lax.rsqrt(head_mean(raw * raw) + 1e-6)
    normed = raw * scale
    if cos is not None:
        grad = grad * cos - partner(grad) * sin
    gain_grad = jnp.sum(grad * normed, axis=0, keepdims=True)
    grad = grad * gain
    return scale * (grad - normed * head_mean(grad * normed)), gain_grad


def text_back_kernel(pre, gain, grad, out):
    wide = pre.shape[1] // 2
    for p in range(wide // 128):
        cols = slice(p * 128, p * 128 + 128)
        out[:, cols] = norm_back(pre[:, cols].astype(f32), gain[...], grad[:, cols])[0].astype(bf16)
    out[:, wide:] = grad[:, wide:].astype(bf16)


def text_back(pre, gain, grad):
    return pl.pallas_call(
        text_back_kernel,
        out_shape=jax.ShapeDtypeStruct(grad.shape, bf16),
        name="text_back",
        cost_estimate=CHEAP,
    )(pre, gain, grad)


def project_back_kernel(wide, starts, pre, qgain, kgain, cos, sin, dqt, x, scale, weight, *rest):
    kvs, (out, qgrad, kgrad, sums, *acts) = rest[: len(starts)], rest[len(starts) :]
    tokens = pre.shape[0]
    total = [jnp.zeros((1, 128), f32), jnp.zeros((1, 128), f32)]
    summed = lambda cols: sum(kv[start : start + tokens, cols].astype(f32) for kv, start in zip(kvs, starts))
    for p in range(wide // 128):
        cols = slice(p * 128, p * 128 + 128)
        grads = (dqt[cols, :] * HD**-0.5).T, summed(cols)
        for which, gain in ((0, qgain), (1, kgain)):
            at = slice(which * wide + p * 128, which * wide + p * 128 + 128)
            value, extra = norm_back(pre[:, at], gain[...], grads[which], cos[...], sin[...])
            out[:, at] = value.astype(bf16)
            total[which] = total[which] + extra
    out[:, 2 * wide :] = summed(slice(wide, 2 * wide)).astype(bf16)
    qgrad[...] = total[0]
    kgrad[...] = total[1]
    value = dot_rows(out[...], weight[...])
    rows = acts[0].shape[0]
    for n, act in enumerate(acts):
        act[...] = value[n * rows : n * rows + rows, :].astype(bf16)
    sums[...] = jnp.sum(value * (x[...].astype(f32) * scale[...]), axis=0, keepdims=True)


def project_back(pre, qgain, kgain, cos, sin, dqt, x, scale, weight, kvs, starts):
    tokens, wide = pre.shape[0], pre.shape[1] // 2
    shape = jax.ShapeDtypeStruct
    return pl.pallas_call(
        functools.partial(project_back_kernel, wide, tuple(starts)),
        out_shape=(
            shape((tokens, 3 * wide), bf16),
            shape((1, 128), f32),
            shape((1, 128), f32),
            shape((1, x.shape[1]), f32),
        )
        + (shape((tokens // 4, x.shape[1]), bf16),) * 4,
        name="project_back",
        cost_estimate=CHEAP,
        compiler_params=pltpu.CompilerParams(vmem_limit_bytes=60 << 20),
    )(pre, qgain, kgain, cos, sin, dqt, x, scale, weight, *kvs)


def finish_kernel(k, end, total, got, x, gain, mid, mark, *rest):
    out, done, value, sem = rest[-4:]
    rows = mid.shape[0]
    value_x = x[...].astype(f32)
    inverse = rms(value_x)
    normed = value_x * inverse
    grad = picked(end, total, got)[:rows] * gain[0:1, :]
    mean = jnp.mean(grad * normed, axis=-1, keepdims=True)
    value[...] = mid[...] + inverse * (grad - normed * mean)
    copy = pltpu.make_async_copy(value, out.at[pl.ds(k * rows, rows), :], sem)
    copy.start()
    done[...] = mark[...]
    copy.wait()


def finish(k, end, total, got, x, gain, mid, mark, tokens, before):
    before = [] if before is None else [before]
    vmem = pl.BlockSpec(memory_space=pltpu.VMEM)
    return pl.pallas_call(
        functools.partial(finish_kernel, k),
        out_shape=[jax.ShapeDtypeStruct((tokens, mid.shape[1]), f32), jax.ShapeDtypeStruct(mark.shape, f32)],
        in_specs=[pl.BlockSpec(memory_space=pltpu.SMEM)] + [vmem] * 6 + [pl.BlockSpec(memory_space=pl.ANY)] * len(before),
        out_specs=[pl.BlockSpec(memory_space=pl.ANY), vmem],
        scratch_shapes=[pltpu.VMEM(mid.shape, f32), pltpu.SemaphoreType.DMA(())],
        input_output_aliases={7: 0} if before else {},
        name="finish",
        cost_estimate=CHEAP,
        compiler_params=pltpu.CompilerParams(vmem_limit_bytes=SMALL_MIB << 20),
    )(end, total, got, x, gain, mid, mark, *before)


def text_weights_kernel(count, rows, roles, *rest):
    pieces, (own, key_grad, value_grad, held, sem) = rest[:count], rest[count:]
    copies = []
    for k in range(count):
        to = pl.ds(pl.multiple_of(roles[k] * rows, rows), rows)
        copies.append(pltpu.make_async_copy(pieces[k], held.at[to, :], sem.at[k]))
    for c in copies:
        c.start()
    for c in copies:
        c.wait()
    wide = key_grad.shape[1]
    key_grad[...] = lax.dot_general(own[...], held[:, :wide], COLS, preferred_element_type=f32)
    value_grad[...] = lax.dot_general(own[...], held[:, wide:], COLS, preferred_element_type=f32)


def text_weight_grads(pieces, roles, own):
    count = len(pieces)
    rows, width = pieces[0].shape
    vmem = pl.BlockSpec(memory_space=pltpu.VMEM)
    return pl.pallas_call(
        functools.partial(text_weights_kernel, count, rows),
        out_shape=[jax.ShapeDtypeStruct((own.shape[1], width // 2), f32)] * 2,
        in_specs=[pl.BlockSpec(memory_space=pltpu.SMEM)] + [pl.BlockSpec(memory_space=pl.ANY)] * count + [vmem],
        out_specs=[vmem] * 2,
        scratch_shapes=[pltpu.VMEM((count * rows, width), bf16), pltpu.SemaphoreType.DMA((count,))],
        compiler_params=pltpu.CompilerParams(vmem_limit_bytes=60 << 20),
        cost_estimate=CHEAP,
        name="text_weight_grads",
    )(roles, *pieces, own)


def touch_kernel(*refs):
    refs[-1][...] = refs[0][...]


def touch(value, arrays):
    return pl.pallas_call(
        touch_kernel,
        out_shape=jax.ShapeDtypeStruct(value.shape, value.dtype),
        in_specs=[pl.BlockSpec(memory_space=pltpu.VMEM)] * (1 + len(arrays)),
        cost_estimate=CHEAP,
        compiler_params=pltpu.CompilerParams(vmem_limit_bytes=SMALL_MIB << 20),
        name="touch",
    )(value, *arrays)


def gains_back_kernel(sums, mods, gains, gain_grad, mod_grad):
    for n in range(4):
        row = slice(n, n + 1)
        if n % 2 == 0:
            gain_grad[row, :] = sums[row, :] * (1.0 + mods[row, :])
            mod_grad[row, :] = sums[row, :] * gains[row, :]
        else:
            gate = jnp.tanh(mods[row, :])
            gain_grad[row, :] = sums[row, :] * gate
            mod_grad[row, :] = sums[row, :] * gains[row, :] * (1.0 - gate * gate)


def gains_back(sums, mods, gains):
    return pl.pallas_call(
        gains_back_kernel,
        out_shape=[jax.ShapeDtypeStruct(gains.shape, f32)] * 2,
        cost_estimate=CHEAP,
        name="gains_back",
    )(sums, mods, gains)


def vectors_kernel(mods, gains, out):
    out[0:1, :] = gains[0:1, :] * (1.0 + mods[0:1, :])
    out[1:2, :] = jnp.tanh(mods[1:2, :]) * gains[1:2, :]
    out[2:3, :] = gains[2:3, :] * (1.0 + mods[2:3, :])
    out[3:4, :] = jnp.tanh(mods[3:4, :]) * gains[3:4, :]


def vectors(mods, gains):
    return pl.pallas_call(
        vectors_kernel,
        out_shape=jax.ShapeDtypeStruct(gains.shape, f32),
        cost_estimate=CHEAP,
        name="vectors",
    )(mods, gains)


def per_device(
    seq_count,
    head_count,
    hidden_in,
    cond,
    captions,
    clip_lengths,
    ada_weight,
    norm_gains,
    qk_gains,
    w_query,
    w_key,
    w_value,
    w_out,
    cross_gate,
    w_text_key,
    w_text_value,
    w_gate,
    w_up,
    w_down,
    out_cotangent,
):
    local_rows, model_width = hidden_in.shape
    seq_index = lax.axis_index("seq")
    head_index = lax.axis_index("head")
    clips = clip_lengths.shape[0]
    cols = w_query.shape[1]
    heads = cols // HD
    wide = (cols + 127) // 128 * 128
    units = w_gate.shape[1]
    roles = seq_roles(seq_index, seq_count)
    pad = lambda v: jnp.pad(v, ((0, 0), (0, wide - cols))) if wide > cols else v
    cut = lambda v: v[:, :cols]

    spread = seq_count == 8
    core = lambda v: swap(v, "seq", 8, lambda i: i ^ 1)
    hold = lax.optimization_barrier
    axes = (("seq", seq_count), ("head", head_count))
    seq_hops, head_hops = hops("seq", seq_count), hops("head", head_count)
    finish_sum = lambda v: lax.psum_scatter(v, "seq", scatter_dimension=0, tiled=True)

    def hop(value, steps):
        for axis, bit in steps:
            value = value + swap(value, axis, dict(axes)[axis], lambda i: i ^ bit)
        return value

    clip_ends = jnp.cumsum(clip_lengths, dtype=jnp.int32)
    starts = clip_ends - clip_lengths
    text_rows = captions.reshape(-1, captions.shape[2])
    text_block = text_rows.shape[0] // seq_count
    text_ids = jnp.arange(clips, dtype=jnp.int32) * captions.shape[1]
    first_row = seq_index * local_rows
    place_info = jnp.concatenate([first_row[None], starts, clip_ends]).astype(jnp.int32)
    text_info = jnp.concatenate(
        [place_info, text_ids, text_ids + captions.shape[1], jnp.zeros((1,), jnp.int32)]
    )

    infos = {}

    def self_info(which):
        which = tuple(which)
        if which not in infos:
            infos[which] = jnp.concatenate([place_info, starts, clip_ends, roles[jnp.array(which)] * local_rows])
        return infos[which]

    places = first_row + jnp.arange(local_rows, dtype=jnp.int32)
    inside = (places[:, None] >= starts[None, :]) & (places[:, None] < clip_ends[None, :])
    position = places - jnp.sum(jnp.where(inside, starts[None, :], 0), axis=1, dtype=jnp.int32)
    lane = jnp.arange(128)
    frequency = 10000.0 ** (-(lane % (HD // 2)).astype(f32) / (HD // 2))
    angles = position.astype(f32)[:, None] * frequency[None, :]
    cos = jnp.cos(angles)
    sin = jnp.where(lane % HD < HD // 2, -1.0, 1.0)[None, :] * jnp.sin(angles)
    query_gain = jnp.tile(qk_gains[0], 2)[None, :]
    key_gain = jnp.tile(qk_gains[1], 2)[None, :]

    cond_act = jax.nn.silu(cond).astype(bf16)
    piece_width = ada_weight.shape[1]
    mod_piece = matmul(cond_act[None, :], ada_weight)
    mine = lax.broadcasted_iota(jnp.int32, (seq_count * head_count, 1), 0) == seq_index * head_count + head_index
    modulation = jnp.where(mine, mod_piece, 0.0)
    modulation, w_query = hold((modulation, w_query))
    qkv_block = jnp.concatenate([pad(w_query), pad(w_key), pad(w_value)], axis=1)
    out_block = pad(w_out.T)
    slab_width = text_rows.shape[1] // seq_count
    if spread:
        modulation = hop(modulation, seq_hops[:1])
        modulation, text_rows = hold((modulation, text_rows))
    own_text = lax.dynamic_slice_in_dim(text_rows, seq_index * slab_width, slab_width, 1)
    text_part = matmul(own_text, jnp.concatenate([pad(w_text_key), pad(w_text_value)], axis=1)).astype(bf16)

    def queries_keys(pieces):
        return project(roles, hidden_in, rows, query_gain, key_gain, cos, sin, pieces, wide)

    def part_sums(group, blocks, before=None):
        return attend(self_info(group), query_t, blocks, heads, clips, before)

    if spread:
        near = swap(qkv_block, "seq", 8, first_way)
        next_ = swap(qkv_block, "seq", 8, other_way)
        modulation = hop(modulation, head_hops[:1])
        text_pre = lax.psum(text_part, "seq")
        gate_w = lax.all_gather(w_gate, "seq", axis=0, tiled=True)
        near, next_, modulation = hold((near, next_, modulation))
        far = swap(near, "seq", 8, other_way)
        modulation = hop(modulation, head_hops[1:])
        modulation = hop(modulation, seq_hops[1:])
        qkv_pieces = [qkv_block, near, next_, far]
        qkv_pieces = qkv_pieces + [core(v) for v in qkv_pieces]
        modulation, qkv_pieces, out_block = hold((modulation, qkv_pieces, out_block))
        modulation = modulation.reshape(4, model_width)
        rows = vectors(modulation, norm_gains)
        act_a, x_scale, pre, kv_own, queries, query_t, w_qkv = queries_keys(qkv_pieces)
        kv_own, modulation, out_block = hold((kv_own, modulation, out_block))
        near = swap(kv_own, "seq", 8, first_way)
        next_ = swap(kv_own, "seq", 8, other_way)
        kv_peer = core(kv_own)
        out_near = swap(out_block, "seq", 8, first_way)
        out_next = swap(out_block, "seq", 8, other_way)
        sums = part_sums((0, 4), [kv_own, kv_peer])
        for group in ((1, 2, 5, 6), (3, 7), (3, 2, 7, 6), (1, 5)):
            self_info(group)
        chip = seq_index // 2
        near_chip = jnp.where(seq_index % 2 == 0, chip ^ 1, chip ^ 2)
        next_chip = jnp.where(seq_index % 2 == 0, chip ^ 2, chip ^ 1)
        wheres = [[1 - seq_index % 2], [seq_index % 2, chip ^ 3, next_chip], [chip, near_chip]]
        wheres = [jnp.stack(where).astype(jnp.int32) for where in wheres]
        ready = (near, next_, sums, out_near, out_next, infos, text_info, wheres)
        near, next_, sums, out_near, out_next, infos_held, text_info, wheres = hold(ready)
        infos.update(infos_held)
        far = swap(near, "seq", 8, other_way)
        out_far = swap(out_near, "seq", 8, other_way)
        near_peer, next_peer = core(near), core(next_)
        out_peers = [core(out_block), core(out_near), core(out_next)]
        sums = part_sums((1, 2, 5, 6), [near, next_, near_peer, next_peer], sums)
        ud_block = jnp.concatenate([w_up, w_down.T], axis=1)
        far, sums, out_far, text_pre, ud_block = hold((far, sums, out_far, text_pre, ud_block))
        far_peer = core(far)
        ud_near = swap(ud_block, "seq", 8, first_way)
        ud_next = swap(ud_block, "seq", 8, other_way)
        out_t = place([out_block, out_near, out_next, out_far] + out_peers + [core(out_far)], roles)
        text_pieces = [text_norm(text_pre, key_gain)]
        cross_sums = attend(text_info, query_t, text_pieces, heads, clips)
        sums = part_sums((3, 7), [far, far_peer], sums)
        pieces = [kv_own, near, next_, far, kv_peer, near_peer, next_peer, far_peer]
    else:
        modulation = lax.psum(modulation, ("seq", "head"))
        text_pre = lax.psum(text_part, "seq")
        qkv_pieces = gather_pieces(qkv_block, seq_count)
        modulation = modulation.reshape(4, model_width)
        rows = vectors(modulation, norm_gains)
        act_a, x_scale, pre, kv_own, queries, query_t, w_qkv = queries_keys(qkv_pieces)
        pieces = gather_pieces(kv_own, seq_count)
        text_pieces = [text_norm(text_pre, key_gain)]
        out_t = place(gather_pieces(out_block, seq_count), roles)
        sums = part_sums(tuple(range(seq_count)), pieces)
        cross_sums = attend(text_info, query_t, text_pieces, heads, clips)
        gate_w = lax.all_gather(w_gate, "seq", axis=0, tiled=True)
    gate_local = jnp.tanh(cross_gate)
    mixed, self_t, cross_t, self_lse, cross_lse = mix(gate_local, sums, cross_sums, wide)
    attn_part = matmul(mixed, out_t, ROWS).astype(bf16)

    late = {}

    def split_weights(pieces):
        return place(pieces, roles, (units, units), 40)

    def fill_near(carry):
        return [ud_near, ud_next]

    def fill_far(carry):
        near, next_ = carry
        return [near, next_, swap(near, "seq", 8, other_way), core(ud_block), core(near), core(next_)]

    def fill_weights(carry):
        late["up"], late["down"] = split_weights([ud_block] + carry + [core(carry[2])])
        late["rows"] = touch(rows, [gate_w, late["up"], late["down"]])
        return [late["rows"]]

    if not spread:
        weights = gather_pieces(jnp.concatenate([w_up, w_down.T], axis=1), seq_count)
        late["up"], late["down"] = split_weights(weights)
        late["rows"] = rows
    chunk_count = 4
    chunk = local_rows // chunk_count
    rows_of = lambda v, k: v[k * chunk : (k + 1) * chunk]
    kept = [{} for _ in range(chunk_count)]


    tall, thin = (chunk, model_width), (chunk, units)
    whole = lambda width: (local_rows, chunk, width, bf16)

    def feed_forward(k, end, total, got, before):
        keep = kept[k]
        outs = [((chunk, 2 * model_width), f32), ((chunk, 128), f32), ((chunk, 2 * units), f32), (tall, bf16)]
        arrays = [total, got, rows_of(hidden_in, k), late["rows"], gate_w, late["up"], late["down"]]
        keep["norms"], keep["stats"], keep["pre"], part, late["first"] = staged(
            forward_kernel, k, outs, [whole(units + model_width)], [end], arrays,
            [late["first"]] if k else None, "feed_forward",
        )
        return part

    def feed_back(k, end, total, got, before):
        keep = kept[k]
        arrays = [total, got, keep["norms"], keep["pre"], rows_of(out_cotangent, k), late["rows"]]
        keep["uf"], part, late["second"], late["hidden"] = staged(
            backward_kernel, k, [((1, model_width), f32), (tall, bf16)],
            [whole(2 * units + model_width), whole(model_width)], [end], arrays + [gate_w, late["up"], late["down"]],
            [late["second"], late["hidden"]] if k else None, "feed_back",
        )
        return part

    def attn_back(k, end, total, got, before):
        keep = kept[k]
        arrays = [total, got, keep["norms"], keep["stats"], rows_of(out_cotangent, k), rows]
        keep["sums"], keep["dmid"], late["dattn"] = staged(
            attn_back_kernel, k, [((2, model_width), f32), (tall, f32)], [whole(model_width)], [end], arrays,
            [late["dattn"]] if k else None, "attn_back", 60,
        )
        return keep["sums"]

    total_of = lambda name, n: sum(keep[name][n] for keep in kept)

    def fill_down(carry):
        return [weight_grad(late["second"], 2 * units, model_width, late["first"], 0, units)]

    def fill_gate(carry):
        late["down_sum"] = finish_sum(carry[0])
        (first, second), carry = hold(((late["first"], late["second"]), carry))
        late["first"], late["second"] = first, second
        return [weight_grad(first, units, model_width, second, 0, units)]

    def fill_up(carry):
        late["gate_sum"] = finish_sum(carry[0])
        (first, second), carry = hold(((late["first"], late["second"]), carry))
        return [weight_grad(first, units, model_width, second, 1, units)]

    def fill_last(carry):
        late["up_sum"] = finish_sum(carry[0])
        return []

    fills = {8 + chunk_count - 1: fill_down, 8 + chunk_count: fill_gate, 8 + chunk_count + 1: fill_up, 8 + chunk_count + 2: fill_last}
    first_parts = [rows_of(attn_part, k) for k in range(chunk_count)]
    if spread:
        fills.update({0: fill_near, 1: fill_far, 2: fill_weights})
    run_ticks(
        first_parts, [feed_forward, feed_back, attn_back], head_index, head_count, fills
    )
    grad_attn_low, hidden_out = late["dattn"], late["hidden"]
    down_grad, gate_grad, up_grad = late["down_sum"], late["gate_sum"], late["up_sum"]

    grad_self_tok, grad_self_t, grad_cross_tok, grad_cross_t, self_delta, cross_delta, gate_rows = unmix(
        gate_local, grad_attn_low, out_t, self_t, cross_t
    )
    cross_gate_part = jnp.sum(gate_rows, axis=1) * (1.0 - gate_local * gate_local)

    def back(group, parts, before=None):
        return attend_back(
            self_info(group), query_t, grad_self_t, queries, grad_self_tok, self_lse, self_delta,
            [pieces[g] for g in group], heads, clips, bf16, parts, before,
        )

    def cross_back(before):
        return attend_back(
            text_info, query_t, grad_cross_t, queries, grad_cross_tok, cross_lse, cross_delta,
            text_pieces, heads, clips, f32, 1, before,
        )

    if spread:
        dq, _, kv_mine, kv_theirs = back((3, 2, 7, 6), 2)
        kv_got = core(kv_theirs)
        kv_mine, low = hold((kv_mine, grad_attn_low))
        out_part = matmul(low, mixed, COLS).astype(bf16)
        total = [add_low(kv_mine[:local_rows], kv_got[:local_rows]), add_low(kv_mine[local_rows:], kv_got[local_rows:])]
        total, dq, out_part = hold((total, dq, out_part))
        first = swap(total[0], "seq", 8, other_way)
        dq, text_dot, cross_kv = cross_back(dq)
        dq, cross_kv, down_grad, total = hold((dq, cross_kv, down_grad, total))
        own_first = swap(total[1], "seq", 8, other_way)
        dq, _, kv_mine, kv_theirs = back((1, 5), 2, dq)
        first, kv_mine, kv_theirs = hold((first, kv_mine, kv_theirs))
        total = kv_mine.astype(f32) + core(kv_theirs).astype(f32) + first.astype(f32)
        total = total.astype(bf16)
        second = swap(total, "seq", 8, first_way)
        dq, _, kv_mine, kv_theirs = back((0, 4), 2, dq)
        text_low = text_back(text_pre, key_gain, cross_kv)
        ready = (second, kv_mine, kv_theirs, gate_grad, own_first, text_low)
        second, kv_mine, kv_theirs, gate_grad, own_first, text_low = hold(ready)
        kv_parts, kv_starts = [kv_mine, core(kv_theirs), own_first, second], (0, 0, 0, 0)
    else:
        dq, _, kv_all = back(tuple(range(seq_count)), 1)
        dq, text_dot, cross_kv = cross_back(dq)
        text_low = text_back(text_pre, key_gain, cross_kv)
        out_part = weight_grad(grad_attn_low, 0, model_width, mixed, 0, wide)
        kv_parts, kv_starts = [finish_sum(kv_all)], (0,)
    qkv_low, grad_query_gain, grad_key_gain, sum_a, *act_low = project_back(
        pre, query_gain, key_gain, cos, sin, dq, hidden_in, x_scale, w_qkv, kv_parts, kv_starts
    )
    act_low, qkv_low, gate_grad, out_part = hold((act_low, qkv_low, gate_grad, out_part))
    fold = lambda v: v[0, :HD] + v[0, HD:]
    pair_gains = jnp.concatenate([fold(grad_query_gain), fold(grad_key_gain + text_dot / key_gain)])
    tail = jnp.stack([sum_a[0], jnp.pad(pair_gains, (0, model_width - 2 * HD))])
    tail = jnp.pad(tail, ((0, 14), (0, 0))).astype(bf16)
    small = [total_of("sums", 1), total_of("sums", 0), total_of("uf", 0)]
    cross_row = jnp.pad(cross_gate_part, (2 * HD, model_width - 2 * HD - heads))

    def collect(k, end, total, got, before):
        if k == 1:
            late["tail"] = jnp.where(end[0] == 1, got, total)[chunk:].astype(f32)
        arrays = rows_of(hidden_in, k), rows, kept[k]["dmid"]
        mark = jnp.zeros((8, 128), f32) if before is None else before
        late["input"], mark = finish(k, end, total, got, *arrays, mark, local_rows, late.get("input"))
        return mark


    def fill0(carry):
        out = scatter_start(out_part, wheres[0]) if spread else out_part
        return [text_low, weight_grad(act_a, 0, model_width, qkv_low, 0, 3 * wide), out]

    def fill1(carry):
        late["qkv"] = finish_sum(carry[1])
        late["out"] = scatter_first(carry[2], wheres[1]) if spread else carry[2]
        gate, down, text = hold((gate_grad, down_grad, carry[0]))
        late["gate"], late["down"] = widen([gate]), widen([down]).T
        if not spread:
            return [lax.psum(text, "seq"), late["gate"], late["down"]]
        return [scatter_first(scatter_start(text, wheres[0]), wheres[1]), late["gate"], late["down"]]

    def fill2(carry):
        text, late["gate"], late["down"] = carry
        up, text = hold((up_grad, text))
        late["up"] = widen([up])
        if not spread:
            return [text, late["up"]]
        own = add_low(*scatter_second(text, wheres[2]))
        return [[own, swap(own, "seq", 8, first_way), swap(own, "seq", 8, other_way)], late["up"]]

    def fill3(carry):
        text, late["up"] = carry
        if not spread:
            return [text]
        text = text + [swap(text[1], "seq", 8, other_way)]
        out, text = hold((late["out"], text))
        late["out"] = scatter_second(out, wheres[2])
        return [text + [core(v) for v in text[:3]]]

    def fill4(carry):
        (text,) = carry
        tail_rows = [late["tail"][0]] + small + [jnp.pad(late["tail"][1, : 2 * HD], (0, model_width - 2 * HD)) + cross_row]
        values = jnp.pad(jnp.stack(tail_rows), ((0, 3), (0, 0)))
        out, text = hold((late["out"], text))
        late["out"] = widen(list(out)).T if spread else finish_sum(out).astype(f32).T
        if not spread:
            return [lax.psum(values, "seq"), text, late["out"]]
        return [hop(values, seq_hops[:2]), text + [core(text[3])], late["out"]]

    def fill5(carry):
        values, text, late["out"] = carry
        values = hop(values, seq_hops[2:]) if spread else values
        gain_grad, mod_grad = gains_back(values[:4], modulation, norm_gains)
        own_mod = lax.dynamic_slice_in_dim(
            mod_grad.reshape(-1), (seq_index * head_count + head_index) * piece_width, piece_width
        )
        text_grads = text_weight_grads(text if spread else [text], roles if spread else jnp.zeros((1,), jnp.int32), own_text)
        return [gain_grad, values[4], text_grads, cond_act.astype(f32)[:, None] * own_mod[None, :]]

    parts = list(act_low)
    parts[1] = jnp.concatenate([parts[1], tail])
    fills = dict(enumerate([fill0, fill1, fill2, fill3, fill4, fill5]))
    _, (norm_gains_grad, values, text_grad, ada_grad) = run_ticks(parts, [collect], head_index, head_count, fills)
    input_grad = late["input"]
    own_qkv = widen([late["qkv"]])

    qk_gains_grad = values[: 2 * HD].reshape(2, HD)
    cross_gate_grad = values[2 * HD : 2 * HD + heads]
    return (
        hidden_out,
        input_grad,
        ada_grad,
        norm_gains_grad,
        qk_gains_grad,
        cut(own_qkv[:, :wide]),
        cut(own_qkv[:, wide : 2 * wide]),
        cut(own_qkv[:, 2 * wide : 3 * wide]),
        late["out"][:cols],
        cross_gate_grad,
        cut(text_grad[0]),
        cut(text_grad[1]),
        late["gate"],
        late["up"],
        late["down"],
    )


def solution(mesh):
    in_specs = (
        P("seq", None),
        P(),
        P(),
        P(),
        P(None, ("seq", "head")),
        P(),
        P(),
        P("seq", "head"),
        P("seq", "head"),
        P("seq", "head"),
        P("head", "seq"),
        P("head"),
        P("seq", "head"),
        P("seq", "head"),
        P("seq", "head"),
        P("seq", "head"),
        P("head", "seq"),
        P("seq", None),
    )
    out_specs = (
        P("seq", None),
        P("seq", None),
        P(None, ("seq", "head")),
        P(),
        P(),
        P("seq", "head"),
        P("seq", "head"),
        P("seq", "head"),
        P("head", "seq"),
        P("head"),
        P("seq", "head"),
        P("seq", "head"),
        P("seq", "head"),
        P("seq", "head"),
        P("head", "seq"),
    )
    body = functools.partial(per_device, mesh.shape["seq"], mesh.shape["head"])
    return jax.shard_map(body, mesh=mesh, in_specs=in_specs, out_specs=out_specs, check_vma=False)
```
